256 devices in a mesh: item: 64 (over z, y, x_lo), user: 4 (over x_hi, core).
Axes of the slice: x: 4 (x_hi: 2, x_lo: 2; x = x_hi * 2 + x_lo), y: 4, z: 8, core: 2. Of those that a mesh axis runs over, the one named last changes fastest.
Arguments:
- query_a: bfloat16 [4096, 256], P(('item', 'user')), may hold values from -8 to 8
- query_b: bfloat16 [4096, 256], P(('item', 'user')), may hold values from -8 to 8
- items: bfloat16 [131072, 256], P('item'), may hold values from -1 to 1
- positive_a: int32 [4096], replicated, may hold values from 0 to 131071
- positive_b: int32 [4096], replicated, may hold values from 0 to 131071
- loss_cotangent: float32 [4096], replicated, may hold values from -4 to 4
Outputs:
- loss_a: float32 [4096], P(('item', 'user'))
- grad_query_b: float32 [4096, 256], P(('item', 'user'))
- grad_items: float32 [131072, 256], P(('item', 'user'))
The draws below stay inside these ranges and needn't reach their ends.
All inputs are finite; a program needn't handle non-finite values.
Results may differ from the reference program's by a relative error of at most 0.003.
Values may be sent and summed in bfloat16 or wider, within the bound.
A program may use at most 64 MiB of HBM per device.

```python
import math
import jax
import jax.numpy as jnp
from jax import lax

E = 256
ITEM_DEV = 2048
ITEMS = 131072
USERS = 4096


def shared_parts(key):
    key_sign, key_dir = jax.random.split(key)
    signs = (jax.random.randint(key_sign, (E,), 0, 2) * 2 - 1).astype(jnp.float32)
    directions = (jax.random.randint(key_dir, (16, E), 0, 2) * 2 - 1).astype(jnp.float32)
    return (signs, directions)


def draw_items(key, part):
    signs, directions = shared_parts(key)
    key = jax.random.fold_in(key, 11)
    key_scale, key_value, key_pick = jax.random.split(key, 3)
    index = jnp.arange(ITEMS, dtype=jnp.int32)
    region = index * 16 // ITEMS
    cluster = (region + jax.random.randint(key_pick, (ITEMS,), 0, 3)) % 16
    member = jnp.take(directions, cluster, axis=0)
    ramp = jnp.exp(math.log(0.5) + math.log(4.0) * index.astype(jnp.float32) / (ITEMS - 1))[:, None]
    scale = ramp * jnp.exp(jax.random.uniform(key_scale, (ITEMS, 1), jnp.float32, math.log(0.7), math.log(1.4)))
    base = jax.random.normal(key_value, (ITEMS, E), jnp.float32)
    table = jnp.clip(0.125 * scale * base + 0.0625 * member, -1.0, 1.0)
    table = table.at[ITEMS - 1].set(signs).at[ITEMS - 2].set(0.99 * signs).at[ITEMS // 2 - 1].set(0.97 * signs)
    return table.astype(jnp.bfloat16)


def query_rows(key, directions):
    key_scale, key_value, key_pick, key_amp = jax.random.split(key, 4)
    scale = jnp.exp(jax.random.uniform(key_scale, (USERS, 1), jnp.float32, 0.0, math.log(10.0)))
    cluster = jax.random.randint(key_pick, (USERS,), 0, 16)
    amount = jax.random.uniform(key_amp, (USERS, 1), jnp.float32, 0.15, 0.35)
    base = jax.random.normal(key_value, (USERS, E), jnp.float32)
    return jnp.clip(0.1 * scale * base + amount * jnp.take(directions, cluster, axis=0), -8.0, 8.0)


def draw_query_a(key, part):
    signs, directions = shared_parts(key)
    key = jax.random.fold_in(key, 23)
    rows = query_rows(key, directions)
    strong = 230.0 / E * signs
    rows = rows.at[0].set(strong).at[USERS // 2].set(0.9 * strong).at[USERS - 1].set(0.8 * strong)
    return rows.astype(jnp.bfloat16)


def draw_query_b(key, part):
    signs, directions = shared_parts(key)
    key = jax.random.fold_in(key, 37)
    rows = query_rows(key, directions)
    strong = 230.0 / E * signs
    rows = rows.at[1].set(0.85 * strong).at[USERS // 3].set(strong).at[USERS - 2].set(0.95 * strong)
    return rows.astype(jnp.bfloat16)


def place_ends(result, rng, smallest, largest):
    dims = result.shape
    spot = [jax.random.randint(jax.random.fold_in(rng, axis), (), 0, dims[axis]) for axis in range(len(dims))]
    result = result.at[tuple(spot)].set(smallest)
    longest = dims.index(max(dims))
    spot[longest] = (spot[longest] + 1) % dims[longest]
    return result.at[tuple(spot)].set(largest)


def scatter_about(own_key, extent, scale, reach, kind=jnp.bfloat16):
    return jnp.clip(scale * jax.random.normal(own_key, extent, jnp.float32), -reach, reach).astype(kind)


def setup_inputs(seed: int = 0) -> dict:
    key_list = jax.random.split(jax.random.key(seed), 7)
    query_a = draw_query_a(jax.random.fold_in(key_list[6], 71), 0)
    query_b = draw_query_b(jax.random.fold_in(key_list[6], 71), 0)
    items = draw_items(jax.random.fold_in(key_list[6], 71), 0)
    positive_a = place_ends(jax.random.randint(key_list[3], (USERS,), 0, ITEMS), jax.random.fold_in(key_list[3], 1), 0, ITEMS - 1).astype(jnp.int32)
    positive_b = place_ends(jax.random.randint(key_list[4], (USERS,), 0, ITEMS), jax.random.fold_in(key_list[4], 1), 0, ITEMS - 1).astype(jnp.int32)
    loss_cotangent = scatter_about(key_list[5], (USERS,), 1.0, 4.0, jnp.float32)
    return {"query_a": query_a, "query_b": query_b, "items": items, "positive_a": positive_a, "positive_b": positive_b, "loss_cotangent": loss_cotangent}


def block_scores(queries, block):
    return lax.dot_general(queries, block, (((1,), (1,)), ((), ())), preferred_element_type=jnp.float32)


def reference(query_a, query_b, items, positive_a, positive_b, loss_cotangent):
    count = ITEMS // ITEM_DEV
    blocks = items.reshape(count, ITEM_DEV, items.shape[1])
    starts = jnp.arange(count, dtype=jnp.int32) * ITEM_DEV
    columns = jnp.arange(ITEM_DEV, dtype=jnp.int32)

    def update(queries, ids, state, block, start):
        top, total, hit = state
        score = block_scores(queries, block)
        new_top = jnp.maximum(top, jnp.max(score, axis=1))
        total = total * jnp.exp(top - new_top) + jnp.sum(jnp.exp(score - new_top[:, None]), axis=1)
        match = ids[:, None] == (columns + start)[None, :]
        hit = hit + jnp.sum(jnp.where(match, score, 0.0), axis=1)
        return (new_top, total, hit)

    def first_pass(carry, inputs):
        block, start = inputs
        state_a, state_b = carry
        return (update(query_a, positive_a, state_a, block, start), update(query_b, positive_b, state_b, block, start)), None

    empty = (jnp.full((USERS,), -jnp.inf, jnp.float32), jnp.zeros((USERS,), jnp.float32), jnp.zeros((USERS,), jnp.float32))
    (state_a, state_b), unused = lax.scan(first_pass, (empty, empty), (blocks, starts))
    loss_a = state_a[0] + jnp.log(state_a[1]) - state_a[2]
    lse_b = state_b[0] + jnp.log(state_b[1])

    def second_pass(grad_query, inputs):
        block, start = inputs
        score = block_scores(query_b, block)
        match = (positive_b[:, None] == (columns + start)[None, :]).astype(jnp.float32)
        dscore = (loss_cotangent[:, None] * (jnp.exp(score - lse_b[:, None]) - match)).astype(jnp.bfloat16)
        grad_query = grad_query + jnp.dot(dscore, block, preferred_element_type=jnp.float32)
        grad_block = lax.dot_general(dscore, query_b, (((0,), (0,)), ((), ())), preferred_element_type=jnp.float32)
        return grad_query, grad_block

    grad_query_b, grad_blocks = lax.scan(second_pass, jnp.zeros((USERS, items.shape[1]), jnp.float32), (blocks, starts))
    return loss_a, grad_query_b, grad_blocks.reshape(ITEMS, items.shape[1])
```

```python
import functools

import jax
import jax.numpy as jnp
from jax import lax
from jax.experimental import pallas as pl
from jax.experimental.pallas import tpu as pltpu
from jax.sharding import PartitionSpec as P

MESH = pl.DeviceIdType.MESH
F32 = jnp.float32
BF16 = jnp.bfloat16
HIGHEST = lax.Precision.HIGHEST

NZ, NY, NX = 8, 4, 2
OWN = 16
E = 256
GROUP = NZ * NY * NX * OWN
CHUNK = 256
QUARTER = 512


def remote(src, dst, send_sem, recv_sem, device):
    return pltpu.make_async_remote_copy(
        src_ref=src,
        dst_ref=dst,
        send_sem=send_sem,
        recv_sem=recv_sem,
        device_id=device,
        device_id_type=MESH,
    )


def group_row(table, selector, row_of):
    picked = jnp.dot(table, selector, precision=HIGHEST, preferred_element_type=F32)
    rows = lax.broadcasted_iota(jnp.int32, picked.shape, 0)
    return jnp.sum(jnp.where(rows == row_of, picked, 0.0), axis=0, keepdims=True)


def lse_of(parts):
    top = jnp.max(parts, axis=0)
    return top + jnp.log(jnp.sum(jnp.exp(parts - top[None]), axis=0))


def kernel(
    qa_in, qb_in, items_in, pa_in, pb_in, w_in,
    loss_out, gq_out, gi_out,
    items_v, items_t, qa, qb, probs, acc_t, gq_f, gq_s,
    rx0, ry0, ry1, rx1, rz, h_s, k_s,
    gi_s, gi_core, gi_far,
    zb, yb, za, ya,
    tops,
    items_sem, g_zs, g_zr, g_ys, g_yr, g_fs, g_fr, g_xs, g_xr,
    b_zs, b_zr, b_ys, b_yr, a_zs, a_zr, a_ys, a_yr,
    s1s, s1r, s2s, s2r, s3s, s3r, gi_ss, gi_rs,
):
    item = lax.axis_index("item")
    user = lax.axis_index("user")
    z, y, x = item // (NY * NX), (item // NX) % NY, item % NX
    far, core = user // 2, user % 2
    items_rows = items_v.shape[0]
    offset = item * items_rows

    def at(zz, yy, xx):
        return {"item": (zz * NY + yy) * NX + xx}

    def z_peer(k):
        return lax.rem(z + k, NZ)

    def y_peer(k):
        return lax.rem(y + k, NY)

    def plane_peer(k):
        return lax.rem(y * NX + x + k, NY * NX)

    load = pltpu.make_async_copy(items_in, items_v, items_sem)
    load.start()

    barrier = pltpu.get_barrier_semaphore()

    @pl.loop(1, NZ)
    def _(k):
        pl.semaphore_signal(barrier, inc=1, device_id=at(z_peer(k), y, x), device_id_type=MESH)

    @pl.loop(1, NY * NX)
    def _(k):
        p = plane_peer(k)
        pl.semaphore_signal(barrier, inc=1, device_id=at(z, p // NX, p % NX), device_id_type=MESH)

    other_core = {"user": far * 2 + 1 - core}
    other_far = {"user": (1 - far) * 2 + core}
    pl.semaphore_signal(barrier, inc=1, device_id=other_core, device_id_type=MESH)
    pl.semaphore_signal(barrier, inc=1, device_id=other_far, device_id_type=MESH)

    qb[x, y, z] = qb_in[...]
    qa[x, y, z] = qa_in[...]

    pl.semaphore_wait(barrier, (NZ - 1) + (NY * NX - 1) + 2)

    def gather_z_start(n, q):
        @pl.loop(1, NZ)
        def _(k):
            block = q.at[x, y, z]
            remote(block, block, g_zs.at[n, k], g_zr.at[n, z], at(z_peer(k), y, x)).start()

    def gather_z_wait(n, q):
        @pl.loop(1, NZ)
        def _(k):
            zz = z_peer(k)
            block = q.at[x, y, zz]
            remote(block, block, g_zs.at[n, k], g_zr.at[n, zz], at(zz, y, x)).wait_recv()

    def x_copy(n, q, xx, yy):
        block = q.at[xx, yy]
        return remote(block, block, g_xs.at[n, yy], g_xr.at[n, yy], at(z, y, 1 - x))

    def y_copy(n, q, k, src_y):
        block = q.at[x, src_y]
        return remote(block, block, g_ys.at[n, k], g_yr.at[n, src_y], at(z, y_peer(k), x))

    def f_copy(n, q, k, src_y):
        block = q.at[1 - x, src_y]
        return remote(block, block, g_fs.at[n, k], g_fr.at[n, src_y], at(z, y_peer(k), x))

    def gather_plane_start(n, q):
        x_copy(n, q, x, y).start()

        @pl.loop(1, NY)
        def _(k):
            y_copy(n, q, k, y).start()

    def gather_forward(n, q):
        @pl.when(core == 0)
        def _():
            @pl.loop(1, NY)
            def _(k):
                yy = y_peer(k)
                y_copy(n, q, k, yy).wait_recv()
                x_copy(n, q, x, yy).start()

        @pl.when(core == 1)
        def _():
            x_copy(n, q, 1 - x, y).wait_recv()

            @pl.loop(1, NY)
            def _(k):
                f_copy(n, q, k, y).start()

    def gather_finish(n, q):
        @pl.when(core == 0)
        def _():
            @pl.loop(0, NY)
            def _(yy):
                x_copy(n, q, 1 - x, yy).wait_recv()

        @pl.when(core == 1)
        def _():
            @pl.loop(1, NY)
            def _(k):
                yy = y_peer(k)
                y_copy(n, q, k, yy).wait_recv()
                f_copy(n, q, k, yy).wait_recv()

    def gather_drain(n, q):
        @pl.loop(1, NZ)
        def _(k):
            block = q.at[x, y, z]
            remote(block, block, g_zs.at[n, k], g_zr.at[n, z], at(z_peer(k), y, x)).wait_send()

        x_copy(n, q, x, y).wait_send()

        @pl.loop(1, NY)
        def _(k):
            y_copy(n, q, k, y).wait_send()

            @pl.when(core == 0)
            def _():
                x_copy(n, q, x, y_peer(k)).wait_send()

            @pl.when(core == 1)
            def _():
                f_copy(n, q, k, y).wait_send()

    gather_z_start(0, qb)
    gather_z_start(1, qa)

    lanes = lax.broadcasted_iota(jnp.int32, (1, GROUP), 1)
    own_of = lanes % OWN
    z_of = (lanes // OWN) % NZ
    y_of = (lanes // (OWN * NZ)) % NY
    x_of = lanes // (OWN * NZ * NY)
    ks = lax.broadcasted_iota(jnp.int32, (128, GROUP), 0)
    selector = (ks == x_of * (4 * OWN) + user * OWN + own_of).astype(F32)
    row_of = z_of * NY + y_of
    pos_a = group_row(pa_in[...].astype(F32), selector, row_of).astype(jnp.int32) - offset
    pos_b = group_row(pb_in[...].astype(F32), selector, row_of).astype(jnp.int32) - offset
    weight = group_row(w_in[...], selector, row_of)

    gather_z_wait(0, qb)
    gather_plane_start(0, qb)

    load.wait()
    for part in range(items_rows // QUARTER):
        rows = pl.ds(part * QUARTER, QUARTER)
        items_t[:, rows] = items_v[rows, :].T

    gather_forward(0, qb)
    gather_z_wait(1, qa)
    gather_plane_start(1, qa)
    gather_finish(0, qb)

    def scores(q, c):
        rows = q[c // 2, (c % 2) * 2 : (c % 2) * 2 + 2].reshape(CHUNK, E)
        return lax.dot_general(
            items_v[...], rows, (((1,), (1,)), ((), ())), preferred_element_type=F32
        )

    for c in range(GROUP // CHUNK):
        cols = slice(c * CHUNK, (c + 1) * CHUNK)
        score = scores(qb, c)
        top = jnp.max(score, axis=0, keepdims=True)
        p = jnp.exp(score - top)
        probs[:, cols] = p
        tops[:, cols] = top
        zb[z, :, cols] = top + jnp.log(jnp.sum(p, axis=0, keepdims=True))

    def round_copy(buf, k, ss, rs, src, device):
        return remote(buf.at[src], buf.at[src], ss.at[k], rs.at[src], device)

    def z_round(buf, ss, rs, verb):
        @pl.loop(1, NZ)
        def _(k):
            zz = z_peer(k)
            if verb == "recv":
                round_copy(buf, k, ss, rs, zz, at(zz, y, x)).wait_recv()
            elif verb == "send":
                round_copy(buf, k, ss, rs, z, at(zz, y, x)).wait_send()
            else:
                round_copy(buf, k, ss, rs, z, at(zz, y, x)).start()

    def plane_round(buf, ss, rs, verb):
        @pl.loop(1, NY * NX)
        def _(k):
            p = plane_peer(k)
            device = at(z, p // NX, p % NX)
            if verb == "recv":
                round_copy(buf, k, ss, rs, p, device).wait_recv()
            elif verb == "send":
                round_copy(buf, k, ss, rs, y * NX + x, device).wait_send()
            else:
                round_copy(buf, k, ss, rs, y * NX + x, device).start()

    z_round(zb, b_zs, b_zr, "start")
    gather_forward(1, qa)
    z_round(zb, b_zs, b_zr, "recv")
    yb[y * NX + x] = lse_of(zb[...])
    plane_round(yb, b_ys, b_yr, "start")
    gather_finish(1, qa)

    for c in range(GROUP // CHUNK):
        cols = slice(c * CHUNK, (c + 1) * CHUNK)
        score = scores(qa, c)
        top = jnp.max(score, axis=0, keepdims=True)
        total = jnp.sum(jnp.exp(score - top), axis=0, keepdims=True)
        ids = lax.broadcasted_iota(jnp.int32, score.shape, 0)
        hit = jnp.sum(jnp.where(ids == pos_a[:, cols], score, 0.0), axis=0, keepdims=True)
        za[z, 0:1, cols] = top + jnp.log(total)
        za[z, 1:2, cols] = hit
    z_round(za, a_zs, a_zr, "start")

    plane_round(yb, b_ys, b_yr, "recv")
    lse_b = lse_of(yb[...])
    factor = weight * jnp.exp(tops[...] - lse_b)

    def far_copy():
        return remote(gi_s.at[1], gi_far, gi_ss.at[1], gi_rs.at[1], other_far)

    def core_copy(n):
        return remote(gi_s.at[2 * n], gi_core.at[n], gi_ss.at[2 * n], gi_rs.at[2 * n], other_core)

    quarters = (
        (1 - far) * 2 + 1 - core,
        (1 - far) * 2 + core,
        far * 2 + 1 - core,
        far * 2 + core,
    )
    for step, quarter in enumerate(quarters):
        start = pl.multiple_of(quarter * QUARTER, QUARTER)
        rows = pl.ds(start, QUARTER)
        ids = lax.broadcasted_iota(jnp.int32, (QUARTER, GROUP), 0)
        dscore = probs[rows, :] * factor - jnp.where(ids == pos_b - start, weight, 0.0)
        dscore = dscore.astype(BF16)
        part = jnp.dot(dscore, qb[...].reshape(GROUP, E), preferred_element_type=F32)
        if step == 0:
            gi_s[0] = part.astype(BF16)
            core_copy(0).start()
        elif step == 1:
            core_copy(0).wait_recv()
            gi_s[1] = (part + gi_core[0].astype(F32)).astype(BF16)
            far_copy().start()
        elif step == 2:
            gi_s[2] = part.astype(BF16)
            core_copy(1).start()
        else:
            gi_out[...] = part
        part_t = jnp.dot(items_t[:, rows], dscore, preferred_element_type=F32)
        if step == 0:
            acc_t[...] = part_t
        else:
            acc_t[...] += part_t

    for xx in range(NX):
        for yy in range(NY):
            j = (xx * NY + yy) * NZ * OWN
            block = acc_t[:, j : j + NZ * OWN].T.reshape(NZ, OWN, E)
            gq_f[xx, yy] = block
            gq_s[xx, yy] = block.astype(BF16)

    def sx0(yy):
        return remote(gq_s.at[1 - x, yy], rx0.at[yy], s1s.at[yy], s1r.at[yy], at(z, y, 1 - x))

    def sy0(k, yy, src):
        return remote(h_s.at[yy], ry0.at[src], s2s.at[yy], s2r.at[src], at(z, y_peer(k), x))

    def sy1(k, yy, src):
        return remote(gq_s.at[:, yy], ry1.at[src], s1s.at[yy], s1r.at[src], at(z, y_peer(k), x))

    def sx1():
        return remote(h_s.at[0], rx1, s2s.at[0], s2r.at[0], at(z, y, 1 - x))

    def sz(zz, src):
        return remote(k_s.at[zz], rz.at[src], s3s.at[zz], s3r.at[src], at(zz, y, x))

    @pl.when(core == 0)
    def _():
        @pl.loop(1, NY + 1)
        def _(k):
            sx0(y_peer(k)).start()

        @pl.loop(1, NY)
        def _(k):
            yy = y_peer(k)
            sx0(yy).wait_recv()
            h_s[yy] = (gq_f[x, yy] + rx0[yy].astype(F32)).astype(BF16)
            sy0(k, yy, y).start()

        sx0(y).wait_recv()
        gq_f[x, y] += rx0[y].astype(F32)

        @pl.loop(1, NY)
        def _(k):
            yy = y_peer(k)
            sy0(k, yy, yy).wait_recv()
            gq_f[x, y] += ry0[yy].astype(F32)

    @pl.when(core == 1)
    def _():
        @pl.loop(1, NY)
        def _(k):
            sy1(k, y_peer(k), y).start()

        @pl.loop(1, NY)
        def _(k):
            yy = y_peer(k)
            sy1(k, yy, yy).wait_recv()
            gq_f[0, y] += ry1[yy, 0].astype(F32)
            gq_f[1, y] += ry1[yy, 1].astype(F32)

        h_s[0] = gq_f[1 - x, y].astype(BF16)
        sx1().start()
        sx1().wait_recv()
        gq_f[x, y] += rx1[...].astype(F32)

    k_s[...] = gq_f[x, y].astype(BF16)

    @pl.loop(1, NZ)
    def _(k):
        sz(z_peer(k), z).start()

    z_round(za, a_zs, a_zr, "recv")
    z_parts = za[...]
    ya[y * NX + x, 0:1] = lse_of(z_parts[:, 0:1])
    ya[y * NX + x, 1:2] = jnp.sum(z_parts[:, 1:2], axis=0)
    plane_round(ya, a_ys, a_yr, "start")

    core_copy(1).wait_recv()
    gi_out[...] += gi_core[1].astype(F32)
    far_copy().wait_recv()
    gi_out[...] += gi_far[...].astype(F32)

    plane_round(ya, a_ys, a_yr, "recv")
    y_parts = ya[...]
    tops[...] = lse_of(y_parts[:, 0:1]) - jnp.sum(y_parts[:, 1:2], axis=0)
    mine = tops[:, pl.ds(pl.multiple_of((x * NY + y) * NZ * OWN, NZ * OWN), NZ * OWN)]
    pick_row = lax.broadcasted_iota(jnp.int32, (NZ * OWN, OWN), 0)
    pick_col = lax.broadcasted_iota(jnp.int32, (NZ * OWN, OWN), 1)
    pick = (pick_row == z * OWN + pick_col).astype(F32)
    loss_out[...] = jnp.dot(mine, pick, precision=HIGHEST, preferred_element_type=F32)

    @pl.loop(1, NZ)
    def _(k):
        zz = z_peer(k)
        sz(zz, zz).wait_recv()

    total = gq_f[x, y, z]
    rz[z] = jnp.zeros((OWN, E), BF16)
    for zz in range(NZ):
        total = total + rz[zz].astype(F32)
    gq_out[...] = total

    gather_drain(0, qb)
    gather_drain(1, qa)
    z_round(zb, b_zs, b_zr, "send")
    plane_round(yb, b_ys, b_yr, "send")
    z_round(za, a_zs, a_zr, "send")
    plane_round(ya, a_ys, a_yr, "send")
    core_copy(0).wait_send()
    core_copy(1).wait_send()
    far_copy().wait_send()

    @pl.when(core == 0)
    def _():
        @pl.loop(0, NY)
        def _(yy):
            sx0(yy).wait_send()

        @pl.loop(1, NY)
        def _(k):
            sy0(k, y_peer(k), y).wait_send()

    @pl.when(core == 1)
    def _():
        @pl.loop(1, NY)
        def _(k):
            sy1(k, y_peer(k), y).wait_send()

        sx1().wait_send()

    @pl.loop(1, NZ)
    def _(k):
        sz(z_peer(k), z).wait_send()


def per_device(query_a, query_b, items, positive_a, positive_b, loss_cotangent):
    rows = items.shape[0]
    vmem = pl.BlockSpec(memory_space=pltpu.VMEM)
    dma = pltpu.SemaphoreType.DMA
    block = (NX, NY, NZ, OWN, E)
    loss, gq, gi = pl.pallas_call(
        kernel,
        out_shape=(
            jax.ShapeDtypeStruct((1, OWN), F32),
            jax.ShapeDtypeStruct((OWN, E), F32),
            jax.ShapeDtypeStruct((QUARTER, E), F32),
        ),
        in_specs=[vmem, vmem, pl.BlockSpec(memory_space=pl.ANY), vmem, vmem, vmem],
        out_specs=(vmem, vmem, vmem),
        scratch_shapes=[
            pltpu.VMEM((rows, E), BF16),
            pltpu.VMEM((E, rows), BF16),
            pltpu.VMEM(block, BF16),
            pltpu.VMEM(block, BF16),
            pltpu.VMEM((rows, GROUP), F32),
            pltpu.VMEM((E, GROUP), F32),
            pltpu.VMEM(block, F32),
            pltpu.VMEM(block, BF16),
            pltpu.VMEM((NY, NZ, OWN, E), BF16),
            pltpu.VMEM((NY, NZ, OWN, E), BF16),
            pltpu.VMEM((NY, NX, NZ, OWN, E), BF16),
            pltpu.VMEM((NZ, OWN, E), BF16),
            pltpu.VMEM((NZ, OWN, E), BF16),
            pltpu.VMEM((NY, NZ, OWN, E), BF16),
            pltpu.VMEM((NZ, OWN, E), BF16),
            pltpu.VMEM((3, QUARTER, E), BF16),
            pltpu.VMEM((2, QUARTER, E), BF16),
            pltpu.VMEM((QUARTER, E), BF16),
            pltpu.VMEM((NZ, 1, GROUP), F32),
            pltpu.VMEM((NY * NX, 1, GROUP), F32),
            pltpu.VMEM((NZ, 2, GROUP), F32),
            pltpu.VMEM((NY * NX, 2, GROUP), F32),
            pltpu.VMEM((1, GROUP), F32),
            dma,
            dma((2, NZ)), dma((2, NZ)),
            dma((2, NY)), dma((2, NY)),
            dma((2, NY)), dma((2, NY)),
            dma((2, NY)), dma((2, NY)),
            dma((NZ,)), dma((NZ,)),
            dma((NY * NX,)), dma((NY * NX,)),
            dma((NZ,)), dma((NZ,)),
            dma((NY * NX,)), dma((NY * NX,)),
            dma((NY,)), dma((NY,)),
            dma((NY,)), dma((NY,)),
            dma((NZ,)), dma((NZ,)),
            dma((3,)), dma((3,)),
        ],
        compiler_params=pltpu.CompilerParams(
            collective_id=0, has_side_effects=True, vmem_limit_bytes=48 * 1024 * 1024
        ),
    )(
        query_a,
        query_b,
        items,
        positive_a.reshape(32, 128),
        positive_b.reshape(32, 128),
        loss_cotangent.reshape(32, 128),
    )
    return loss.reshape(OWN), gq, gi


def solution(mesh):
    return jax.shard_map(
        per_device,
        mesh=mesh,
        in_specs=(
            P(("item", "user"), None),
            P(("item", "user"), None),
            P("item", None),
            P(),
            P(),
            P(),
        ),
        out_specs=(P(("item", "user")), P(("item", "user"), None), P(("item", "user"), None)),
        check_vma=False,
    )
```

```python
import functools

import jax
import jax.numpy as jnp
from jax import lax
from jax.experimental import pallas as pl
from jax.experimental.pallas import tpu as pltpu
from jax.sharding import PartitionSpec as P

MESH = pl.DeviceIdType.MESH
F32 = jnp.float32
BF16 = jnp.bfloat16
HIGHEST = lax.Precision.HIGHEST

NZ, NY, NX = 8, 4, 2
OWN = 16
E = 256
GROUP = NZ * NY * NX * OWN
CHUNK = 256
QUARTER = 512


def remote(src, dst, send_sem, recv_sem, device):
    return pltpu.make_async_remote_copy(
        src_ref=src,
        dst_ref=dst,
        send_sem=send_sem,
        recv_sem=recv_sem,
        device_id=device,
        device_id_type=MESH,
    )


def group_row(table, selector, row_of):
    picked = jnp.dot(table, selector, precision=HIGHEST, preferred_element_type=F32)
    rows = lax.broadcasted_iota(jnp.int32, picked.shape, 0)
    return jnp.sum(jnp.where(rows == row_of, picked, 0.0), axis=0, keepdims=True)


def lse_of(parts):
    top = jnp.max(parts, axis=0)
    return top + jnp.log(jnp.sum(jnp.exp(parts - top[None]), axis=0))


def kernel(
    qa_in, qb_in, items_in, pa_in, pb_in, w_in,
    loss_hbm, gq_hbm, gi_hbm,
    items_v, items_t, qa, qb, pa_v, pb_v, w_v, probs, dsc, gq_f, gq_s,
    ry, rz, r2, k_s,
    gi_s, gi_core, gi_far, loss_out, gq_out, gi_out,
    zb, yb, za, ya,
    tops,
    in_sem, out_sem, g_zs, g_zr, g_ys, g_yr, g_fs, g_fr, g_xs, g_xr,
    b_zs, b_zr, b_ys, b_yr, a_zs, a_zr, a_ys, a_yr,
    ys_s, ys_r, zs_s, zs_r, s2s, s2r, gi_ss, gi_rs,
):
    item = lax.axis_index("item")
    user = lax.axis_index("user")
    z, y, x = item // (NY * NX), (item // NX) % NY, item % NX
    far, core = user // 2, user % 2
    items_rows = items_v.shape[0]
    offset = item * items_rows

    def at(zz, yy, xx):
        return {"item": (zz * NY + yy) * NX + xx}

    def z_peer(k):
        return lax.rem(z + k, NZ)

    def y_peer(k):
        return lax.rem(y + k, NY)

    def zx_peer(k):
        return lax.rem(z * NX + x + k, NZ * NX)

    def plane_peer(k):
        return lax.rem(y * NX + x + k, NY * NX)

    loads = [
        pltpu.make_async_copy(source, target, in_sem.at[n])
        for n, (source, target) in enumerate(
            (
                (qb_in, qb.at[x, y, z]),
                (qa_in, qa.at[x, y, z]),
                (pa_in, pa_v),
                (pb_in, pb_v),
                (w_in, w_v),
                (items_in, items_v),
            )
        )
    ]

    barrier = pltpu.get_barrier_semaphore()

    @pl.loop(1, NZ)
    def _(k):
        pl.semaphore_signal(barrier, inc=1, device_id=at(z_peer(k), y, x), device_id_type=MESH)

    @pl.loop(1, NY * NX)
    def _(k):
        p = plane_peer(k)
        pl.semaphore_signal(barrier, inc=1, device_id=at(z, p // NX, p % NX), device_id_type=MESH)

    @pl.loop(1, NZ)
    def _(k):
        pl.semaphore_signal(barrier, inc=1, device_id=at(z_peer(k), y, 1 - x), device_id_type=MESH)

    other_core = {"user": far * 2 + 1 - core}
    other_far = {"user": (1 - far) * 2 + core}
    pl.semaphore_signal(barrier, inc=1, device_id=other_core, device_id_type=MESH)
    pl.semaphore_signal(barrier, inc=1, device_id=other_far, device_id_type=MESH)

    for load in loads:
        load.start()
    loads[0].wait()
    loads[1].wait()

    pl.semaphore_wait(barrier, 2 * (NZ - 1) + (NY * NX - 1) + 2)

    def gather_z_start(n, q):
        @pl.loop(1, NZ)
        def _(k):
            block = q.at[x, y, z]
            remote(block, block, g_zs.at[n, k], g_zr.at[n, z], at(z_peer(k), y, x)).start()

    def gather_z_wait(n, q):
        @pl.loop(1, NZ)
        def _(k):
            zz = z_peer(k)
            block = q.at[x, y, zz]
            remote(block, block, g_zs.at[n, k], g_zr.at[n, zz], at(zz, y, x)).wait_recv()

    def x_copy(n, q, xx, yy):
        block = q.at[xx, yy]
        return remote(block, block, g_xs.at[n, yy], g_xr.at[n, yy], at(z, y, 1 - x))

    def y_copy(n, q, k, src_y):
        block = q.at[x, src_y]
        return remote(block, block, g_ys.at[n, k], g_yr.at[n, src_y], at(z, y_peer(k), x))

    def f_copy(n, q, k, src_y):
        block = q.at[1 - x, src_y]
        return remote(block, block, g_fs.at[n, k], g_fr.at[n, src_y], at(z, y_peer(k), x))

    def gather_plane_start(n, q):
        x_copy(n, q, x, y).start()

        @pl.loop(1, NY)
        def _(k):
            y_copy(n, q, k, y).start()

    def gather_forward(n, q):
        @pl.when(core == 0)
        def _():
            @pl.loop(1, NY)
            def _(k):
                yy = y_peer(k)
                y_copy(n, q, k, yy).wait_recv()
                x_copy(n, q, x, yy).start()

        @pl.when(core == 1)
        def _():
            x_copy(n, q, 1 - x, y).wait_recv()

            @pl.loop(1, NY)
            def _(k):
                f_copy(n, q, k, y).start()

    def gather_finish(n, q):
        @pl.when(core == 0)
        def _():
            @pl.loop(0, NY)
            def _(yy):
                x_copy(n, q, 1 - x, yy).wait_recv()

        @pl.when(core == 1)
        def _():
            @pl.loop(1, NY)
            def _(k):
                yy = y_peer(k)
                y_copy(n, q, k, yy).wait_recv()
                f_copy(n, q, k, yy).wait_recv()

    def gather_drain(n, q):
        @pl.loop(1, NZ)
        def _(k):
            block = q.at[x, y, z]
            remote(block, block, g_zs.at[n, k], g_zr.at[n, z], at(z_peer(k), y, x)).wait_send()

        x_copy(n, q, x, y).wait_send()

        @pl.loop(1, NY)
        def _(k):
            y_copy(n, q, k, y).wait_send()

            @pl.when(core == 0)
            def _():
                x_copy(n, q, x, y_peer(k)).wait_send()

            @pl.when(core == 1)
            def _():
                f_copy(n, q, k, y).wait_send()

    gather_z_start(0, qb)
    gather_z_start(1, qa)

    lanes = lax.broadcasted_iota(jnp.int32, (1, GROUP), 1)
    own_of = lanes % OWN
    z_of = (lanes // OWN) % NZ
    y_of = (lanes // (OWN * NZ)) % NY
    x_of = lanes // (OWN * NZ * NY)
    ks = lax.broadcasted_iota(jnp.int32, (128, GROUP), 0)
    selector = (ks == x_of * (4 * OWN) + user * OWN + own_of).astype(F32)
    row_of = z_of * NY + y_of
    for load in loads[2:5]:
        load.wait()
    pos_a = group_row(pa_v[...].astype(F32), selector, row_of).astype(jnp.int32) - offset
    pos_b = group_row(pb_v[...].astype(F32), selector, row_of).astype(jnp.int32) - offset
    weight = group_row(w_v[...], selector, row_of)

    gather_z_wait(0, qb)
    gather_plane_start(0, qb)

    loads[5].wait()
    for part in range(items_rows // QUARTER):
        rows = pl.ds(part * QUARTER, QUARTER)
        items_t[:, rows] = items_v[rows, :].T

    gather_forward(0, qb)
    gather_z_wait(1, qa)
    gather_plane_start(1, qa)
    gather_finish(0, qb)

    def scores(q, c):
        rows = q[c // 2, (c % 2) * 2 : (c % 2) * 2 + 2].reshape(CHUNK, E)
        return lax.dot_general(
            items_v[...], rows, (((1,), (1,)), ((), ())), preferred_element_type=F32
        )

    for c in range(GROUP // CHUNK):
        cols = slice(c * CHUNK, (c + 1) * CHUNK)
        score = scores(qb, c)
        top = jnp.max(score, axis=0, keepdims=True)
        p = jnp.exp(score - top)
        probs[:, cols] = p
        tops[:, cols] = top
        zb[z, :, cols] = top + jnp.log(jnp.sum(p, axis=0, keepdims=True))

    def round_copy(buf, k, ss, rs, src, device):
        return remote(buf.at[src], buf.at[src], ss.at[k], rs.at[src], device)

    def z_round(buf, ss, rs, verb):
        @pl.loop(1, NZ)
        def _(k):
            zz = z_peer(k)
            if verb == "recv":
                round_copy(buf, k, ss, rs, zz, at(zz, y, x)).wait_recv()
            elif verb == "send":
                round_copy(buf, k, ss, rs, z, at(zz, y, x)).wait_send()
            else:
                round_copy(buf, k, ss, rs, z, at(zz, y, x)).start()

    def plane_round(buf, ss, rs, verb):
        @pl.loop(1, NY * NX)
        def _(k):
            p = plane_peer(k)
            device = at(z, p // NX, p % NX)
            if verb == "recv":
                round_copy(buf, k, ss, rs, p, device).wait_recv()
            elif verb == "send":
                round_copy(buf, k, ss, rs, y * NX + x, device).wait_send()
            else:
                round_copy(buf, k, ss, rs, y * NX + x, device).start()

    z_round(zb, b_zs, b_zr, "start")
    gather_forward(1, qa)
    z_round(zb, b_zs, b_zr, "recv")
    yb[y * NX + x] = lse_of(zb[...])
    plane_round(yb, b_ys, b_yr, "start")
    gather_finish(1, qa)

    for c in range(GROUP // CHUNK):
        cols = slice(c * CHUNK, (c + 1) * CHUNK)
        score = scores(qa, c)
        top = jnp.max(score, axis=0, keepdims=True)
        total = jnp.sum(jnp.exp(score - top), axis=0, keepdims=True)
        ids = lax.broadcasted_iota(jnp.int32, score.shape, 0)
        hit = jnp.sum(jnp.where(ids == pos_a[:, cols], score, 0.0), axis=0, keepdims=True)
        za[z, 0:1, cols] = top + jnp.log(total)
        za[z, 1:2, cols] = hit
    z_round(za, a_zs, a_zr, "start")

    plane_round(yb, b_ys, b_yr, "recv")
    lse_b = lse_of(yb[...])
    factor = weight * jnp.exp(tops[...] - lse_b)

    def far_copy():
        return remote(gi_s.at[1], gi_far, gi_ss.at[1], gi_rs.at[1], other_far)

    def core_copy(n):
        return remote(gi_s.at[2 * n], gi_core.at[n], gi_ss.at[2 * n], gi_rs.at[2 * n], other_core)

    quarters = (
        (1 - far) * 2 + 1 - core,
        (1 - far) * 2 + core,
        far * 2 + 1 - core,
        far * 2 + core,
    )

    def item_grads(step):
        rows = pl.ds(pl.multiple_of(quarters[step] * QUARTER, QUARTER), QUARTER)
        return jnp.dot(dsc[rows, :], qb[...].reshape(GROUP, E), preferred_element_type=F32)

    def y_send(k, xx, yy, src):
        return remote(
            gq_s.at[xx, yy], ry.at[src, xx], ys_s.at[xx, yy], ys_r.at[xx, src],
            at(z, y_peer(k), x),
        )

    def z_send(k, xx, zz, src):
        return remote(
            gq_s.at[xx, :, zz], rz.at[src, xx], zs_s.at[xx, zz], zs_r.at[xx, src],
            at(z_peer(k), y, x),
        )

    def query_grads(c):
        cols = slice(c * CHUNK, (c + 1) * CHUNK)
        block = jnp.dot(items_t[...], dsc[:, cols], preferred_element_type=F32).T
        block = block.reshape(2, NZ, OWN, E)
        xx, yy = c // 2, (c % 2) * 2
        gq_f[xx, yy : yy + 2] = block
        gq_s[xx, yy : yy + 2] = block.astype(BF16)

    def query_sends(xx):
        @pl.when(core == 0)
        def _():
            @pl.loop(1, NY)
            def _(k):
                y_send(k, xx, y_peer(k), y).start()

        @pl.when(core == 1)
        def _():
            @pl.loop(1, NZ)
            def _(k):
                z_send(k, xx, z_peer(k), z).start()

    ids = lax.broadcasted_iota(jnp.int32, (items_rows, CHUNK), 0)
    for c in range(GROUP // CHUNK):
        cols = slice(c * CHUNK, (c + 1) * CHUNK)
        match = jnp.where(ids == pos_b[:, cols], weight[:, cols], 0.0)
        dsc[:, cols] = (probs[:, cols] * factor[:, cols] - match).astype(BF16)

    gi_s[0] = item_grads(0).astype(BF16)
    core_copy(0).start()
    part = item_grads(1)
    query_grads(0)
    query_grads(1)
    query_sends(0)
    core_copy(0).wait_recv()
    gi_s[1] = (part + gi_core[0].astype(F32)).astype(BF16)
    far_copy().start()
    query_grads(2)
    query_grads(3)
    query_sends(1)
    gi_s[2] = item_grads(2).astype(BF16)
    core_copy(1).start()
    gi_out[...] = item_grads(3)

    def zx_copy(p, src):
        return remote(
            k_s.at[p], r2.at[src], s2s.at[p], s2r.at[src], at(p // NX, y, p % NX)
        )

    def yx_copy(p, src):
        return remote(
            k_s.at[p], r2.at[src], s2s.at[p], s2r.at[src], at(z, p // NX, p % NX)
        )

    @pl.when(core == 0)
    def _():
        for xx in range(NX):
            @pl.loop(1, NY)
            def _(k):
                yy = y_peer(k)
                y_send(k, xx, yy, yy).wait_recv()
                gq_f[xx, y] += ry[yy, xx].astype(F32)

            @pl.loop(0, NZ)
            def _(zz):
                k_s[zz * NX + xx] = gq_f[xx, y, zz].astype(BF16)

        @pl.loop(1, NZ * NX)
        def _(k):
            zx_copy(zx_peer(k), z * NX + x).start()

    @pl.when(core == 1)
    def _():
        for xx in range(NX):
            @pl.loop(1, NZ)
            def _(k):
                zz = z_peer(k)
                z_send(k, xx, zz, zz).wait_recv()
                gq_f[xx, :, z] += rz[zz, xx].astype(F32)

            @pl.loop(0, NY)
            def _(yy):
                k_s[yy * NX + xx] = gq_f[xx, yy, z].astype(BF16)

        @pl.loop(1, NY * NX)
        def _(k):
            yx_copy(plane_peer(k), y * NX + x).start()

    z_round(za, a_zs, a_zr, "recv")
    z_parts = za[...]
    ya[y * NX + x, 0:1] = lse_of(z_parts[:, 0:1])
    ya[y * NX + x, 1:2] = jnp.sum(z_parts[:, 1:2], axis=0)
    plane_round(ya, a_ys, a_yr, "start")

    core_copy(1).wait_recv()
    gi_out[...] += gi_core[1].astype(F32)
    far_copy().wait_recv()
    gi_out[...] += gi_far[...].astype(F32)
    stores = [
        pltpu.make_async_copy(source, target, out_sem.at[n])
        for n, (source, target) in enumerate(
            ((gi_out, gi_hbm), (loss_out, loss_hbm), (gq_out, gq_hbm))
        )
    ]
    stores[0].start()

    plane_round(ya, a_ys, a_yr, "recv")
    y_parts = ya[...]
    tops[...] = lse_of(y_parts[:, 0:1]) - jnp.sum(y_parts[:, 1:2], axis=0)
    mine = tops[:, pl.ds(pl.multiple_of((x * NY + y) * NZ * OWN, NZ * OWN), NZ * OWN)]
    pick_row = lax.broadcasted_iota(jnp.int32, (NZ * OWN, OWN), 0)
    pick_col = lax.broadcasted_iota(jnp.int32, (NZ * OWN, OWN), 1)
    pick = (pick_row == z * OWN + pick_col).astype(F32)
    loss_out[...] = jnp.dot(mine, pick, precision=HIGHEST, preferred_element_type=F32)
    stores[1].start()

    gq_out[...] = gq_f[x, y, z]

    @pl.when(core == 0)
    def _():
        @pl.loop(1, NZ * NX)
        def _(k):
            p = zx_peer(k)
            zx_copy(p, p).wait_recv()
            gq_out[...] += r2[p].astype(F32)

    @pl.when(core == 1)
    def _():
        @pl.loop(1, NY * NX)
        def _(k):
            p = plane_peer(k)
            yx_copy(p, p).wait_recv()
            gq_out[...] += r2[p].astype(F32)

    stores[2].start()

    gather_drain(0, qb)
    gather_drain(1, qa)
    z_round(zb, b_zs, b_zr, "send")
    plane_round(yb, b_ys, b_yr, "send")
    z_round(za, a_zs, a_zr, "send")
    plane_round(ya, a_ys, a_yr, "send")
    core_copy(0).wait_send()
    core_copy(1).wait_send()
    far_copy().wait_send()

    @pl.when(core == 0)
    def _():
        for xx in range(NX):
            @pl.loop(1, NY)
            def _(k):
                y_send(k, xx, y_peer(k), y).wait_send()

        @pl.loop(1, NZ * NX)
        def _(k):
            zx_copy(zx_peer(k), z * NX + x).wait_send()

    @pl.when(core == 1)
    def _():
        for xx in range(NX):
            @pl.loop(1, NZ)
            def _(k):
                z_send(k, xx, z_peer(k), z).wait_send()

        @pl.loop(1, NY * NX)
        def _(k):
            yx_copy(plane_peer(k), y * NX + x).wait_send()


    for store in stores:
        store.wait()


def hand_over(*refs):
    sources, targets, sem = refs[:3], refs[3:6], refs[6]
    copies = [
        pltpu.make_async_copy(source, target, sem.at[n])
        for n, (source, target) in enumerate(zip(sources, targets))
    ]
    for copy in copies:
        copy.start()
    for copy in copies:
        copy.wait()


def per_device(query_a, query_b, items, positive_a, positive_b, loss_cotangent):
    rows = items.shape[0]
    hbm = pl.BlockSpec(memory_space=pl.ANY)
    results = (
        jax.ShapeDtypeStruct((1, OWN), F32),
        jax.ShapeDtypeStruct((OWN, E), F32),
        jax.ShapeDtypeStruct((QUARTER, E), F32),
    )
    dma = pltpu.SemaphoreType.DMA
    block = (NX, NY, NZ, OWN, E)
    loss, gq, gi = pl.pallas_call(
        kernel,
        out_shape=results,
        in_specs=[hbm] * 6,
        out_specs=[hbm] * 3,
        scratch_shapes=[
            pltpu.VMEM((rows, E), BF16),
            pltpu.VMEM((E, rows), BF16),
            pltpu.VMEM(block, BF16),
            pltpu.VMEM(block, BF16),
            pltpu.VMEM((32, 128), jnp.int32),
            pltpu.VMEM((32, 128), jnp.int32),
            pltpu.VMEM((32, 128), F32),
            pltpu.VMEM((rows, GROUP), F32),
            pltpu.VMEM((rows, GROUP), BF16),
            pltpu.VMEM(block, F32),
            pltpu.VMEM(block, BF16),
            pltpu.VMEM((NY, NX, NZ, OWN, E), BF16),
            pltpu.VMEM((NZ, NX, NY, OWN, E), BF16),
            pltpu.VMEM((NZ * NX, OWN, E), BF16),
            pltpu.VMEM((NZ * NX, OWN, E), BF16),
            pltpu.VMEM((3, QUARTER, E), BF16),
            pltpu.VMEM((2, QUARTER, E), BF16),
            pltpu.VMEM((QUARTER, E), BF16),
            pltpu.VMEM((1, OWN), F32),
            pltpu.VMEM((OWN, E), F32),
            pltpu.VMEM((QUARTER, E), F32),
            pltpu.VMEM((NZ, 1, GROUP), F32),
            pltpu.VMEM((NY * NX, 1, GROUP), F32),
            pltpu.VMEM((NZ, 2, GROUP), F32),
            pltpu.VMEM((NY * NX, 2, GROUP), F32),
            pltpu.VMEM((1, GROUP), F32),
            dma((6,)),
            dma((3,)),
            dma((2, NZ)), dma((2, NZ)),
            dma((2, NY)), dma((2, NY)),
            dma((2, NY)), dma((2, NY)),
            dma((2, NY)), dma((2, NY)),
            dma((NZ,)), dma((NZ,)),
            dma((NY * NX,)), dma((NY * NX,)),
            dma((NZ,)), dma((NZ,)),
            dma((NY * NX,)), dma((NY * NX,)),
            dma((NX, NY)), dma((NX, NY)),
            dma((NX, NZ)), dma((NX, NZ)),
            dma((NZ * NX,)), dma((NZ * NX,)),
            dma((3,)), dma((3,)),
        ],
        compiler_params=pltpu.CompilerParams(
            collective_id=0, has_side_effects=True, vmem_limit_bytes=64 * 1024 * 1024
        ),
    )(
        query_a,
        query_b,
        items,
        positive_a.reshape(32, 128),
        positive_b.reshape(32, 128),
        loss_cotangent.reshape(32, 128),
    )
    loss, gq, gi = pl.pallas_call(
        hand_over,
        out_shape=results,
        in_specs=[hbm] * 3,
        out_specs=[hbm] * 3,
        scratch_shapes=[dma((3,))],
        compiler_params=pltpu.CompilerParams(vmem_limit_bytes=64 * 1024 * 1024),
    )(loss, gq, gi)
    return loss.reshape(OWN), gq, gi


def solution(mesh):
    return jax.shard_map(
        per_device,
        mesh=mesh,
        in_specs=(
            P(("item", "user"), None),
            P(("item", "user"), None),
            P("item", None),
            P(),
            P(),
            P(),
        ),
        out_specs=(P(("item", "user")), P(("item", "user"), None), P(("item", "user"), None)),
        check_vma=False,
    )
```

```python
import functools

import jax
import jax.numpy as jnp
from jax import lax
from jax.experimental import pallas as pl
from jax.experimental.pallas import tpu as pltpu
from jax.sharding import PartitionSpec as P

MESH = pl.DeviceIdType.MESH
F32 = jnp.float32
BF16 = jnp.bfloat16
HIGHEST = lax.Precision.HIGHEST

NZ, NY, NX = 8, 4, 2
OWN = 16
E = 256
GROUP = NZ * NY * NX * OWN
CHUNK = 256
TILE = 512
QUARTER = 512
PIECE = 128


def remote(src, dst, send_sem, recv_sem, device):
    return pltpu.make_async_remote_copy(
        src_ref=src,
        dst_ref=dst,
        send_sem=send_sem,
        recv_sem=recv_sem,
        device_id=device,
        device_id_type=MESH,
    )


def group_row(table, selector, row_of):
    picked = jnp.dot(table, selector, precision=HIGHEST, preferred_element_type=F32)
    rows = lax.broadcasted_iota(jnp.int32, picked.shape, 0)
    return jnp.sum(jnp.where(rows == row_of, picked, 0.0), axis=0, keepdims=True)


def lse_of(parts):
    top = jnp.max(parts, axis=0)
    return top + jnp.log(jnp.sum(jnp.exp(parts - top[None]), axis=0))


def kernel(
    qa_in, qb_in, items_in, pa_in, pb_in, w_in,
    loss_hbm, gq_hbm, gi_hbm,
    items_v, items_t, qa, qb, pa_v, pb_v, w_v, probs, score0, score1, dsc, gq_f, gq_s,
    ry, rz, r2, k_s,
    gi_s, gi_core, gi_far, loss_out, gq_out, gi_out,
    zb, yb, za, ya,
    tops,
    in_sem, out_sem, g_zs, g_zr, g_ys, g_yr, g_fs, g_fr, g_xs, g_xr,
    b_zs, b_zr, b_ys, b_yr, a_zs, a_zr, a_ys, a_yr,
    ys_s, ys_r, zs_s, zs_r, s2s, s2r, gi_ss, gi_rs,
):
    item = lax.axis_index("item")
    user = lax.axis_index("user")
    z, y, x = item // (NY * NX), (item // NX) % NY, item % NX
    far, core = user // 2, user % 2
    items_rows = items_v.shape[0]
    offset = item * items_rows

    def at(zz, yy, xx):
        return {"item": (zz * NY + yy) * NX + xx}

    def z_peer(k):
        return lax.rem(z + k, NZ)

    def y_peer(k):
        return lax.rem(y + k, NY)

    def zx_peer(k):
        return lax.rem(z * NX + x + k, NZ * NX)

    def plane_peer(k):
        return lax.rem(y * NX + x + k, NY * NX)

    loads = [
        pltpu.make_async_copy(source, target, in_sem.at[n])
        for n, (source, target) in enumerate(
            (
                (qb_in, qb.at[x, y, z]),
                (qa_in, qa.at[x, y, z]),
                (pa_in, pa_v),
                (pb_in, pb_v),
                (w_in, w_v),
                (items_in, items_v),
            )
        )
    ]

    barrier = pltpu.get_barrier_semaphore()

    @pl.loop(1, NZ)
    def _(k):
        pl.semaphore_signal(barrier, inc=1, device_id=at(z_peer(k), y, x), device_id_type=MESH)

    @pl.loop(1, NY * NX)
    def _(k):
        p = plane_peer(k)
        pl.semaphore_signal(barrier, inc=1, device_id=at(z, p // NX, p % NX), device_id_type=MESH)

    @pl.loop(1, NZ)
    def _(k):
        pl.semaphore_signal(barrier, inc=1, device_id=at(z_peer(k), y, 1 - x), device_id_type=MESH)

    other_core = {"user": far * 2 + 1 - core}
    other_far = {"user": (1 - far) * 2 + core}
    pl.semaphore_signal(barrier, inc=1, device_id=other_core, device_id_type=MESH)
    pl.semaphore_signal(barrier, inc=1, device_id=other_far, device_id_type=MESH)

    for load in loads:
        load.start()
    loads[0].wait()
    loads[1].wait()

    pl.semaphore_wait(barrier, 2 * (NZ - 1) + (NY * NX - 1) + 2)

    def gather_z_start(n, q):
        @pl.loop(1, NZ)
        def _(k):
            block = q.at[x, y, z]
            remote(block, block, g_zs.at[n, k], g_zr.at[n, z], at(z_peer(k), y, x)).start()

    def gather_z_wait(n, q):
        @pl.loop(1, NZ)
        def _(k):
            zz = z_peer(k)
            block = q.at[x, y, zz]
            remote(block, block, g_zs.at[n, k], g_zr.at[n, zz], at(zz, y, x)).wait_recv()

    def x_copy(n, q, xx, yy):
        block = q.at[xx, yy]
        return remote(block, block, g_xs.at[n, yy], g_xr.at[n, yy], at(z, y, 1 - x))

    def y_copy(n, q, k, src_y):
        block = q.at[x, src_y]
        return remote(block, block, g_ys.at[n, k], g_yr.at[n, src_y], at(z, y_peer(k), x))

    def f_copy(n, q, k, src_y):
        block = q.at[1 - x, src_y]
        return remote(block, block, g_fs.at[n, k], g_fr.at[n, src_y], at(z, y_peer(k), x))

    def gather_plane_start(n, q):
        x_copy(n, q, x, y).start()

        @pl.loop(1, NY)
        def _(k):
            y_copy(n, q, k, y).start()

    def gather_forward(n, q):
        @pl.when(core == 0)
        def _():
            @pl.loop(1, NY)
            def _(k):
                yy = y_peer(k)
                y_copy(n, q, k, yy).wait_recv()
                x_copy(n, q, x, yy).start()

        @pl.when(core == 1)
        def _():
            x_copy(n, q, 1 - x, y).wait_recv()

            @pl.loop(1, NY)
            def _(k):
                f_copy(n, q, k, y).start()

    def gather_finish(n, q):
        @pl.when(core == 0)
        def _():
            @pl.loop(0, NY)
            def _(yy):
                x_copy(n, q, 1 - x, yy).wait_recv()

        @pl.when(core == 1)
        def _():
            @pl.loop(1, NY)
            def _(k):
                yy = y_peer(k)
                y_copy(n, q, k, yy).wait_recv()
                f_copy(n, q, k, yy).wait_recv()

    def gather_drain(n, q):
        @pl.loop(1, NZ)
        def _(k):
            block = q.at[x, y, z]
            remote(block, block, g_zs.at[n, k], g_zr.at[n, z], at(z_peer(k), y, x)).wait_send()

        x_copy(n, q, x, y).wait_send()

        @pl.loop(1, NY)
        def _(k):
            y_copy(n, q, k, y).wait_send()

            @pl.when(core == 0)
            def _():
                x_copy(n, q, x, y_peer(k)).wait_send()

            @pl.when(core == 1)
            def _():
                f_copy(n, q, k, y).wait_send()

    gather_z_start(0, qb)
    gather_z_start(1, qa)

    lanes = lax.broadcasted_iota(jnp.int32, (1, GROUP), 1)
    own_of = lanes % OWN
    z_of = (lanes // OWN) % NZ
    y_of = (lanes // (OWN * NZ)) % NY
    x_of = lanes // (OWN * NZ * NY)
    ks = lax.broadcasted_iota(jnp.int32, (128, GROUP), 0)
    selector = (ks == x_of * (4 * OWN) + user * OWN + own_of).astype(F32)
    row_of = z_of * NY + y_of
    for load in loads[2:5]:
        load.wait()
    pos_a = group_row(pa_v[...].astype(F32), selector, row_of).astype(jnp.int32) - offset
    pos_b = group_row(pb_v[...].astype(F32), selector, row_of).astype(jnp.int32) - offset
    weight = group_row(w_v[...], selector, row_of)

    gather_z_wait(0, qb)
    gather_plane_start(0, qb)

    loads[5].wait()
    for part in range(items_rows // QUARTER):
        rows = pl.ds(part * QUARTER, QUARTER)
        items_t[:, rows] = items_v[rows, :].T

    gather_forward(0, qb)
    gather_z_wait(1, qa)
    gather_plane_start(1, qa)
    gather_finish(0, qb)

    tiles = items_rows // TILE

    def chunk_of(c):
        return slice(c * CHUNK, (c + 1) * CHUNK)

    def fold(values, op):
        return op(values.reshape(TILE // 8, 8, CHUNK), axis=0)

    def softmax_parts(q, pos, keep, finish):
        tops_row, held = None, None
        for c in range(GROUP // CHUNK + 1):
            now, before = (score0, score1) if c % 2 == 0 else (score1, score0)
            ahead = c < GROUP // CHUNK

            def tile(t, carry):
                top, hit, total = carry
                rows = pl.ds(pl.multiple_of(t * TILE, TILE), TILE)
                if ahead:
                    users = q[c // 2, (c % 2) * 2 : (c % 2) * 2 + 2].reshape(CHUNK, E)
                    score = lax.dot_general(
                        items_v[rows, :], users, (((1,), (1,)), ((), ())),
                        preferred_element_type=F32,
                    )
                    now[rows, :] = score
                    top = jnp.maximum(top, fold(score, jnp.max))
                    if pos is not None:
                        ids = lax.broadcasted_iota(jnp.int32, score.shape, 0)
                        match = ids == pos[:, chunk_of(c)] - t * TILE
                        hit = hit + fold(jnp.where(match, score, 0.0), jnp.sum)
                if c > 0:
                    p = jnp.exp(before[rows, :] - tops_row)
                    if keep:
                        probs[rows, chunk_of(c - 1)] = p
                    total = total + fold(p, jnp.sum)
                return top, hit, total

            zero = jnp.zeros((8, CHUNK), F32)
            top, hit, total = lax.fori_loop(
                0, tiles, tile, (jnp.full((8, CHUNK), -jnp.inf, F32), zero, zero)
            )
            if c > 0:
                finish(c - 1, tops_row, jnp.sum(total, axis=0, keepdims=True), held)
            tops_row = jnp.max(top, axis=0, keepdims=True)
            held = jnp.sum(hit, axis=0, keepdims=True)

    def finish_b(c, top, total, hit):
        tops[:, chunk_of(c)] = top
        zb[z, :, chunk_of(c)] = top + jnp.log(total)

    def finish_a(c, top, total, hit):
        za[z, 0:1, chunk_of(c)] = top + jnp.log(total)
        za[z, 1:2, chunk_of(c)] = hit

    softmax_parts(qb, None, True, finish_b)

    def round_copy(buf, k, ss, rs, src, device):
        return remote(buf.at[src], buf.at[src], ss.at[k], rs.at[src], device)

    def z_round(buf, ss, rs, verb):
        @pl.loop(1, NZ)
        def _(k):
            zz = z_peer(k)
            if verb == "recv":
                round_copy(buf, k, ss, rs, zz, at(zz, y, x)).wait_recv()
            elif verb == "send":
                round_copy(buf, k, ss, rs, z, at(zz, y, x)).wait_send()
            else:
                round_copy(buf, k, ss, rs, z, at(zz, y, x)).start()

    def plane_round(buf, ss, rs, verb):
        @pl.loop(1, NY * NX)
        def _(k):
            p = plane_peer(k)
            device = at(z, p // NX, p % NX)
            if verb == "recv":
                round_copy(buf, k, ss, rs, p, device).wait_recv()
            elif verb == "send":
                round_copy(buf, k, ss, rs, y * NX + x, device).wait_send()
            else:
                round_copy(buf, k, ss, rs, y * NX + x, device).start()

    z_round(zb, b_zs, b_zr, "start")
    gather_forward(1, qa)
    z_round(zb, b_zs, b_zr, "recv")
    yb[y * NX + x] = lse_of(zb[...])
    plane_round(yb, b_ys, b_yr, "start")
    gather_finish(1, qa)

    softmax_parts(qa, pos_a, False, finish_a)
    z_round(za, a_zs, a_zr, "start")

    plane_round(yb, b_ys, b_yr, "recv")
    lse_b = lse_of(yb[...])
    factor = weight * jnp.exp(tops[...] - lse_b)

    def far_copy():
        return remote(gi_s.at[1], gi_far, gi_ss.at[1], gi_rs.at[1], other_far)

    def core_copy(n):
        return remote(gi_s.at[2 * n], gi_core.at[n], gi_ss.at[2 * n], gi_rs.at[2 * n], other_core)

    quarters = (
        (1 - far) * 2 + 1 - core,
        (1 - far) * 2 + core,
        far * 2 + 1 - core,
        far * 2 + core,
    )

    def item_grads(step):
        rows = pl.ds(pl.multiple_of(quarters[step] * QUARTER, QUARTER), QUARTER)
        return jnp.dot(dsc[rows, :], qb[...].reshape(GROUP, E), preferred_element_type=F32)

    def y_send(k, xx, yy, src):
        return remote(
            gq_s.at[xx, yy], ry.at[src, xx], ys_s.at[xx, yy], ys_r.at[xx, src],
            at(z, y_peer(k), x),
        )

    def z_send(k, xx, zz, src):
        return remote(
            gq_s.at[xx, :, zz], rz.at[src, xx], zs_s.at[xx, zz], zs_r.at[xx, src],
            at(z_peer(k), y, x),
        )

    def query_grads(xx, pair):
        cols = pl.ds(pl.multiple_of((xx * 2 + pair) * CHUNK, CHUNK), CHUNK)
        block = jnp.dot(items_t[...], dsc[:, cols], preferred_element_type=F32).T
        block = block.reshape(2, NZ, OWN, E)
        yy = pair * 2
        gq_f[xx, pl.ds(yy, 2)] = block
        gq_s[xx, pl.ds(yy, 2)] = block.astype(BF16)

    def query_sends(xx):
        @pl.loop(0, 2)
        def _(pair):
            query_grads(xx, pair)

        @pl.when(core == 0)
        def _():
            @pl.loop(1, NY)
            def _(k):
                y_send(k, xx, y_peer(k), y).start()

        @pl.when(core == 1)
        def _():
            @pl.loop(1, NZ)
            def _(k):
                z_send(k, xx, z_peer(k), z).start()

    @pl.loop(0, tiles)
    def _(t):
        rows = pl.ds(pl.multiple_of(t * TILE, TILE), TILE)
        ids = lax.broadcasted_iota(jnp.int32, (TILE, CHUNK), 0)
        for c in range(GROUP // CHUNK):
            cols = chunk_of(c)
            match = jnp.where(ids == pos_b[:, cols] - t * TILE, weight[:, cols], 0.0)
            dsc[rows, cols] = (probs[rows, cols] * factor[:, cols] - match).astype(BF16)

    gi_s[0] = item_grads(0).astype(BF16)
    core_copy(0).start()
    part = item_grads(1)
    query_sends(0)
    core_copy(0).wait_recv()
    gi_s[1] = (part + gi_core[0].astype(F32)).astype(BF16)
    far_copy().start()
    query_sends(1)
    gi_s[2] = item_grads(2).astype(BF16)
    core_copy(1).start()
    gi_out[...] = item_grads(3)

    def zx_copy(p, src):
        return remote(
            k_s.at[p], r2.at[src], s2s.at[p], s2r.at[src], at(p // NX, y, p % NX)
        )

    def yx_copy(p, src):
        return remote(
            k_s.at[p], r2.at[src], s2s.at[p], s2r.at[src], at(z, p // NX, p % NX)
        )

    @pl.when(core == 0)
    def _():
        for xx in range(NX):
            @pl.loop(1, NY)
            def _(k):
                yy = y_peer(k)
                y_send(k, xx, yy, yy).wait_recv()
                gq_f[xx, y] += ry[yy, xx].astype(F32)

            @pl.loop(0, NZ)
            def _(zz):
                k_s[zz * NX + xx] = gq_f[xx, y, zz].astype(BF16)

        @pl.loop(1, NZ * NX)
        def _(k):
            zx_copy(zx_peer(k), z * NX + x).start()

    @pl.when(core == 1)
    def _():
        for xx in range(NX):
            @pl.loop(1, NZ)
            def _(k):
                zz = z_peer(k)
                z_send(k, xx, zz, zz).wait_recv()
                gq_f[xx, :, z] += rz[zz, xx].astype(F32)

            @pl.loop(0, NY)
            def _(yy):
                k_s[yy * NX + xx] = gq_f[xx, yy, z].astype(BF16)

        @pl.loop(1, NY * NX)
        def _(k):
            yx_copy(plane_peer(k), y * NX + x).start()

    z_round(za, a_zs, a_zr, "recv")
    z_parts = za[...]
    ya[y * NX + x, 0:1] = lse_of(z_parts[:, 0:1])
    ya[y * NX + x, 1:2] = jnp.sum(z_parts[:, 1:2], axis=0)
    plane_round(ya, a_ys, a_yr, "start")

    core_copy(1).wait_recv()
    gi_out[...] += gi_core[1].astype(F32)
    far_copy().wait_recv()
    gi_out[...] += gi_far[...].astype(F32)
    stores = [
        pltpu.make_async_copy(source, target, out_sem.at[n])
        for n, (source, target) in enumerate(
            ((gi_out, gi_hbm), (loss_out, loss_hbm), (gq_out, gq_hbm))
        )
    ]
    stores[0].start()

    plane_round(ya, a_ys, a_yr, "recv")
    y_parts = ya[...]
    tops[...] = lse_of(y_parts[:, 0:1]) - jnp.sum(y_parts[:, 1:2], axis=0)
    mine = tops[:, pl.ds(pl.multiple_of((x * NY + y) * NZ * OWN, NZ * OWN), NZ * OWN)]
    pick_row = lax.broadcasted_iota(jnp.int32, (NZ * OWN, OWN), 0)
    pick_col = lax.broadcasted_iota(jnp.int32, (NZ * OWN, OWN), 1)
    pick = (pick_row == z * OWN + pick_col).astype(F32)
    loss_out[...] = jnp.dot(mine, pick, precision=HIGHEST, preferred_element_type=F32)
    stores[1].start()

    gq_out[...] = gq_f[x, y, z]

    @pl.when(core == 0)
    def _():
        @pl.loop(1, NZ * NX)
        def _(k):
            p = zx_peer(k)
            zx_copy(p, p).wait_recv()
            gq_out[...] += r2[p].astype(F32)

    @pl.when(core == 1)
    def _():
        @pl.loop(1, NY * NX)
        def _(k):
            p = plane_peer(k)
            yx_copy(p, p).wait_recv()
            gq_out[...] += r2[p].astype(F32)

    stores[2].start()

    gather_drain(0, qb)
    gather_drain(1, qa)
    z_round(zb, b_zs, b_zr, "send")
    plane_round(yb, b_ys, b_yr, "send")
    z_round(za, a_zs, a_zr, "send")
    plane_round(ya, a_ys, a_yr, "send")
    core_copy(0).wait_send()
    core_copy(1).wait_send()
    far_copy().wait_send()

    @pl.when(core == 0)
    def _():
        for xx in range(NX):
            @pl.loop(1, NY)
            def _(k):
                y_send(k, xx, y_peer(k), y).wait_send()

        @pl.loop(1, NZ * NX)
        def _(k):
            zx_copy(zx_peer(k), z * NX + x).wait_send()

    @pl.when(core == 1)
    def _():
        for xx in range(NX):
            @pl.loop(1, NZ)
            def _(k):
                z_send(k, xx, z_peer(k), z).wait_send()

        @pl.loop(1, NY * NX)
        def _(k):
            yx_copy(plane_peer(k), y * NX + x).wait_send()


    for store in stores:
        store.wait()


def hand_over(*refs):
    sources, targets, held, (in_sem, out_sem) = refs[:3], refs[3:6], refs[6:9], refs[9:]
    ways = list(zip(sources, held, targets))
    steps = QUARTER // PIECE
    parts = [tuple(r.at[pl.ds(n * PIECE, PIECE)] for r in ways[2]) for n in range(steps)]
    parts = parts + ways[:2]
    reads = [
        pltpu.make_async_copy(source, middle, in_sem.at[n])
        for n, (source, middle, target) in enumerate(parts)
    ]
    writes = [
        pltpu.make_async_copy(middle, target, out_sem.at[n])
        for n, (source, middle, target) in enumerate(parts)
    ]
    for read in reads:
        read.start()
    for read, write in zip(reads, writes):
        read.wait()
        write.start()
    for write in writes:
        write.wait()


def per_device(query_a, query_b, items, positive_a, positive_b, loss_cotangent):
    rows = items.shape[0]
    hbm = pl.BlockSpec(memory_space=pl.ANY)
    results = (
        jax.ShapeDtypeStruct((1, OWN), F32),
        jax.ShapeDtypeStruct((OWN, E), F32),
        jax.ShapeDtypeStruct((QUARTER, E), F32),
    )
    dma = pltpu.SemaphoreType.DMA
    block = (NX, NY, NZ, OWN, E)
    loss, gq, gi = pl.pallas_call(
        kernel,
        out_shape=results,
        in_specs=[hbm] * 6,
        out_specs=[hbm] * 3,
        scratch_shapes=[
            pltpu.VMEM((rows, E), BF16),
            pltpu.VMEM((E, rows), BF16),
            pltpu.VMEM(block, BF16),
            pltpu.VMEM(block, BF16),
            pltpu.VMEM((32, 128), jnp.int32),
            pltpu.VMEM((32, 128), jnp.int32),
            pltpu.VMEM((32, 128), F32),
            pltpu.VMEM((rows, GROUP), F32),
            pltpu.VMEM((rows, CHUNK), F32),
            pltpu.VMEM((rows, CHUNK), F32),
            pltpu.VMEM((rows, GROUP), BF16),
            pltpu.VMEM(block, F32),
            pltpu.VMEM(block, BF16),
            pltpu.VMEM((NY, NX, NZ, OWN, E), BF16),
            pltpu.VMEM((NZ, NX, NY, OWN, E), BF16),
            pltpu.VMEM((NZ * NX, OWN, E), BF16),
            pltpu.VMEM((NZ * NX, OWN, E), BF16),
            pltpu.VMEM((3, QUARTER, E), BF16),
            pltpu.VMEM((2, QUARTER, E), BF16),
            pltpu.VMEM((QUARTER, E), BF16),
            pltpu.VMEM((1, OWN), F32),
            pltpu.VMEM((OWN, E), F32),
            pltpu.VMEM((QUARTER, E), F32),
            pltpu.VMEM((NZ, 1, GROUP), F32),
            pltpu.VMEM((NY * NX, 1, GROUP), F32),
            pltpu.VMEM((NZ, 2, GROUP), F32),
            pltpu.VMEM((NY * NX, 2, GROUP), F32),
            pltpu.VMEM((1, GROUP), F32),
            dma((6,)),
            dma((3,)),
            dma((2, NZ)), dma((2, NZ)),
            dma((2, NY)), dma((2, NY)),
            dma((2, NY)), dma((2, NY)),
            dma((2, NY)), dma((2, NY)),
            dma((NZ,)), dma((NZ,)),
            dma((NY * NX,)), dma((NY * NX,)),
            dma((NZ,)), dma((NZ,)),
            dma((NY * NX,)), dma((NY * NX,)),
            dma((NX, NY)), dma((NX, NY)),
            dma((NX, NZ)), dma((NX, NZ)),
            dma((NZ * NX,)), dma((NZ * NX,)),
            dma((3,)), dma((3,)),
        ],
        compiler_params=pltpu.CompilerParams(
            collective_id=0, has_side_effects=True, vmem_limit_bytes=64 * 1024 * 1024
        ),
    )(
        query_a,
        query_b,
        items,
        positive_a.reshape(32, 128),
        positive_b.reshape(32, 128),
        loss_cotangent.reshape(32, 128),
    )
    pieces = QUARTER // PIECE + 2
    loss, gq, gi = pl.pallas_call(
        hand_over,
        out_shape=results,
        in_specs=[hbm] * 3,
        out_specs=[hbm] * 3,
        scratch_shapes=[pltpu.VMEM(r.shape, r.dtype) for r in results] + [dma((pieces,))] * 2,
        compiler_params=pltpu.CompilerParams(vmem_limit_bytes=64 * 1024 * 1024),
    )(loss, gq, gi)
    return loss.reshape(OWN), gq, gi


def solution(mesh):
    return jax.shard_map(
        per_device,
        mesh=mesh,
        in_specs=(
            P(("item", "user"), None),
            P(("item", "user"), None),
            P("item", None),
            P(),
            P(),
            P(),
        ),
        out_specs=(P(("item", "user")), P(("item", "user"), None), P(("item", "user"), None)),
        check_vma=False,
    )
```

```python
import functools

import jax
import jax.numpy as jnp
from jax import lax
from jax.experimental import pallas as pl
from jax.experimental.pallas import tpu as pltpu
from jax.sharding import PartitionSpec as P

MESH = pl.DeviceIdType.MESH
F32 = jnp.float32
BF16 = jnp.bfloat16
HIGHEST = lax.Precision.HIGHEST

NZ, NY, NX = 8, 4, 2
OWN = 16
E = 256
GROUP = NZ * NY * NX * OWN
HALF = GROUP // NX
TILE = 512
QUARTER = 512
PIECE = 128


def remote(src, dst, send_sem, recv_sem, device):
    return pltpu.make_async_remote_copy(
        src_ref=src,
        dst_ref=dst,
        send_sem=send_sem,
        recv_sem=recv_sem,
        device_id=device,
        device_id_type=MESH,
    )


def group_row(table, selector, row_of):
    picked = jnp.dot(table, selector, precision=HIGHEST, preferred_element_type=F32)
    rows = lax.broadcasted_iota(jnp.int32, picked.shape, 0)
    return jnp.sum(jnp.where(rows == row_of, picked, 0.0), axis=0, keepdims=True)


def lse_of(parts):
    top = jnp.max(parts, axis=0)
    return top + jnp.log(jnp.sum(jnp.exp(parts - top[None]), axis=0))


def act(copy, verb):
    if verb == "start":
        copy.start()
    elif verb == "send":
        copy.wait_send()
    else:
        copy.wait_recv()


def kernel(
    qa_in, qb_in, items_in, pa_in, pb_in, w_in,
    loss_hbm, gq_hbm, gi_hbm,
    items_v, items_t, qa, qb, pa_v, pb_v, w_v, pos_a, pos_b, weight,
    probs, score_a, dsc, gq_f, gq_s,
    ry, rz, r2, k_s,
    gi_f, gi_s, gi_core, gi_far, loss_out, gq_out, gi_out,
    zb, yb, za, ya,
    tops,
    in_sem, out_sem, g_zs, g_zr, g_ps, g_pr,
    b_zs, b_zr, b_ys, b_yr, a_zs, a_zr, a_ys, a_yr,
    ys_s, ys_r, zs_s, zs_r, s2s, s2r, gi_ss, gi_rs,
):
    item = lax.axis_index("item")
    user = lax.axis_index("user")
    z, y, x = item // (NY * NX), (item // NX) % NY, item % NX
    far, core = user // 2, user % 2
    items_rows = items_v.shape[0]
    offset = item * items_rows

    def at(zz, yy, xx):
        return {"item": (zz * NY + yy) * NX + xx}

    def z_peer(k):
        return lax.rem(z + k, NZ)

    def y_peer(k):
        return lax.rem(y + k, NY)

    def zx_peer(k):
        return lax.rem(z * NX + x + k, NZ * NX)

    def plane_peer(k):
        return lax.rem(y * NX + x + k, NY * NX)

    loads = [
        pltpu.make_async_copy(source, target, in_sem.at[n])
        for n, (source, target) in enumerate(
            (
                (qb_in, qb.at[x, y, z]),
                (qa_in, qa.at[x, y, z]),
                (pa_in, pa_v),
                (pb_in, pb_v),
                (w_in, w_v),
                (items_in, items_v),
            )
        )
    ]

    barrier = pltpu.get_barrier_semaphore()

    @pl.loop(1, NZ)
    def _(k):
        pl.semaphore_signal(barrier, inc=1, device_id=at(z_peer(k), y, x), device_id_type=MESH)
        pl.semaphore_signal(barrier, inc=1, device_id=at(z_peer(k), y, 1 - x), device_id_type=MESH)

    @pl.loop(1, NY * NX)
    def _(k):
        p = plane_peer(k)
        pl.semaphore_signal(barrier, inc=1, device_id=at(z, p // NX, p % NX), device_id_type=MESH)

    other_core = {"user": far * 2 + 1 - core}
    other_far = {"user": (1 - far) * 2 + core}
    pl.semaphore_signal(barrier, inc=1, device_id=other_core, device_id_type=MESH)
    pl.semaphore_signal(barrier, inc=1, device_id=other_far, device_id_type=MESH)

    for load in loads:
        load.start()
    loads[0].wait()
    loads[1].wait()

    pl.semaphore_wait(barrier, 2 * (NZ - 1) + (NY * NX - 1) + 2)

    def gather_z(n, q, verb):
        @pl.loop(1, NZ)
        def _(k):
            zz = z_peer(k)
            block = q.at[x, y, zz if verb == "recv" else z]
            source = zz if verb == "recv" else z
            copy = remote(block, block, g_zs.at[n, k], g_zr.at[n, source], at(zz, y, x))
            act(copy, verb)

    def plane_copy(n, q, yy, xx, source):
        block = q.at[source % NX, source // NX]
        place = yy * NX + xx
        return remote(block, block, g_ps.at[n, place], g_pr.at[n, source], at(z, yy, xx))

    def gather_plane(n, q, verb):
        mine = y * NX + x

        @pl.loop(1, NY)
        def _(k):
            act(plane_copy(n, q, y_peer(k), x, mine), verb)

        @pl.loop(0, NY)
        def _(k):
            act(plane_copy(n, q, y_peer(k), 1 - x, mine), verb)

    def gather_wait(n, q, xx, first):
        @pl.loop(first, NY)
        def _(k):
            yy = y_peer(k)
            plane_copy(n, q, yy, xx, yy * NX + xx).wait_recv()

    gather_z(0, qb, "start")
    gather_z(1, qa, "start")

    lanes = lax.broadcasted_iota(jnp.int32, (1, GROUP), 1)
    own_of = lanes % OWN
    z_of = (lanes // OWN) % NZ
    y_of = (lanes // (OWN * NZ)) % NY
    x_of = lanes // (OWN * NZ * NY)
    ks = lax.broadcasted_iota(jnp.int32, (128, GROUP), 0)
    selector = (ks == x_of * (4 * OWN) + user * OWN + own_of).astype(F32)
    row_of = z_of * NY + y_of
    for load in loads[2:5]:
        load.wait()
    pos_a[...] = group_row(pa_v[...].astype(F32), selector, row_of).astype(jnp.int32) - offset
    pos_b[...] = group_row(pb_v[...].astype(F32), selector, row_of).astype(jnp.int32) - offset
    weight[...] = group_row(w_v[...], selector, row_of)

    gather_z(0, qb, "recv")
    gather_plane(0, qb, "start")

    loads[5].wait()
    for part in range(items_rows // QUARTER):
        rows = pl.ds(part * QUARTER, QUARTER)
        items_t[:, rows] = items_v[rows, :].T
    gather_z(1, qa, "recv")

    tiles = items_rows // TILE

    def half_of(xx):
        return pl.ds(pl.multiple_of(xx * HALF, HALF), HALF)

    def tile_of(t):
        return pl.ds(pl.multiple_of(t * TILE, TILE), TILE)

    def fold(values, op):
        return op(values.reshape(TILE // 8, 8, HALF), axis=0)

    def scores(q, xx):
        users = q[xx].reshape(HALF, E)
        return lax.dot_general(
            items_v[...], users, (((1,), (1,)), ((), ())), preferred_element_type=F32
        )

    zero = jnp.zeros((8, HALF), F32)
    least = jnp.full((8, HALF), -jnp.inf, F32)

    def half_b(xx):
        probs[xx] = scores(qb, xx)

        def largest(t, top):
            return jnp.maximum(top, fold(probs[xx, tile_of(t), :], jnp.max))

        top = jnp.max(lax.fori_loop(0, tiles, largest, least), axis=0, keepdims=True)

        def exponentials(t, total):
            p = jnp.exp(probs[xx, tile_of(t), :] - top)
            probs[xx, tile_of(t), :] = p
            return total + fold(p, jnp.sum)

        total = jnp.sum(lax.fori_loop(0, tiles, exponentials, zero), axis=0, keepdims=True)
        tops[:, half_of(xx)] = top
        zb[z, :, half_of(xx)] = top + jnp.log(total)

    def half_a(xx):
        score_a[...] = scores(qa, xx)
        pos = pos_a[:, half_of(xx)]
        ids = lax.broadcasted_iota(jnp.int32, (TILE, HALF), 0)

        def largest(t, carry):
            top, hit = carry
            score = score_a[tile_of(t), :]
            match = jnp.where(ids == pos - t * TILE, score, 0.0)
            return jnp.maximum(top, fold(score, jnp.max)), hit + fold(match, jnp.sum)

        top, hit = lax.fori_loop(0, tiles, largest, (least, zero))
        top = jnp.max(top, axis=0, keepdims=True)

        def exponentials(t, total):
            return total + fold(jnp.exp(score_a[tile_of(t), :] - top), jnp.sum)

        total = jnp.sum(lax.fori_loop(0, tiles, exponentials, zero), axis=0, keepdims=True)
        za[z, 0:1, half_of(xx)] = top + jnp.log(total)
        za[z, 1:2, half_of(xx)] = jnp.sum(hit, axis=0, keepdims=True)

    def z_round(buf, ss, rs, verb):
        @pl.loop(1, NZ)
        def _(k):
            zz = z_peer(k)
            src = zz if verb == "recv" else z
            act(remote(buf.at[src], buf.at[src], ss.at[k], rs.at[src], at(zz, y, x)), verb)

    def plane_round(buf, ss, rs, verb):
        @pl.loop(1, NY * NX)
        def _(k):
            p = plane_peer(k)
            src = p if verb == "recv" else y * NX + x
            device = at(z, p // NX, p % NX)
            act(remote(buf.at[src], buf.at[src], ss.at[k], rs.at[src], device), verb)

    gather_wait(0, qb, x, 1)
    half_b(x)
    gather_wait(0, qb, 1 - x, 0)
    gather_plane(1, qa, "start")
    half_b(1 - x)
    z_round(zb, b_zs, b_zr, "start")
    gather_z(0, qb, "send")
    gather_z(1, qa, "send")
    gather_plane(0, qb, "send")
    z_round(zb, b_zs, b_zr, "recv")
    yb[y * NX + x] = lse_of(zb[...])
    plane_round(yb, b_ys, b_yr, "start")
    gather_wait(1, qa, x, 1)
    half_a(x)
    z_round(zb, b_zs, b_zr, "send")

    plane_round(yb, b_ys, b_yr, "recv")
    factor = weight[...] * jnp.exp(tops[...] - lse_of(yb[...]))

    ids = lax.broadcasted_iota(jnp.int32, (TILE, HALF), 0)

    def dscores(ff):
        @pl.loop(ff * 2 * QUARTER // TILE, (ff + 1) * 2 * QUARTER // TILE)
        def _(t):
            for xx in range(NX):
                cols = slice(xx * HALF, (xx + 1) * HALF)
                match = jnp.where(ids == pos_b[:, cols] - t * TILE, weight[:, cols], 0.0)
                score = probs[xx, tile_of(t), :] * factor[:, cols] - match
                dsc[tile_of(t), cols] = score.astype(BF16)

    def far_copy():
        return remote(gi_s.at[1], gi_far, gi_ss.at[1], gi_rs.at[1], other_far)

    def core_copy(n):
        return remote(gi_s.at[2 * n], gi_core.at[n], gi_ss.at[2 * n], gi_rs.at[2 * n], other_core)

    def item_grads(ff):
        rows = pl.ds(pl.multiple_of(ff * (2 * QUARTER), 2 * QUARTER), 2 * QUARTER)
        gi_f[...] = jnp.dot(dsc[rows, :], qb[...].reshape(GROUP, E), preferred_element_type=F32)

    def gi_part(cc):
        return gi_f[pl.ds(pl.multiple_of(cc * QUARTER, QUARTER), QUARTER), :]

    def y_send(k, xx, yy, src):
        return remote(
            gq_s.at[xx, yy], ry.at[src, xx], ys_s.at[xx, yy], ys_r.at[xx, src],
            at(z, y_peer(k), x),
        )

    def z_send(k, xx, zz, src):
        return remote(
            gq_s.at[xx, :, zz], rz.at[src, xx], zs_s.at[xx, zz], zs_r.at[xx, src],
            at(z_peer(k), y, x),
        )

    def query_grads(xx):
        block = jnp.dot(
            items_t[...], dsc[:, xx * HALF : (xx + 1) * HALF], preferred_element_type=F32
        ).T.reshape(NY, NZ, OWN, E)
        gq_f[xx] = block
        gq_s[xx] = block.astype(BF16)

        @pl.when(core == 0)
        def _():
            @pl.loop(1, NY)
            def _(k):
                y_send(k, xx, y_peer(k), y).start()

        @pl.when(core == 1)
        def _():
            @pl.loop(1, NZ)
            def _(k):
                z_send(k, xx, z_peer(k), z).start()

    dscores(1 - far)
    item_grads(1 - far)
    gi_s[0] = gi_part(1 - core).astype(BF16)
    core_copy(0).start()
    dscores(far)
    query_grads(0)
    core_copy(0).wait_recv()
    gi_s[1] = (gi_part(core) + gi_core[0].astype(F32)).astype(BF16)
    far_copy().start()
    query_grads(1)
    item_grads(far)
    gi_s[2] = gi_part(1 - core).astype(BF16)
    core_copy(1).start()

    gather_wait(1, qa, 1 - x, 0)
    half_a(1 - x)
    z_round(za, a_zs, a_zr, "start")

    def zx_copy(p, src):
        return remote(
            k_s.at[p], r2.at[src], s2s.at[p], s2r.at[src], at(p // NX, y, p % NX)
        )

    def yx_copy(p, src):
        return remote(
            k_s.at[p], r2.at[src], s2s.at[p], s2r.at[src], at(z, p // NX, p % NX)
        )

    @pl.when(core == 0)
    def _():
        for xx in range(NX):
            @pl.loop(1, NY)
            def _(k):
                yy = y_peer(k)
                y_send(k, xx, yy, yy).wait_recv()
                gq_f[xx, y] += ry[yy, xx].astype(F32)

            @pl.loop(0, NZ)
            def _(zz):
                k_s[zz * NX + xx] = gq_f[xx, y, zz].astype(BF16)

        @pl.loop(1, NZ * NX)
        def _(k):
            zx_copy(zx_peer(k), z * NX + x).start()

    @pl.when(core == 1)
    def _():
        for xx in range(NX):
            @pl.loop(1, NZ)
            def _(k):
                zz = z_peer(k)
                z_send(k, xx, zz, zz).wait_recv()
                gq_f[xx, :, z] += rz[zz, xx].astype(F32)

            @pl.loop(0, NY)
            def _(yy):
                k_s[yy * NX + xx] = gq_f[xx, yy, z].astype(BF16)

        @pl.loop(1, NY * NX)
        def _(k):
            yx_copy(plane_peer(k), y * NX + x).start()

    z_round(za, a_zs, a_zr, "recv")
    z_parts = za[...]
    ya[y * NX + x, 0:1] = lse_of(z_parts[:, 0:1])
    ya[y * NX + x, 1:2] = jnp.sum(z_parts[:, 1:2], axis=0)
    plane_round(ya, a_ys, a_yr, "start")

    core_copy(1).wait_recv()
    gi_out[...] = gi_part(core) + gi_core[1].astype(F32)
    gather_plane(1, qa, "send")
    plane_round(yb, b_ys, b_yr, "send")
    z_round(za, a_zs, a_zr, "send")
    core_copy(0).wait_send()
    core_copy(1).wait_send()
    far_copy().wait_recv()
    gi_out[...] += gi_far[...].astype(F32)
    stores = [
        pltpu.make_async_copy(source, target, out_sem.at[n])
        for n, (source, target) in enumerate(
            ((gi_out, gi_hbm), (loss_out, loss_hbm), (gq_out, gq_hbm))
        )
    ]
    stores[0].start()

    plane_round(ya, a_ys, a_yr, "recv")
    y_parts = ya[...]
    tops[...] = lse_of(y_parts[:, 0:1]) - jnp.sum(y_parts[:, 1:2], axis=0)
    mine = tops[:, pl.ds(pl.multiple_of((x * NY + y) * NZ * OWN, NZ * OWN), NZ * OWN)]
    pick_row = lax.broadcasted_iota(jnp.int32, (NZ * OWN, OWN), 0)
    pick_col = lax.broadcasted_iota(jnp.int32, (NZ * OWN, OWN), 1)
    pick = (pick_row == z * OWN + pick_col).astype(F32)
    loss_out[...] = jnp.dot(mine, pick, precision=HIGHEST, preferred_element_type=F32)
    stores[1].start()

    gq_out[...] = gq_f[x, y, z]

    @pl.when(core == 0)
    def _():
        @pl.loop(1, NZ * NX)
        def _(k):
            p = zx_peer(k)
            zx_copy(p, p).wait_recv()
            gq_out[...] += r2[p].astype(F32)

    @pl.when(core == 1)
    def _():
        @pl.loop(1, NY * NX)
        def _(k):
            p = plane_peer(k)
            yx_copy(p, p).wait_recv()
            gq_out[...] += r2[p].astype(F32)

    stores[2].start()

    plane_round(ya, a_ys, a_yr, "send")
    far_copy().wait_send()

    @pl.when(core == 0)
    def _():
        for xx in range(NX):
            @pl.loop(1, NY)
            def _(k):
                y_send(k, xx, y_peer(k), y).wait_send()

        @pl.loop(1, NZ * NX)
        def _(k):
            zx_copy(zx_peer(k), z * NX + x).wait_send()

    @pl.when(core == 1)
    def _():
        for xx in range(NX):
            @pl.loop(1, NZ)
            def _(k):
                z_send(k, xx, z_peer(k), z).wait_send()

        @pl.loop(1, NY * NX)
        def _(k):
            yx_copy(plane_peer(k), y * NX + x).wait_send()

    for store in stores:
        store.wait()


def hand_over(*refs):
    sources, targets, held, (in_sem, out_sem) = refs[:3], refs[3:6], refs[6:9], refs[9:]
    ways = list(zip(sources, held, targets))
    steps = QUARTER // PIECE
    parts = [tuple(r.at[pl.ds(n * PIECE, PIECE)] for r in ways[2]) for n in range(steps)]
    parts = parts + ways[:2]
    reads = [
        pltpu.make_async_copy(source, middle, in_sem.at[n])
        for n, (source, middle, target) in enumerate(parts)
    ]
    writes = [
        pltpu.make_async_copy(middle, target, out_sem.at[n])
        for n, (source, middle, target) in enumerate(parts)
    ]
    for read in reads:
        read.start()
    for read, write in zip(reads, writes):
        read.wait()
        write.start()
    for write in writes:
        write.wait()


def per_device(query_a, query_b, items, positive_a, positive_b, loss_cotangent):
    rows = items.shape[0]
    hbm = pl.BlockSpec(memory_space=pl.ANY)
    results = (
        jax.ShapeDtypeStruct((1, OWN), F32),
        jax.ShapeDtypeStruct((OWN, E), F32),
        jax.ShapeDtypeStruct((QUARTER, E), F32),
    )
    dma = pltpu.SemaphoreType.DMA
    block = (NX, NY, NZ, OWN, E)
    loss, gq, gi = pl.pallas_call(
        kernel,
        out_shape=results,
        in_specs=[hbm] * 6,
        out_specs=[hbm] * 3,
        scratch_shapes=[
            pltpu.VMEM((rows, E), BF16),
            pltpu.VMEM((E, rows), BF16),
            pltpu.VMEM(block, BF16),
            pltpu.VMEM(block, BF16),
            pltpu.VMEM((32, 128), jnp.int32),
            pltpu.VMEM((32, 128), jnp.int32),
            pltpu.VMEM((32, 128), F32),
            pltpu.VMEM((1, GROUP), jnp.int32),
            pltpu.VMEM((1, GROUP), jnp.int32),
            pltpu.VMEM((1, GROUP), F32),
            pltpu.VMEM((NX, rows, HALF), F32),
            pltpu.VMEM((rows, HALF), F32),
            pltpu.VMEM((rows, GROUP), BF16),
            pltpu.VMEM(block, F32),
            pltpu.VMEM(block, BF16),
            pltpu.VMEM((NY, NX, NZ, OWN, E), BF16),
            pltpu.VMEM((NZ, NX, NY, OWN, E), BF16),
            pltpu.VMEM((NZ * NX, OWN, E), BF16),
            pltpu.VMEM((NZ * NX, OWN, E), BF16),
            pltpu.VMEM((2 * QUARTER, E), F32),
            pltpu.VMEM((3, QUARTER, E), BF16),
            pltpu.VMEM((2, QUARTER, E), BF16),
            pltpu.VMEM((QUARTER, E), BF16),
            pltpu.VMEM((1, OWN), F32),
            pltpu.VMEM((OWN, E), F32),
            pltpu.VMEM((QUARTER, E), F32),
            pltpu.VMEM((NZ, 1, GROUP), F32),
            pltpu.VMEM((NY * NX, 1, GROUP), F32),
            pltpu.VMEM((NZ, 2, GROUP), F32),
            pltpu.VMEM((NY * NX, 2, GROUP), F32),
            pltpu.VMEM((1, GROUP), F32),
            dma((6,)),
            dma((3,)),
            dma((2, NZ)), dma((2, NZ)),
            dma((2, NY * NX)), dma((2, NY * NX)),
            dma((NZ,)), dma((NZ,)),
            dma((NY * NX,)), dma((NY * NX,)),
            dma((NZ,)), dma((NZ,)),
            dma((NY * NX,)), dma((NY * NX,)),
            dma((NX, NY)), dma((NX, NY)),
            dma((NX, NZ)), dma((NX, NZ)),
            dma((NZ * NX,)), dma((NZ * NX,)),
            dma((3,)), dma((3,)),
        ],
        compiler_params=pltpu.CompilerParams(
            collective_id=0, has_side_effects=True, vmem_limit_bytes=64 * 1024 * 1024
        ),
    )(
        query_a,
        query_b,
        items,
        positive_a.reshape(32, 128),
        positive_b.reshape(32, 128),
        loss_cotangent.reshape(32, 128),
    )
    pieces = QUARTER // PIECE + 2
    loss, gq, gi = pl.pallas_call(
        hand_over,
        out_shape=results,
        in_specs=[hbm] * 3,
        out_specs=[hbm] * 3,
        scratch_shapes=[pltpu.VMEM(r.shape, r.dtype) for r in results] + [dma((pieces,))] * 2,
        compiler_params=pltpu.CompilerParams(vmem_limit_bytes=64 * 1024 * 1024),
    )(loss, gq, gi)
    return loss.reshape(OWN), gq, gi


def solution(mesh):
    return jax.shard_map(
        per_device,
        mesh=mesh,
        in_specs=(
            P(("item", "user"), None),
            P(("item", "user"), None),
            P("item", None),
            P(),
            P(),
            P(),
        ),
        out_specs=(P(("item", "user")), P(("item", "user"), None), P(("item", "user"), None)),
        check_vma=False,
    )
```

```python
import functools

import jax
import jax.numpy as jnp
from jax import lax
from jax.experimental import pallas as pl
from jax.experimental.pallas import tpu as pltpu
from jax.sharding import PartitionSpec as P

MESH = pl.DeviceIdType.MESH
F32 = jnp.float32
BF16 = jnp.bfloat16
HIGHEST = lax.Precision.HIGHEST

NZ, NY, NX = 8, 4, 2
OWN = 16
E = 256
GROUP = NZ * NY * NX * OWN
HALF = GROUP // NX
TILE = 512
QUARTER = 512
PIECE = 128


def remote(src, dst, send_sem, recv_sem, device):
    return pltpu.make_async_remote_copy(
        src_ref=src,
        dst_ref=dst,
        send_sem=send_sem,
        recv_sem=recv_sem,
        device_id=device,
        device_id_type=MESH,
    )


def group_row(table, selector, row_of):
    picked = jnp.dot(table, selector, precision=HIGHEST, preferred_element_type=F32)
    rows = lax.broadcasted_iota(jnp.int32, picked.shape, 0)
    return jnp.sum(jnp.where(rows == row_of, picked, 0.0), axis=0, keepdims=True)


def lse_of(parts):
    top = jnp.max(parts, axis=0)
    return top + jnp.log(jnp.sum(jnp.exp(parts - top[None]), axis=0))


def act(copy, verb):
    if verb == "start":
        copy.start()
    elif verb == "send":
        copy.wait_send()
    else:
        copy.wait_recv()


def kernel(
    qa_in, qb_in, items_in, pa_in, pb_in, w_in,
    loss_hbm, gq_hbm, gi_hbm,
    items_v, items_t, qa, qb, pa_v, pb_v, w_v, pos_a, pos_b, weight,
    probs, score_a, dsc, gq_f, gq_s,
    ry, r2,
    gi_f, gi_s, gi_core, gi_relay, gi_far, loss_out, gq_out, gi_out,
    zb, yb, za, ya,
    tops,
    in_sem, out_sem, g_zs, g_zr, g_ps, g_pr,
    b_zs, b_zr, b_ys, b_yr, a_zs, a_zr, a_ys, a_yr,
    ys_s, ys_r, s2s, s2r, gi_ss, gi_rs, far_s, far_r,
):
    item = lax.axis_index("item")
    user = lax.axis_index("user")
    z, y, x = item // (NY * NX), (item // NX) % NY, item % NX
    far, core = user // 2, user % 2
    items_rows = items_v.shape[0]
    offset = item * items_rows

    def at(zz, yy, xx):
        return {"item": (zz * NY + yy) * NX + xx}

    def z_peer(k):
        return lax.rem(z + k, NZ)

    def y_peer(k):
        return lax.rem(y + k, NY)

    def plane_peer(k):
        return lax.rem(y * NX + x + k, NY * NX)

    loads = [
        pltpu.make_async_copy(source, target, in_sem.at[n])
        for n, (source, target) in enumerate(
            (
                (qb_in, qb.at[x, y, z]),
                (qa_in, qa.at[x, y, z]),
                (pa_in, pa_v),
                (pb_in, pb_v),
                (w_in, w_v),
                (items_in, items_v),
            )
        )
    ]

    barrier = pltpu.get_barrier_semaphore()

    @pl.loop(1, NZ)
    def _(k):
        pl.semaphore_signal(barrier, inc=1, device_id=at(z_peer(k), y, x), device_id_type=MESH)
        pl.semaphore_signal(barrier, inc=1, device_id=at(z_peer(k), y, 1 - x), device_id_type=MESH)

    @pl.loop(1, NY * NX)
    def _(k):
        p = plane_peer(k)
        pl.semaphore_signal(barrier, inc=1, device_id=at(z, p // NX, p % NX), device_id_type=MESH)

    other_core = {"user": far * 2 + 1 - core}
    other_far = {"item": (z * NY + y) * NX + 1 - x, "user": (1 - far) * 2 + core}
    next_x = lax.rem(far * NX + x + 1 + 2 * core, 4)
    next_chip = {"item": (z * NY + y) * NX + next_x % NX, "user": next_x // NX * 2 + core}
    pl.semaphore_signal(barrier, inc=1, device_id=other_core, device_id_type=MESH)
    pl.semaphore_signal(barrier, inc=1, device_id=other_far, device_id_type=MESH)

    for load in loads:
        load.start()
    loads[0].wait()
    loads[1].wait()

    pl.semaphore_wait(barrier, 2 * (NZ - 1) + (NY * NX - 1) + 2)

    def gather_z(n, q, verb):
        @pl.loop(1, NZ)
        def _(k):
            zz = z_peer(k)
            block = q.at[x, y, zz if verb == "recv" else z]
            source = zz if verb == "recv" else z
            copy = remote(block, block, g_zs.at[n, k], g_zr.at[n, source], at(zz, y, x))
            act(copy, verb)

    def plane_copy(n, q, yy, xx, source):
        block = q.at[source % NX, source // NX]
        place = yy * NX + xx
        return remote(block, block, g_ps.at[n, place], g_pr.at[n, source], at(z, yy, xx))

    def gather_plane(n, q, verb):
        mine = y * NX + x

        @pl.loop(1, NY)
        def _(k):
            act(plane_copy(n, q, y_peer(k), x, mine), verb)

        @pl.loop(0, NY)
        def _(k):
            act(plane_copy(n, q, y_peer(k), 1 - x, mine), verb)

    def gather_wait(n, q, xx, first):
        @pl.loop(first, NY)
        def _(k):
            yy = y_peer(k)
            plane_copy(n, q, yy, xx, yy * NX + xx).wait_recv()

    gather_z(0, qb, "start")
    gather_z(1, qa, "start")

    lanes = lax.broadcasted_iota(jnp.int32, (1, GROUP), 1)
    own_of = lanes % OWN
    z_of = (lanes // OWN) % NZ
    y_of = (lanes // (OWN * NZ)) % NY
    x_of = lanes // (OWN * NZ * NY)
    ks = lax.broadcasted_iota(jnp.int32, (128, GROUP), 0)
    selector = (ks == x_of * (4 * OWN) + user * OWN + own_of).astype(F32)
    row_of = z_of * NY + y_of
    for load in loads[2:5]:
        load.wait()
    pos_a[...] = group_row(pa_v[...].astype(F32), selector, row_of).astype(jnp.int32) - offset
    pos_b[...] = group_row(pb_v[...].astype(F32), selector, row_of).astype(jnp.int32) - offset
    weight[...] = group_row(w_v[...], selector, row_of)

    gather_z(0, qb, "recv")
    gather_plane(0, qb, "start")

    loads[5].wait()
    for part in range(items_rows // QUARTER):
        rows = pl.ds(part * QUARTER, QUARTER)
        items_t[:, rows] = items_v[rows, :].T
    gather_z(1, qa, "recv")

    tiles = items_rows // TILE

    def half_of(xx):
        return pl.ds(pl.multiple_of(xx * HALF, HALF), HALF)

    def tile_of(t):
        return pl.ds(pl.multiple_of(t * TILE, TILE), TILE)

    def fold(values, op):
        return op(values.reshape(TILE // 8, 8, HALF), axis=0)

    def scores(q, xx):
        users = q[xx].reshape(HALF, E)
        return lax.dot_general(
            items_v[...], users, (((1,), (1,)), ((), ())), preferred_element_type=F32
        )

    zero = jnp.zeros((8, HALF), F32)
    least = jnp.full((8, HALF), -jnp.inf, F32)

    def half_b(xx):
        probs[xx] = scores(qb, xx)

        def largest(t, top):
            return jnp.maximum(top, fold(probs[xx, tile_of(t), :], jnp.max))

        top = jnp.max(lax.fori_loop(0, tiles, largest, least), axis=0, keepdims=True)

        def exponentials(t, total):
            p = jnp.exp(probs[xx, tile_of(t), :] - top)
            probs[xx, tile_of(t), :] = p
            return total + fold(p, jnp.sum)

        total = jnp.sum(lax.fori_loop(0, tiles, exponentials, zero), axis=0, keepdims=True)
        tops[:, half_of(xx)] = top
        zb[z, :, half_of(xx)] = top + jnp.log(total)

    def half_a(xx):
        score_a[...] = scores(qa, xx)
        pos = pos_a[:, half_of(xx)]
        ids = lax.broadcasted_iota(jnp.int32, (TILE, HALF), 0)

        def largest(t, carry):
            top, hit = carry
            score = score_a[tile_of(t), :]
            match = jnp.where(ids == pos - t * TILE, score, 0.0)
            return jnp.maximum(top, fold(score, jnp.max)), hit + fold(match, jnp.sum)

        top, hit = lax.fori_loop(0, tiles, largest, (least, zero))
        top = jnp.max(top, axis=0, keepdims=True)

        def exponentials(t, total):
            return total + fold(jnp.exp(score_a[tile_of(t), :] - top), jnp.sum)

        total = jnp.sum(lax.fori_loop(0, tiles, exponentials, zero), axis=0, keepdims=True)
        za[z, 0:1, half_of(xx)] = top + jnp.log(total)
        za[z, 1:2, half_of(xx)] = jnp.sum(hit, axis=0, keepdims=True)

    def z_round(buf, ss, rs, verb):
        @pl.loop(1, NZ)
        def _(k):
            zz = z_peer(k)
            src = zz if verb == "recv" else z
            act(remote(buf.at[src], buf.at[src], ss.at[k], rs.at[src], at(zz, y, x)), verb)

    def plane_round(buf, ss, rs, verb):
        @pl.loop(1, NY * NX)
        def _(k):
            p = plane_peer(k)
            src = p if verb == "recv" else y * NX + x
            device = at(z, p // NX, p % NX)
            act(remote(buf.at[src], buf.at[src], ss.at[k], rs.at[src], device), verb)

    gather_wait(0, qb, x, 1)
    half_b(x)
    gather_wait(0, qb, 1 - x, 0)
    gather_plane(1, qa, "start")
    half_b(1 - x)
    z_round(zb, b_zs, b_zr, "start")
    gather_z(0, qb, "send")
    gather_z(1, qa, "send")
    gather_plane(0, qb, "send")
    z_round(zb, b_zs, b_zr, "recv")
    yb[y * NX + x] = lse_of(zb[...])
    plane_round(yb, b_ys, b_yr, "start")
    gather_wait(1, qa, x, 1)
    half_a(x)
    z_round(zb, b_zs, b_zr, "send")

    plane_round(yb, b_ys, b_yr, "recv")
    factor = weight[...] * jnp.exp(tops[...] - lse_of(yb[...]))

    ids = lax.broadcasted_iota(jnp.int32, (TILE, HALF), 0)

    def dscores(ff):
        @pl.loop(ff * 2 * QUARTER // TILE, (ff + 1) * 2 * QUARTER // TILE)
        def _(t):
            for xx in range(NX):
                cols = slice(xx * HALF, (xx + 1) * HALF)
                match = jnp.where(ids == pos_b[:, cols] - t * TILE, weight[:, cols], 0.0)
                score = probs[xx, tile_of(t), :] * factor[:, cols] - match
                dsc[tile_of(t), cols] = score.astype(BF16)

    def far_copy(hop, n):
        piece = pl.ds(pl.multiple_of(n * PIECE, PIECE), PIECE)
        source, target = (gi_s, gi_relay) if hop == 0 else (gi_relay, gi_far)
        return remote(
            source.at[piece], target.at[piece], far_s.at[hop, n], far_r.at[hop, n], next_chip
        )

    def core_copy(n):
        return remote(gi_f.at[n, 1 - core], gi_core.at[n], gi_ss.at[n], gi_rs.at[n], other_core)

    def item_grads(n, ff):
        rows = pl.ds(pl.multiple_of(ff * (2 * QUARTER), 2 * QUARTER), 2 * QUARTER)
        part = jnp.dot(dsc[rows, :], qb[...].reshape(GROUP, E), preferred_element_type=F32)
        gi_f[n] = part.reshape(2, QUARTER, E)
        core_copy(n).start()

    def y_send(k, xx, yy, src):
        return remote(
            gq_s.at[xx, yy], ry.at[src, xx], ys_s.at[xx, yy], ys_r.at[xx, src],
            at(z, y_peer(k), x),
        )

    def query_grads(xx):
        block = jnp.dot(
            items_t[...], dsc[:, xx * HALF : (xx + 1) * HALF], preferred_element_type=F32
        ).T.reshape(NY, NZ, OWN, E)
        gq_f[xx] = block
        gq_s[xx] = block.astype(BF16)

        @pl.loop(1, NY)
        def _(k):
            y_send(k, xx, y_peer(k), y).start()

    dscores(1 - far)
    item_grads(0, 1 - far)
    dscores(far)
    query_grads(0)
    core_copy(0).wait_recv()
    gi_s[...] = (gi_f[0, core] + gi_core[0]).astype(BF16)

    @pl.loop(0, QUARTER // PIECE)
    def _(n):
        far_copy(0, n).start()

    query_grads(1)
    item_grads(1, far)

    gather_wait(1, qa, 1 - x, 0)
    half_a(1 - x)
    z_round(za, a_zs, a_zr, "start")

    @pl.loop(0, QUARTER // PIECE)
    def _(n):
        far_copy(0, n).wait_recv()
        far_copy(1, n).start()

    def zx_copy(xx, zz, verb):
        slot = (xx, zz) if verb == "recv" else (x, z)
        act(
            remote(gq_f.at[xx, y, zz], r2.at[slot], s2s.at[xx, zz], s2r.at[slot], at(zz, y, xx)),
            verb,
        )

    def second_stage(xx, verb):
        @pl.loop(1, NZ)
        def _(k):
            zx_copy(xx, z_peer(k), verb)

        @pl.when(x != xx)
        def _():
            zx_copy(xx, z, verb)

    for half in range(NX):
        @pl.loop(1, NY)
        def _(k):
            yy = y_peer(k)
            y_send(k, half, yy, yy).wait_recv()
            gq_f[half, y] += ry[yy, half].astype(F32)

        second_stage(half, "start")

    z_round(za, a_zs, a_zr, "recv")
    z_parts = za[...]
    ya[y * NX + x, 0:1] = lse_of(z_parts[:, 0:1])
    ya[y * NX + x, 1:2] = jnp.sum(z_parts[:, 1:2], axis=0)
    plane_round(ya, a_ys, a_yr, "start")

    core_copy(1).wait_recv()
    gi_out[...] = gi_f[1, core] + gi_core[1]
    gather_plane(1, qa, "send")
    plane_round(yb, b_ys, b_yr, "send")
    z_round(za, a_zs, a_zr, "send")
    core_copy(0).wait_send()
    core_copy(1).wait_send()

    @pl.loop(0, QUARTER // PIECE)
    def _(n):
        piece = pl.ds(pl.multiple_of(n * PIECE, PIECE), PIECE)
        far_copy(1, n).wait_recv()
        gi_out[piece, :] += gi_far[piece, :].astype(F32)

    stores = [
        pltpu.make_async_copy(source, target, out_sem.at[n])
        for n, (source, target) in enumerate(
            ((gi_out, gi_hbm), (loss_out, loss_hbm), (gq_out, gq_hbm))
        )
    ]
    stores[0].start()

    plane_round(ya, a_ys, a_yr, "recv")
    y_parts = ya[...]
    tops[...] = lse_of(y_parts[:, 0:1]) - jnp.sum(y_parts[:, 1:2], axis=0)
    mine = tops[:, pl.ds(pl.multiple_of((x * NY + y) * NZ * OWN, NZ * OWN), NZ * OWN)]
    pick_row = lax.broadcasted_iota(jnp.int32, (NZ * OWN, OWN), 0)
    pick_col = lax.broadcasted_iota(jnp.int32, (NZ * OWN, OWN), 1)
    pick = (pick_row == z * OWN + pick_col).astype(F32)
    loss_out[...] = jnp.dot(mine, pick, precision=HIGHEST, preferred_element_type=F32)
    stores[1].start()

    gq_out[...] = gq_f[x, y, z]

    for half in range(NX):
        @pl.loop(1, NZ)
        def _(k):
            zz = z_peer(k)
            zx_copy(half, zz, "recv")
            gq_out[...] += r2[half, zz]

        @pl.when(x != half)
        def _():
            zx_copy(half, z, "recv")
            gq_out[...] += r2[half, z]

    stores[2].start()

    plane_round(ya, a_ys, a_yr, "send")

    @pl.loop(0, QUARTER // PIECE)
    def _(n):
        far_copy(0, n).wait_send()
        far_copy(1, n).wait_send()

    for half in range(NX):
        @pl.loop(1, NY)
        def _(k):
            y_send(k, half, y_peer(k), y).wait_send()

        second_stage(half, "send")

    for store in stores:
        store.wait()


def hand_over(*refs):
    sources, targets, held, (in_sem, out_sem) = refs[:3], refs[3:6], refs[6:9], refs[9:]
    ways = list(zip(sources, held, targets))
    steps = QUARTER // PIECE
    parts = [tuple(r.at[pl.ds(n * PIECE, PIECE)] for r in ways[2]) for n in range(steps)]
    parts = parts + ways[:2]
    reads = [
        pltpu.make_async_copy(source, middle, in_sem.at[n])
        for n, (source, middle, target) in enumerate(parts)
    ]
    writes = [
        pltpu.make_async_copy(middle, target, out_sem.at[n])
        for n, (source, middle, target) in enumerate(parts)
    ]
    for read in reads:
        read.start()
    for read, write in zip(reads, writes):
        read.wait()
        write.start()
    for write in writes:
        write.wait()


def per_device(query_a, query_b, items, positive_a, positive_b, loss_cotangent):
    rows = items.shape[0]
    hbm = pl.BlockSpec(memory_space=pl.ANY)
    results = (
        jax.ShapeDtypeStruct((1, OWN), F32),
        jax.ShapeDtypeStruct((OWN, E), F32),
        jax.ShapeDtypeStruct((QUARTER, E), F32),
    )
    dma = pltpu.SemaphoreType.DMA
    block = (NX, NY, NZ, OWN, E)
    loss, gq, gi = pl.pallas_call(
        kernel,
        out_shape=results,
        in_specs=[hbm] * 6,
        out_specs=[hbm] * 3,
        scratch_shapes=[
            pltpu.VMEM((rows, E), BF16),
            pltpu.VMEM((E, rows), BF16),
            pltpu.VMEM(block, BF16),
            pltpu.VMEM(block, BF16),
            pltpu.VMEM((32, 128), jnp.int32),
            pltpu.VMEM((32, 128), jnp.int32),
            pltpu.VMEM((32, 128), F32),
            pltpu.VMEM((1, GROUP), jnp.int32),
            pltpu.VMEM((1, GROUP), jnp.int32),
            pltpu.VMEM((1, GROUP), F32),
            pltpu.VMEM((NX, rows, HALF), F32),
            pltpu.VMEM((rows, HALF), F32),
            pltpu.VMEM((rows, GROUP), BF16),
            pltpu.VMEM(block, F32),
            pltpu.VMEM(block, BF16),
            pltpu.VMEM((NY, NX, NZ, OWN, E), BF16),
            pltpu.VMEM((NX, NZ, OWN, E), F32),
            pltpu.VMEM((2, 2, QUARTER, E), F32),
            pltpu.VMEM((QUARTER, E), BF16),
            pltpu.VMEM((2, QUARTER, E), F32),
            pltpu.VMEM((QUARTER, E), BF16),
            pltpu.VMEM((QUARTER, E), BF16),
            pltpu.VMEM((1, OWN), F32),
            pltpu.VMEM((OWN, E), F32),
            pltpu.VMEM((QUARTER, E), F32),
            pltpu.VMEM((NZ, 1, GROUP), F32),
            pltpu.VMEM((NY * NX, 1, GROUP), F32),
            pltpu.VMEM((NZ, 2, GROUP), F32),
            pltpu.VMEM((NY * NX, 2, GROUP), F32),
            pltpu.VMEM((1, GROUP), F32),
            dma((6,)),
            dma((3,)),
            dma((2, NZ)), dma((2, NZ)),
            dma((2, NY * NX)), dma((2, NY * NX)),
            dma((NZ,)), dma((NZ,)),
            dma((NY * NX,)), dma((NY * NX,)),
            dma((NZ,)), dma((NZ,)),
            dma((NY * NX,)), dma((NY * NX,)),
            dma((NX, NY)), dma((NX, NY)),
            dma((NX, NZ)), dma((NX, NZ)),
            dma((2,)), dma((2,)),
            dma((2, QUARTER // PIECE)), dma((2, QUARTER // PIECE)),
        ],
        compiler_params=pltpu.CompilerParams(
            collective_id=0, has_side_effects=True, vmem_limit_bytes=64 * 1024 * 1024
        ),
    )(
        query_a,
        query_b,
        items,
        positive_a.reshape(32, 128),
        positive_b.reshape(32, 128),
        loss_cotangent.reshape(32, 128),
    )
    pieces = QUARTER // PIECE + 2
    loss, gq, gi = pl.pallas_call(
        hand_over,
        out_shape=results,
        in_specs=[hbm] * 3,
        out_specs=[hbm] * 3,
        scratch_shapes=[pltpu.VMEM(r.shape, r.dtype) for r in results] + [dma((pieces,))] * 2,
        compiler_params=pltpu.CompilerParams(vmem_limit_bytes=64 * 1024 * 1024),
    )(loss, gq, gi)
    return loss.reshape(OWN), gq, gi


def solution(mesh):
    return jax.shard_map(
        per_device,
        mesh=mesh,
        in_specs=(
            P(("item", "user"), None),
            P(("item", "user"), None),
            P("item", None),
            P(),
            P(),
            P(),
        ),
        out_specs=(P(("item", "user")), P(("item", "user"), None), P(("item", "user"), None)),
        check_vma=False,
    )
```

```python
import functools

import jax
import jax.numpy as jnp
from jax import lax
from jax.experimental import pallas as pl
from jax.experimental.pallas import tpu as pltpu
from jax.sharding import PartitionSpec as P

MESH = pl.DeviceIdType.MESH
F32 = jnp.float32
BF16 = jnp.bfloat16
HIGHEST = lax.Precision.HIGHEST

NZ, NY, NX = 8, 4, 2
OWN = 16
E = 256
GROUP = NZ * NY * NX * OWN
HALF = GROUP // NX
TILE = 512
QUARTER = 512
PIECE = 128


def remote(src, dst, send_sem, recv_sem, device):
    return pltpu.make_async_remote_copy(
        src_ref=src,
        dst_ref=dst,
        send_sem=send_sem,
        recv_sem=recv_sem,
        device_id=device,
        device_id_type=MESH,
    )


def group_row(table, selector, row_of):
    picked = jnp.dot(table, selector, precision=HIGHEST, preferred_element_type=F32)
    rows = lax.broadcasted_iota(jnp.int32, picked.shape, 0)
    return jnp.sum(jnp.where(rows == row_of, picked, 0.0), axis=0, keepdims=True)


def lse_of(parts):
    top = jnp.max(parts, axis=0)
    return top + jnp.log(jnp.sum(jnp.exp(parts - top[None]), axis=0))


def kernel(
    qa_in, qb_in, items_in, pa_in, pb_in, w_in,
    loss_hbm, gq_hbm, gi_hbm,
    items_v, items_t, qa, qb, pa_v, pb_v, w_v, pos_a, pos_b, weight,
    probs, score_a, dsc, gq_f, gq_s,
    r1, gq_h, r2,
    gi_f, gi_s, gi_core, gi_relay, gi_far, loss_out, gq_out, gi_out,
    zb, yb, za, ya,
    tops,
    in_sem, out_sem, g_zs, g_zr, g_ps, g_pr,
    b_zs, b_zr, b_ys, b_yr, a_zs, a_zr, a_ys, a_yr,
    s1s, s1r, s2s, s2r, gi_ss, gi_rs, far_s, far_r,
):
    item = lax.axis_index("item")
    user = lax.axis_index("user")
    z, y, x = item // (NY * NX), (item // NX) % NY, item % NX
    place = y * NX + x
    far, core = user // 2, user % 2
    items_rows = items_v.shape[0]
    offset = item * items_rows

    def at(zz, yy, xx):
        return {"item": (zz * NY + yy) * NX + xx}

    def z_peer(k):
        return lax.rem(z + k, NZ)

    def y_peer(k):
        return lax.rem(y + k, NY)

    def plane_peer(k):
        return lax.rem(place + k, NY * NX)

    loads = [
        pltpu.make_async_copy(source, target, in_sem.at[n])
        for n, (source, target) in enumerate(
            (
                (qb_in, qb.at[x, y, z]),
                (qa_in, qa.at[x, y, z]),
                (pa_in, pa_v),
                (pb_in, pb_v),
                (w_in, w_v),
                (items_in, items_v),
            )
        )
    ]

    barrier = pltpu.get_barrier_semaphore()

    @pl.loop(1, NZ)
    def _(k):
        pl.semaphore_signal(barrier, inc=1, device_id=at(z_peer(k), y, x), device_id_type=MESH)
        pl.semaphore_signal(barrier, inc=1, device_id=at(z_peer(k), y, 1 - x), device_id_type=MESH)

    @pl.loop(1, NY * NX)
    def _(k):
        p = plane_peer(k)
        pl.semaphore_signal(barrier, inc=1, device_id=at(z, p // NX, p % NX), device_id_type=MESH)

    other_core = {"user": far * 2 + 1 - core}
    other_far = {"item": (z * NY + y) * NX + 1 - x, "user": (1 - far) * 2 + core}
    next_x = lax.rem(far * NX + x + 1 + 2 * core, 4)
    next_chip = {"item": (z * NY + y) * NX + next_x % NX, "user": next_x // NX * 2 + core}
    pl.semaphore_signal(barrier, inc=1, device_id=other_core, device_id_type=MESH)
    pl.semaphore_signal(barrier, inc=1, device_id=other_far, device_id_type=MESH)

    for load in loads:
        load.start()

    pl.semaphore_wait(barrier, 2 * (NZ - 1) + (NY * NX - 1) + 2)

    def sent(refs, send_sem, recv_sem):
        remote(refs, refs, send_sem, recv_sem, other_core).wait_send()

    def arrived(refs, send_sem, recv_sem):
        remote(refs, refs, send_sem, recv_sem, other_core).wait_recv()

    def gather_z(n, q, source):
        @pl.loop(1, NZ)
        def _(k):
            target = at(z_peer(k), y, x)
            remote(source, q.at[x, y, z], g_zs.at[n], g_zr.at[n], target).start()

    def gather_plane(n, q):
        block = q.at[x, y]

        @pl.loop(1, NY)
        def _(k):
            remote(block, block, g_ps.at[n], g_pr.at[n, x], at(z, y_peer(k), x)).start()

        @pl.loop(0, NY)
        def _(k):
            remote(block, block, g_ps.at[n], g_pr.at[n, x], at(z, y_peer(k), 1 - x)).start()

    def gather_z_wait(n, q):
        arrived(q.at[x, y, pl.ds(0, NZ - 1)], g_zs.at[n], g_zr.at[n])

    def gather_own_wait(n, q):
        arrived(q.at[x, pl.ds(0, NY - 1)], g_ps.at[n], g_pr.at[n, x])

    def gather_other_wait(n, q):
        arrived(q.at[1 - x], g_ps.at[n], g_pr.at[n, 1 - x])

    def gather_z_drain(n, q):
        sent(q.at[x, y, pl.ds(0, NZ - 1)], g_zs.at[n], g_zr.at[n])

    def gather_plane_drain(n, q):
        sent(q.at[x], g_ps.at[n], g_pr.at[n, 0])
        sent(q.at[x, pl.ds(0, NY - 1)], g_ps.at[n], g_pr.at[n, 0])

    gather_z(0, qb, qb_in)
    gather_z(1, qa, qa_in)

    lanes = lax.broadcasted_iota(jnp.int32, (1, GROUP), 1)
    own_of = lanes % OWN
    z_of = (lanes // OWN) % NZ
    y_of = (lanes // (OWN * NZ)) % NY
    x_of = lanes // (OWN * NZ * NY)
    ks = lax.broadcasted_iota(jnp.int32, (128, GROUP), 0)
    selector = (ks == x_of * (4 * OWN) + user * OWN + own_of).astype(F32)
    row_of = z_of * NY + y_of
    for load in loads[2:5]:
        load.wait()
    pos_a[...] = group_row(pa_v[...].astype(F32), selector, row_of).astype(jnp.int32) - offset
    pos_b[...] = group_row(pb_v[...].astype(F32), selector, row_of).astype(jnp.int32) - offset
    weight[...] = group_row(w_v[...], selector, row_of)

    loads[0].wait()
    gather_z_wait(0, qb)
    gather_plane(0, qb)

    loads[5].wait()
    for part in range(items_rows // QUARTER):
        rows = pl.ds(part * QUARTER, QUARTER)
        items_t[:, rows] = items_v[rows, :].T
    loads[1].wait()
    gather_z_wait(1, qa)

    tiles = items_rows // TILE

    def half_of(xx):
        return pl.ds(pl.multiple_of(xx * HALF, HALF), HALF)

    def tile_of(t):
        return pl.ds(pl.multiple_of(t * TILE, TILE), TILE)

    def fold(values, op):
        return op(values.reshape(TILE // 8, 8, HALF), axis=0)

    def scores(q, xx):
        users = q[xx].reshape(HALF, E)
        return lax.dot_general(
            items_v[...], users, (((1,), (1,)), ((), ())), preferred_element_type=F32
        )

    zero = jnp.zeros((8, HALF), F32)
    least = jnp.full((8, HALF), -jnp.inf, F32)

    def half_b(xx):
        probs[xx] = scores(qb, xx)

        def largest(t, top):
            return jnp.maximum(top, fold(probs[xx, tile_of(t), :], jnp.max))

        top = jnp.max(lax.fori_loop(0, tiles, largest, least), axis=0, keepdims=True)

        def exponentials(t, total):
            p = jnp.exp(probs[xx, tile_of(t), :] - top)
            probs[xx, tile_of(t), :] = p
            return total + fold(p, jnp.sum)

        total = jnp.sum(lax.fori_loop(0, tiles, exponentials, zero), axis=0, keepdims=True)
        tops[:, half_of(xx)] = top
        zb[z, :, half_of(xx)] = top + jnp.log(total)

    def half_a(xx):
        score_a[...] = scores(qa, xx)
        pos = pos_a[:, half_of(xx)]
        ids = lax.broadcasted_iota(jnp.int32, (TILE, HALF), 0)

        def largest(t, carry):
            top, hit = carry
            score = score_a[tile_of(t), :]
            match = jnp.where(ids == pos - t * TILE, score, 0.0)
            return jnp.maximum(top, fold(score, jnp.max)), hit + fold(match, jnp.sum)

        top, hit = lax.fori_loop(0, tiles, largest, (least, zero))
        top = jnp.max(top, axis=0, keepdims=True)

        def exponentials(t, total):
            return total + fold(jnp.exp(score_a[tile_of(t), :] - top), jnp.sum)

        total = jnp.sum(lax.fori_loop(0, tiles, exponentials, zero), axis=0, keepdims=True)
        za[z, 0:1, half_of(xx)] = top + jnp.log(total)
        za[z, 1:2, half_of(xx)] = jnp.sum(hit, axis=0, keepdims=True)

    def z_round(buf, ss, rs):
        @pl.loop(1, NZ)
        def _(k):
            remote(buf.at[z], buf.at[z], ss, rs, at(z_peer(k), y, x)).start()

    def plane_round(buf, ss, rs):
        @pl.loop(1, NY * NX)
        def _(k):
            p = plane_peer(k)
            remote(buf.at[place], buf.at[place], ss, rs, at(z, p // NX, p % NX)).start()

    others = pl.ds(0, NZ - 1)

    gather_own_wait(0, qb)
    half_b(x)
    gather_other_wait(0, qb)
    gather_plane(1, qa)
    half_b(1 - x)
    z_round(zb, b_zs, b_zr)
    gather_z_drain(0, qb)
    gather_z_drain(1, qa)
    gather_plane_drain(0, qb)
    arrived(zb.at[others], b_zs, b_zr)
    yb[place] = lse_of(zb[...])
    plane_round(yb, b_ys, b_yr)
    gather_own_wait(1, qa)
    half_a(x)
    sent(zb.at[others], b_zs, b_zr)

    arrived(yb.at[others], b_ys, b_yr)
    factor = weight[...] * jnp.exp(tops[...] - lse_of(yb[...]))

    ids = lax.broadcasted_iota(jnp.int32, (TILE, HALF), 0)

    def dscores(ff):
        @pl.loop(ff * 2 * QUARTER // TILE, (ff + 1) * 2 * QUARTER // TILE)
        def _(t):
            for xx in range(NX):
                cols = slice(xx * HALF, (xx + 1) * HALF)
                match = jnp.where(ids == pos_b[:, cols] - t * TILE, weight[:, cols], 0.0)
                score = probs[xx, tile_of(t), :] * factor[:, cols] - match
                dsc[tile_of(t), cols] = score.astype(BF16)

    def far_copy(hop, n):
        piece = pl.ds(pl.multiple_of(n * PIECE, PIECE), PIECE)
        source, target = (gi_s, gi_relay) if hop == 0 else (gi_relay, gi_far)
        return remote(
            source.at[piece], target.at[piece], far_s.at[hop, n], far_r.at[hop, n], next_chip
        )

    def core_copy(n):
        return remote(gi_f.at[n, 1 - core], gi_core.at[n], gi_ss.at[n], gi_rs.at[n], other_core)

    def item_grads(n, ff):
        rows = pl.ds(pl.multiple_of(ff * (2 * QUARTER), 2 * QUARTER), 2 * QUARTER)
        part = jnp.dot(dsc[rows, :], qb[...].reshape(GROUP, E), preferred_element_type=F32)
        gi_f[n] = part.reshape(2, QUARTER, E)
        core_copy(n).start()

    def query_grads(xx):
        block = jnp.dot(
            items_t[...], dsc[:, xx * HALF : (xx + 1) * HALF], preferred_element_type=F32
        ).T.reshape(NY, NZ, OWN, E)
        gq_f[xx] = block
        gq_s[xx] = block.astype(BF16)

        @pl.loop(1, NY)
        def _(k):
            yy = y_peer(k)
            remote(gq_s.at[xx, yy], r1.at[place], s1s, s1r, at(z, yy, xx)).start()

        @pl.when(x != xx)
        def _():
            remote(gq_s.at[xx, y], r1.at[place], s1s, s1r, at(z, y, xx)).start()

    dscores(1 - far)
    item_grads(0, 1 - far)
    dscores(far)
    query_grads(0)
    core_copy(0).wait_recv()
    gi_s[...] = (gi_f[0, core] + gi_core[0]).astype(BF16)

    @pl.loop(0, QUARTER // PIECE)
    def _(n):
        far_copy(0, n).start()

    query_grads(1)
    item_grads(1, far)

    gather_other_wait(1, qa)
    half_a(1 - x)
    z_round(za, a_zs, a_zr)

    @pl.loop(0, QUARTER // PIECE)
    def _(n):
        far_copy(0, n).wait_recv()
        far_copy(1, n).start()

    r1[place] = jnp.zeros((NZ, OWN, E), BF16)
    r2[z] = jnp.zeros((OWN, E), F32)
    arrived(r1.at[others], s1s, s1r)
    gq_h[...] = gq_f[x, y] + jnp.sum(r1[...].astype(F32), axis=0)

    @pl.loop(1, NZ)
    def _(k):
        zz = z_peer(k)
        remote(gq_h.at[zz], r2.at[z], s2s, s2r, at(zz, y, x)).start()

    arrived(za.at[others], a_zs, a_zr)
    z_parts = za[...]
    ya[place, 0:1] = lse_of(z_parts[:, 0:1])
    ya[place, 1:2] = jnp.sum(z_parts[:, 1:2], axis=0)
    plane_round(ya, a_ys, a_yr)

    core_copy(1).wait_recv()
    gi_out[...] = gi_f[1, core] + gi_core[1]
    gather_plane_drain(1, qa)
    sent(yb.at[others], b_ys, b_yr)
    sent(za.at[others], a_zs, a_zr)
    sent(r1.at[others], s1s, s1r)
    core_copy(0).wait_send()
    core_copy(1).wait_send()

    @pl.loop(0, QUARTER // PIECE)
    def _(n):
        far_copy(0, n).wait_send()

    @pl.loop(0, QUARTER // PIECE)
    def _(n):
        piece = pl.ds(pl.multiple_of(n * PIECE, PIECE), PIECE)
        far_copy(1, n).wait_recv()
        gi_out[piece, :] += gi_far[piece, :].astype(F32)

    stores = [
        pltpu.make_async_copy(source, target, out_sem.at[n])
        for n, (source, target) in enumerate(
            ((gi_out, gi_hbm), (loss_out, loss_hbm), (gq_out, gq_hbm))
        )
    ]
    stores[0].start()

    arrived(ya.at[others], a_ys, a_yr)
    y_parts = ya[...]
    tops[...] = lse_of(y_parts[:, 0:1]) - jnp.sum(y_parts[:, 1:2], axis=0)
    mine = tops[:, pl.ds(pl.multiple_of((x * NY + y) * NZ * OWN, NZ * OWN), NZ * OWN)]
    pick_row = lax.broadcasted_iota(jnp.int32, (NZ * OWN, OWN), 0)
    pick_col = lax.broadcasted_iota(jnp.int32, (NZ * OWN, OWN), 1)
    pick = (pick_row == z * OWN + pick_col).astype(F32)
    loss_out[...] = jnp.dot(mine, pick, precision=HIGHEST, preferred_element_type=F32)
    stores[1].start()

    arrived(r2.at[others], s2s, s2r)
    gq_out[...] = gq_h[z] + jnp.sum(r2[...], axis=0)
    stores[2].start()

    sent(ya.at[others], a_ys, a_yr)
    sent(r2.at[others], s2s, s2r)

    @pl.loop(0, QUARTER // PIECE)
    def _(n):
        far_copy(1, n).wait_send()

    for store in stores:
        store.wait()


def hand_over(*refs):
    sources, targets, held, (in_sem, out_sem) = refs[:3], refs[3:6], refs[6:9], refs[9:]
    ways = list(zip(sources, held, targets))
    steps = QUARTER // PIECE
    parts = [tuple(r.at[pl.ds(n * PIECE, PIECE)] for r in ways[2]) for n in range(steps)]
    parts = parts + ways[:2]
    reads = [
        pltpu.make_async_copy(source, middle, in_sem.at[n])
        for n, (source, middle, target) in enumerate(parts)
    ]
    writes = [
        pltpu.make_async_copy(middle, target, out_sem.at[n])
        for n, (source, middle, target) in enumerate(parts)
    ]
    for read in reads:
        read.start()
    for read, write in zip(reads, writes):
        read.wait()
        write.start()
    for write in writes:
        write.wait()


def per_device(query_a, query_b, items, positive_a, positive_b, loss_cotangent):
    rows = items.shape[0]
    hbm = pl.BlockSpec(memory_space=pl.ANY)
    results = (
        jax.ShapeDtypeStruct((1, OWN), F32),
        jax.ShapeDtypeStruct((OWN, E), F32),
        jax.ShapeDtypeStruct((QUARTER, E), F32),
    )
    dma = pltpu.SemaphoreType.DMA
    block = (NX, NY, NZ, OWN, E)
    loss, gq, gi = pl.pallas_call(
        kernel,
        out_shape=results,
        in_specs=[hbm] * 6,
        out_specs=[hbm] * 3,
        scratch_shapes=[
            pltpu.VMEM((rows, E), BF16),
            pltpu.VMEM((E, rows), BF16),
            pltpu.VMEM(block, BF16),
            pltpu.VMEM(block, BF16),
            pltpu.VMEM((32, 128), jnp.int32),
            pltpu.VMEM((32, 128), jnp.int32),
            pltpu.VMEM((32, 128), F32),
            pltpu.VMEM((1, GROUP), jnp.int32),
            pltpu.VMEM((1, GROUP), jnp.int32),
            pltpu.VMEM((1, GROUP), F32),
            pltpu.VMEM((NX, rows, HALF), F32),
            pltpu.VMEM((rows, HALF), F32),
            pltpu.VMEM((rows, GROUP), BF16),
            pltpu.VMEM(block, F32),
            pltpu.VMEM(block, BF16),
            pltpu.VMEM((NY * NX, NZ, OWN, E), BF16),
            pltpu.VMEM((NZ, OWN, E), F32),
            pltpu.VMEM((NZ, OWN, E), F32),
            pltpu.VMEM((2, 2, QUARTER, E), F32),
            pltpu.VMEM((QUARTER, E), BF16),
            pltpu.VMEM((2, QUARTER, E), F32),
            pltpu.VMEM((QUARTER, E), BF16),
            pltpu.VMEM((QUARTER, E), BF16),
            pltpu.VMEM((1, OWN), F32),
            pltpu.VMEM((OWN, E), F32),
            pltpu.VMEM((QUARTER, E), F32),
            pltpu.VMEM((NZ, 1, GROUP), F32),
            pltpu.VMEM((NY * NX, 1, GROUP), F32),
            pltpu.VMEM((NZ, 2, GROUP), F32),
            pltpu.VMEM((NY * NX, 2, GROUP), F32),
            pltpu.VMEM((1, GROUP), F32),
            dma((6,)),
            dma((3,)),
            dma((2,)), dma((2,)),
            dma((2,)), dma((2, NX)),
            dma, dma,
            dma, dma,
            dma, dma,
            dma, dma,
            dma, dma,
            dma, dma,
            dma((2,)), dma((2,)),
            dma((2, QUARTER // PIECE)), dma((2, QUARTER // PIECE)),
        ],
        compiler_params=pltpu.CompilerParams(
            collective_id=0, has_side_effects=True, vmem_limit_bytes=64 * 1024 * 1024
        ),
    )(
        query_a,
        query_b,
        items,
        positive_a.reshape(32, 128),
        positive_b.reshape(32, 128),
        loss_cotangent.reshape(32, 128),
    )
    pieces = QUARTER // PIECE + 2
    loss, gq, gi = pl.pallas_call(
        hand_over,
        out_shape=results,
        in_specs=[hbm] * 3,
        out_specs=[hbm] * 3,
        scratch_shapes=[pltpu.VMEM(r.shape, r.dtype) for r in results] + [dma((pieces,))] * 2,
        compiler_params=pltpu.CompilerParams(vmem_limit_bytes=64 * 1024 * 1024),
    )(loss, gq, gi)
    return loss.reshape(OWN), gq, gi


def solution(mesh):
    return jax.shard_map(
        per_device,
        mesh=mesh,
        in_specs=(
            P(("item", "user"), None),
            P(("item", "user"), None),
            P("item", None),
            P(),
            P(),
            P(),
        ),
        out_specs=(P(("item", "user")), P(("item", "user"), None), P(("item", "user"), None)),
        check_vma=False,
    )
```

```python
import functools

import jax
import jax.numpy as jnp
from jax import lax
from jax.experimental import pallas as pl
from jax.experimental.pallas import tpu as pltpu
from jax.sharding import PartitionSpec as P

MESH = pl.DeviceIdType.MESH
F32 = jnp.float32
BF16 = jnp.bfloat16
HIGHEST = lax.Precision.HIGHEST

NZ, NY, NX = 8, 4, 2
OWN = 16
E = 256
GROUP = NZ * NY * NX * OWN
HALF = GROUP // NX
TILE = 512
QUARTER = 512
PIECE = 128


def remote(src, dst, send_sem, recv_sem, device):
    return pltpu.make_async_remote_copy(
        src_ref=src,
        dst_ref=dst,
        send_sem=send_sem,
        recv_sem=recv_sem,
        device_id=device,
        device_id_type=MESH,
    )


def group_row(table, selector, row_of):
    picked = jnp.dot(table, selector, precision=HIGHEST, preferred_element_type=F32)
    rows = lax.broadcasted_iota(jnp.int32, picked.shape, 0)
    return jnp.sum(jnp.where(rows == row_of, picked, 0.0), axis=0, keepdims=True)


def lse_of(parts):
    top = jnp.max(parts, axis=0)
    return top + jnp.log(jnp.sum(jnp.exp(parts - top[None]), axis=0))


def kernel(
    qa_in, qb_in, items_in, pa_in, pb_in, w_in,
    loss_hbm, gq_hbm, gi_hbm,
    items_v, items_t, qa, qb, pa_v, pb_v, w_v, pos_a, pos_b, weight,
    probs, score_a, dsc, gq_f, gq_s,
    r1, gq_h, r2,
    gi_f, gi_s, gi_core, gi_relay, gi_far, loss_out, gq_out, gi_out,
    zb, yb, za, ya,
    tops,
    in_sem, out_sem, b1_s, b1_r, b2_s, b2_r, a1_s, a1_r, a2_s, a2_r,
    b_zs, b_zr, b_ys, b_yr, a_zs, a_zr, a_ys, a_yr,
    s1s, s1r, s2s, s2r, gi_ss, gi_rs, far_s, far_r,
):
    item = lax.axis_index("item")
    user = lax.axis_index("user")
    z, y, x = item // (NY * NX), (item // NX) % NY, item % NX
    place = y * NX + x
    far, core = user // 2, user % 2
    items_rows = items_v.shape[0]
    offset = item * items_rows

    def at(zz, yy, xx):
        return {"item": (zz * NY + yy) * NX + xx}

    def z_peer(k):
        return lax.rem(z + k, NZ)

    def y_peer(k):
        return lax.rem(y + k, NY)

    def plane_peer(k):
        return lax.rem(place + k, NY * NX)

    loads = [
        pltpu.make_async_copy(source, target, in_sem.at[n])
        for n, (source, target) in enumerate(
            (
                (qb_in, qb.at[x, y, z]),
                (qa_in, qa.at[x, y, z]),
                (pa_in, pa_v),
                (pb_in, pb_v),
                (w_in, w_v),
                (items_in, items_v),
            )
        )
    ]

    barrier = pltpu.get_barrier_semaphore()

    @pl.loop(1, NZ)
    def _(k):
        pl.semaphore_signal(barrier, inc=1, device_id=at(z_peer(k), y, x), device_id_type=MESH)
        pl.semaphore_signal(barrier, inc=1, device_id=at(z_peer(k), y, 1 - x), device_id_type=MESH)

    @pl.loop(1, NY * NX)
    def _(k):
        p = plane_peer(k)
        pl.semaphore_signal(barrier, inc=1, device_id=at(z, p // NX, p % NX), device_id_type=MESH)

    other_core = {"user": far * 2 + 1 - core}
    other_far = {"item": (z * NY + y) * NX + 1 - x, "user": (1 - far) * 2 + core}
    next_x = lax.rem(far * NX + x + 1 + 2 * core, 4)
    next_chip = {"item": (z * NY + y) * NX + next_x % NX, "user": next_x // NX * 2 + core}
    pl.semaphore_signal(barrier, inc=1, device_id=other_core, device_id_type=MESH)
    pl.semaphore_signal(barrier, inc=1, device_id=other_far, device_id_type=MESH)

    for load in loads:
        load.start()

    pl.semaphore_wait(barrier, 2 * (NZ - 1) + (NY * NX - 1) + 2)

    def sent(refs, send_sem, recv_sem):
        remote(refs, refs, send_sem, recv_sem, other_core).wait_send()

    def arrived(refs, send_sem, recv_sem):
        remote(refs, refs, send_sem, recv_sem, other_core).wait_recv()

    @pl.loop(1, NZ)
    def _(k):
        remote(qb_in, qb.at[x, y, z], b1_s, b1_r, at(z_peer(k), y, x)).start()

    def gather_b_bulk():
        block = qb.at[x, y]

        @pl.loop(1, NY)
        def _(k):
            remote(block, block, b2_s, b2_r.at[x], at(z, y_peer(k), x)).start()

        @pl.loop(0, NY)
        def _(k):
            remote(block, block, b2_s, b2_r.at[x], at(z, y_peer(k), 1 - x)).start()

    @pl.loop(1, NY * NX)
    def _(k):
        p = plane_peer(k)
        remote(qa_in, qa.at[x, y, z], a1_s, a1_r, at(z, p // NX, p % NX)).start()

    def gather_a_bulk(xx):
        block = qa.at[xx, :, z]

        @pl.loop(1, NZ)
        def _(k):
            remote(block, block, a2_s, a2_r.at[xx], at(z_peer(k), y, x)).start()

    others = pl.ds(0, NZ - 1)

    lanes = lax.broadcasted_iota(jnp.int32, (1, GROUP), 1)
    own_of = lanes % OWN
    z_of = (lanes // OWN) % NZ
    y_of = (lanes // (OWN * NZ)) % NY
    x_of = lanes // (OWN * NZ * NY)
    ks = lax.broadcasted_iota(jnp.int32, (128, GROUP), 0)
    selector = (ks == x_of * (4 * OWN) + user * OWN + own_of).astype(F32)
    row_of = z_of * NY + y_of
    for load in loads[2:5]:
        load.wait()
    pos_a[...] = group_row(pa_v[...].astype(F32), selector, row_of).astype(jnp.int32) - offset
    pos_b[...] = group_row(pb_v[...].astype(F32), selector, row_of).astype(jnp.int32) - offset
    weight[...] = group_row(w_v[...], selector, row_of)

    loads[0].wait()
    arrived(qb.at[x, y, others], b1_s, b1_r)
    gather_b_bulk()
    loads[1].wait()
    arrived(qa.at[x, y, others], a1_s, a1_r)
    gather_a_bulk(x)

    loads[5].wait()
    for part in range(items_rows // QUARTER):
        rows = pl.ds(part * QUARTER, QUARTER)
        items_t[:, rows] = items_v[rows, :].T

    tiles = items_rows // TILE

    def half_of(xx):
        return pl.ds(pl.multiple_of(xx * HALF, HALF), HALF)

    def tile_of(t):
        return pl.ds(pl.multiple_of(t * TILE, TILE), TILE)

    def fold(values, op):
        return op(values.reshape(TILE // 8, 8, HALF), axis=0)

    def scores(q, xx):
        users = q[xx].reshape(HALF, E)
        return lax.dot_general(
            items_v[...], users, (((1,), (1,)), ((), ())), preferred_element_type=F32
        )

    zero = jnp.zeros((8, HALF), F32)
    least = jnp.full((8, HALF), -jnp.inf, F32)

    def half_b(xx):
        probs[xx] = scores(qb, xx)

        def largest(t, top):
            return jnp.maximum(top, fold(probs[xx, tile_of(t), :], jnp.max))

        top = jnp.max(lax.fori_loop(0, tiles, largest, least), axis=0, keepdims=True)

        def exponentials(t, total):
            p = jnp.exp(probs[xx, tile_of(t), :] - top)
            probs[xx, tile_of(t), :] = p
            return total + fold(p, jnp.sum)

        total = jnp.sum(lax.fori_loop(0, tiles, exponentials, zero), axis=0, keepdims=True)
        tops[:, half_of(xx)] = top
        zb[z, :, half_of(xx)] = top + jnp.log(total)

    def half_a(xx):
        score_a[...] = scores(qa, xx)
        pos = pos_a[:, half_of(xx)]
        ids = lax.broadcasted_iota(jnp.int32, (TILE, HALF), 0)

        def largest(t, carry):
            top, hit = carry
            score = score_a[tile_of(t), :]
            match = jnp.where(ids == pos - t * TILE, score, 0.0)
            return jnp.maximum(top, fold(score, jnp.max)), hit + fold(match, jnp.sum)

        top, hit = lax.fori_loop(0, tiles, largest, (least, zero))
        top = jnp.max(top, axis=0, keepdims=True)

        def exponentials(t, total):
            return total + fold(jnp.exp(score_a[tile_of(t), :] - top), jnp.sum)

        total = jnp.sum(lax.fori_loop(0, tiles, exponentials, zero), axis=0, keepdims=True)
        za[z, 0:1, half_of(xx)] = top + jnp.log(total)
        za[z, 1:2, half_of(xx)] = jnp.sum(hit, axis=0, keepdims=True)

    def z_round(buf, ss, rs):
        @pl.loop(1, NZ)
        def _(k):
            remote(buf.at[z], buf.at[z], ss, rs, at(z_peer(k), y, x)).start()

    def plane_round(buf, ss, rs):
        @pl.loop(1, NY * NX)
        def _(k):
            p = plane_peer(k)
            remote(buf.at[place], buf.at[place], ss, rs, at(z, p // NX, p % NX)).start()

    arrived(qb.at[x, pl.ds(0, NY - 1)], b2_s, b2_r.at[x])
    half_b(x)
    arrived(qb.at[1 - x], b2_s, b2_r.at[1 - x])
    half_b(1 - x)
    z_round(zb, b_zs, b_zr)
    gather_a_bulk(1 - x)
    sent(qb.at[x, y, others], b1_s, b1_r)
    sent(qa.at[x, y, others], a1_s, a1_r)
    sent(qb.at[0], b2_s, b2_r.at[0])
    sent(qb.at[0, pl.ds(0, NY - 1)], b2_s, b2_r.at[0])
    arrived(zb.at[others], b_zs, b_zr)
    yb[place] = lse_of(zb[...])
    plane_round(yb, b_ys, b_yr)
    arrived(qa.at[x, :, others], a2_s, a2_r.at[x])
    half_a(x)
    sent(zb.at[others], b_zs, b_zr)

    arrived(yb.at[others], b_ys, b_yr)
    factor = weight[...] * jnp.exp(tops[...] - lse_of(yb[...]))

    ids = lax.broadcasted_iota(jnp.int32, (TILE, HALF), 0)

    def dscores(ff):
        @pl.loop(ff * 2 * QUARTER // TILE, (ff + 1) * 2 * QUARTER // TILE)
        def _(t):
            for xx in range(NX):
                cols = slice(xx * HALF, (xx + 1) * HALF)
                match = jnp.where(ids == pos_b[:, cols] - t * TILE, weight[:, cols], 0.0)
                score = probs[xx, tile_of(t), :] * factor[:, cols] - match
                dsc[tile_of(t), cols] = score.astype(BF16)

    def far_copy(hop, n):
        piece = pl.ds(pl.multiple_of(n * PIECE, PIECE), PIECE)
        source, target = (gi_s, gi_relay) if hop == 0 else (gi_relay, gi_far)
        return remote(
            source.at[piece], target.at[piece], far_s.at[hop, n], far_r.at[hop, n], next_chip
        )

    def core_copy(n):
        return remote(gi_f.at[n, 1 - core], gi_core.at[n], gi_ss.at[n], gi_rs.at[n], other_core)

    def item_grads(n, ff):
        rows = pl.ds(pl.multiple_of(ff * (2 * QUARTER), 2 * QUARTER), 2 * QUARTER)
        part = jnp.dot(dsc[rows, :], qb[...].reshape(GROUP, E), preferred_element_type=F32)
        gi_f[n] = part.reshape(2, QUARTER, E)
        core_copy(n).start()

    def query_grads(xx):
        block = jnp.dot(
            items_t[...], dsc[:, xx * HALF : (xx + 1) * HALF], preferred_element_type=F32
        ).T.reshape(NY, NZ, OWN, E)
        gq_f[xx] = block
        gq_s[xx] = block.astype(BF16)

        @pl.loop(1, NY)
        def _(k):
            yy = y_peer(k)
            remote(gq_s.at[xx, yy], r1.at[place], s1s, s1r, at(z, yy, xx)).start()

        @pl.when(x != xx)
        def _():
            remote(gq_s.at[xx, y], r1.at[place], s1s, s1r, at(z, y, xx)).start()

    dscores(1 - far)
    item_grads(0, 1 - far)
    dscores(far)
    query_grads(0)
    core_copy(0).wait_recv()
    gi_s[...] = (gi_f[0, core] + gi_core[0]).astype(BF16)

    @pl.loop(0, QUARTER // PIECE)
    def _(n):
        far_copy(0, n).start()

    query_grads(1)
    item_grads(1, far)

    arrived(qa.at[1 - x, :, others], a2_s, a2_r.at[1 - x])
    half_a(1 - x)
    z_round(za, a_zs, a_zr)

    @pl.loop(0, QUARTER // PIECE)
    def _(n):
        far_copy(0, n).wait_recv()
        far_copy(1, n).start()

    r1[place] = jnp.zeros((NZ, OWN, E), BF16)
    r2[z] = jnp.zeros((OWN, E), F32)
    arrived(r1.at[others], s1s, s1r)
    gq_h[...] = gq_f[x, y] + jnp.sum(r1[...].astype(F32), axis=0)

    @pl.loop(1, NZ)
    def _(k):
        zz = z_peer(k)
        remote(gq_h.at[zz], r2.at[z], s2s, s2r, at(zz, y, x)).start()

    arrived(za.at[others], a_zs, a_zr)
    z_parts = za[...]
    ya[place, 0:1] = lse_of(z_parts[:, 0:1])
    ya[place, 1:2] = jnp.sum(z_parts[:, 1:2], axis=0)
    plane_round(ya, a_ys, a_yr)

    core_copy(1).wait_recv()
    gi_out[...] = gi_f[1, core] + gi_core[1]
    sent(qa.at[0, :, others], a2_s, a2_r.at[0])
    sent(qa.at[1, :, others], a2_s, a2_r.at[0])
    sent(yb.at[others], b_ys, b_yr)
    sent(za.at[others], a_zs, a_zr)
    sent(r1.at[others], s1s, s1r)
    core_copy(0).wait_send()
    core_copy(1).wait_send()

    @pl.loop(0, QUARTER // PIECE)
    def _(n):
        far_copy(0, n).wait_send()

    @pl.loop(0, QUARTER // PIECE)
    def _(n):
        piece = pl.ds(pl.multiple_of(n * PIECE, PIECE), PIECE)
        far_copy(1, n).wait_recv()
        gi_out[piece, :] += gi_far[piece, :].astype(F32)

    stores = [
        pltpu.make_async_copy(source, target, out_sem.at[n])
        for n, (source, target) in enumerate(
            ((gi_out, gi_hbm), (loss_out, loss_hbm), (gq_out, gq_hbm))
        )
    ]
    stores[0].start()

    arrived(ya.at[others], a_ys, a_yr)
    y_parts = ya[...]
    tops[...] = lse_of(y_parts[:, 0:1]) - jnp.sum(y_parts[:, 1:2], axis=0)
    mine = tops[:, pl.ds(pl.multiple_of((x * NY + y) * NZ * OWN, NZ * OWN), NZ * OWN)]
    pick_row = lax.broadcasted_iota(jnp.int32, (NZ * OWN, OWN), 0)
    pick_col = lax.broadcasted_iota(jnp.int32, (NZ * OWN, OWN), 1)
    pick = (pick_row == z * OWN + pick_col).astype(F32)
    loss_out[...] = jnp.dot(mine, pick, precision=HIGHEST, preferred_element_type=F32)
    stores[1].start()

    arrived(r2.at[others], s2s, s2r)
    gq_out[...] = gq_h[z] + jnp.sum(r2[...], axis=0)
    stores[2].start()

    sent(ya.at[others], a_ys, a_yr)
    sent(r2.at[others], s2s, s2r)

    @pl.loop(0, QUARTER // PIECE)
    def _(n):
        far_copy(1, n).wait_send()

    for store in stores:
        store.wait()


def hand_over(*refs):
    sources, targets, held, (in_sem, out_sem) = refs[:3], refs[3:6], refs[6:9], refs[9:]
    ways = list(zip(sources, held, targets))
    steps = QUARTER // PIECE
    parts = [tuple(r.at[pl.ds(n * PIECE, PIECE)] for r in ways[2]) for n in range(steps)]
    parts = parts + ways[:2]
    reads = [
        pltpu.make_async_copy(source, middle, in_sem.at[n])
        for n, (source, middle, target) in enumerate(parts)
    ]
    writes = [
        pltpu.make_async_copy(middle, target, out_sem.at[n])
        for n, (source, middle, target) in enumerate(parts)
    ]
    for read in reads:
        read.start()
    for read, write in zip(reads, writes):
        read.wait()
        write.start()
    for write in writes:
        write.wait()


def per_device(query_a, query_b, items, positive_a, positive_b, loss_cotangent):
    rows = items.shape[0]
    hbm = pl.BlockSpec(memory_space=pl.ANY)
    results = (
        jax.ShapeDtypeStruct((1, OWN), F32),
        jax.ShapeDtypeStruct((OWN, E), F32),
        jax.ShapeDtypeStruct((QUARTER, E), F32),
    )
    dma = pltpu.SemaphoreType.DMA
    block = (NX, NY, NZ, OWN, E)
    loss, gq, gi = pl.pallas_call(
        kernel,
        out_shape=results,
        in_specs=[hbm] * 6,
        out_specs=[hbm] * 3,
        scratch_shapes=[
            pltpu.VMEM((rows, E), BF16),
            pltpu.VMEM((E, rows), BF16),
            pltpu.VMEM(block, BF16),
            pltpu.VMEM(block, BF16),
            pltpu.VMEM((32, 128), jnp.int32),
            pltpu.VMEM((32, 128), jnp.int32),
            pltpu.VMEM((32, 128), F32),
            pltpu.VMEM((1, GROUP), jnp.int32),
            pltpu.VMEM((1, GROUP), jnp.int32),
            pltpu.VMEM((1, GROUP), F32),
            pltpu.VMEM((NX, rows, HALF), F32),
            pltpu.VMEM((rows, HALF), F32),
            pltpu.VMEM((rows, GROUP), BF16),
            pltpu.VMEM(block, F32),
            pltpu.VMEM(block, BF16),
            pltpu.VMEM((NY * NX, NZ, OWN, E), BF16),
            pltpu.VMEM((NZ, OWN, E), F32),
            pltpu.VMEM((NZ, OWN, E), F32),
            pltpu.VMEM((2, 2, QUARTER, E), F32),
            pltpu.VMEM((QUARTER, E), BF16),
            pltpu.VMEM((2, QUARTER, E), F32),
            pltpu.VMEM((QUARTER, E), BF16),
            pltpu.VMEM((QUARTER, E), BF16),
            pltpu.VMEM((1, OWN), F32),
            pltpu.VMEM((OWN, E), F32),
            pltpu.VMEM((QUARTER, E), F32),
            pltpu.VMEM((NZ, 1, GROUP), F32),
            pltpu.VMEM((NY * NX, 1, GROUP), F32),
            pltpu.VMEM((NZ, 2, GROUP), F32),
            pltpu.VMEM((NY * NX, 2, GROUP), F32),
            pltpu.VMEM((1, GROUP), F32),
            dma((6,)),
            dma((3,)),
            dma, dma,
            dma, dma((NX,)),
            dma, dma,
            dma, dma((NX,)),
            dma, dma,
            dma, dma,
            dma, dma,
            dma, dma,
            dma, dma,
            dma, dma,
            dma((2,)), dma((2,)),
            dma((2, QUARTER // PIECE)), dma((2, QUARTER // PIECE)),
        ],
        compiler_params=pltpu.CompilerParams(
            collective_id=0, has_side_effects=True, vmem_limit_bytes=64 * 1024 * 1024
        ),
    )(
        query_a,
        query_b,
        items,
        positive_a.reshape(32, 128),
        positive_b.reshape(32, 128),
        loss_cotangent.reshape(32, 128),
    )
    pieces = QUARTER // PIECE + 2
    loss, gq, gi = pl.pallas_call(
        hand_over,
        out_shape=results,
        in_specs=[hbm] * 3,
        out_specs=[hbm] * 3,
        scratch_shapes=[pltpu.VMEM(r.shape, r.dtype) for r in results] + [dma((pieces,))] * 2,
        compiler_params=pltpu.CompilerParams(vmem_limit_bytes=64 * 1024 * 1024),
    )(loss, gq, gi)
    return loss.reshape(OWN), gq, gi


def solution(mesh):
    return jax.shard_map(
        per_device,
        mesh=mesh,
        in_specs=(
            P(("item", "user"), None),
            P(("item", "user"), None),
            P("item", None),
            P(),
            P(),
            P(),
        ),
        out_specs=(P(("item", "user")), P(("item", "user"), None), P(("item", "user"), None)),
        check_vma=False,
    )
```

```python
import functools

import jax
import jax.numpy as jnp
from jax import lax
from jax.experimental import pallas as pl
from jax.experimental.pallas import tpu as pltpu
from jax.sharding import PartitionSpec as P

MESH = pl.DeviceIdType.MESH
F32 = jnp.float32
BF16 = jnp.bfloat16
HIGHEST = lax.Precision.HIGHEST

NZ, NY, NX = 8, 4, 2
OWN = 16
E = 256
GROUP = NZ * NY * NX * OWN
HALF = GROUP // NX
TILE = 512
QUARTER = 512
PIECE = 128


def remote(src, dst, send_sem, recv_sem, device):
    return pltpu.make_async_remote_copy(
        src_ref=src,
        dst_ref=dst,
        send_sem=send_sem,
        recv_sem=recv_sem,
        device_id=device,
        device_id_type=MESH,
    )


def group_row(table, selector, row_of):
    picked = jnp.dot(table, selector, precision=HIGHEST, preferred_element_type=F32)
    rows = lax.broadcasted_iota(jnp.int32, picked.shape, 0)
    return jnp.sum(jnp.where(rows == row_of, picked, 0.0), axis=0, keepdims=True)


def lse_of(parts):
    top = jnp.max(parts, axis=0)
    return top + jnp.log(jnp.sum(jnp.exp(parts - top[None]), axis=0))


def kernel(
    qa_in, qb_in, items_in, pa_in, pb_in, w_in,
    loss_hbm, gq_hbm, gi_hbm,
    items_v, items_t, qa, qb, pa_v, pb_v, w_v, pos_a, pos_b, weight,
    probs, score_a, dsc, gq_f, gq_s,
    r1, gq_h, r2,
    gi_f, gi_s, gi_core, gi_relay, gi_far, loss_out, gq_out, gi_out,
    zb, yb, za, ya,
    tops,
    in_sem, out_sem, b1_s, b1_r, b2_s, b2_r, a1_s, a1_r, a2_s, a2_r,
    b_zs, b_zr, b_ys, b_yr, a_zs, a_zr, a_ys, a_yr,
    s1s, s1r, s2s, s2r, gi_ss, gi_rs, far_s, far_r,
):
    item = lax.axis_index("item")
    user = lax.axis_index("user")
    z, y, x = item // (NY * NX), (item // NX) % NY, item % NX
    place = y * NX + x
    far, core = user // 2, user % 2
    items_rows = items_v.shape[0]
    offset = item * items_rows

    def at(zz, yy, xx):
        return {"item": (zz * NY + yy) * NX + xx}

    def z_peer(k):
        return lax.rem(z + k, NZ)

    def y_peer(k):
        return lax.rem(y + k, NY)

    def plane_peer(k):
        return lax.rem(place + k, NY * NX)

    loads = [
        pltpu.make_async_copy(source, target, in_sem.at[n])
        for n, (source, target) in enumerate(
            (
                (qb_in, qb.at[x, y, z]),
                (qa_in, qa.at[x, y, z]),
                (pa_in, pa_v),
                (pb_in, pb_v),
                (w_in, w_v),
                (items_in, items_v),
            )
        )
    ]

    barrier = pltpu.get_barrier_semaphore()

    @pl.loop(1, NZ)
    def _(k):
        pl.semaphore_signal(barrier, inc=1, device_id=at(z_peer(k), y, x), device_id_type=MESH)
        pl.semaphore_signal(barrier, inc=1, device_id=at(z_peer(k), y, 1 - x), device_id_type=MESH)

    @pl.loop(1, NY * NX)
    def _(k):
        p = plane_peer(k)
        pl.semaphore_signal(barrier, inc=1, device_id=at(z, p // NX, p % NX), device_id_type=MESH)

    other_core = {"user": far * 2 + 1 - core}
    other_far = {"item": (z * NY + y) * NX + 1 - x, "user": (1 - far) * 2 + core}
    next_x = lax.rem(far * NX + x + 1 + 2 * core, 4)
    next_chip = {"item": (z * NY + y) * NX + next_x % NX, "user": next_x // NX * 2 + core}
    pl.semaphore_signal(barrier, inc=1, device_id=other_core, device_id_type=MESH)
    pl.semaphore_signal(barrier, inc=1, device_id=other_far, device_id_type=MESH)

    for load in loads:
        load.start()

    pl.semaphore_wait(barrier, 2 * (NZ - 1) + (NY * NX - 1) + 2)

    def sent(refs, send_sem, recv_sem):
        remote(refs, refs, send_sem, recv_sem, other_core).wait_send()

    def arrived(refs, send_sem, recv_sem):
        remote(refs, refs, send_sem, recv_sem, other_core).wait_recv()

    @pl.loop(1, NZ)
    def _(k):
        remote(qb_in, qb.at[x, y, z], b1_s, b1_r, at(z_peer(k), y, x)).start()

    def gather_b_bulk():
        block = qb.at[x, y]

        @pl.loop(1, NY)
        def _(k):
            remote(block, block, b2_s, b2_r.at[x], at(z, y_peer(k), x)).start()

        @pl.loop(0, NY)
        def _(k):
            remote(block, block, b2_s, b2_r.at[x], at(z, y_peer(k), 1 - x)).start()

    @pl.loop(1, NY * NX)
    def _(k):
        p = plane_peer(k)
        remote(qa_in, qa.at[x, y, z], a1_s, a1_r, at(z, p // NX, p % NX)).start()

    def gather_a_bulk(xx):
        block = qa.at[xx, :, z]

        @pl.loop(1, NZ)
        def _(k):
            remote(block, block, a2_s, a2_r.at[xx], at(z_peer(k), y, x)).start()

    others = pl.ds(0, NZ - 1)

    lanes = lax.broadcasted_iota(jnp.int32, (1, GROUP), 1)
    own_of = lanes % OWN
    z_of = (lanes // OWN) % NZ
    y_of = (lanes // (OWN * NZ)) % NY
    x_of = lanes // (OWN * NZ * NY)
    ks = lax.broadcasted_iota(jnp.int32, (128, GROUP), 0)
    selector = (ks == x_of * (4 * OWN) + user * OWN + own_of).astype(F32)
    row_of = z_of * NY + y_of
    for load in loads[2:5]:
        load.wait()
    pos_a[...] = group_row(pa_v[...].astype(F32), selector, row_of).astype(jnp.int32) - offset
    pos_b[...] = group_row(pb_v[...].astype(F32), selector, row_of).astype(jnp.int32) - offset
    weight[...] = group_row(w_v[...], selector, row_of)

    loads[0].wait()
    arrived(qb.at[x, y, others], b1_s, b1_r)
    gather_b_bulk()
    loads[1].wait()
    arrived(qa.at[x, y, others], a1_s, a1_r)
    gather_a_bulk(x)

    loads[5].wait()
    for part in range(items_rows // QUARTER):
        rows = pl.ds(part * QUARTER, QUARTER)
        items_t[:, rows] = items_v[rows, :].T

    tiles = items_rows // TILE

    def half_of(xx):
        return pl.ds(pl.multiple_of(xx * HALF, HALF), HALF)

    def tile_of(t):
        return pl.ds(pl.multiple_of(t * TILE, TILE), TILE)

    def fold(values, op):
        return op(values.reshape(TILE // 8, 8, HALF), axis=0)

    def scores(q, xx):
        users = q[xx].reshape(HALF, E)
        return lax.dot_general(
            items_v[...], users, (((1,), (1,)), ((), ())), preferred_element_type=F32
        )

    zero = jnp.zeros((8, HALF), F32)
    least = jnp.full((8, HALF), -jnp.inf, F32)

    def half_b(xx):
        probs[xx] = scores(qb, xx)

        def largest(t, top):
            return jnp.maximum(top, fold(probs[xx, tile_of(t), :], jnp.max))

        top = jnp.max(lax.fori_loop(0, tiles, largest, least), axis=0, keepdims=True)

        def exponentials(t, total):
            p = jnp.exp(probs[xx, tile_of(t), :] - top)
            probs[xx, tile_of(t), :] = p
            return total + fold(p, jnp.sum)

        total = jnp.sum(lax.fori_loop(0, tiles, exponentials, zero), axis=0, keepdims=True)
        tops[:, half_of(xx)] = top
        zb[z, :, half_of(xx)] = top + jnp.log(total)

    def half_a(xx):
        score_a[...] = scores(qa, xx)
        pos = pos_a[:, half_of(xx)]
        ids = lax.broadcasted_iota(jnp.int32, (TILE, HALF), 0)

        def largest(t, carry):
            top, hit = carry
            score = score_a[tile_of(t), :]
            match = jnp.where(ids == pos - t * TILE, score, 0.0)
            return jnp.maximum(top, fold(score, jnp.max)), hit + fold(match, jnp.sum)

        top, hit = lax.fori_loop(0, tiles, largest, (least, zero))
        top = jnp.max(top, axis=0, keepdims=True)

        def exponentials(t, total):
            return total + fold(jnp.exp(score_a[tile_of(t), :] - top), jnp.sum)

        total = jnp.sum(lax.fori_loop(0, tiles, exponentials, zero), axis=0, keepdims=True)
        za[z, 0:1, half_of(xx)] = top + jnp.log(total)
        za[z, 1:2, half_of(xx)] = jnp.sum(hit, axis=0, keepdims=True)

    def z_round(buf, ss, rs):
        @pl.loop(1, NZ)
        def _(k):
            remote(buf.at[z], buf.at[z], ss, rs, at(z_peer(k), y, x)).start()

    def plane_round(buf, ss, rs):
        @pl.loop(1, NY * NX)
        def _(k):
            p = plane_peer(k)
            remote(buf.at[place], buf.at[place], ss, rs, at(z, p // NX, p % NX)).start()

    arrived(qb.at[x, pl.ds(0, NY - 1)], b2_s, b2_r.at[x])
    half_b(x)
    arrived(qb.at[1 - x], b2_s, b2_r.at[1 - x])
    half_b(1 - x)
    z_round(zb, b_zs, b_zr)
    gather_a_bulk(1 - x)
    sent(qb.at[x, y, others], b1_s, b1_r)
    sent(qa.at[x, y, others], a1_s, a1_r)
    sent(qb.at[0], b2_s, b2_r.at[0])
    sent(qb.at[0, pl.ds(0, NY - 1)], b2_s, b2_r.at[0])
    arrived(zb.at[others], b_zs, b_zr)
    yb[place] = lse_of(zb[...])
    plane_round(yb, b_ys, b_yr)
    arrived(qa.at[x, :, others], a2_s, a2_r.at[x])
    half_a(x)
    sent(zb.at[others], b_zs, b_zr)

    arrived(yb.at[others], b_ys, b_yr)
    factor = weight[...] * jnp.exp(tops[...] - lse_of(yb[...]))

    ids = lax.broadcasted_iota(jnp.int32, (TILE, HALF), 0)

    def quarter_of(ff, cc):
        return pl.ds(pl.multiple_of((ff * 2 + cc) * QUARTER, QUARTER), QUARTER)

    def dscores(ff, cc):
        rows = quarter_of(ff, cc)
        for xx in range(NX):
            cols = slice(xx * HALF, (xx + 1) * HALF)
            match = jnp.where(
                ids == pos_b[:, cols] - (ff * 2 + cc) * QUARTER, weight[:, cols], 0.0
            )
            dsc[rows, cols] = (probs[xx, rows, :] * factor[:, cols] - match).astype(BF16)

    def far_copy(hop, n):
        piece = pl.ds(pl.multiple_of(n * PIECE, PIECE), PIECE)
        source, target = (gi_s, gi_relay) if hop == 0 else (gi_relay, gi_far)
        return remote(
            source.at[piece], target.at[piece], far_s.at[hop, n], far_r.at[hop, n], next_chip
        )

    def core_copy(n):
        return remote(gi_f.at[n, 1 - core], gi_core.at[n], gi_ss.at[n], gi_rs.at[n], other_core)

    def item_grads(n, ff, cc):
        gi_f[n, cc] = jnp.dot(
            dsc[quarter_of(ff, cc), :], qb[...].reshape(GROUP, E), preferred_element_type=F32
        )

    def query_grads(xx):
        block = jnp.dot(
            items_t[...], dsc[:, half_of(xx)], preferred_element_type=F32
        ).T.reshape(NY, NZ, OWN, E)
        gq_f[xx] = block
        gq_s[xx] = block.astype(BF16)

        @pl.loop(1, NY)
        def _(k):
            yy = y_peer(k)
            remote(gq_s.at[xx, yy], r1.at[place], s1s, s1r, at(z, yy, xx)).start()

        @pl.when(x != xx)
        def _():
            remote(gq_s.at[xx, y], r1.at[place], s1s, s1r, at(z, y, xx)).start()

    dscores(1 - far, 1 - core)
    item_grads(0, 1 - far, 1 - core)
    core_copy(0).start()
    dscores(1 - far, core)
    item_grads(0, 1 - far, core)
    dscores(far, 1 - core)
    dscores(far, core)
    query_grads(1 - x)
    core_copy(0).wait_recv()
    gi_s[...] = (gi_f[0, core] + gi_core[0]).astype(BF16)

    @pl.loop(0, QUARTER // PIECE)
    def _(n):
        far_copy(0, n).start()

    query_grads(x)
    item_grads(1, far, 1 - core)
    core_copy(1).start()
    item_grads(1, far, core)

    arrived(qa.at[1 - x, :, others], a2_s, a2_r.at[1 - x])
    half_a(1 - x)
    z_round(za, a_zs, a_zr)

    @pl.loop(0, QUARTER // PIECE)
    def _(n):
        far_copy(0, n).wait_recv()
        far_copy(1, n).start()

    r1[place] = jnp.zeros((NZ, OWN, E), BF16)
    r2[z] = jnp.zeros((OWN, E), F32)
    arrived(r1.at[others], s1s, s1r)
    gq_h[...] = gq_f[x, y] + jnp.sum(r1[...].astype(F32), axis=0)

    @pl.loop(1, NZ)
    def _(k):
        zz = z_peer(k)
        remote(gq_h.at[zz], r2.at[z], s2s, s2r, at(zz, y, x)).start()

    arrived(za.at[others], a_zs, a_zr)
    z_parts = za[...]
    ya[place, 0:1] = lse_of(z_parts[:, 0:1])
    ya[place, 1:2] = jnp.sum(z_parts[:, 1:2], axis=0)
    plane_round(ya, a_ys, a_yr)

    core_copy(1).wait_recv()
    gi_out[...] = gi_f[1, core] + gi_core[1]
    sent(qa.at[0, :, others], a2_s, a2_r.at[0])
    sent(qa.at[1, :, others], a2_s, a2_r.at[0])
    sent(yb.at[others], b_ys, b_yr)
    sent(za.at[others], a_zs, a_zr)
    sent(r1.at[others], s1s, s1r)
    core_copy(0).wait_send()
    core_copy(1).wait_send()

    @pl.loop(0, QUARTER // PIECE)
    def _(n):
        far_copy(0, n).wait_send()

    @pl.loop(0, QUARTER // PIECE)
    def _(n):
        piece = pl.ds(pl.multiple_of(n * PIECE, PIECE), PIECE)
        far_copy(1, n).wait_recv()
        gi_out[piece, :] += gi_far[piece, :].astype(F32)

    stores = [
        pltpu.make_async_copy(source, target, out_sem.at[n])
        for n, (source, target) in enumerate(
            ((gi_out, gi_hbm), (loss_out, loss_hbm), (gq_out, gq_hbm))
        )
    ]
    stores[0].start()

    arrived(ya.at[others], a_ys, a_yr)
    y_parts = ya[...]
    tops[...] = lse_of(y_parts[:, 0:1]) - jnp.sum(y_parts[:, 1:2], axis=0)
    mine = tops[:, pl.ds(pl.multiple_of((x * NY + y) * NZ * OWN, NZ * OWN), NZ * OWN)]
    pick_row = lax.broadcasted_iota(jnp.int32, (NZ * OWN, OWN), 0)
    pick_col = lax.broadcasted_iota(jnp.int32, (NZ * OWN, OWN), 1)
    pick = (pick_row == z * OWN + pick_col).astype(F32)
    loss_out[...] = jnp.dot(mine, pick, precision=HIGHEST, preferred_element_type=F32)
    stores[1].start()

    arrived(r2.at[others], s2s, s2r)
    gq_out[...] = gq_h[z] + jnp.sum(r2[...], axis=0)
    stores[2].start()

    sent(ya.at[others], a_ys, a_yr)
    sent(r2.at[others], s2s, s2r)

    @pl.loop(0, QUARTER // PIECE)
    def _(n):
        far_copy(1, n).wait_send()

    for store in stores:
        store.wait()


def hand_over(*refs):
    sources, targets, held, (in_sem, out_sem) = refs[:3], refs[3:6], refs[6:9], refs[9:]
    ways = list(zip(sources, held, targets))
    steps = QUARTER // PIECE
    parts = [tuple(r.at[pl.ds(n * PIECE, PIECE)] for r in ways[2]) for n in range(steps)]
    parts = parts + ways[:2]
    reads = [
        pltpu.make_async_copy(source, middle, in_sem.at[n])
        for n, (source, middle, target) in enumerate(parts)
    ]
    writes = [
        pltpu.make_async_copy(middle, target, out_sem.at[n])
        for n, (source, middle, target) in enumerate(parts)
    ]
    for read in reads:
        read.start()
    for read, write in zip(reads, writes):
        read.wait()
        write.start()
    for write in writes:
        write.wait()


def per_device(query_a, query_b, items, positive_a, positive_b, loss_cotangent):
    rows = items.shape[0]
    hbm = pl.BlockSpec(memory_space=pl.ANY)
    results = (
        jax.ShapeDtypeStruct((1, OWN), F32),
        jax.ShapeDtypeStruct((OWN, E), F32),
        jax.ShapeDtypeStruct((QUARTER, E), F32),
    )
    dma = pltpu.SemaphoreType.DMA
    block = (NX, NY, NZ, OWN, E)
    loss, gq, gi = pl.pallas_call(
        kernel,
        out_shape=results,
        in_specs=[hbm] * 6,
        out_specs=[hbm] * 3,
        scratch_shapes=[
            pltpu.VMEM((rows, E), BF16),
            pltpu.VMEM((E, rows), BF16),
            pltpu.VMEM(block, BF16),
            pltpu.VMEM(block, BF16),
            pltpu.VMEM((32, 128), jnp.int32),
            pltpu.VMEM((32, 128), jnp.int32),
            pltpu.VMEM((32, 128), F32),
            pltpu.VMEM((1, GROUP), jnp.int32),
            pltpu.VMEM((1, GROUP), jnp.int32),
            pltpu.VMEM((1, GROUP), F32),
            pltpu.VMEM((NX, rows, HALF), F32),
            pltpu.VMEM((rows, HALF), F32),
            pltpu.VMEM((rows, GROUP), BF16),
            pltpu.VMEM(block, F32),
            pltpu.VMEM(block, BF16),
            pltpu.VMEM((NY * NX, NZ, OWN, E), BF16),
            pltpu.VMEM((NZ, OWN, E), F32),
            pltpu.VMEM((NZ, OWN, E), F32),
            pltpu.VMEM((2, 2, QUARTER, E), F32),
            pltpu.VMEM((QUARTER, E), BF16),
            pltpu.VMEM((2, QUARTER, E), F32),
            pltpu.VMEM((QUARTER, E), BF16),
            pltpu.VMEM((QUARTER, E), BF16),
            pltpu.VMEM((1, OWN), F32),
            pltpu.VMEM((OWN, E), F32),
            pltpu.VMEM((QUARTER, E), F32),
            pltpu.VMEM((NZ, 1, GROUP), F32),
            pltpu.VMEM((NY * NX, 1, GROUP), F32),
            pltpu.VMEM((NZ, 2, GROUP), F32),
            pltpu.VMEM((NY * NX, 2, GROUP), F32),
            pltpu.VMEM((1, GROUP), F32),
            dma((6,)),
            dma((3,)),
            dma, dma,
            dma, dma((NX,)),
            dma, dma,
            dma, dma((NX,)),
            dma, dma,
            dma, dma,
            dma, dma,
            dma, dma,
            dma, dma,
            dma, dma,
            dma((2,)), dma((2,)),
            dma((2, QUARTER // PIECE)), dma((2, QUARTER // PIECE)),
        ],
        compiler_params=pltpu.CompilerParams(
            collective_id=0, has_side_effects=True, vmem_limit_bytes=64 * 1024 * 1024
        ),
    )(
        query_a,
        query_b,
        items,
        positive_a.reshape(32, 128),
        positive_b.reshape(32, 128),
        loss_cotangent.reshape(32, 128),
    )
    pieces = QUARTER // PIECE + 2
    loss, gq, gi = pl.pallas_call(
        hand_over,
        out_shape=results,
        in_specs=[hbm] * 3,
        out_specs=[hbm] * 3,
        scratch_shapes=[pltpu.VMEM(r.shape, r.dtype) for r in results] + [dma((pieces,))] * 2,
        compiler_params=pltpu.CompilerParams(vmem_limit_bytes=64 * 1024 * 1024),
    )(loss, gq, gi)
    return loss.reshape(OWN), gq, gi


def solution(mesh):
    return jax.shard_map(
        per_device,
        mesh=mesh,
        in_specs=(
            P(("item", "user"), None),
            P(("item", "user"), None),
            P("item", None),
            P(),
            P(),
            P(),
        ),
        out_specs=(P(("item", "user")), P(("item", "user"), None), P(("item", "user"), None)),
        check_vma=False,
    )
```

```python
import functools

import jax
import jax.numpy as jnp
from jax import lax
from jax.experimental import pallas as pl
from jax.experimental.pallas import tpu as pltpu
from jax.sharding import PartitionSpec as P

MESH = pl.DeviceIdType.MESH
F32 = jnp.float32
BF16 = jnp.bfloat16
HIGHEST = lax.Precision.HIGHEST

NZ, NY, NX = 8, 4, 2
OWN = 16
E = 256
GROUP = NZ * NY * NX * OWN
HALF = GROUP // NX
TILE = 512
QUARTER = 512
PIECE = 128


def remote(src, dst, send_sem, recv_sem, device):
    return pltpu.make_async_remote_copy(
        src_ref=src,
        dst_ref=dst,
        send_sem=send_sem,
        recv_sem=recv_sem,
        device_id=device,
        device_id_type=MESH,
    )


def group_row(table, selector, row_of):
    picked = jnp.dot(table, selector, precision=HIGHEST, preferred_element_type=F32)
    rows = lax.broadcasted_iota(jnp.int32, picked.shape, 0)
    return jnp.sum(jnp.where(rows == row_of, picked, 0.0), axis=0, keepdims=True)


def lse_of(parts):
    top = jnp.max(parts, axis=0)
    return top + jnp.log(jnp.sum(jnp.exp(parts - top[None]), axis=0))


def kernel(
    qa_in, qb_in, items_in, pa_in, pb_in, w_in,
    loss_out, gq_out, gi_out,
    items_v, items_t, qa, qb, pa_v, pb_v, w_v, pos_a, pos_b, weight,
    probs, score_a, dsc, gq_f, gq_s,
    r1, gq_h, r2,
    gi_f, gi_s, gi_core, gi_relay, gi_far,
    zb, yb, za, ya,
    tops,
    in_sem, b1_s, b1_r, b2_s, b2_r, a1_s, a1_r, a2_s, a2_r,
    b_zs, b_zr, b_ys, b_yr, a_zs, a_zr, a_ys, a_yr,
    s1s, s1r, s2s, s2r, gi_ss, gi_rs, far_s, far_r,
):
    item = lax.axis_index("item")
    user = lax.axis_index("user")
    z, y, x = item // (NY * NX), (item // NX) % NY, item % NX
    place = y * NX + x
    far, core = user // 2, user % 2
    items_rows = items_v.shape[0]
    offset = item * items_rows

    def at(zz, yy, xx):
        return {"item": (zz * NY + yy) * NX + xx}

    def z_peer(k):
        return lax.rem(z + k, NZ)

    def y_peer(k):
        return lax.rem(y + k, NY)

    def plane_peer(k):
        return lax.rem(place + k, NY * NX)

    loads = [
        pltpu.make_async_copy(source, target, in_sem.at[n])
        for n, (source, target) in enumerate(
            (
                (qb_in, qb.at[x, y, z]),
                (qa_in, qa.at[x, y, z]),
                (pa_in, pa_v),
                (pb_in, pb_v),
                (w_in, w_v),
                (items_in, items_v),
            )
        )
    ]

    barrier = pltpu.get_barrier_semaphore()

    @pl.loop(1, NZ)
    def _(k):
        pl.semaphore_signal(barrier, inc=1, device_id=at(z_peer(k), y, x), device_id_type=MESH)
        pl.semaphore_signal(barrier, inc=1, device_id=at(z_peer(k), y, 1 - x), device_id_type=MESH)

    @pl.loop(1, NY * NX)
    def _(k):
        p = plane_peer(k)
        pl.semaphore_signal(barrier, inc=1, device_id=at(z, p // NX, p % NX), device_id_type=MESH)

    other_core = {"user": far * 2 + 1 - core}
    other_far = {"item": (z * NY + y) * NX + 1 - x, "user": (1 - far) * 2 + core}
    next_x = lax.rem(far * NX + x + 1 + 2 * core, 4)
    next_chip = {"item": (z * NY + y) * NX + next_x % NX, "user": next_x // NX * 2 + core}
    pl.semaphore_signal(barrier, inc=1, device_id=other_core, device_id_type=MESH)
    pl.semaphore_signal(barrier, inc=1, device_id=other_far, device_id_type=MESH)

    for load in loads:
        load.start()

    pl.semaphore_wait(barrier, 2 * (NZ - 1) + (NY * NX - 1) + 2)

    def sent(refs, send_sem, recv_sem):
        remote(refs, refs, send_sem, recv_sem, other_core).wait_send()

    def arrived(refs, send_sem, recv_sem):
        remote(refs, refs, send_sem, recv_sem, other_core).wait_recv()

    @pl.loop(1, NZ)
    def _(k):
        remote(qb_in, qb.at[x, y, z], b1_s, b1_r, at(z_peer(k), y, x)).start()

    def gather_b_bulk():
        block = qb.at[x, y]

        @pl.loop(1, NY)
        def _(k):
            remote(block, block, b2_s, b2_r.at[x], at(z, y_peer(k), x)).start()

        @pl.loop(0, NY)
        def _(k):
            remote(block, block, b2_s, b2_r.at[x], at(z, y_peer(k), 1 - x)).start()

    @pl.loop(1, NY * NX)
    def _(k):
        p = plane_peer(k)
        remote(qa_in, qa.at[x, y, z], a1_s, a1_r, at(z, p // NX, p % NX)).start()

    def gather_a_bulk(xx):
        block = qa.at[xx, :, z]

        @pl.loop(1, NZ)
        def _(k):
            remote(block, block, a2_s, a2_r.at[xx], at(z_peer(k), y, x)).start()

    others = pl.ds(0, NZ - 1)

    lanes = lax.broadcasted_iota(jnp.int32, (1, GROUP), 1)
    own_of = lanes % OWN
    z_of = (lanes // OWN) % NZ
    y_of = (lanes // (OWN * NZ)) % NY
    x_of = lanes // (OWN * NZ * NY)
    ks = lax.broadcasted_iota(jnp.int32, (128, GROUP), 0)
    selector = (ks == x_of * (4 * OWN) + user * OWN + own_of).astype(F32)
    row_of = z_of * NY + y_of
    for load in loads[2:5]:
        load.wait()
    pos_a[...] = group_row(pa_v[...].astype(F32), selector, row_of).astype(jnp.int32) - offset
    pos_b[...] = group_row(pb_v[...].astype(F32), selector, row_of).astype(jnp.int32) - offset
    weight[...] = group_row(w_v[...], selector, row_of)

    loads[0].wait()
    arrived(qb.at[x, y, others], b1_s, b1_r)
    gather_b_bulk()
    loads[1].wait()
    arrived(qa.at[x, y, others], a1_s, a1_r)
    gather_a_bulk(x)

    loads[5].wait()
    for part in range(items_rows // QUARTER):
        rows = pl.ds(part * QUARTER, QUARTER)
        items_t[:, rows] = items_v[rows, :].T

    tiles = items_rows // TILE

    def half_of(xx):
        return pl.ds(pl.multiple_of(xx * HALF, HALF), HALF)

    def tile_of(t):
        return pl.ds(pl.multiple_of(t * TILE, TILE), TILE)

    def fold(values, op):
        return op(values.reshape(TILE // 8, 8, HALF), axis=0)

    def scores(q, xx):
        users = q[xx].reshape(HALF, E)
        return lax.dot_general(
            items_v[...], users, (((1,), (1,)), ((), ())), preferred_element_type=F32
        )

    zero = jnp.zeros((8, HALF), F32)
    least = jnp.full((8, HALF), -jnp.inf, F32)

    def half_b(xx):
        probs[xx] = scores(qb, xx)

        def largest(t, top):
            return jnp.maximum(top, fold(probs[xx, tile_of(t), :], jnp.max))

        top = jnp.max(lax.fori_loop(0, tiles, largest, least), axis=0, keepdims=True)

        def exponentials(t, total):
            p = jnp.exp(probs[xx, tile_of(t), :] - top)
            probs[xx, tile_of(t), :] = p
            return total + fold(p, jnp.sum)

        total = jnp.sum(lax.fori_loop(0, tiles, exponentials, zero), axis=0, keepdims=True)
        tops[:, half_of(xx)] = top
        zb[z, :, half_of(xx)] = top + jnp.log(total)

    def half_a(xx):
        score_a[...] = scores(qa, xx)
        pos = pos_a[:, half_of(xx)]
        ids = lax.broadcasted_iota(jnp.int32, (TILE, HALF), 0)

        def largest(t, carry):
            top, hit = carry
            score = score_a[tile_of(t), :]
            match = jnp.where(ids == pos - t * TILE, score, 0.0)
            return jnp.maximum(top, fold(score, jnp.max)), hit + fold(match, jnp.sum)

        top, hit = lax.fori_loop(0, tiles, largest, (least, zero))
        top = jnp.max(top, axis=0, keepdims=True)

        def exponentials(t, total):
            return total + fold(jnp.exp(score_a[tile_of(t), :] - top), jnp.sum)

        total = jnp.sum(lax.fori_loop(0, tiles, exponentials, zero), axis=0, keepdims=True)
        za[z, 0:1, half_of(xx)] = top + jnp.log(total)
        za[z, 1:2, half_of(xx)] = jnp.sum(hit, axis=0, keepdims=True)

    def z_round(buf, ss, rs):
        @pl.loop(1, NZ)
        def _(k):
            remote(buf.at[z], buf.at[z], ss, rs, at(z_peer(k), y, x)).start()

    def plane_round(buf, ss, rs):
        @pl.loop(1, NY * NX)
        def _(k):
            p = plane_peer(k)
            remote(buf.at[place], buf.at[place], ss, rs, at(z, p // NX, p % NX)).start()

    arrived(qb.at[x, pl.ds(0, NY - 1)], b2_s, b2_r.at[x])
    half_b(x)
    arrived(qb.at[1 - x], b2_s, b2_r.at[1 - x])
    half_b(1 - x)
    z_round(zb, b_zs, b_zr)
    gather_a_bulk(1 - x)
    sent(qb.at[x, y, others], b1_s, b1_r)
    sent(qa.at[x, y, others], a1_s, a1_r)
    sent(qb.at[0], b2_s, b2_r.at[0])
    sent(qb.at[0, pl.ds(0, NY - 1)], b2_s, b2_r.at[0])
    arrived(zb.at[others], b_zs, b_zr)
    yb[place] = lse_of(zb[...])
    plane_round(yb, b_ys, b_yr)
    arrived(qa.at[x, :, others], a2_s, a2_r.at[x])
    half_a(x)
    sent(zb.at[others], b_zs, b_zr)

    arrived(yb.at[others], b_ys, b_yr)
    factor = weight[...] * jnp.exp(tops[...] - lse_of(yb[...]))

    ids = lax.broadcasted_iota(jnp.int32, (TILE, HALF), 0)

    def quarter_of(ff, cc):
        return pl.ds(pl.multiple_of((ff * 2 + cc) * QUARTER, QUARTER), QUARTER)

    def dscores(ff, cc):
        rows = quarter_of(ff, cc)
        for xx in range(NX):
            cols = slice(xx * HALF, (xx + 1) * HALF)
            match = jnp.where(
                ids == pos_b[:, cols] - (ff * 2 + cc) * QUARTER, weight[:, cols], 0.0
            )
            dsc[rows, cols] = (probs[xx, rows, :] * factor[:, cols] - match).astype(BF16)

    def far_copy(hop, n):
        piece = pl.ds(pl.multiple_of(n * PIECE, PIECE), PIECE)
        source, target = (gi_s, gi_relay) if hop == 0 else (gi_relay, gi_far)
        return remote(
            source.at[piece], target.at[piece], far_s.at[hop, n], far_r.at[hop, n], next_chip
        )

    def core_copy(n):
        return remote(gi_f.at[n, 1 - core], gi_core.at[n], gi_ss.at[n], gi_rs.at[n], other_core)

    def item_grads(n, ff, cc):
        gi_f[n, cc] = jnp.dot(
            dsc[quarter_of(ff, cc), :], qb[...].reshape(GROUP, E), preferred_element_type=F32
        )

    def query_grads(xx):
        block = jnp.dot(
            items_t[...], dsc[:, half_of(xx)], preferred_element_type=F32
        ).T.reshape(NY, NZ, OWN, E)
        gq_f[xx] = block
        gq_s[xx] = block.astype(BF16)

        @pl.loop(1, NY)
        def _(k):
            yy = y_peer(k)
            remote(gq_s.at[xx, yy], r1.at[place], s1s, s1r, at(z, yy, xx)).start()

        @pl.when(x != xx)
        def _():
            remote(gq_s.at[xx, y], r1.at[place], s1s, s1r, at(z, y, xx)).start()

    dscores(1 - far, 1 - core)
    item_grads(0, 1 - far, 1 - core)
    core_copy(0).start()
    dscores(1 - far, core)
    item_grads(0, 1 - far, core)
    dscores(far, 1 - core)
    dscores(far, core)
    query_grads(1 - x)
    core_copy(0).wait_recv()
    gi_s[...] = (gi_f[0, core] + gi_core[0]).astype(BF16)

    @pl.loop(0, QUARTER // PIECE)
    def _(n):
        far_copy(0, n).start()

    query_grads(x)
    item_grads(1, far, 1 - core)
    core_copy(1).start()
    item_grads(1, far, core)

    arrived(qa.at[1 - x, :, others], a2_s, a2_r.at[1 - x])
    half_a(1 - x)
    z_round(za, a_zs, a_zr)

    @pl.loop(0, QUARTER // PIECE)
    def _(n):
        far_copy(0, n).wait_recv()
        far_copy(1, n).start()

    r1[place] = jnp.zeros((NZ, OWN, E), BF16)
    r2[z] = jnp.zeros((OWN, E), F32)
    arrived(r1.at[others], s1s, s1r)
    gq_h[...] = gq_f[x, y] + jnp.sum(r1[...].astype(F32), axis=0)

    @pl.loop(1, NZ)
    def _(k):
        zz = z_peer(k)
        remote(gq_h.at[zz], r2.at[z], s2s, s2r, at(zz, y, x)).start()

    arrived(za.at[others], a_zs, a_zr)
    z_parts = za[...]
    ya[place, 0:1] = lse_of(z_parts[:, 0:1])
    ya[place, 1:2] = jnp.sum(z_parts[:, 1:2], axis=0)
    plane_round(ya, a_ys, a_yr)

    core_copy(1).wait_recv()
    gi_out[...] = gi_f[1, core] + gi_core[1]
    sent(qa.at[0, :, others], a2_s, a2_r.at[0])
    sent(qa.at[1, :, others], a2_s, a2_r.at[0])
    sent(yb.at[others], b_ys, b_yr)
    sent(za.at[others], a_zs, a_zr)
    sent(r1.at[others], s1s, s1r)
    core_copy(0).wait_send()
    core_copy(1).wait_send()

    @pl.loop(0, QUARTER // PIECE)
    def _(n):
        far_copy(0, n).wait_send()

    @pl.loop(0, QUARTER // PIECE)
    def _(n):
        piece = pl.ds(pl.multiple_of(n * PIECE, PIECE), PIECE)
        far_copy(1, n).wait_recv()
        gi_out[piece, :] += gi_far[piece, :].astype(F32)

    arrived(ya.at[others], a_ys, a_yr)
    y_parts = ya[...]
    tops[...] = lse_of(y_parts[:, 0:1]) - jnp.sum(y_parts[:, 1:2], axis=0)
    mine = tops[:, pl.ds(pl.multiple_of((x * NY + y) * NZ * OWN, NZ * OWN), NZ * OWN)]
    pick_row = lax.broadcasted_iota(jnp.int32, (NZ * OWN, OWN), 0)
    pick_col = lax.broadcasted_iota(jnp.int32, (NZ * OWN, OWN), 1)
    pick = (pick_row == z * OWN + pick_col).astype(F32)
    loss_out[...] = jnp.dot(mine, pick, precision=HIGHEST, preferred_element_type=F32)

    arrived(r2.at[others], s2s, s2r)
    gq_out[...] = gq_h[z] + jnp.sum(r2[...], axis=0)

    sent(ya.at[others], a_ys, a_yr)
    sent(r2.at[others], s2s, s2r)

    @pl.loop(0, QUARTER // PIECE)
    def _(n):
        far_copy(1, n).wait_send()


def hand_over(*refs):
    copies = [
        pltpu.make_async_copy(source, target, refs[6].at[n])
        for n, (source, target) in enumerate(zip(refs[:3], refs[3:6]))
    ]
    for copy in copies:
        copy.start()
    for copy in copies:
        copy.wait()


def per_device(query_a, query_b, items, positive_a, positive_b, loss_cotangent):
    rows = items.shape[0]
    hbm, vmem = pl.BlockSpec(memory_space=pltpu.HBM), pl.BlockSpec(memory_space=pltpu.VMEM)
    results = (
        jax.ShapeDtypeStruct((1, OWN), F32),
        jax.ShapeDtypeStruct((OWN, E), F32),
        jax.ShapeDtypeStruct((QUARTER, E), F32),
    )
    dma = pltpu.SemaphoreType.DMA
    block = (NX, NY, NZ, OWN, E)
    loss, gq, gi = pl.pallas_call(
        kernel,
        out_shape=[pltpu.VMEM(r.shape, r.dtype) for r in results],
        in_specs=[hbm] * 6,
        out_specs=[vmem] * 3,
        scratch_shapes=[
            pltpu.VMEM((rows, E), BF16),
            pltpu.VMEM((E, rows), BF16),
            pltpu.VMEM(block, BF16),
            pltpu.VMEM(block, BF16),
            pltpu.VMEM((32, 128), jnp.int32),
            pltpu.VMEM((32, 128), jnp.int32),
            pltpu.VMEM((32, 128), F32),
            pltpu.VMEM((1, GROUP), jnp.int32),
            pltpu.VMEM((1, GROUP), jnp.int32),
            pltpu.VMEM((1, GROUP), F32),
            pltpu.VMEM((NX, rows, HALF), F32),
            pltpu.VMEM((rows, HALF), F32),
            pltpu.VMEM((rows, GROUP), BF16),
            pltpu.VMEM(block, F32),
            pltpu.VMEM(block, BF16),
            pltpu.VMEM((NY * NX, NZ, OWN, E), BF16),
            pltpu.VMEM((NZ, OWN, E), F32),
            pltpu.VMEM((NZ, OWN, E), F32),
            pltpu.VMEM((2, 2, QUARTER, E), F32),
            pltpu.VMEM((QUARTER, E), BF16),
            pltpu.VMEM((2, QUARTER, E), F32),
            pltpu.VMEM((QUARTER, E), BF16),
            pltpu.VMEM((QUARTER, E), BF16),
            pltpu.VMEM((NZ, 1, GROUP), F32),
            pltpu.VMEM((NY * NX, 1, GROUP), F32),
            pltpu.VMEM((NZ, 2, GROUP), F32),
            pltpu.VMEM((NY * NX, 2, GROUP), F32),
            pltpu.VMEM((1, GROUP), F32),
            dma((6,)),
            dma, dma,
            dma, dma((NX,)),
            dma, dma,
            dma, dma((NX,)),
            dma, dma,
            dma, dma,
            dma, dma,
            dma, dma,
            dma, dma,
            dma, dma,
            dma((2,)), dma((2,)),
            dma((2, QUARTER // PIECE)), dma((2, QUARTER // PIECE)),
        ],
        compiler_params=pltpu.CompilerParams(
            collective_id=0, has_side_effects=True, vmem_limit_bytes=56 * 1024 * 1024
        ),
    )(
        *(
            pltpu.with_memory_space_constraint(operand, pltpu.HBM)
            for operand in (
                query_a,
                query_b,
                items,
                positive_a.reshape(32, 128),
                positive_b.reshape(32, 128),
                loss_cotangent.reshape(32, 128),
            )
        )
    )
    loss, gq, gi = pl.pallas_call(
        hand_over,
        out_shape=results,
        in_specs=[vmem] * 3,
        out_specs=[hbm] * 3,
        scratch_shapes=[dma((3,))],
    )(loss, gq, gi)
    return loss.reshape(OWN), gq, gi


def solution(mesh):
    return jax.shard_map(
        per_device,
        mesh=mesh,
        in_specs=(
            P(("item", "user"), None),
            P(("item", "user"), None),
            P("item", None),
            P(),
            P(),
            P(),
        ),
        out_specs=(P(("item", "user")), P(("item", "user"), None), P(("item", "user"), None)),
        check_vma=False,
    )
```

```python
import functools

import jax
import jax.numpy as jnp
from jax import lax
from jax.experimental import pallas as pl
from jax.experimental.pallas import tpu as pltpu
from jax.sharding import PartitionSpec as P

MESH = pl.DeviceIdType.MESH
F32 = jnp.float32
BF16 = jnp.bfloat16
HIGHEST = lax.Precision.HIGHEST

NZ, NY, NX = 8, 4, 2
OWN = 16
E = 256
GROUP = NZ * NY * NX * OWN
HALF = GROUP // NX
TILE = 512
QUARTER = 512


def remote(src, dst, send_sem, recv_sem, device):
    return pltpu.make_async_remote_copy(
        src_ref=src,
        dst_ref=dst,
        send_sem=send_sem,
        recv_sem=recv_sem,
        device_id=device,
        device_id_type=MESH,
    )


def group_row(table, selector, row_of):
    picked = jnp.dot(table, selector, precision=HIGHEST, preferred_element_type=F32)
    rows = lax.broadcasted_iota(jnp.int32, picked.shape, 0)
    return jnp.sum(jnp.where(rows == row_of, picked, 0.0), axis=0, keepdims=True)


def lse_of(parts):
    top = jnp.max(parts, axis=0)
    return top + jnp.log(jnp.sum(jnp.exp(parts - top[None]), axis=0))


def kernel(
    qa_in, qb_in, items_in, pa_in, pb_in, w_in,
    loss_out, gq_out, gi_out,
    items_v, items_t, qa, qb, pa_v, pb_v, w_v, pos_a, pos_b, weight,
    probs, score_a, dsc, gq_f, gq_s,
    r1, gq_h, r2,
    gi_f, gi_s, gi_core, gi_far,
    zb, yb, za, ya,
    tops,
    in_sem, b1_s, b1_r, b2_s, b2_r, a1_s, a1_r, a2_s, a2_r,
    b_zs, b_zr, b_ys, b_yr, a_zs, a_zr, a_ys, a_yr,
    s1s, s1r, s2s, s2r, gi_ss, gi_rs, far_s, far_r,
):
    item = lax.axis_index("item")
    user = lax.axis_index("user")
    z, y, x = item // (NY * NX), (item // NX) % NY, item % NX
    place = y * NX + x
    far, core = user // 2, user % 2
    items_rows = items_v.shape[0]
    offset = item * items_rows

    def at(zz, yy, xx):
        return {"item": (zz * NY + yy) * NX + xx}

    def z_peer(k):
        return lax.rem(z + k, NZ)

    def y_peer(k):
        return lax.rem(y + k, NY)

    def plane_peer(k):
        return lax.rem(place + k, NY * NX)

    loads = [
        pltpu.make_async_copy(source, target, in_sem.at[n])
        for n, (source, target) in enumerate(
            (
                (qb_in, qb.at[x, y, z]),
                (qa_in, qa.at[x, y, z]),
                (pa_in, pa_v),
                (pb_in, pb_v),
                (w_in, w_v),
                (items_in, items_v),
            )
        )
    ]

    barrier = pltpu.get_barrier_semaphore()

    @pl.loop(1, NZ)
    def _(k):
        pl.semaphore_signal(barrier, inc=1, device_id=at(z_peer(k), y, x), device_id_type=MESH)
        pl.semaphore_signal(barrier, inc=1, device_id=at(z_peer(k), y, 1 - x), device_id_type=MESH)

    @pl.loop(1, NY * NX)
    def _(k):
        p = plane_peer(k)
        pl.semaphore_signal(barrier, inc=1, device_id=at(z, p // NX, p % NX), device_id_type=MESH)

    other_core = {"user": far * 2 + 1 - core}
    other_far = {"user": (1 - far) * 2 + core}
    pl.semaphore_signal(barrier, inc=1, device_id=other_core, device_id_type=MESH)
    pl.semaphore_signal(barrier, inc=1, device_id=other_far, device_id_type=MESH)

    for load in loads:
        load.start()

    pl.semaphore_wait(barrier, 2 * (NZ - 1) + (NY * NX - 1) + 2)

    def sent(refs, send_sem, recv_sem):
        remote(refs, refs, send_sem, recv_sem, other_core).wait_send()

    def arrived(refs, send_sem, recv_sem):
        remote(refs, refs, send_sem, recv_sem, other_core).wait_recv()

    @pl.loop(1, NZ)
    def _(k):
        remote(qb_in, qb.at[x, y, z], b1_s, b1_r, at(z_peer(k), y, x)).start()

    def gather_b_bulk():
        block = qb.at[x, y]

        @pl.loop(1, NY)
        def _(k):
            remote(block, block, b2_s, b2_r.at[x], at(z, y_peer(k), x)).start()

        @pl.loop(0, NY)
        def _(k):
            remote(block, block, b2_s, b2_r.at[x], at(z, y_peer(k), 1 - x)).start()

    @pl.loop(1, NY * NX)
    def _(k):
        p = plane_peer(k)
        remote(qa_in, qa.at[x, y, z], a1_s, a1_r, at(z, p // NX, p % NX)).start()

    def gather_a_bulk(xx):
        block = qa.at[xx, :, z]

        @pl.loop(1, NZ)
        def _(k):
            remote(block, block, a2_s, a2_r.at[xx], at(z_peer(k), y, x)).start()

    others = pl.ds(0, NZ - 1)

    lanes = lax.broadcasted_iota(jnp.int32, (1, GROUP), 1)
    own_of = lanes % OWN
    z_of = (lanes // OWN) % NZ
    y_of = (lanes // (OWN * NZ)) % NY
    x_of = lanes // (OWN * NZ * NY)
    ks = lax.broadcasted_iota(jnp.int32, (128, GROUP), 0)
    selector = (ks == x_of * (4 * OWN) + user * OWN + own_of).astype(F32)
    row_of = z_of * NY + y_of
    for load in loads[2:5]:
        load.wait()
    pos_a[...] = group_row(pa_v[...].astype(F32), selector, row_of).astype(jnp.int32) - offset
    pos_b[...] = group_row(pb_v[...].astype(F32), selector, row_of).astype(jnp.int32) - offset
    weight[...] = group_row(w_v[...], selector, row_of)

    loads[0].wait()
    arrived(qb.at[x, y, others], b1_s, b1_r)
    gather_b_bulk()
    loads[1].wait()
    arrived(qa.at[x, y, others], a1_s, a1_r)
    gather_a_bulk(x)

    loads[5].wait()
    for part in range(items_rows // QUARTER):
        rows = pl.ds(part * QUARTER, QUARTER)
        items_t[:, rows] = items_v[rows, :].T

    tiles = items_rows // TILE

    def half_of(xx):
        return pl.ds(pl.multiple_of(xx * HALF, HALF), HALF)

    def tile_of(t):
        return pl.ds(pl.multiple_of(t * TILE, TILE), TILE)

    def fold(values, op):
        return op(values.reshape(TILE // 8, 8, HALF), axis=0)

    def scores(q, xx):
        users = q[xx].reshape(HALF, E)
        return lax.dot_general(
            items_v[...], users, (((1,), (1,)), ((), ())), preferred_element_type=F32
        )

    zero = jnp.zeros((8, HALF), F32)
    least = jnp.full((8, HALF), -jnp.inf, F32)

    def half_b(xx):
        probs[xx] = scores(qb, xx)

        def largest(t, top):
            return jnp.maximum(top, fold(probs[xx, tile_of(t), :], jnp.max))

        top = jnp.max(lax.fori_loop(0, tiles, largest, least), axis=0, keepdims=True)

        def exponentials(t, total):
            p = jnp.exp(probs[xx, tile_of(t), :] - top)
            probs[xx, tile_of(t), :] = p
            return total + fold(p, jnp.sum)

        total = jnp.sum(lax.fori_loop(0, tiles, exponentials, zero), axis=0, keepdims=True)
        tops[:, half_of(xx)] = top
        zb[z, :, half_of(xx)] = top + jnp.log(total)

    def half_a(xx):
        score_a[...] = scores(qa, xx)
        pos = pos_a[:, half_of(xx)]
        ids = lax.broadcasted_iota(jnp.int32, (TILE, HALF), 0)

        def largest(t, carry):
            top, hit = carry
            score = score_a[tile_of(t), :]
            match = jnp.where(ids == pos - t * TILE, score, 0.0)
            return jnp.maximum(top, fold(score, jnp.max)), hit + fold(match, jnp.sum)

        top, hit = lax.fori_loop(0, tiles, largest, (least, zero))
        top = jnp.max(top, axis=0, keepdims=True)

        def exponentials(t, total):
            return total + fold(jnp.exp(score_a[tile_of(t), :] - top), jnp.sum)

        total = jnp.sum(lax.fori_loop(0, tiles, exponentials, zero), axis=0, keepdims=True)
        za[z, 0:1, half_of(xx)] = top + jnp.log(total)
        za[z, 1:2, half_of(xx)] = jnp.sum(hit, axis=0, keepdims=True)

    def z_round(buf, ss, rs):
        @pl.loop(1, NZ)
        def _(k):
            remote(buf.at[z], buf.at[z], ss, rs, at(z_peer(k), y, x)).start()

    def plane_round(buf, ss, rs):
        @pl.loop(1, NY * NX)
        def _(k):
            p = plane_peer(k)
            remote(buf.at[place], buf.at[place], ss, rs, at(z, p // NX, p % NX)).start()

    arrived(qb.at[x, pl.ds(0, NY - 1)], b2_s, b2_r.at[x])
    half_b(x)
    arrived(qb.at[1 - x], b2_s, b2_r.at[1 - x])
    half_b(1 - x)
    z_round(zb, b_zs, b_zr)
    gather_a_bulk(1 - x)
    sent(qb.at[x, y, others], b1_s, b1_r)
    sent(qa.at[x, y, others], a1_s, a1_r)
    sent(qb.at[0], b2_s, b2_r.at[0])
    sent(qb.at[0, pl.ds(0, NY - 1)], b2_s, b2_r.at[0])
    arrived(zb.at[others], b_zs, b_zr)
    yb[place] = lse_of(zb[...])
    plane_round(yb, b_ys, b_yr)
    arrived(qa.at[x, :, others], a2_s, a2_r.at[x])
    half_a(x)
    sent(zb.at[others], b_zs, b_zr)

    arrived(yb.at[others], b_ys, b_yr)
    factor = weight[...] * jnp.exp(tops[...] - lse_of(yb[...]))

    ids = lax.broadcasted_iota(jnp.int32, (TILE, HALF), 0)

    def quarter_of(ff, cc):
        return pl.ds(pl.multiple_of((ff * 2 + cc) * QUARTER, QUARTER), QUARTER)

    def dscores(ff, cc):
        rows = quarter_of(ff, cc)
        for xx in range(NX):
            cols = slice(xx * HALF, (xx + 1) * HALF)
            match = jnp.where(
                ids == pos_b[:, cols] - (ff * 2 + cc) * QUARTER, weight[:, cols], 0.0
            )
            dsc[rows, cols] = (probs[xx, rows, :] * factor[:, cols] - match).astype(BF16)

    def far_copy():
        return remote(gi_s, gi_far, far_s, far_r, other_far)

    def core_copy(n):
        return remote(gi_f.at[n, 1 - core], gi_core.at[n], gi_ss.at[n], gi_rs.at[n], other_core)

    def item_grads(n, ff, cc):
        gi_f[n, cc] = jnp.dot(
            dsc[quarter_of(ff, cc), :], qb[...].reshape(GROUP, E), preferred_element_type=F32
        )

    def query_grads(xx):
        block = jnp.dot(
            items_t[...], dsc[:, half_of(xx)], preferred_element_type=F32
        ).T.reshape(NY, NZ, OWN, E)
        gq_f[xx] = block
        gq_s[xx] = block.astype(BF16)

        @pl.loop(1, NY)
        def _(k):
            yy = y_peer(k)
            remote(gq_s.at[xx, yy], r1.at[place], s1s, s1r, at(z, yy, xx)).start()

        @pl.when(x != xx)
        def _():
            remote(gq_s.at[xx, y], r1.at[place], s1s, s1r, at(z, y, xx)).start()

    dscores(1 - far, 1 - core)
    item_grads(0, 1 - far, 1 - core)
    core_copy(0).start()
    dscores(1 - far, core)
    item_grads(0, 1 - far, core)
    dscores(far, 1 - core)
    dscores(far, core)
    query_grads(1 - x)
    core_copy(0).wait_recv()
    gi_s[...] = (gi_f[0, core] + gi_core[0]).astype(BF16)
    far_copy().start()

    query_grads(x)
    item_grads(1, far, 1 - core)
    core_copy(1).start()
    item_grads(1, far, core)

    arrived(qa.at[1 - x, :, others], a2_s, a2_r.at[1 - x])
    half_a(1 - x)
    z_round(za, a_zs, a_zr)

    r1[place] = jnp.zeros((NZ, OWN, E), BF16)
    r2[z] = jnp.zeros((OWN, E), F32)
    arrived(r1.at[others], s1s, s1r)
    gq_h[...] = gq_f[x, y] + jnp.sum(r1[...].astype(F32), axis=0)

    @pl.loop(1, NZ)
    def _(k):
        zz = z_peer(k)
        remote(gq_h.at[zz], r2.at[z], s2s, s2r, at(zz, y, x)).start()

    arrived(za.at[others], a_zs, a_zr)
    z_parts = za[...]
    ya[place, 0:1] = lse_of(z_parts[:, 0:1])
    ya[place, 1:2] = jnp.sum(z_parts[:, 1:2], axis=0)
    plane_round(ya, a_ys, a_yr)

    core_copy(1).wait_recv()
    gi_out[...] = gi_f[1, core] + gi_core[1]
    sent(qa.at[0, :, others], a2_s, a2_r.at[0])
    sent(qa.at[1, :, others], a2_s, a2_r.at[0])
    sent(yb.at[others], b_ys, b_yr)
    sent(za.at[others], a_zs, a_zr)
    sent(r1.at[others], s1s, s1r)
    core_copy(0).wait_send()
    core_copy(1).wait_send()
    far_copy().wait_recv()
    gi_out[...] += gi_far[...].astype(F32)

    arrived(ya.at[others], a_ys, a_yr)
    y_parts = ya[...]
    tops[...] = lse_of(y_parts[:, 0:1]) - jnp.sum(y_parts[:, 1:2], axis=0)
    mine = tops[:, pl.ds(pl.multiple_of((x * NY + y) * NZ * OWN, NZ * OWN), NZ * OWN)]
    pick_row = lax.broadcasted_iota(jnp.int32, (NZ * OWN, OWN), 0)
    pick_col = lax.broadcasted_iota(jnp.int32, (NZ * OWN, OWN), 1)
    pick = (pick_row == z * OWN + pick_col).astype(F32)
    loss_out[...] = jnp.dot(mine, pick, precision=HIGHEST, preferred_element_type=F32)

    arrived(r2.at[others], s2s, s2r)
    gq_out[...] = gq_h[z] + jnp.sum(r2[...], axis=0)

    sent(ya.at[others], a_ys, a_yr)
    sent(r2.at[others], s2s, s2r)

    far_copy().wait_send()


def hand_over(*refs):
    copies = [
        pltpu.make_async_copy(source, target, refs[6].at[n])
        for n, (source, target) in enumerate(zip(refs[:3], refs[3:6]))
    ]
    for copy in copies:
        copy.start()
    for copy in copies:
        copy.wait()


def per_device(query_a, query_b, items, positive_a, positive_b, loss_cotangent):
    rows = items.shape[0]
    hbm, vmem = pl.BlockSpec(memory_space=pltpu.HBM), pl.BlockSpec(memory_space=pltpu.VMEM)
    results = (
        jax.ShapeDtypeStruct((1, OWN), F32),
        jax.ShapeDtypeStruct((OWN, E), F32),
        jax.ShapeDtypeStruct((QUARTER, E), F32),
    )
    dma = pltpu.SemaphoreType.DMA
    block = (NX, NY, NZ, OWN, E)
    loss, gq, gi = pl.pallas_call(
        kernel,
        out_shape=[pltpu.VMEM(r.shape, r.dtype) for r in results],
        in_specs=[hbm] * 6,
        out_specs=[vmem] * 3,
        scratch_shapes=[
            pltpu.VMEM((rows, E), BF16),
            pltpu.VMEM((E, rows), BF16),
            pltpu.VMEM(block, BF16),
            pltpu.VMEM(block, BF16),
            pltpu.VMEM((32, 128), jnp.int32),
            pltpu.VMEM((32, 128), jnp.int32),
            pltpu.VMEM((32, 128), F32),
            pltpu.VMEM((1, GROUP), jnp.int32),
            pltpu.VMEM((1, GROUP), jnp.int32),
            pltpu.VMEM((1, GROUP), F32),
            pltpu.VMEM((NX, rows, HALF), F32),
            pltpu.VMEM((rows, HALF), F32),
            pltpu.VMEM((rows, GROUP), BF16),
            pltpu.VMEM(block, F32),
            pltpu.VMEM(block, BF16),
            pltpu.VMEM((NY * NX, NZ, OWN, E), BF16),
            pltpu.VMEM((NZ, OWN, E), F32),
            pltpu.VMEM((NZ, OWN, E), F32),
            pltpu.VMEM((2, 2, QUARTER, E), F32),
            pltpu.VMEM((QUARTER, E), BF16),
            pltpu.VMEM((2, QUARTER, E), F32),
            pltpu.VMEM((QUARTER, E), BF16),
            pltpu.VMEM((NZ, 1, GROUP), F32),
            pltpu.VMEM((NY * NX, 1, GROUP), F32),
            pltpu.VMEM((NZ, 2, GROUP), F32),
            pltpu.VMEM((NY * NX, 2, GROUP), F32),
            pltpu.VMEM((1, GROUP), F32),
            dma((6,)),
            dma, dma,
            dma, dma((NX,)),
            dma, dma,
            dma, dma((NX,)),
            dma, dma,
            dma, dma,
            dma, dma,
            dma, dma,
            dma, dma,
            dma, dma,
            dma((2,)), dma((2,)),
            dma, dma,
        ],
        compiler_params=pltpu.CompilerParams(
            collective_id=0, has_side_effects=True, vmem_limit_bytes=56 * 1024 * 1024
        ),
    )(
        *(
            pltpu.with_memory_space_constraint(operand, pltpu.HBM)
            for operand in (
                query_a,
                query_b,
                items,
                positive_a.reshape(32, 128),
                positive_b.reshape(32, 128),
                loss_cotangent.reshape(32, 128),
            )
        )
    )
    loss, gq, gi = pl.pallas_call(
        hand_over,
        out_shape=results,
        in_specs=[vmem] * 3,
        out_specs=[hbm] * 3,
        scratch_shapes=[dma((3,))],
        compiler_params=pltpu.CompilerParams(vmem_limit_bytes=1024 * 1024),
    )(*(pltpu.with_memory_space_constraint(result, pltpu.VMEM) for result in (loss, gq, gi)))
    return loss.reshape(OWN), gq, gi


def solution(mesh):
    return jax.shard_map(
        per_device,
        mesh=mesh,
        in_specs=(
            P(("item", "user"), None),
            P(("item", "user"), None),
            P("item", None),
            P(),
            P(),
            P(),
        ),
        out_specs=(P(("item", "user")), P(("item", "user"), None), P(("item", "user"), None)),
        check_vma=False,
    )
```

```python
import functools

import jax
import jax.numpy as jnp
from jax import lax
from jax.experimental import pallas as pl
from jax.experimental.pallas import tpu as pltpu
from jax.sharding import PartitionSpec as P

MESH = pl.DeviceIdType.MESH
F32 = jnp.float32
BF16 = jnp.bfloat16
HIGHEST = lax.Precision.HIGHEST

NZ, NY, NX = 8, 4, 2
OWN = 16
E = 256
GROUP = NZ * NY * NX * OWN
HALF = GROUP // NX
TILE = 512
QUARTER = 512


def remote(src, dst, send_sem, recv_sem, device):
    return pltpu.make_async_remote_copy(
        src_ref=src,
        dst_ref=dst,
        send_sem=send_sem,
        recv_sem=recv_sem,
        device_id=device,
        device_id_type=MESH,
    )


def group_row(table, selector, row_of):
    picked = jnp.dot(table, selector, precision=HIGHEST, preferred_element_type=F32)
    rows = lax.broadcasted_iota(jnp.int32, picked.shape, 0)
    return jnp.sum(jnp.where(rows == row_of, picked, 0.0), axis=0, keepdims=True)


def lse_of(parts):
    top = jnp.max(parts, axis=0)
    return top + jnp.log(jnp.sum(jnp.exp(parts - top[None]), axis=0))


def kernel(
    qa_in, qb_in, items_in, pa_in, pb_in, w_in,
    loss_out, gq_out, gi_out,
    items_v, items_t, qa, qb, pa_v, pb_v, w_v, pos_a, pos_b, weight,
    probs, score_a, dsc, gq_f, gq_s,
    r1, gq_h, r2,
    gi_f, gi_s, gi_core, gi_far,
    zb, yb, za, ya,
    tops, top_a,
    in_sem, b1_s, b1_r, b2_s, b2_r, a1_s, a1_r, a2_s, a2_r,
    b_zs, b_zr, b_ys, b_yr, a_zs, a_zr, a_ys, a_yr,
    s1s, s1r, s2s, s2r, gi_ss, gi_rs, far_s, far_r,
):
    item = lax.axis_index("item")
    user = lax.axis_index("user")
    z, y, x = item // (NY * NX), (item // NX) % NY, item % NX
    place = y * NX + x
    far, core = user // 2, user % 2
    items_rows = items_v.shape[0]
    offset = item * items_rows

    def at(zz, yy, xx):
        return {"item": (zz * NY + yy) * NX + xx}

    def z_peer(k):
        return lax.rem(z + k, NZ)

    def y_peer(k):
        return lax.rem(y + k, NY)

    def plane_peer(k):
        return lax.rem(place + k, NY * NX)

    loads = [
        pltpu.make_async_copy(source, target, in_sem.at[n])
        for n, (source, target) in enumerate(
            (
                (qb_in, qb.at[x, y, z]),
                (qa_in, qa.at[x, y, z]),
                (pa_in, pa_v),
                (pb_in, pb_v),
                (w_in, w_v),
                (items_in, items_v),
            )
        )
    ]

    barrier = pltpu.get_barrier_semaphore()

    @pl.loop(1, NZ)
    def _(k):
        pl.semaphore_signal(barrier, inc=1, device_id=at(z_peer(k), y, x), device_id_type=MESH)
        pl.semaphore_signal(barrier, inc=1, device_id=at(z_peer(k), y, 1 - x), device_id_type=MESH)

    @pl.loop(1, NY * NX)
    def _(k):
        p = plane_peer(k)
        pl.semaphore_signal(barrier, inc=1, device_id=at(z, p // NX, p % NX), device_id_type=MESH)

    other_core = {"user": far * 2 + 1 - core}
    other_far = {"user": (1 - far) * 2 + core}
    pl.semaphore_signal(barrier, inc=1, device_id=other_core, device_id_type=MESH)
    pl.semaphore_signal(barrier, inc=1, device_id=other_far, device_id_type=MESH)

    for load in loads:
        load.start()

    pl.semaphore_wait(barrier, 2 * (NZ - 1) + (NY * NX - 1) + 2)

    def sent(refs, send_sem, recv_sem):
        remote(refs, refs, send_sem, recv_sem, other_core).wait_send()

    def arrived(refs, send_sem, recv_sem):
        remote(refs, refs, send_sem, recv_sem, other_core).wait_recv()

    @pl.loop(1, NZ)
    def _(k):
        remote(qb_in, qb.at[x, y, z], b1_s, b1_r, at(z_peer(k), y, x)).start()

    def gather_b_bulk():
        block = qb.at[x, y]

        @pl.loop(1, NY)
        def _(k):
            remote(block, block, b2_s, b2_r.at[x], at(z, y_peer(k), x)).start()

        @pl.loop(0, NY)
        def _(k):
            remote(block, block, b2_s, b2_r.at[x], at(z, y_peer(k), 1 - x)).start()

    @pl.loop(1, NY * NX)
    def _(k):
        p = plane_peer(k)
        remote(qa_in, qa.at[x, y, z], a1_s, a1_r, at(z, p // NX, p % NX)).start()

    def gather_a_bulk(xx):
        block = qa.at[xx, :, z]

        @pl.loop(1, NZ)
        def _(k):
            remote(block, block, a2_s, a2_r.at[xx], at(z_peer(k), y, x)).start()

    others = pl.ds(0, NZ - 1)

    lanes = lax.broadcasted_iota(jnp.int32, (1, GROUP), 1)
    own_of = lanes % OWN
    z_of = (lanes // OWN) % NZ
    y_of = (lanes // (OWN * NZ)) % NY
    x_of = lanes // (OWN * NZ * NY)
    ks = lax.broadcasted_iota(jnp.int32, (128, GROUP), 0)
    selector = (ks == x_of * (4 * OWN) + user * OWN + own_of).astype(F32)
    row_of = z_of * NY + y_of
    for load in loads[2:5]:
        load.wait()
    pos_a[...] = group_row(pa_v[...].astype(F32), selector, row_of).astype(jnp.int32) - offset
    pos_b[...] = group_row(pb_v[...].astype(F32), selector, row_of).astype(jnp.int32) - offset
    weight[...] = group_row(w_v[...], selector, row_of)

    loads[0].wait()
    arrived(qb.at[x, y, others], b1_s, b1_r)
    gather_b_bulk()
    loads[1].wait()
    arrived(qa.at[x, y, others], a1_s, a1_r)
    gather_a_bulk(x)

    loads[5].wait()
    for part in range(items_rows // QUARTER):
        rows = pl.ds(part * QUARTER, QUARTER)
        items_t[:, rows] = items_v[rows, :].T

    tiles = items_rows // TILE

    def half_of(xx):
        return pl.ds(pl.multiple_of(xx * HALF, HALF), HALF)

    def tile_of(t):
        return pl.ds(pl.multiple_of(t * TILE, TILE), TILE)

    def fold(values, op):
        return op(values.reshape(TILE // 8, 8, HALF), axis=0)

    def scores(q, xx):
        users = q[xx].reshape(HALF, E)
        return lax.dot_general(
            items_v[...], users, (((1,), (1,)), ((), ())), preferred_element_type=F32
        )

    zero = jnp.zeros((8, HALF), F32)
    least = jnp.full((8, HALF), -jnp.inf, F32)
    ids = lax.broadcasted_iota(jnp.int32, (TILE, HALF), 0)

    def half_b(xx):
        probs[xx] = scores(qb, xx)

        def largest(t, top):
            return jnp.maximum(top, fold(probs[xx, tile_of(t), :], jnp.max))

        top = jnp.max(lax.fori_loop(0, tiles, largest, least), axis=0, keepdims=True)

        def exponentials(t, total):
            p = jnp.exp(probs[xx, tile_of(t), :] - top)
            probs[xx, tile_of(t), :] = p
            return total + fold(p, jnp.sum)

        total = jnp.sum(lax.fori_loop(0, tiles, exponentials, zero), axis=0, keepdims=True)
        tops[:, half_of(xx)] = top
        zb[xx, z] = top + jnp.log(total)

    def scores_a(xx):
        score_a[...] = scores(qa, xx)

    def tops_a(xx):
        pos = pos_a[:, half_of(xx)]

        def largest(t, carry):
            top, hit = carry
            score = score_a[tile_of(t), :]
            match = jnp.where(ids == pos - t * TILE, score, 0.0)
            return jnp.maximum(top, fold(score, jnp.max)), hit + fold(match, jnp.sum)

        top, hit = lax.fori_loop(0, tiles, largest, (least, zero))
        top_a[...] = jnp.max(top, axis=0, keepdims=True)
        za[z, 1:2, half_of(xx)] = jnp.sum(hit, axis=0, keepdims=True)

    def sums_a(xx):
        top = top_a[...]

        def exponentials(t, total):
            return total + fold(jnp.exp(score_a[tile_of(t), :] - top), jnp.sum)

        total = jnp.sum(lax.fori_loop(0, tiles, exponentials, zero), axis=0, keepdims=True)
        za[z, 0:1, half_of(xx)] = top + jnp.log(total)

    def z_round(buf, ss, rs):
        @pl.loop(1, NZ)
        def _(k):
            remote(buf.at[z], buf.at[z], ss, rs, at(z_peer(k), y, x)).start()

    def plane_round(buf, ss, rs):
        @pl.loop(1, NY * NX)
        def _(k):
            p = plane_peer(k)
            remote(buf.at[place], buf.at[place], ss, rs, at(z, p // NX, p % NX)).start()

    def lse_z(xx):
        z_round(zb.at[xx], b_zs.at[xx], b_zr.at[xx])

    def lse_plane(xx):
        arrived(zb.at[xx, others], b_zs.at[xx], b_zr.at[xx])
        yb[xx, place] = lse_of(zb[xx])
        plane_round(yb.at[xx], b_ys.at[xx], b_yr.at[xx])

    def dscores(xx):
        arrived(yb.at[xx, others], b_ys.at[xx], b_yr.at[xx])
        cols = half_of(xx)
        pos, scale = pos_b[:, cols], weight[:, cols]
        factor = scale * jnp.exp(tops[:, cols] - lse_of(yb[xx]))

        @pl.loop(0, tiles)
        def _(t):
            match = jnp.where(ids == pos - t * TILE, scale, 0.0)
            dsc[tile_of(t), cols] = (probs[xx, tile_of(t), :] * factor - match).astype(BF16)

    arrived(qb.at[x, pl.ds(0, NY - 1)], b2_s, b2_r.at[x])
    half_b(x)
    lse_z(x)
    arrived(qb.at[1 - x], b2_s, b2_r.at[1 - x])
    half_b(1 - x)
    lse_z(1 - x)
    gather_a_bulk(1 - x)
    sent(qb.at[x, y, others], b1_s, b1_r)
    sent(qa.at[x, y, others], a1_s, a1_r)
    sent(qb.at[0], b2_s, b2_r.at[0])
    sent(qb.at[0, pl.ds(0, NY - 1)], b2_s, b2_r.at[0])
    arrived(qa.at[x, :, others], a2_s, a2_r.at[x])
    scores_a(x)
    lse_plane(x)
    tops_a(x)
    lse_plane(1 - x)
    sums_a(x)

    def far_copy():
        return remote(gi_s, gi_far, far_s, far_r, other_far)

    def core_copy(n):
        return remote(gi_f.at[n, 1 - core], gi_core.at[n], gi_ss.at[n], gi_rs.at[n], other_core)

    def item_grads(n, ff, cc):
        rows = pl.ds(pl.multiple_of((ff * 2 + cc) * QUARTER, QUARTER), QUARTER)
        gi_f[n, cc] = jnp.dot(
            dsc[rows, :], qb[...].reshape(GROUP, E), preferred_element_type=F32
        )

    def query_grads(xx):
        block = jnp.dot(
            items_t[...], dsc[:, half_of(xx)], preferred_element_type=F32
        ).T.reshape(NY, NZ, OWN, E)
        gq_f[xx] = block
        gq_s[xx] = block.astype(BF16)

        @pl.loop(1, NY)
        def _(k):
            yy = y_peer(k)
            remote(gq_s.at[xx, yy], r1.at[xx, y], s1s, s1r.at[xx], at(z, yy, x)).start()

    def second_stage(xx):
        r1[xx, y] = jnp.zeros((NZ, OWN, E), BF16)
        arrived(r1.at[xx, pl.ds(0, NY - 1)], s1s, s1r.at[xx])
        gq_h[xx] = gq_f[xx, y] + jnp.sum(r1[xx].astype(F32), axis=0)

        @pl.loop(1, NZ)
        def _(k):
            zz = z_peer(k)
            remote(gq_h.at[xx, zz], r2.at[x, z], s2s, s2r.at[x], at(zz, y, xx)).start()

    dscores(x)
    query_grads(x)
    dscores(1 - x)
    item_grads(0, 1 - far, 1 - core)
    core_copy(0).start()
    query_grads(1 - x)
    item_grads(0, 1 - far, core)
    core_copy(0).wait_recv()
    gi_s[...] = (gi_f[0, core] + gi_core[0]).astype(BF16)
    far_copy().start()
    item_grads(1, far, 1 - core)
    core_copy(1).start()
    second_stage(x)
    item_grads(1, far, core)

    arrived(qa.at[1 - x, :, others], a2_s, a2_r.at[1 - x])
    scores_a(1 - x)
    tops_a(1 - x)
    sums_a(1 - x)
    z_round(za, a_zs, a_zr)

    second_stage(1 - x)
    remote(gq_h.at[1 - x, z], r2.at[x, z], s2s, s2r.at[x], at(z, y, 1 - x)).start()

    arrived(za.at[others], a_zs, a_zr)
    z_parts = za[...]
    ya[place, 0:1] = lse_of(z_parts[:, 0:1])
    ya[place, 1:2] = jnp.sum(z_parts[:, 1:2], axis=0)
    plane_round(ya, a_ys, a_yr)

    core_copy(1).wait_recv()
    gi_out[...] = gi_f[1, core] + gi_core[1]
    sent(qa.at[0, :, others], a2_s, a2_r.at[0])
    sent(qa.at[1, :, others], a2_s, a2_r.at[0])
    for half in range(NX):
        sent(zb.at[half, others], b_zs.at[half], b_zr.at[half])
        sent(yb.at[half, others], b_ys.at[half], b_yr.at[half])
    sent(za.at[others], a_zs, a_zr)
    for half in range(NX):
        sent(r1.at[half, pl.ds(0, NY - 1)], s1s, s1r.at[half])
    core_copy(0).wait_send()
    core_copy(1).wait_send()
    far_copy().wait_recv()
    gi_out[...] += gi_far[...].astype(F32)

    arrived(ya.at[others], a_ys, a_yr)
    y_parts = ya[...]
    tops[...] = lse_of(y_parts[:, 0:1]) - jnp.sum(y_parts[:, 1:2], axis=0)
    mine = tops[:, pl.ds(pl.multiple_of((x * NY + y) * NZ * OWN, NZ * OWN), NZ * OWN)]
    pick_row = lax.broadcasted_iota(jnp.int32, (NZ * OWN, OWN), 0)
    pick_col = lax.broadcasted_iota(jnp.int32, (NZ * OWN, OWN), 1)
    pick = (pick_row == z * OWN + pick_col).astype(F32)
    loss_out[...] = jnp.dot(mine, pick, precision=HIGHEST, preferred_element_type=F32)

    r2[x, z] = jnp.zeros((OWN, E), F32)
    arrived(r2.at[x, others], s2s, s2r.at[x])
    arrived(r2.at[1 - x], s2s, s2r.at[1 - x])
    gq_out[...] = gq_h[x, z] + jnp.sum(r2[...].reshape(NX * NZ, OWN, E), axis=0)

    sent(ya.at[others], a_ys, a_yr)
    sent(r2.at[0], s2s, s2r.at[0])
    sent(r2.at[1, others], s2s, s2r.at[1])

    far_copy().wait_send()


def hand_over(*refs):
    copies = [
        pltpu.make_async_copy(source, target, refs[6].at[n])
        for n, (source, target) in enumerate(zip(refs[:3], refs[3:6]))
    ]
    for copy in copies:
        copy.start()
    for copy in copies:
        copy.wait()


def per_device(query_a, query_b, items, positive_a, positive_b, loss_cotangent):
    rows = items.shape[0]
    hbm, vmem = pl.BlockSpec(memory_space=pltpu.HBM), pl.BlockSpec(memory_space=pltpu.VMEM)
    results = (
        jax.ShapeDtypeStruct((1, OWN), F32),
        jax.ShapeDtypeStruct((OWN, E), F32),
        jax.ShapeDtypeStruct((QUARTER, E), F32),
    )
    dma = pltpu.SemaphoreType.DMA
    block = (NX, NY, NZ, OWN, E)
    loss, gq, gi = pl.pallas_call(
        kernel,
        out_shape=[pltpu.VMEM(r.shape, r.dtype) for r in results],
        in_specs=[hbm] * 6,
        out_specs=[vmem] * 3,
        scratch_shapes=[
            pltpu.VMEM((rows, E), BF16),
            pltpu.VMEM((E, rows), BF16),
            pltpu.VMEM(block, BF16),
            pltpu.VMEM(block, BF16),
            pltpu.VMEM((32, 128), jnp.int32),
            pltpu.VMEM((32, 128), jnp.int32),
            pltpu.VMEM((32, 128), F32),
            pltpu.VMEM((1, GROUP), jnp.int32),
            pltpu.VMEM((1, GROUP), jnp.int32),
            pltpu.VMEM((1, GROUP), F32),
            pltpu.VMEM((NX, rows, HALF), F32),
            pltpu.VMEM((rows, HALF), F32),
            pltpu.VMEM((rows, GROUP), BF16),
            pltpu.VMEM(block, F32),
            pltpu.VMEM(block, BF16),
            pltpu.VMEM(block, BF16),
            pltpu.VMEM((NX, NZ, OWN, E), F32),
            pltpu.VMEM((NX, NZ, OWN, E), F32),
            pltpu.VMEM((2, 2, QUARTER, E), F32),
            pltpu.VMEM((QUARTER, E), BF16),
            pltpu.VMEM((2, QUARTER, E), F32),
            pltpu.VMEM((QUARTER, E), BF16),
            pltpu.VMEM((NX, NZ, 1, HALF), F32),
            pltpu.VMEM((NX, NY * NX, 1, HALF), F32),
            pltpu.VMEM((NZ, 2, GROUP), F32),
            pltpu.VMEM((NY * NX, 2, GROUP), F32),
            pltpu.VMEM((1, GROUP), F32),
            pltpu.VMEM((1, HALF), F32),
            dma((6,)),
            dma, dma,
            dma, dma((NX,)),
            dma, dma,
            dma, dma((NX,)),
            dma((NX,)), dma((NX,)),
            dma((NX,)), dma((NX,)),
            dma, dma,
            dma, dma,
            dma, dma((NX,)),
            dma, dma((NX,)),
            dma((2,)), dma((2,)),
            dma, dma,
        ],
        compiler_params=pltpu.CompilerParams(
            collective_id=0, has_side_effects=True, vmem_limit_bytes=56 * 1024 * 1024
        ),
    )(
        *(
            pltpu.with_memory_space_constraint(operand, pltpu.HBM)
            for operand in (
                query_a,
                query_b,
                items,
                positive_a.reshape(32, 128),
                positive_b.reshape(32, 128),
                loss_cotangent.reshape(32, 128),
            )
        )
    )
    loss, gq, gi = pl.pallas_call(
        hand_over,
        out_shape=results,
        in_specs=[vmem] * 3,
        out_specs=[hbm] * 3,
        scratch_shapes=[dma((3,))],
        compiler_params=pltpu.CompilerParams(vmem_limit_bytes=1024 * 1024),
    )(*(pltpu.with_memory_space_constraint(result, pltpu.VMEM) for result in (loss, gq, gi)))
    return loss.reshape(OWN), gq, gi


def solution(mesh):
    return jax.shard_map(
        per_device,
        mesh=mesh,
        in_specs=(
            P(("item", "user"), None),
            P(("item", "user"), None),
            P("item", None),
            P(),
            P(),
            P(),
        ),
        out_specs=(P(("item", "user")), P(("item", "user"), None), P(("item", "user"), None)),
        check_vma=False,
    )
```

```python
import functools

import jax
import jax.numpy as jnp
from jax import lax
from jax.experimental import pallas as pl
from jax.experimental.pallas import tpu as pltpu
from jax.sharding import PartitionSpec as P

MESH = pl.DeviceIdType.MESH
F32 = jnp.float32
BF16 = jnp.bfloat16
HIGHEST = lax.Precision.HIGHEST

NZ, NY, NX = 8, 4, 2
OWN = 16
E = 256
GROUP = NZ * NY * NX * OWN
HALF = GROUP // NX
TILE = 32
QUARTER = 512


def remote(src, dst, send_sem, recv_sem, device):
    return pltpu.make_async_remote_copy(
        src_ref=src,
        dst_ref=dst,
        send_sem=send_sem,
        recv_sem=recv_sem,
        device_id=device,
        device_id_type=MESH,
    )


def group_row(table, selector, row_of):
    picked = jnp.dot(table, selector, precision=HIGHEST, preferred_element_type=F32)
    rows = lax.broadcasted_iota(jnp.int32, picked.shape, 0)
    return jnp.sum(jnp.where(rows == row_of, picked, 0.0), axis=0, keepdims=True)


def lse_of(parts):
    top = jnp.max(parts, axis=0)
    return top + jnp.log(jnp.sum(jnp.exp(parts - top[None]), axis=0))


def kernel(
    qa_in, qb_in, items_in, pa_in, pb_in, w_in,
    loss_out, gq_out, gi_out,
    items_v, items_t, qa, qb, pa_v, pb_v, w_v, pos_a, pos_b, weight,
    probs, score_a, dsc, gq_f, gq_s,
    r1, gq_h, r2,
    gi_f, gi_s, gi_core, gi_far,
    zb, yb, za, ya,
    tops,
    in_sem, b1_s, b1_r, b2_s, b2_r, a1_s, a1_r, a2_s, a2_r,
    b_zs, b_zr, b_ys, b_yr, a_zs, a_zr, a_ys, a_yr,
    s1s, s1r, s2s, s2r, gi_ss, gi_rs, far_s, far_r,
):
    item = lax.axis_index("item")
    user = lax.axis_index("user")
    z, y, x = item // (NY * NX), (item // NX) % NY, item % NX
    place = y * NX + x
    far, core = user // 2, user % 2
    items_rows = items_v.shape[0]
    offset = item * items_rows

    def at(zz, yy, xx):
        return {"item": (zz * NY + yy) * NX + xx}

    def z_peer(k):
        return lax.rem(z + k, NZ)

    def y_peer(k):
        return lax.rem(y + k, NY)

    def plane_peer(k):
        return lax.rem(place + k, NY * NX)

    loads = [
        pltpu.make_async_copy(source, target, in_sem.at[n])
        for n, (source, target) in enumerate(
            (
                (qb_in, qb.at[x, y, z]),
                (qa_in, qa.at[x, y, z]),
                (pa_in, pa_v),
                (pb_in, pb_v),
                (w_in, w_v),
                (items_in, items_v),
            )
        )
    ]

    barrier = pltpu.get_barrier_semaphore()

    @pl.loop(1, NZ)
    def _(k):
        pl.semaphore_signal(barrier, inc=1, device_id=at(z_peer(k), y, x), device_id_type=MESH)
        pl.semaphore_signal(barrier, inc=1, device_id=at(z_peer(k), y, 1 - x), device_id_type=MESH)

    @pl.loop(1, NY * NX)
    def _(k):
        p = plane_peer(k)
        pl.semaphore_signal(barrier, inc=1, device_id=at(z, p // NX, p % NX), device_id_type=MESH)

    other_core = {"user": far * 2 + 1 - core}
    other_far = {"user": (1 - far) * 2 + core}
    pl.semaphore_signal(barrier, inc=1, device_id=other_core, device_id_type=MESH)
    pl.semaphore_signal(barrier, inc=1, device_id=other_far, device_id_type=MESH)

    for load in loads:
        load.start()

    pl.semaphore_wait(barrier, 2 * (NZ - 1) + (NY * NX - 1) + 2)

    def sent(refs, send_sem, recv_sem):
        remote(refs, refs, send_sem, recv_sem, other_core).wait_send()

    def arrived(refs, send_sem, recv_sem):
        remote(refs, refs, send_sem, recv_sem, other_core).wait_recv()

    @pl.loop(1, NZ)
    def _(k):
        remote(qb_in, qb.at[x, y, z], b1_s, b1_r, at(z_peer(k), y, x)).start()

    def gather_b_bulk():
        block = qb.at[x, y]

        @pl.loop(1, NY)
        def _(k):
            remote(block, block, b2_s, b2_r.at[x], at(z, y_peer(k), x)).start()

        @pl.loop(0, NY)
        def _(k):
            remote(block, block, b2_s, b2_r.at[x], at(z, y_peer(k), 1 - x)).start()

    @pl.loop(1, NY * NX)
    def _(k):
        p = plane_peer(k)
        remote(qa_in, qa.at[x, y, z], a1_s, a1_r, at(z, p // NX, p % NX)).start()

    def gather_a_bulk(xx):
        block = qa.at[xx, :, z]

        @pl.loop(1, NZ)
        def _(k):
            remote(block, block, a2_s, a2_r.at[xx], at(z_peer(k), y, x)).start()

    others = pl.ds(0, NZ - 1)

    lanes = lax.broadcasted_iota(jnp.int32, (1, GROUP), 1)
    own_of = lanes % OWN
    z_of = (lanes // OWN) % NZ
    y_of = (lanes // (OWN * NZ)) % NY
    x_of = lanes // (OWN * NZ * NY)
    ks = lax.broadcasted_iota(jnp.int32, (128, GROUP), 0)
    selector = (ks == x_of * (4 * OWN) + user * OWN + own_of).astype(F32)
    row_of = z_of * NY + y_of
    for load in loads[2:5]:
        load.wait()
    pos_a[...] = group_row(pa_v[...].astype(F32), selector, row_of).astype(jnp.int32) - offset
    pos_b[...] = group_row(pb_v[...].astype(F32), selector, row_of).astype(jnp.int32) - offset
    weight[...] = group_row(w_v[...], selector, row_of)

    loads[0].wait()
    arrived(qb.at[x, y, others], b1_s, b1_r)
    gather_b_bulk()
    loads[1].wait()
    arrived(qa.at[x, y, others], a1_s, a1_r)
    gather_a_bulk(x)

    loads[5].wait()
    for part in range(items_rows // QUARTER):
        rows = pl.ds(part * QUARTER, QUARTER)
        items_t[:, rows] = items_v[rows, :].T

    tiles = [slice(r, r + TILE) for r in range(0, items_rows, TILE)]
    ids = lax.broadcasted_iota(jnp.int32, (TILE, HALF), 0)

    def half_of(xx):
        return pl.ds(pl.multiple_of(xx * HALF, HALF), HALF)

    def fold(values, op):
        return op(values.reshape(TILE // 8, 8, HALF), axis=0)

    def scores(q, xx):
        users = q[xx].reshape(HALF, E)
        return lax.dot_general(
            items_v[...], users, (((1,), (1,)), ((), ())), preferred_element_type=F32
        )

    zero = jnp.zeros((8, HALF), F32)
    least = jnp.full((8, HALF), -jnp.inf, F32)

    def half_b(xx):
        probs[xx] = scores(qb, xx)

        top = least
        for rows in tiles:
            top = jnp.maximum(top, fold(probs[xx, rows, :], jnp.max))
        top = jnp.max(top, axis=0, keepdims=True)
        total = zero
        for rows in tiles:
            p = jnp.exp(probs[xx, rows, :] - top)
            probs[xx, rows, :] = p
            total = total + fold(p, jnp.sum)
        total = jnp.sum(total, axis=0, keepdims=True)
        tops[:, half_of(xx)] = top
        zb[z, :, half_of(xx)] = top + jnp.log(total)

    def half_a(xx):
        score_a[...] = scores(qa, xx)
        pos = pos_a[:, half_of(xx)]
        top, hit = least, zero
        for rows in tiles:
            score = score_a[rows, :]
            top = jnp.maximum(top, fold(score, jnp.max))
            hit = hit + fold(jnp.where(ids == pos - rows.start, score, 0.0), jnp.sum)
        top = jnp.max(top, axis=0, keepdims=True)
        total = zero
        for rows in tiles:
            total = total + fold(jnp.exp(score_a[rows, :] - top), jnp.sum)
        total = jnp.sum(total, axis=0, keepdims=True)
        za[z, 0:1, half_of(xx)] = top + jnp.log(total)
        za[z, 1:2, half_of(xx)] = jnp.sum(hit, axis=0, keepdims=True)

    def z_round(buf, ss, rs):
        @pl.loop(1, NZ)
        def _(k):
            remote(buf.at[z], buf.at[z], ss, rs, at(z_peer(k), y, x)).start()

    def plane_round(buf, ss, rs):
        @pl.loop(1, NY * NX)
        def _(k):
            p = plane_peer(k)
            remote(buf.at[place], buf.at[place], ss, rs, at(z, p // NX, p % NX)).start()

    arrived(qb.at[x, pl.ds(0, NY - 1)], b2_s, b2_r.at[x])
    half_b(x)
    arrived(qb.at[1 - x], b2_s, b2_r.at[1 - x])
    half_b(1 - x)
    z_round(zb, b_zs, b_zr)
    gather_a_bulk(1 - x)
    sent(qb.at[x, y, others], b1_s, b1_r)
    sent(qa.at[x, y, others], a1_s, a1_r)
    sent(qb.at[0], b2_s, b2_r.at[0])
    sent(qb.at[0, pl.ds(0, NY - 1)], b2_s, b2_r.at[0])
    arrived(zb.at[others], b_zs, b_zr)
    yb[place] = lse_of(zb[...])
    plane_round(yb, b_ys, b_yr)
    arrived(qa.at[x, :, others], a2_s, a2_r.at[x])
    half_a(x)
    sent(zb.at[others], b_zs, b_zr)

    arrived(yb.at[others], b_ys, b_yr)
    factor = weight[...] * jnp.exp(tops[...] - lse_of(yb[...]))

    def quarter_of(ff, cc):
        return pl.ds(pl.multiple_of((ff * 2 + cc) * QUARTER, QUARTER), QUARTER)

    def dscores(ff, cc):
        start = (ff * 2 + cc) * QUARTER
        for xx in range(NX):
            cols = slice(xx * HALF, (xx + 1) * HALF)
            pos, scale, ratio = pos_b[:, cols] - start, weight[:, cols], factor[:, cols]
            for r in range(0, QUARTER, TILE):
                rows = pl.ds(pl.multiple_of(start + r, TILE), TILE)
                match = jnp.where(ids == pos - r, scale, 0.0)
                dsc[rows, cols] = (probs[xx, rows, :] * ratio - match).astype(BF16)

    def far_copy():
        return remote(gi_s, gi_far, far_s, far_r, other_far)

    def core_copy(n):
        return remote(gi_f.at[n, 1 - core], gi_core.at[n], gi_ss.at[n], gi_rs.at[n], other_core)

    def item_grads(n, ff, cc):
        gi_f[n, cc] = jnp.dot(
            dsc[quarter_of(ff, cc), :], qb[...].reshape(GROUP, E), preferred_element_type=F32
        )

    def query_grads(xx):
        block = jnp.dot(
            items_t[...], dsc[:, half_of(xx)], preferred_element_type=F32
        ).T.reshape(NY, NZ, OWN, E)
        gq_f[xx] = block
        gq_s[xx] = block.astype(BF16)

        @pl.loop(1, NY)
        def _(k):
            yy = y_peer(k)
            remote(gq_s.at[xx, yy], r1.at[place], s1s, s1r, at(z, yy, xx)).start()

        @pl.when(x != xx)
        def _():
            remote(gq_s.at[xx, y], r1.at[place], s1s, s1r, at(z, y, xx)).start()

    dscores(1 - far, 1 - core)
    item_grads(0, 1 - far, 1 - core)
    core_copy(0).start()
    dscores(1 - far, core)
    item_grads(0, 1 - far, core)
    dscores(far, 1 - core)
    dscores(far, core)
    query_grads(1 - x)
    core_copy(0).wait_recv()
    gi_s[...] = (gi_f[0, core] + gi_core[0]).astype(BF16)
    far_copy().start()

    query_grads(x)
    item_grads(1, far, 1 - core)
    core_copy(1).start()
    item_grads(1, far, core)

    arrived(qa.at[1 - x, :, others], a2_s, a2_r.at[1 - x])
    half_a(1 - x)
    z_round(za, a_zs, a_zr)

    r1[place] = jnp.zeros((NZ, OWN, E), BF16)
    r2[z] = jnp.zeros((OWN, E), F32)
    arrived(r1.at[others], s1s, s1r)
    gq_h[...] = gq_f[x, y] + jnp.sum(r1[...].astype(F32), axis=0)

    @pl.loop(1, NZ)
    def _(k):
        zz = z_peer(k)
        remote(gq_h.at[zz], r2.at[z], s2s, s2r, at(zz, y, x)).start()

    arrived(za.at[others], a_zs, a_zr)
    z_parts = za[...]
    ya[place, 0:1] = lse_of(z_parts[:, 0:1])
    ya[place, 1:2] = jnp.sum(z_parts[:, 1:2], axis=0)
    plane_round(ya, a_ys, a_yr)

    core_copy(1).wait_recv()
    gi_out[...] = gi_f[1, core] + gi_core[1]
    sent(qa.at[0, :, others], a2_s, a2_r.at[0])
    sent(qa.at[1, :, others], a2_s, a2_r.at[0])
    sent(yb.at[others], b_ys, b_yr)
    sent(za.at[others], a_zs, a_zr)
    sent(r1.at[others], s1s, s1r)
    core_copy(0).wait_send()
    core_copy(1).wait_send()
    far_copy().wait_recv()
    gi_out[...] += gi_far[...].astype(F32)

    arrived(ya.at[others], a_ys, a_yr)
    y_parts = ya[...]
    tops[...] = lse_of(y_parts[:, 0:1]) - jnp.sum(y_parts[:, 1:2], axis=0)
    mine = tops[:, pl.ds(pl.multiple_of((x * NY + y) * NZ * OWN, NZ * OWN), NZ * OWN)]
    pick_row = lax.broadcasted_iota(jnp.int32, (NZ * OWN, OWN), 0)
    pick_col = lax.broadcasted_iota(jnp.int32, (NZ * OWN, OWN), 1)
    pick = (pick_row == z * OWN + pick_col).astype(F32)
    loss_out[...] = jnp.dot(mine, pick, precision=HIGHEST, preferred_element_type=F32)

    arrived(r2.at[others], s2s, s2r)
    gq_out[...] = gq_h[z] + jnp.sum(r2[...], axis=0)

    sent(ya.at[others], a_ys, a_yr)
    sent(r2.at[others], s2s, s2r)

    far_copy().wait_send()


def hand_over(*refs):
    copies = [
        pltpu.make_async_copy(source, target, refs[6].at[n])
        for n, (source, target) in enumerate(zip(refs[:3], refs[3:6]))
    ]
    for copy in copies:
        copy.start()
    for copy in copies:
        copy.wait()


def per_device(query_a, query_b, items, positive_a, positive_b, loss_cotangent):
    rows = items.shape[0]
    hbm, vmem = pl.BlockSpec(memory_space=pltpu.HBM), pl.BlockSpec(memory_space=pltpu.VMEM)
    results = (
        jax.ShapeDtypeStruct((1, OWN), F32),
        jax.ShapeDtypeStruct((OWN, E), F32),
        jax.ShapeDtypeStruct((QUARTER, E), F32),
    )
    dma = pltpu.SemaphoreType.DMA
    block = (NX, NY, NZ, OWN, E)
    loss, gq, gi = pl.pallas_call(
        kernel,
        out_shape=[pltpu.VMEM(r.shape, r.dtype) for r in results],
        in_specs=[hbm] * 6,
        out_specs=[vmem] * 3,
        scratch_shapes=[
            pltpu.VMEM((rows, E), BF16),
            pltpu.VMEM((E, rows), BF16),
            pltpu.VMEM(block, BF16),
            pltpu.VMEM(block, BF16),
            pltpu.VMEM((32, 128), jnp.int32),
            pltpu.VMEM((32, 128), jnp.int32),
            pltpu.VMEM((32, 128), F32),
            pltpu.VMEM((1, GROUP), jnp.int32),
            pltpu.VMEM((1, GROUP), jnp.int32),
            pltpu.VMEM((1, GROUP), F32),
            pltpu.VMEM((NX, rows, HALF), F32),
            pltpu.VMEM((rows, HALF), F32),
            pltpu.VMEM((rows, GROUP), BF16),
            pltpu.VMEM(block, F32),
            pltpu.VMEM(block, BF16),
            pltpu.VMEM((NY * NX, NZ, OWN, E), BF16),
            pltpu.VMEM((NZ, OWN, E), F32),
            pltpu.VMEM((NZ, OWN, E), F32),
            pltpu.VMEM((2, 2, QUARTER, E), F32),
            pltpu.VMEM((QUARTER, E), BF16),
            pltpu.VMEM((2, QUARTER, E), F32),
            pltpu.VMEM((QUARTER, E), BF16),
            pltpu.VMEM((NZ, 1, GROUP), F32),
            pltpu.VMEM((NY * NX, 1, GROUP), F32),
            pltpu.VMEM((NZ, 2, GROUP), F32),
            pltpu.VMEM((NY * NX, 2, GROUP), F32),
            pltpu.VMEM((1, GROUP), F32),
            dma((6,)),
            dma, dma,
            dma, dma((NX,)),
            dma, dma,
            dma, dma((NX,)),
            dma, dma,
            dma, dma,
            dma, dma,
            dma, dma,
            dma, dma,
            dma, dma,
            dma((2,)), dma((2,)),
            dma, dma,
        ],
        compiler_params=pltpu.CompilerParams(
            collective_id=0, has_side_effects=True, vmem_limit_bytes=56 * 1024 * 1024
        ),
    )(
        *(
            pltpu.with_memory_space_constraint(operand, pltpu.HBM)
            for operand in (
                query_a,
                query_b,
                items,
                positive_a.reshape(32, 128),
                positive_b.reshape(32, 128),
                loss_cotangent.reshape(32, 128),
            )
        )
    )
    loss, gq, gi = pl.pallas_call(
        hand_over,
        out_shape=results,
        in_specs=[vmem] * 3,
        out_specs=[hbm] * 3,
        scratch_shapes=[dma((3,))],
        compiler_params=pltpu.CompilerParams(vmem_limit_bytes=1024 * 1024),
    )(*(pltpu.with_memory_space_constraint(result, pltpu.VMEM) for result in (loss, gq, gi)))
    return loss.reshape(OWN), gq, gi


def solution(mesh):
    return jax.shard_map(
        per_device,
        mesh=mesh,
        in_specs=(
            P(("item", "user"), None),
            P(("item", "user"), None),
            P("item", None),
            P(),
            P(),
            P(),
        ),
        out_specs=(P(("item", "user")), P(("item", "user"), None), P(("item", "user"), None)),
        check_vma=False,
    )
```

```python
import functools

import jax
import jax.numpy as jnp
from jax import lax
from jax.experimental import pallas as pl
from jax.experimental.pallas import tpu as pltpu
from jax.sharding import PartitionSpec as P

MESH = pl.DeviceIdType.MESH
F32 = jnp.float32
BF16 = jnp.bfloat16

NZ, NY, NX = 8, 4, 2
OWN = 16
E = 256
GROUP = NZ * NY * NX * OWN
HALF = GROUP // NX
TILE = 32
QUARTER = 512


def remote(src, dst, send_sem, recv_sem, device):
    return pltpu.make_async_remote_copy(
        src_ref=src,
        dst_ref=dst,
        send_sem=send_sem,
        recv_sem=recv_sem,
        device_id=device,
        device_id_type=MESH,
    )


def exact_parts(table):
    if table.dtype == jnp.int32:
        parts = (table & 63, table & (63 << 6), table & (63 << 12))
        return [part.astype(F32).astype(BF16) for part in parts]
    high = table.astype(BF16)
    rest = table - high.astype(F32)
    middle = rest.astype(BF16)
    return [high, middle, (rest - middle.astype(F32)).astype(BF16)]


def group_rows(tables, selector, row_of):
    parts = [part for table in tables for part in exact_parts(table)]
    picked = jnp.dot(jnp.concatenate(parts, axis=0), selector, preferred_element_type=F32)
    picked = picked.reshape(len(tables), 3, 32, GROUP)
    rows = lax.broadcasted_iota(jnp.int32, (32, GROUP), 0) == row_of
    return [
        jnp.sum(jnp.where(rows, (p[0] + p[1]) + p[2], 0.0), axis=0, keepdims=True) for p in picked
    ]


def lse_of(parts):
    top = jnp.max(parts, axis=0)
    return top + jnp.log(jnp.sum(jnp.exp(parts - top[None]), axis=0))


def kernel(
    qa_in, qb_in, items_in, pa_in, pb_in, w_in,
    loss_out, gq_out, gi_out,
    items_v, items_t, qa, qb, pa_v, pb_v, w_v, pos_a, pos_b, weight,
    probs, score_a, dsc, gq_f, gq_s,
    r1, gq_h, r2,
    gi_f, gi_s, gi_core, gi_far,
    zb, yb, za, ya,
    tops,
    in_sem, b1_s, b1_r, b2_s, b2_r, a1_s, a1_r, a2_s, a2_r,
    b_zs, b_zr, b_ys, b_yr, a_zs, a_zr, a_ys, a_yr,
    s1s, s1r, s2s, s2r, gi_ss, gi_rs, far_s, far_r,
):
    item = lax.axis_index("item")
    user = lax.axis_index("user")
    z, y, x = item // (NY * NX), (item // NX) % NY, item % NX
    place = y * NX + x
    far, core = user // 2, user % 2
    items_rows = items_v.shape[0]
    offset = item * items_rows

    def at(zz, yy, xx):
        return {"item": (zz * NY + yy) * NX + xx}

    def z_peer(k):
        return lax.rem(z + k, NZ)

    def y_peer(k):
        return lax.rem(y + k, NY)

    def plane_peer(k):
        return lax.rem(place + k, NY * NX)

    loads = [
        pltpu.make_async_copy(source, target, in_sem.at[n])
        for n, (source, target) in enumerate(
            (
                (qb_in, qb.at[x, y, z]),
                (qa_in, qa.at[x, y, z]),
                (pa_in, pa_v),
                (pb_in, pb_v),
                (w_in, w_v),
                (items_in, items_v),
            )
        )
    ]

    barrier = pltpu.get_barrier_semaphore()

    @pl.loop(1, NZ)
    def _(k):
        pl.semaphore_signal(barrier, inc=1, device_id=at(z_peer(k), y, x), device_id_type=MESH)
        pl.semaphore_signal(barrier, inc=1, device_id=at(z_peer(k), y, 1 - x), device_id_type=MESH)

    @pl.loop(1, NY * NX)
    def _(k):
        p = plane_peer(k)
        pl.semaphore_signal(barrier, inc=1, device_id=at(z, p // NX, p % NX), device_id_type=MESH)

    other_core = {"user": far * 2 + 1 - core}
    other_far = {"user": (1 - far) * 2 + core}
    pl.semaphore_signal(barrier, inc=1, device_id=other_core, device_id_type=MESH)
    pl.semaphore_signal(barrier, inc=1, device_id=other_far, device_id_type=MESH)

    for load in loads:
        load.start()

    pl.semaphore_wait(barrier, 2 * (NZ - 1) + (NY * NX - 1) + 2)

    def sent(refs, send_sem, recv_sem):
        remote(refs, refs, send_sem, recv_sem, other_core).wait_send()

    def arrived(refs, send_sem, recv_sem):
        remote(refs, refs, send_sem, recv_sem, other_core).wait_recv()

    @pl.loop(1, NZ)
    def _(k):
        remote(qb_in, qb.at[x, y, z], b1_s, b1_r, at(z_peer(k), y, x)).start()

    def gather_b_bulk():
        block = qb.at[x, y]

        @pl.loop(1, NY)
        def _(k):
            remote(block, block, b2_s, b2_r.at[x], at(z, y_peer(k), x)).start()

        @pl.loop(0, NY)
        def _(k):
            remote(block, block, b2_s, b2_r.at[x], at(z, y_peer(k), 1 - x)).start()

    @pl.loop(1, NY * NX)
    def _(k):
        p = plane_peer(k)
        remote(qa_in, qa.at[x, y, z], a1_s, a1_r, at(z, p // NX, p % NX)).start()

    def gather_a_bulk(xx):
        block = qa.at[xx, :, z]

        @pl.loop(1, NZ)
        def _(k):
            remote(block, block, a2_s, a2_r.at[xx], at(z_peer(k), y, x)).start()

    others = pl.ds(0, NZ - 1)

    loads[0].wait()
    arrived(qb.at[x, y, others], b1_s, b1_r)
    gather_b_bulk()
    loads[1].wait()
    arrived(qa.at[x, y, others], a1_s, a1_r)
    gather_a_bulk(x)

    lanes = lax.broadcasted_iota(jnp.int32, (1, GROUP), 1)
    own_of = lanes % OWN
    z_of = (lanes // OWN) % NZ
    y_of = (lanes // (OWN * NZ)) % NY
    x_of = lanes // (OWN * NZ * NY)
    ks = lax.broadcasted_iota(jnp.int32, (128, GROUP), 0)
    selector = (ks == x_of * (4 * OWN) + user * OWN + own_of).astype(F32).astype(BF16)
    for load in loads[2:5]:
        load.wait()
    row_a, row_b, weight[...] = group_rows(
        (pa_v[...], pb_v[...], w_v[...]), selector, z_of * NY + y_of
    )
    pos_a[...] = row_a.astype(jnp.int32) - offset
    pos_b[...] = row_b.astype(jnp.int32) - offset

    loads[5].wait()
    for part in range(items_rows // QUARTER):
        rows = pl.ds(part * QUARTER, QUARTER)
        items_t[:, rows] = items_v[rows, :].T

    tiles = [slice(r, r + TILE) for r in range(0, items_rows, TILE)]
    ids = lax.broadcasted_iota(jnp.int32, (TILE, HALF), 0)

    def half_of(xx):
        return pl.ds(pl.multiple_of(xx * HALF, HALF), HALF)

    def fold(values, op):
        return op(values.reshape(TILE // 8, 8, HALF), axis=0)

    def scores(q, xx):
        users = q[xx].reshape(HALF, E)
        return lax.dot_general(
            items_v[...], users, (((1,), (1,)), ((), ())), preferred_element_type=F32
        )

    zero = jnp.zeros((8, HALF), F32)
    least = jnp.full((8, HALF), -jnp.inf, F32)

    def half_b(xx):
        probs[xx] = scores(qb, xx)

        top = least
        for rows in tiles:
            top = jnp.maximum(top, fold(probs[xx, rows, :], jnp.max))
        top = jnp.max(top, axis=0, keepdims=True)
        total = zero
        for rows in tiles:
            p = jnp.exp(probs[xx, rows, :] - top)
            probs[xx, rows, :] = p
            total = total + fold(p, jnp.sum)
        total = jnp.sum(total, axis=0, keepdims=True)
        tops[:, half_of(xx)] = top
        zb[z, :, half_of(xx)] = top + jnp.log(total)

    def half_a(xx):
        score_a[...] = scores(qa, xx)
        pos = pos_a[:, half_of(xx)]
        top, hit = least, zero
        for rows in tiles:
            score = score_a[rows, :]
            top = jnp.maximum(top, fold(score, jnp.max))
            hit = hit + fold(jnp.where(ids == pos - rows.start, score, 0.0), jnp.sum)
        top = jnp.max(top, axis=0, keepdims=True)
        total = zero
        for rows in tiles:
            total = total + fold(jnp.exp(score_a[rows, :] - top), jnp.sum)
        total = jnp.sum(total, axis=0, keepdims=True)
        za[z, 0:1, half_of(xx)] = top + jnp.log(total)
        za[z, 1:2, half_of(xx)] = jnp.sum(hit, axis=0, keepdims=True)

    def z_round(buf, ss, rs):
        @pl.loop(1, NZ)
        def _(k):
            remote(buf.at[z], buf.at[z], ss, rs, at(z_peer(k), y, x)).start()

    def plane_round(buf, ss, rs):
        @pl.loop(1, NY * NX)
        def _(k):
            p = plane_peer(k)
            remote(buf.at[place], buf.at[place], ss, rs, at(z, p // NX, p % NX)).start()

    arrived(qb.at[x, pl.ds(0, NY - 1)], b2_s, b2_r.at[x])
    half_b(x)
    arrived(qb.at[1 - x], b2_s, b2_r.at[1 - x])
    half_b(1 - x)
    z_round(zb, b_zs, b_zr)
    gather_a_bulk(1 - x)
    sent(qb.at[x, y, others], b1_s, b1_r)
    sent(qa.at[x, y, others], a1_s, a1_r)
    sent(qb.at[0], b2_s, b2_r.at[0])
    sent(qb.at[0, pl.ds(0, NY - 1)], b2_s, b2_r.at[0])
    arrived(zb.at[others], b_zs, b_zr)
    yb[place] = lse_of(zb[...])
    plane_round(yb, b_ys, b_yr)
    arrived(qa.at[x, :, others], a2_s, a2_r.at[x])
    half_a(x)
    sent(zb.at[others], b_zs, b_zr)

    arrived(yb.at[others], b_ys, b_yr)
    factor = weight[...] * jnp.exp(tops[...] - lse_of(yb[...]))

    def quarter_of(ff, cc):
        return pl.ds(pl.multiple_of((ff * 2 + cc) * QUARTER, QUARTER), QUARTER)

    def dscores(ff, cc):
        start = (ff * 2 + cc) * QUARTER
        for xx in range(NX):
            cols = slice(xx * HALF, (xx + 1) * HALF)
            pos, scale, ratio = pos_b[:, cols] - start, weight[:, cols], factor[:, cols]
            for r in range(0, QUARTER, TILE):
                rows = pl.ds(pl.multiple_of(start + r, TILE), TILE)
                match = jnp.where(ids == pos - r, scale, 0.0)
                dsc[rows, cols] = (probs[xx, rows, :] * ratio - match).astype(BF16)

    def far_copy():
        return remote(gi_s, gi_far, far_s, far_r, other_far)

    def core_copy(n):
        return remote(gi_f.at[n, 1 - core], gi_core.at[n], gi_ss.at[n], gi_rs.at[n], other_core)

    def item_grads(n, ff, cc):
        gi_f[n, cc] = jnp.dot(
            dsc[quarter_of(ff, cc), :], qb[...].reshape(GROUP, E), preferred_element_type=F32
        )

    def query_grads(xx):
        block = jnp.dot(
            items_t[...], dsc[:, half_of(xx)], preferred_element_type=F32
        ).T.reshape(NY, NZ, OWN, E)
        gq_f[xx] = block
        gq_s[xx] = block.astype(BF16)

        @pl.loop(1, NY)
        def _(k):
            yy = y_peer(k)
            remote(gq_s.at[xx, yy], r1.at[place], s1s, s1r, at(z, yy, xx)).start()

        @pl.when(x != xx)
        def _():
            remote(gq_s.at[xx, y], r1.at[place], s1s, s1r, at(z, y, xx)).start()

    dscores(1 - far, 1 - core)
    item_grads(0, 1 - far, 1 - core)
    core_copy(0).start()
    dscores(1 - far, core)
    item_grads(0, 1 - far, core)
    dscores(far, 1 - core)
    dscores(far, core)
    query_grads(1 - x)
    core_copy(0).wait_recv()
    gi_s[...] = (gi_f[0, core] + gi_core[0]).astype(BF16)
    far_copy().start()

    query_grads(x)
    item_grads(1, far, 1 - core)
    core_copy(1).start()
    item_grads(1, far, core)

    arrived(qa.at[1 - x, :, others], a2_s, a2_r.at[1 - x])
    half_a(1 - x)
    z_round(za, a_zs, a_zr)

    r1[place] = jnp.zeros((NZ, OWN, E), BF16)
    r2[z] = jnp.zeros((OWN, E), F32)
    arrived(r1.at[others], s1s, s1r)
    gq_h[...] = gq_f[x, y] + jnp.sum(r1[...].astype(F32), axis=0)

    @pl.loop(1, NZ)
    def _(k):
        zz = z_peer(k)
        remote(gq_h.at[zz], r2.at[z], s2s, s2r, at(zz, y, x)).start()

    arrived(za.at[others], a_zs, a_zr)
    z_parts = za[...]
    ya[place, 0:1] = lse_of(z_parts[:, 0:1])
    ya[place, 1:2] = jnp.sum(z_parts[:, 1:2], axis=0)
    plane_round(ya, a_ys, a_yr)

    core_copy(1).wait_recv()
    gi_out[...] = gi_f[1, core] + gi_core[1]
    sent(qa.at[0, :, others], a2_s, a2_r.at[0])
    sent(qa.at[1, :, others], a2_s, a2_r.at[0])
    sent(yb.at[others], b_ys, b_yr)
    sent(za.at[others], a_zs, a_zr)
    sent(r1.at[others], s1s, s1r)
    core_copy(0).wait_send()
    core_copy(1).wait_send()
    far_copy().wait_recv()
    gi_out[...] += gi_far[...].astype(F32)

    arrived(ya.at[others], a_ys, a_yr)
    y_parts = ya[...]
    tops[...] = lse_of(y_parts[:, 0:1]) - jnp.sum(y_parts[:, 1:2], axis=0)
    mine = tops[:, pl.ds(pl.multiple_of((x * NY + y) * NZ * OWN, NZ * OWN), NZ * OWN)]
    loss_out[...] = pltpu.roll(
        jnp.broadcast_to(mine, (8, NZ * OWN)), (NZ - z) * OWN % (NZ * OWN), 1
    )[0:1, 0:OWN]

    arrived(r2.at[others], s2s, s2r)
    gq_out[...] = gq_h[z] + jnp.sum(r2[...], axis=0)

    sent(ya.at[others], a_ys, a_yr)
    sent(r2.at[others], s2s, s2r)

    far_copy().wait_send()


def hand_over(*refs):
    copies = [
        pltpu.make_async_copy(source, target, refs[6].at[n])
        for n, (source, target) in enumerate(zip(refs[:3], refs[3:6]))
    ]
    for copy in copies:
        copy.start()
    for copy in copies:
        copy.wait()


def per_device(query_a, query_b, items, positive_a, positive_b, loss_cotangent):
    rows = items.shape[0]
    hbm, vmem = pl.BlockSpec(memory_space=pltpu.HBM), pl.BlockSpec(memory_space=pltpu.VMEM)
    results = (
        jax.ShapeDtypeStruct((1, OWN), F32),
        jax.ShapeDtypeStruct((OWN, E), F32),
        jax.ShapeDtypeStruct((QUARTER, E), F32),
    )
    dma = pltpu.SemaphoreType.DMA
    block = (NX, NY, NZ, OWN, E)
    loss, gq, gi = pl.pallas_call(
        kernel,
        out_shape=[pltpu.VMEM(r.shape, r.dtype) for r in results],
        in_specs=[hbm] * 6,
        out_specs=[vmem] * 3,
        scratch_shapes=[
            pltpu.VMEM((rows, E), BF16),
            pltpu.VMEM((E, rows), BF16),
            pltpu.VMEM(block, BF16),
            pltpu.VMEM(block, BF16),
            pltpu.VMEM((32, 128), jnp.int32),
            pltpu.VMEM((32, 128), jnp.int32),
            pltpu.VMEM((32, 128), F32),
            pltpu.VMEM((1, GROUP), jnp.int32),
            pltpu.VMEM((1, GROUP), jnp.int32),
            pltpu.VMEM((1, GROUP), F32),
            pltpu.VMEM((NX, rows, HALF), F32),
            pltpu.VMEM((rows, HALF), F32),
            pltpu.VMEM((rows, GROUP), BF16),
            pltpu.VMEM(block, F32),
            pltpu.VMEM(block, BF16),
            pltpu.VMEM((NY * NX, NZ, OWN, E), BF16),
            pltpu.VMEM((NZ, OWN, E), F32),
            pltpu.VMEM((NZ, OWN, E), F32),
            pltpu.VMEM((2, 2, QUARTER, E), F32),
            pltpu.VMEM((QUARTER, E), BF16),
            pltpu.VMEM((2, QUARTER, E), F32),
            pltpu.VMEM((QUARTER, E), BF16),
            pltpu.VMEM((NZ, 1, GROUP), F32),
            pltpu.VMEM((NY * NX, 1, GROUP), F32),
            pltpu.VMEM((NZ, 2, GROUP), F32),
            pltpu.VMEM((NY * NX, 2, GROUP), F32),
            pltpu.VMEM((1, GROUP), F32),
            dma((6,)),
            dma, dma,
            dma, dma((NX,)),
            dma, dma,
            dma, dma((NX,)),
            dma, dma,
            dma, dma,
            dma, dma,
            dma, dma,
            dma, dma,
            dma, dma,
            dma((2,)), dma((2,)),
            dma, dma,
        ],
        compiler_params=pltpu.CompilerParams(
            collective_id=0, has_side_effects=True, vmem_limit_bytes=56 * 1024 * 1024
        ),
    )(
        *(
            pltpu.with_memory_space_constraint(operand, pltpu.HBM)
            for operand in (
                query_a,
                query_b,
                items,
                positive_a.reshape(32, 128),
                positive_b.reshape(32, 128),
                loss_cotangent.reshape(32, 128),
            )
        )
    )
    loss, gq, gi = pl.pallas_call(
        hand_over,
        out_shape=results,
        in_specs=[vmem] * 3,
        out_specs=[hbm] * 3,
        scratch_shapes=[dma((3,))],
        compiler_params=pltpu.CompilerParams(vmem_limit_bytes=1024 * 1024),
    )(*(pltpu.with_memory_space_constraint(result, pltpu.VMEM) for result in (loss, gq, gi)))
    return loss.reshape(OWN), gq, gi


def solution(mesh):
    return jax.shard_map(
        per_device,
        mesh=mesh,
        in_specs=(
            P(("item", "user"), None),
            P(("item", "user"), None),
            P("item", None),
            P(),
            P(),
            P(),
        ),
        out_specs=(P(("item", "user")), P(("item", "user"), None), P(("item", "user"), None)),
        check_vma=False,
    )
```

```python
import functools

import jax
import jax.numpy as jnp
from jax import lax
from jax.experimental import pallas as pl
from jax.experimental.pallas import tpu as pltpu
from jax.sharding import PartitionSpec as P

MESH = pl.DeviceIdType.MESH
F32 = jnp.float32
BF16 = jnp.bfloat16

NZ, NY, NX = 8, 4, 2
OWN = 16
E = 256
GROUP = NZ * NY * NX * OWN
HALF = GROUP // NX
TILE = 32
QUARTER = 512


def remote(src, dst, send_sem, recv_sem, device):
    return pltpu.make_async_remote_copy(
        src_ref=src,
        dst_ref=dst,
        send_sem=send_sem,
        recv_sem=recv_sem,
        device_id=device,
        device_id_type=MESH,
    )


def exact_parts(table):
    if table.dtype == jnp.int32:
        parts = (table & 63, table & (63 << 6), table & (63 << 12))
        return [part.astype(F32).astype(BF16) for part in parts]
    high = table.astype(BF16)
    rest = table - high.astype(F32)
    middle = rest.astype(BF16)
    return [high, middle, (rest - middle.astype(F32)).astype(BF16)]


def group_rows(tables, selector, row_of):
    parts = [part for table in tables for part in exact_parts(table)]
    picked = jnp.dot(jnp.concatenate(parts, axis=0), selector, preferred_element_type=F32)
    picked = picked.reshape(len(tables), 3, 32, GROUP)
    rows = lax.broadcasted_iota(jnp.int32, (32, GROUP), 0) == row_of
    return [
        jnp.sum(jnp.where(rows, (p[0] + p[1]) + p[2], 0.0), axis=0, keepdims=True) for p in picked
    ]


def lse_of(parts):
    top = jnp.max(parts, axis=0)
    return top + jnp.log(jnp.sum(jnp.exp(parts - top[None]), axis=0))


def kernel(
    qa_in, qb_in, items_in, pa_in, pb_in, w_in,
    loss_out, gq_out, gi_out,
    items_v, items_t, qa, qb, pa_v, pb_v, w_v, pos_a, pos_b, weight,
    probs, score_a, dsc, gq_f, gq_s,
    r1, gq_h, r2,
    gi_f, gi_s, gi_core, gi_far,
    zb, yb, za, ya,
    tops,
    in_sem, b1_s, b1_r, b2_s, b2_r, a1_s, a1_r, a2_s, a2_r,
    b_zs, b_zr, b_ys, b_yr, a_zs, a_zr, a_ys, a_yr,
    s1s, s1r, s2s, s2r, gi_ss, gi_rs, far_s, far_r,
):
    item = lax.axis_index("item")
    user = lax.axis_index("user")
    z, y, x = item // (NY * NX), (item // NX) % NY, item % NX
    place = y * NX + x
    far, core = user // 2, user % 2
    items_rows = items_v.shape[0]
    offset = item * items_rows

    def at(zz, yy, xx):
        return {"item": (zz * NY + yy) * NX + xx}

    def z_peer(k):
        return lax.rem(z + k, NZ)

    def y_peer(k):
        return lax.rem(y + k, NY)

    def plane_peer(k):
        return lax.rem(place + k, NY * NX)

    loads = [
        pltpu.make_async_copy(source, target, in_sem.at[n])
        for n, (source, target) in enumerate(
            (
                (qb_in, qb.at[x, y, z]),
                (qa_in, qa.at[x, y, z]),
                (pa_in, pa_v),
                (pb_in, pb_v),
                (w_in, w_v),
                (items_in, items_v),
            )
        )
    ]

    barrier = pltpu.get_barrier_semaphore()

    @pl.loop(1, NZ)
    def _(k):
        pl.semaphore_signal(barrier, inc=1, device_id=at(z_peer(k), y, x), device_id_type=MESH)
        pl.semaphore_signal(barrier, inc=1, device_id=at(z_peer(k), y, 1 - x), device_id_type=MESH)

    @pl.loop(1, NY * NX)
    def _(k):
        p = plane_peer(k)
        pl.semaphore_signal(barrier, inc=1, device_id=at(z, p // NX, p % NX), device_id_type=MESH)

    other_core = {"user": far * 2 + 1 - core}
    other_far = {"user": (1 - far) * 2 + core}
    pl.semaphore_signal(barrier, inc=1, device_id=other_core, device_id_type=MESH)
    pl.semaphore_signal(barrier, inc=1, device_id=other_far, device_id_type=MESH)

    for load in loads:
        load.start()

    pl.semaphore_wait(barrier, 2 * (NZ - 1) + (NY * NX - 1) + 2)

    def sent(refs, send_sem, recv_sem):
        remote(refs, refs, send_sem, recv_sem, other_core).wait_send()

    def arrived(refs, send_sem, recv_sem):
        remote(refs, refs, send_sem, recv_sem, other_core).wait_recv()

    @pl.loop(1, NZ)
    def _(k):
        remote(qb_in, qb.at[x, y, z], b1_s, b1_r, at(z_peer(k), y, x)).start()

    def gather_b_bulk():
        block = qb.at[x, y]

        @pl.loop(1, NY)
        def _(k):
            remote(block, block, b2_s, b2_r.at[x], at(z, y_peer(k), x)).start()

        @pl.loop(0, NY)
        def _(k):
            remote(block, block, b2_s, b2_r.at[x], at(z, y_peer(k), 1 - x)).start()

    @pl.loop(1, NY * NX)
    def _(k):
        p = plane_peer(k)
        remote(qa_in, qa.at[x, y, z], a1_s, a1_r, at(z, p // NX, p % NX)).start()

    def gather_a_bulk(xx):
        block = qa.at[xx, :, z]

        @pl.loop(1, NZ)
        def _(k):
            remote(block, block, a2_s, a2_r.at[xx], at(z_peer(k), y, x)).start()

    others = pl.ds(0, NZ - 1)

    loads[0].wait()
    arrived(qb.at[x, y, others], b1_s, b1_r)
    gather_b_bulk()
    loads[1].wait()
    arrived(qa.at[x, y, others], a1_s, a1_r)
    gather_a_bulk(x)

    lanes = lax.broadcasted_iota(jnp.int32, (1, GROUP), 1)
    own_of = lanes % OWN
    z_of = (lanes // OWN) % NZ
    y_of = (lanes // (OWN * NZ)) % NY
    x_of = lanes // (OWN * NZ * NY)
    ks = lax.broadcasted_iota(jnp.int32, (128, GROUP), 0)
    selector = (ks == x_of * (4 * OWN) + user * OWN + own_of).astype(F32).astype(BF16)
    for load in loads[2:5]:
        load.wait()
    row_a, row_b, weight[...] = group_rows(
        (pa_v[...], pb_v[...], w_v[...]), selector, z_of * NY + y_of
    )
    pos_a[...] = row_a.astype(jnp.int32) - offset
    pos_b[...] = row_b.astype(jnp.int32) - offset

    loads[5].wait()
    for part in range(items_rows // QUARTER):
        rows = pl.ds(part * QUARTER, QUARTER)
        items_t[:, rows] = items_v[rows, :].T

    tiles = [slice(r, r + TILE) for r in range(0, items_rows, TILE)]
    ids = lax.broadcasted_iota(jnp.int32, (TILE, HALF), 0)

    def half_of(xx):
        return pl.ds(pl.multiple_of(xx * HALF, HALF), HALF)

    def fold(values, op):
        return op(values.reshape(TILE // 8, 8, HALF), axis=0)

    def scores(q, xx):
        users = q[xx].reshape(HALF, E)
        return lax.dot_general(
            items_v[...], users, (((1,), (1,)), ((), ())), preferred_element_type=F32
        )

    zero = jnp.zeros((8, HALF), F32)
    least = jnp.full((8, HALF), -jnp.inf, F32)

    def half_b(xx):
        probs[xx] = scores(qb, xx)

        top = least
        for rows in tiles:
            top = jnp.maximum(top, fold(probs[xx, rows, :], jnp.max))
        top = jnp.max(top, axis=0, keepdims=True)
        total = zero
        for rows in tiles:
            p = jnp.exp(probs[xx, rows, :] - top)
            probs[xx, rows, :] = p
            total = total + fold(p, jnp.sum)
        total = jnp.sum(total, axis=0, keepdims=True)
        tops[:, half_of(xx)] = top
        zb[z, :, half_of(xx)] = top + jnp.log(total)

    def half_a(xx):
        score_a[...] = scores(qa, xx)
        pos = pos_a[:, half_of(xx)]
        top, hit = least, zero
        for rows in tiles:
            score = score_a[rows, :]
            top = jnp.maximum(top, fold(score, jnp.max))
            hit = hit + fold(jnp.where(ids == pos - rows.start, score, 0.0), jnp.sum)
        top = jnp.max(top, axis=0, keepdims=True)
        total = zero
        for rows in tiles:
            total = total + fold(jnp.exp(score_a[rows, :] - top), jnp.sum)
        total = jnp.sum(total, axis=0, keepdims=True)
        za[z, 0:1, half_of(xx)] = top + jnp.log(total)
        za[z, 1:2, half_of(xx)] = jnp.sum(hit, axis=0, keepdims=True)

    def z_round(buf, ss, rs):
        @pl.loop(1, NZ)
        def _(k):
            remote(buf.at[z], buf.at[z], ss, rs, at(z_peer(k), y, x)).start()

    def plane_round(buf, ss, rs):
        @pl.loop(1, NY * NX)
        def _(k):
            p = plane_peer(k)
            remote(buf.at[place], buf.at[place], ss, rs, at(z, p // NX, p % NX)).start()

    arrived(qb.at[x, pl.ds(0, NY - 1)], b2_s, b2_r.at[x])
    half_b(x)
    arrived(qb.at[1 - x], b2_s, b2_r.at[1 - x])
    half_b(1 - x)
    z_round(zb, b_zs, b_zr)
    gather_a_bulk(1 - x)
    sent(qb.at[x, y, others], b1_s, b1_r)
    sent(qa.at[x, y, others], a1_s, a1_r)
    sent(qb.at[0], b2_s, b2_r.at[0])
    sent(qb.at[0, pl.ds(0, NY - 1)], b2_s, b2_r.at[0])
    arrived(zb.at[others], b_zs, b_zr)
    yb[place] = lse_of(zb[...])
    plane_round(yb, b_ys, b_yr)
    arrived(qa.at[x, :, others], a2_s, a2_r.at[x])
    half_a(x)
    sent(zb.at[others], b_zs, b_zr)

    arrived(yb.at[others], b_ys, b_yr)
    lse_b = lse_of(yb[...])
    tops[...] = weight[...] * jnp.exp(tops[...] - lse_b)

    def quarter_of(ff, cc):
        return pl.ds(pl.multiple_of((ff * 2 + cc) * QUARTER, QUARTER), QUARTER)

    def dscores(xx):
        cols = half_of(xx)
        pos, scale, ratio = pos_b[:, cols], weight[:, cols], tops[:, cols]
        for rows in tiles:
            match = jnp.where(ids == pos - rows.start, scale, 0.0)
            dsc[rows, cols] = (probs[xx, rows, :] * ratio - match).astype(BF16)

    def far_copy():
        return remote(gi_s, gi_far, far_s, far_r, other_far)

    def core_copy(n):
        return remote(gi_f.at[n, 1 - core], gi_core.at[n], gi_ss.at[n], gi_rs.at[n], other_core)

    def item_grads(n, ff, cc):
        gi_f[n, cc] = jnp.dot(
            dsc[quarter_of(ff, cc), :], qb[...].reshape(GROUP, E), preferred_element_type=F32
        )

    def query_grads(xx):
        block = jnp.dot(
            items_t[...], dsc[:, half_of(xx)], preferred_element_type=F32
        ).T.reshape(NY, NZ, OWN, E)
        gq_f[xx] = block
        gq_s[xx] = block.astype(BF16)

        @pl.loop(1, NY)
        def _(k):
            yy = y_peer(k)
            remote(gq_s.at[xx, yy], r1.at[place], s1s, s1r, at(z, yy, xx)).start()

        @pl.when(x != xx)
        def _():
            remote(gq_s.at[xx, y], r1.at[place], s1s, s1r, at(z, y, xx)).start()

    dscores(1 - x)
    query_grads(1 - x)
    dscores(x)
    item_grads(0, 1 - far, 1 - core)
    core_copy(0).start()
    item_grads(0, 1 - far, core)
    query_grads(x)
    core_copy(0).wait_recv()
    gi_s[...] = (gi_f[0, core] + gi_core[0]).astype(BF16)
    far_copy().start()

    item_grads(1, far, 1 - core)
    core_copy(1).start()
    item_grads(1, far, core)

    arrived(qa.at[1 - x, :, others], a2_s, a2_r.at[1 - x])
    half_a(1 - x)
    z_round(za, a_zs, a_zr)

    r1[place] = jnp.zeros((NZ, OWN, E), BF16)
    r2[z] = jnp.zeros((OWN, E), F32)
    arrived(r1.at[others], s1s, s1r)
    gq_h[...] = gq_f[x, y] + jnp.sum(r1[...].astype(F32), axis=0)

    @pl.loop(1, NZ)
    def _(k):
        zz = z_peer(k)
        remote(gq_h.at[zz], r2.at[z], s2s, s2r, at(zz, y, x)).start()

    arrived(za.at[others], a_zs, a_zr)
    z_parts = za[...]
    ya[place, 0:1] = lse_of(z_parts[:, 0:1])
    ya[place, 1:2] = jnp.sum(z_parts[:, 1:2], axis=0)
    plane_round(ya, a_ys, a_yr)

    core_copy(1).wait_recv()
    gi_out[...] = gi_f[1, core] + gi_core[1]
    sent(qa.at[0, :, others], a2_s, a2_r.at[0])
    sent(qa.at[1, :, others], a2_s, a2_r.at[0])
    sent(yb.at[others], b_ys, b_yr)
    sent(za.at[others], a_zs, a_zr)
    sent(r1.at[others], s1s, s1r)
    core_copy(0).wait_send()
    core_copy(1).wait_send()
    far_copy().wait_recv()
    gi_out[...] += gi_far[...].astype(F32)

    arrived(ya.at[others], a_ys, a_yr)
    y_parts = ya[...]
    tops[...] = lse_of(y_parts[:, 0:1]) - jnp.sum(y_parts[:, 1:2], axis=0)
    mine = tops[:, pl.ds(pl.multiple_of((x * NY + y) * NZ * OWN, NZ * OWN), NZ * OWN)]
    loss_out[...] = pltpu.roll(
        jnp.broadcast_to(mine, (8, NZ * OWN)), (NZ - z) * OWN % (NZ * OWN), 1
    )[0:1, 0:OWN]

    arrived(r2.at[others], s2s, s2r)
    gq_out[...] = gq_h[z] + jnp.sum(r2[...], axis=0)

    sent(ya.at[others], a_ys, a_yr)
    sent(r2.at[others], s2s, s2r)

    far_copy().wait_send()


def hand_over(*refs):
    copies = [
        pltpu.make_async_copy(source, target, refs[6].at[n])
        for n, (source, target) in enumerate(zip(refs[:3], refs[3:6]))
    ]
    for copy in copies:
        copy.start()
    for copy in copies:
        copy.wait()


def per_device(query_a, query_b, items, positive_a, positive_b, loss_cotangent):
    rows = items.shape[0]
    hbm, vmem = pl.BlockSpec(memory_space=pltpu.HBM), pl.BlockSpec(memory_space=pltpu.VMEM)
    results = (
        jax.ShapeDtypeStruct((1, OWN), F32),
        jax.ShapeDtypeStruct((OWN, E), F32),
        jax.ShapeDtypeStruct((QUARTER, E), F32),
    )
    dma = pltpu.SemaphoreType.DMA
    block = (NX, NY, NZ, OWN, E)
    loss, gq, gi = pl.pallas_call(
        kernel,
        out_shape=[pltpu.VMEM(r.shape, r.dtype) for r in results],
        in_specs=[hbm] * 6,
        out_specs=[vmem] * 3,
        scratch_shapes=[
            pltpu.VMEM((rows, E), BF16),
            pltpu.VMEM((E, rows), BF16),
            pltpu.VMEM(block, BF16),
            pltpu.VMEM(block, BF16),
            pltpu.VMEM((32, 128), jnp.int32),
            pltpu.VMEM((32, 128), jnp.int32),
            pltpu.VMEM((32, 128), F32),
            pltpu.VMEM((1, GROUP), jnp.int32),
            pltpu.VMEM((1, GROUP), jnp.int32),
            pltpu.VMEM((1, GROUP), F32),
            pltpu.VMEM((NX, rows, HALF), F32),
            pltpu.VMEM((rows, HALF), F32),
            pltpu.VMEM((rows, GROUP), BF16),
            pltpu.VMEM(block, F32),
            pltpu.VMEM(block, BF16),
            pltpu.VMEM((NY * NX, NZ, OWN, E), BF16),
            pltpu.VMEM((NZ, OWN, E), F32),
            pltpu.VMEM((NZ, OWN, E), F32),
            pltpu.VMEM((2, 2, QUARTER, E), F32),
            pltpu.VMEM((QUARTER, E), BF16),
            pltpu.VMEM((2, QUARTER, E), F32),
            pltpu.VMEM((QUARTER, E), BF16),
            pltpu.VMEM((NZ, 1, GROUP), F32),
            pltpu.VMEM((NY * NX, 1, GROUP), F32),
            pltpu.VMEM((NZ, 2, GROUP), F32),
            pltpu.VMEM((NY * NX, 2, GROUP), F32),
            pltpu.VMEM((1, GROUP), F32),
            dma((6,)),
            dma, dma,
            dma, dma((NX,)),
            dma, dma,
            dma, dma((NX,)),
            dma, dma,
            dma, dma,
            dma, dma,
            dma, dma,
            dma, dma,
            dma, dma,
            dma((2,)), dma((2,)),
            dma, dma,
        ],
        compiler_params=pltpu.CompilerParams(
            collective_id=0, has_side_effects=True, vmem_limit_bytes=56 * 1024 * 1024
        ),
    )(
        *(
            pltpu.with_memory_space_constraint(operand, pltpu.HBM)
            for operand in (
                query_a,
                query_b,
                items,
                positive_a.reshape(32, 128),
                positive_b.reshape(32, 128),
                loss_cotangent.reshape(32, 128),
            )
        )
    )
    loss, gq, gi = pl.pallas_call(
        hand_over,
        out_shape=results,
        in_specs=[vmem] * 3,
        out_specs=[hbm] * 3,
        scratch_shapes=[dma((3,))],
        compiler_params=pltpu.CompilerParams(vmem_limit_bytes=1024 * 1024),
    )(*(pltpu.with_memory_space_constraint(result, pltpu.VMEM) for result in (loss, gq, gi)))
    return loss.reshape(OWN), gq, gi


def solution(mesh):
    return jax.shard_map(
        per_device,
        mesh=mesh,
        in_specs=(
            P(("item", "user"), None),
            P(("item", "user"), None),
            P("item", None),
            P(),
            P(),
            P(),
        ),
        out_specs=(P(("item", "user")), P(("item", "user"), None), P(("item", "user"), None)),
        check_vma=False,
    )
```

```python
import functools

import jax
import jax.numpy as jnp
from jax import lax
from jax.experimental import pallas as pl
from jax.experimental.pallas import tpu as pltpu
from jax.sharding import PartitionSpec as P

MESH = pl.DeviceIdType.MESH
F32 = jnp.float32
BF16 = jnp.bfloat16

NZ, NY, NX = 8, 4, 2
OWN = 16
E = 256
GROUP = NZ * NY * NX * OWN
HALF = GROUP // NX
TILE = 32
QUARTER = 512


def remote(src, dst, send_sem, recv_sem, device):
    return pltpu.make_async_remote_copy(
        src_ref=src,
        dst_ref=dst,
        send_sem=send_sem,
        recv_sem=recv_sem,
        device_id=device,
        device_id_type=MESH,
    )


def exact_parts(table):
    if table.dtype == jnp.int32:
        parts = (table & 63, table & (63 << 6), table & (63 << 12))
        return [part.astype(F32).astype(BF16) for part in parts]
    high = table.astype(BF16)
    rest = table - high.astype(F32)
    middle = rest.astype(BF16)
    return [high, middle, (rest - middle.astype(F32)).astype(BF16)]


def group_rows(tables, selector, row_of):
    parts = [part for table in tables for part in exact_parts(table)]
    picked = jnp.dot(jnp.concatenate(parts, axis=0), selector, preferred_element_type=F32)
    picked = picked.reshape(len(tables), 3, 32, GROUP)
    rows = lax.broadcasted_iota(jnp.int32, (32, GROUP), 0) == row_of
    return [
        jnp.sum(jnp.where(rows, (p[0] + p[1]) + p[2], 0.0), axis=0, keepdims=True) for p in picked
    ]


def lse_of(parts):
    top = jnp.max(parts, axis=0)
    return top + jnp.log(jnp.sum(jnp.exp(parts - top[None]), axis=0))


def kernel(
    qa_in, qb_in, items_in, pa_in, pb_in, w_in,
    loss_out, gq_out, gi_out,
    items_v, items_t, qa, qb, pa_v, pb_v, w_v, pos_a, pos_b, weight,
    probs, score_a, dsc, gq_f, gq_s,
    r1, gq_h, r2,
    gi_f, gi_s, gi_core, gi_far,
    zb, yb, za, ya,
    tops, top_a,
    in_sem, b1_s, b1_r, b2_s, b2_r, a1_s, a1_r, a2_s, a2_r,
    b_zs, b_zr, b_ys, b_yr, a_zs, a_zr, a_ys, a_yr,
    s1s, s1r, s2s, s2r, gi_ss, gi_rs, far_s, far_r,
):
    item = lax.axis_index("item")
    user = lax.axis_index("user")
    z, y, x = item // (NY * NX), (item // NX) % NY, item % NX
    place = y * NX + x
    far, core = user // 2, user % 2
    items_rows = items_v.shape[0]
    offset = item * items_rows

    def at(zz, yy, xx):
        return {"item": (zz * NY + yy) * NX + xx}

    def z_peer(k):
        return lax.rem(z + k, NZ)

    def y_peer(k):
        return lax.rem(y + k, NY)

    def plane_peer(k):
        return lax.rem(place + k, NY * NX)

    loads = [
        pltpu.make_async_copy(source, target, in_sem.at[n])
        for n, (source, target) in enumerate(
            (
                (qb_in, qb.at[x, y, z]),
                (qa_in, qa.at[x, y, z]),
                (pa_in, pa_v),
                (pb_in, pb_v),
                (w_in, w_v),
                (items_in, items_v),
            )
        )
    ]

    barrier = pltpu.get_barrier_semaphore()

    @pl.loop(1, NZ)
    def _(k):
        pl.semaphore_signal(barrier, inc=1, device_id=at(z_peer(k), y, x), device_id_type=MESH)

    @pl.loop(1, NY * NX)
    def _(k):
        p = plane_peer(k)
        pl.semaphore_signal(barrier, inc=1, device_id=at(z, p // NX, p % NX), device_id_type=MESH)

    other_core = {"user": far * 2 + 1 - core}
    other_far = {"user": (1 - far) * 2 + core}
    pl.semaphore_signal(barrier, inc=1, device_id=other_core, device_id_type=MESH)
    pl.semaphore_signal(barrier, inc=1, device_id=other_far, device_id_type=MESH)

    for load in loads:
        load.start()

    pl.semaphore_wait(barrier, (NZ - 1) + (NY * NX - 1) + 2)

    def sent(refs, send_sem, recv_sem):
        remote(refs, refs, send_sem, recv_sem, other_core).wait_send()

    def arrived(refs, send_sem, recv_sem):
        remote(refs, refs, send_sem, recv_sem, other_core).wait_recv()

    @pl.loop(1, NZ)
    def _(k):
        remote(qb_in, qb.at[x, y, z], b1_s, b1_r, at(z_peer(k), y, x)).start()

    def gather_b_bulk():
        block = qb.at[x, y]

        @pl.loop(1, NY)
        def _(k):
            remote(block, block, b2_s, b2_r.at[x], at(z, y_peer(k), x)).start()

        @pl.loop(0, NY)
        def _(k):
            remote(block, block, b2_s, b2_r.at[x], at(z, y_peer(k), 1 - x)).start()

    @pl.loop(1, NY * NX)
    def _(k):
        p = plane_peer(k)
        remote(qa_in, qa.at[x, y, z], a1_s, a1_r, at(z, p // NX, p % NX)).start()

    def gather_a_bulk(xx):
        block = qa.at[xx, :, z]

        @pl.loop(1, NZ)
        def _(k):
            remote(block, block, a2_s, a2_r.at[xx], at(z_peer(k), y, x)).start()

    others = pl.ds(0, NZ - 1)

    loads[0].wait()
    arrived(qb.at[x, y, others], b1_s, b1_r)
    gather_b_bulk()
    loads[1].wait()
    arrived(qa.at[x, y, others], a1_s, a1_r)
    gather_a_bulk(x)

    lanes = lax.broadcasted_iota(jnp.int32, (1, GROUP), 1)
    own_of = lanes % OWN
    z_of = (lanes // OWN) % NZ
    y_of = (lanes // (OWN * NZ)) % NY
    x_of = lanes // (OWN * NZ * NY)
    ks = lax.broadcasted_iota(jnp.int32, (128, GROUP), 0)
    selector = (ks == x_of * (4 * OWN) + user * OWN + own_of).astype(F32).astype(BF16)
    for load in loads[2:5]:
        load.wait()
    row_a, row_b, weight[...] = group_rows(
        (pa_v[...], pb_v[...], w_v[...]), selector, z_of * NY + y_of
    )
    pos_a[...] = row_a.astype(jnp.int32) - offset
    pos_b[...] = row_b.astype(jnp.int32) - offset

    loads[5].wait()
    for part in range(items_rows // QUARTER):
        rows = pl.ds(part * QUARTER, QUARTER)
        items_t[:, rows] = items_v[rows, :].T

    tiles = [slice(r, r + TILE) for r in range(0, items_rows, TILE)]
    ids = lax.broadcasted_iota(jnp.int32, (TILE, HALF), 0)

    def half_of(xx):
        return pl.ds(pl.multiple_of(xx * HALF, HALF), HALF)

    def fold(values, op):
        return op(values.reshape(TILE // 8, 8, HALF), axis=0)

    def scores(q, xx):
        users = q[xx].reshape(HALF, E)
        return lax.dot_general(
            items_v[...], users, (((1,), (1,)), ((), ())), preferred_element_type=F32
        )

    zero = jnp.zeros((8, HALF), F32)
    least = jnp.full((8, HALF), -jnp.inf, F32)

    def half_b(xx):
        probs[xx] = scores(qb, xx)

        top = least
        for rows in tiles:
            top = jnp.maximum(top, fold(probs[xx, rows, :], jnp.max))
        top = jnp.max(top, axis=0, keepdims=True)
        total = zero
        for rows in tiles:
            p = jnp.exp(probs[xx, rows, :] - top)
            probs[xx, rows, :] = p
            total = total + fold(p, jnp.sum)
        total = jnp.sum(total, axis=0, keepdims=True)
        tops[:, half_of(xx)] = top
        zb[z, :, half_of(xx)] = top + jnp.log(total)

    def tops_a(xx):
        score_a[...] = scores(qa, xx)
        pos = pos_a[:, half_of(xx)]
        top, hit = least, zero
        for rows in tiles:
            score = score_a[rows, :]
            top = jnp.maximum(top, fold(score, jnp.max))
            hit = hit + fold(jnp.where(ids == pos - rows.start, score, 0.0), jnp.sum)
        top_a[...] = jnp.max(top, axis=0, keepdims=True)
        za[z, 1:2, half_of(xx)] = jnp.sum(hit, axis=0, keepdims=True)

    def sums_a(xx):
        top, total = top_a[...], zero
        for rows in tiles:
            total = total + fold(jnp.exp(score_a[rows, :] - top), jnp.sum)
        total = jnp.sum(total, axis=0, keepdims=True)
        za[z, 0:1, half_of(xx)] = top + jnp.log(total)

    def z_round(buf, ss, rs):
        @pl.loop(1, NZ)
        def _(k):
            remote(buf.at[z], buf.at[z], ss, rs, at(z_peer(k), y, x)).start()

    def plane_round(buf, ss, rs):
        @pl.loop(1, NY * NX)
        def _(k):
            p = plane_peer(k)
            remote(buf.at[place], buf.at[place], ss, rs, at(z, p // NX, p % NX)).start()

    arrived(qb.at[x, pl.ds(0, NY - 1)], b2_s, b2_r.at[x])
    half_b(x)
    arrived(qb.at[1 - x], b2_s, b2_r.at[1 - x])
    half_b(1 - x)
    z_round(zb, b_zs, b_zr)
    gather_a_bulk(1 - x)
    sent(qb.at[x, y, others], b1_s, b1_r)
    sent(qa.at[x, y, others], a1_s, a1_r)
    sent(qb.at[0], b2_s, b2_r.at[0])
    sent(qb.at[0, pl.ds(0, NY - 1)], b2_s, b2_r.at[0])
    arrived(qa.at[x, :, others], a2_s, a2_r.at[x])
    tops_a(x)
    arrived(zb.at[others], b_zs, b_zr)
    yb[place] = lse_of(zb[...])
    plane_round(yb, b_ys, b_yr)
    sums_a(x)
    sent(zb.at[others], b_zs, b_zr)

    arrived(yb.at[others], b_ys, b_yr)
    lse_b = lse_of(yb[...])
    tops[...] = weight[...] * jnp.exp(tops[...] - lse_b)

    def quarter_of(ff, cc):
        return pl.ds(pl.multiple_of((ff * 2 + cc) * QUARTER, QUARTER), QUARTER)

    def dscores(xx, ff, cc):
        cols = half_of(xx)
        start = (ff * 2 + cc) * QUARTER
        pos, scale, ratio = pos_b[:, cols] - start, weight[:, cols], tops[:, cols]
        for r in range(0, QUARTER, TILE):
            rows = pl.ds(pl.multiple_of(start + r, TILE), TILE)
            match = jnp.where(ids == pos - r, scale, 0.0)
            dsc[rows, cols] = (probs[xx, rows, :] * ratio - match).astype(BF16)

    def far_copy():
        return remote(gi_s, gi_far, far_s, far_r, other_far)

    def core_copy(n):
        return remote(gi_f.at[n, 1 - core], gi_core.at[n], gi_ss.at[n], gi_rs.at[n], other_core)

    def item_grads(n, ff, cc):
        gi_f[n, cc] = jnp.dot(
            dsc[quarter_of(ff, cc), :], qb[...].reshape(GROUP, E), preferred_element_type=F32
        )

    def query_grads(xx):
        block = jnp.dot(
            items_t[...], dsc[:, half_of(xx)], preferred_element_type=F32
        ).T.reshape(NY, NZ, OWN, E)
        gq_f[xx] = block
        gq_s[xx] = block.astype(BF16)

        @pl.loop(1, NY)
        def _(k):
            yy = y_peer(k)
            remote(gq_s.at[xx, yy], r1.at[place], s1s, s1r, at(z, yy, xx)).start()

        @pl.when(x != xx)
        def _():
            remote(gq_s.at[xx, y], r1.at[place], s1s, s1r, at(z, y, xx)).start()

    for quarter in range(4):
        dscores(1 - x, quarter // 2, quarter % 2)
    query_grads(1 - x)
    dscores(x, 1 - far, 1 - core)
    item_grads(0, 1 - far, 1 - core)
    core_copy(0).start()
    dscores(x, 1 - far, core)
    item_grads(0, 1 - far, core)
    dscores(x, far, 1 - core)
    dscores(x, far, core)
    query_grads(x)
    core_copy(0).wait_recv()
    gi_s[...] = (gi_f[0, core] + gi_core[0]).astype(BF16)
    far_copy().start()

    item_grads(1, far, 1 - core)
    core_copy(1).start()
    item_grads(1, far, core)

    arrived(qa.at[1 - x, :, others], a2_s, a2_r.at[1 - x])
    tops_a(1 - x)
    sums_a(1 - x)
    z_round(za, a_zs, a_zr)

    r1[place] = jnp.zeros((NZ, OWN, E), BF16)
    r2[z] = jnp.zeros((OWN, E), F32)
    arrived(r1.at[others], s1s, s1r)
    gq_h[...] = gq_f[x, y] + jnp.sum(r1[...].astype(F32), axis=0)

    @pl.loop(1, NZ)
    def _(k):
        zz = z_peer(k)
        remote(gq_h.at[zz], r2.at[z], s2s, s2r, at(zz, y, x)).start()

    arrived(za.at[others], a_zs, a_zr)
    z_parts = za[...]
    ya[place, 0:1] = lse_of(z_parts[:, 0:1])
    ya[place, 1:2] = jnp.sum(z_parts[:, 1:2], axis=0)
    plane_round(ya, a_ys, a_yr)

    core_copy(1).wait_recv()
    gi_out[...] = gi_f[1, core] + gi_core[1]
    sent(qa.at[0, :, others], a2_s, a2_r.at[0])
    sent(qa.at[1, :, others], a2_s, a2_r.at[0])
    sent(yb.at[others], b_ys, b_yr)
    sent(za.at[others], a_zs, a_zr)
    sent(r1.at[others], s1s, s1r)
    core_copy(0).wait_send()
    core_copy(1).wait_send()
    far_copy().wait_recv()
    gi_out[...] += gi_far[...].astype(F32)

    arrived(ya.at[others], a_ys, a_yr)
    y_parts = ya[...]
    tops[...] = lse_of(y_parts[:, 0:1]) - jnp.sum(y_parts[:, 1:2], axis=0)
    mine = tops[:, pl.ds(pl.multiple_of((x * NY + y) * NZ * OWN, NZ * OWN), NZ * OWN)]
    loss_out[...] = pltpu.roll(
        jnp.broadcast_to(mine, (8, NZ * OWN)), (NZ - z) * OWN % (NZ * OWN), 1
    )[0:1, 0:OWN]

    arrived(r2.at[others], s2s, s2r)
    gq_out[...] = gq_h[z] + jnp.sum(r2[...], axis=0)

    sent(ya.at[others], a_ys, a_yr)
    sent(r2.at[others], s2s, s2r)

    far_copy().wait_send()


def hand_over(*refs):
    copies = [
        pltpu.make_async_copy(source, target, refs[6].at[n])
        for n, (source, target) in enumerate(zip(refs[:3], refs[3:6]))
    ]
    for copy in copies:
        copy.start()
    for copy in copies:
        copy.wait()


def per_device(query_a, query_b, items, positive_a, positive_b, loss_cotangent):
    rows = items.shape[0]
    hbm, vmem = pl.BlockSpec(memory_space=pltpu.HBM), pl.BlockSpec(memory_space=pltpu.VMEM)
    results = (
        jax.ShapeDtypeStruct((1, OWN), F32),
        jax.ShapeDtypeStruct((OWN, E), F32),
        jax.ShapeDtypeStruct((QUARTER, E), F32),
    )
    dma = pltpu.SemaphoreType.DMA
    block = (NX, NY, NZ, OWN, E)
    loss, gq, gi = pl.pallas_call(
        kernel,
        out_shape=[pltpu.VMEM(r.shape, r.dtype) for r in results],
        in_specs=[hbm] * 6,
        out_specs=[vmem] * 3,
        scratch_shapes=[
            pltpu.VMEM((rows, E), BF16),
            pltpu.VMEM((E, rows), BF16),
            pltpu.VMEM(block, BF16),
            pltpu.VMEM(block, BF16),
            pltpu.VMEM((32, 128), jnp.int32),
            pltpu.VMEM((32, 128), jnp.int32),
            pltpu.VMEM((32, 128), F32),
            pltpu.VMEM((1, GROUP), jnp.int32),
            pltpu.VMEM((1, GROUP), jnp.int32),
            pltpu.VMEM((1, GROUP), F32),
            pltpu.VMEM((NX, rows, HALF), F32),
            pltpu.VMEM((rows, HALF), F32),
            pltpu.VMEM((rows, GROUP), BF16),
            pltpu.VMEM(block, F32),
            pltpu.VMEM(block, BF16),
            pltpu.VMEM((NY * NX, NZ, OWN, E), BF16),
            pltpu.VMEM((NZ, OWN, E), F32),
            pltpu.VMEM((NZ, OWN, E), F32),
            pltpu.VMEM((2, 2, QUARTER, E), F32),
            pltpu.VMEM((QUARTER, E), BF16),
            pltpu.VMEM((2, QUARTER, E), F32),
            pltpu.VMEM((QUARTER, E), BF16),
            pltpu.VMEM((NZ, 1, GROUP), F32),
            pltpu.VMEM((NY * NX, 1, GROUP), F32),
            pltpu.VMEM((NZ, 2, GROUP), F32),
            pltpu.VMEM((NY * NX, 2, GROUP), F32),
            pltpu.VMEM((1, GROUP), F32),
            pltpu.VMEM((1, HALF), F32),
            dma((6,)),
            dma, dma,
            dma, dma((NX,)),
            dma, dma,
            dma, dma((NX,)),
            dma, dma,
            dma, dma,
            dma, dma,
            dma, dma,
            dma, dma,
            dma, dma,
            dma((2,)), dma((2,)),
            dma, dma,
        ],
        compiler_params=pltpu.CompilerParams(
            collective_id=0, has_side_effects=True, vmem_limit_bytes=56 * 1024 * 1024
        ),
    )(
        *(
            pltpu.with_memory_space_constraint(operand, pltpu.HBM)
            for operand in (
                query_a,
                query_b,
                items,
                positive_a.reshape(32, 128),
                positive_b.reshape(32, 128),
                loss_cotangent.reshape(32, 128),
            )
        )
    )
    loss, gq, gi = pl.pallas_call(
        hand_over,
        out_shape=results,
        in_specs=[vmem] * 3,
        out_specs=[hbm] * 3,
        scratch_shapes=[dma((3,))],
        compiler_params=pltpu.CompilerParams(vmem_limit_bytes=1024 * 1024),
    )(*(pltpu.with_memory_space_constraint(result, pltpu.VMEM) for result in (loss, gq, gi)))
    return loss.reshape(OWN), gq, gi


def solution(mesh):
    return jax.shard_map(
        per_device,
        mesh=mesh,
        in_specs=(
            P(("item", "user"), None),
            P(("item", "user"), None),
            P("item", None),
            P(),
            P(),
            P(),
        ),
        out_specs=(P(("item", "user")), P(("item", "user"), None), P(("item", "user"), None)),
        check_vma=False,
    )
```

```python
import functools

import jax
import jax.numpy as jnp
from jax import lax
from jax.experimental import pallas as pl
from jax.experimental.pallas import tpu as pltpu
from jax.sharding import PartitionSpec as P

MESH = pl.DeviceIdType.MESH
F32 = jnp.float32
BF16 = jnp.bfloat16

NZ, NY, NX = 8, 4, 2
OWN = 16
E = 256
GROUP = NZ * NY * NX * OWN
HALF = GROUP // NX
TILE = 32
QUARTER = 512


def remote(src, dst, send_sem, recv_sem, device):
    return pltpu.make_async_remote_copy(
        src_ref=src,
        dst_ref=dst,
        send_sem=send_sem,
        recv_sem=recv_sem,
        device_id=device,
        device_id_type=MESH,
    )


def exact_parts(table):
    if table.dtype == jnp.int32:
        parts = (table & 63, table & (63 << 6), table & (63 << 12))
        return [part.astype(F32).astype(BF16) for part in parts]
    high = table.astype(BF16)
    rest = table - high.astype(F32)
    middle = rest.astype(BF16)
    return [high, middle, (rest - middle.astype(F32)).astype(BF16)]


def group_rows(tables, selector, row_of):
    parts = [part for table in tables for part in exact_parts(table)]
    picked = jnp.dot(jnp.concatenate(parts, axis=0), selector, preferred_element_type=F32)
    picked = picked.reshape(len(tables), 3, 32, GROUP)
    rows = lax.broadcasted_iota(jnp.int32, (32, GROUP), 0) == row_of
    return [
        jnp.sum(jnp.where(rows, (p[0] + p[1]) + p[2], 0.0), axis=0, keepdims=True) for p in picked
    ]


def lse_of(parts):
    top = jnp.max(parts, axis=0)
    return top + jnp.log(jnp.sum(jnp.exp(parts - top[None]), axis=0))


def kernel(
    qa_in, qb_in, items_in, pa_in, pb_in, w_in,
    loss_out, gq_out, gi_out,
    items_v, items_t, qa, qb, pa_v, pb_v, w_v, pos_a, pos_b, weight,
    probs, score_a, dsc, gq_f, gq_s,
    r1, rz, gq_h, gq_p, r2, r3,
    gi_f, gi_s, gi_core, gi_far,
    zb, yb, za, ya,
    tops, top_a,
    in_sem, b1_s, b1_r, b2_s, b2_r, a1_s, a1_r, a2_s, a2_r,
    b_zs, b_zr, b_ys, b_yr, a_zs, a_zr, a_ys, a_yr,
    s1s, s1r, zs, zr, s2s, s2r, s3s, s3r, gi_ss, gi_rs, far_s, far_r,
):
    item = lax.axis_index("item")
    user = lax.axis_index("user")
    z, y, x = item // (NY * NX), (item // NX) % NY, item % NX
    place = y * NX + x
    far, core = user // 2, user % 2
    items_rows = items_v.shape[0]
    offset = item * items_rows

    def at(zz, yy, xx):
        return {"item": (zz * NY + yy) * NX + xx}

    def z_peer(k):
        return lax.rem(z + k, NZ)

    def y_peer(k):
        return lax.rem(y + k, NY)

    def plane_peer(k):
        return lax.rem(place + k, NY * NX)

    loads = [
        pltpu.make_async_copy(source, target, in_sem.at[n])
        for n, (source, target) in enumerate(
            (
                (qb_in, qb.at[x, y, z]),
                (qa_in, qa.at[x, y, z]),
                (pa_in, pa_v),
                (pb_in, pb_v),
                (w_in, w_v),
                (items_in, items_v),
            )
        )
    ]

    barrier = pltpu.get_barrier_semaphore()

    @pl.loop(1, NZ)
    def _(k):
        pl.semaphore_signal(barrier, inc=1, device_id=at(z_peer(k), y, x), device_id_type=MESH)

    @pl.loop(1, NY * NX)
    def _(k):
        p = plane_peer(k)
        pl.semaphore_signal(barrier, inc=1, device_id=at(z, p // NX, p % NX), device_id_type=MESH)

    other_core = {"user": far * 2 + 1 - core}
    other_far = {"user": (1 - far) * 2 + core}
    pl.semaphore_signal(barrier, inc=1, device_id=other_core, device_id_type=MESH)
    pl.semaphore_signal(barrier, inc=1, device_id=other_far, device_id_type=MESH)

    for load in loads:
        load.start()

    pl.semaphore_wait(barrier, (NZ - 1) + (NY * NX - 1) + 2)

    def sent(refs, send_sem, recv_sem):
        remote(refs, refs, send_sem, recv_sem, other_core).wait_send()

    def arrived(refs, send_sem, recv_sem):
        remote(refs, refs, send_sem, recv_sem, other_core).wait_recv()

    @pl.loop(1, NZ)
    def _(k):
        remote(qb_in, qb.at[x, y, z], b1_s, b1_r, at(z_peer(k), y, x)).start()

    def gather_b_bulk():
        block = qb.at[x, y]

        @pl.loop(1, NY)
        def _(k):
            remote(block, block, b2_s, b2_r.at[x], at(z, y_peer(k), x)).start()

        @pl.loop(0, NY)
        def _(k):
            remote(block, block, b2_s, b2_r.at[x], at(z, y_peer(k), 1 - x)).start()

    @pl.loop(1, NY * NX)
    def _(k):
        p = plane_peer(k)
        remote(qa_in, qa.at[x, y, z], a1_s, a1_r, at(z, p // NX, p % NX)).start()

    def gather_a_bulk(xx):
        block = qa.at[xx, :, z]

        @pl.loop(1, NZ)
        def _(k):
            remote(block, block, a2_s, a2_r.at[xx], at(z_peer(k), y, x)).start()

    others = pl.ds(0, NZ - 1)

    loads[0].wait()
    arrived(qb.at[x, y, others], b1_s, b1_r)
    gather_b_bulk()
    loads[1].wait()
    arrived(qa.at[x, y, others], a1_s, a1_r)
    gather_a_bulk(x)

    lanes = lax.broadcasted_iota(jnp.int32, (1, GROUP), 1)
    own_of = lanes % OWN
    z_of = (lanes // OWN) % NZ
    y_of = (lanes // (OWN * NZ)) % NY
    x_of = lanes // (OWN * NZ * NY)
    ks = lax.broadcasted_iota(jnp.int32, (128, GROUP), 0)
    selector = (ks == x_of * (4 * OWN) + user * OWN + own_of).astype(F32).astype(BF16)
    for load in loads[2:5]:
        load.wait()
    row_a, row_b, weight[...] = group_rows(
        (pa_v[...], pb_v[...], w_v[...]), selector, z_of * NY + y_of
    )
    pos_a[...] = row_a.astype(jnp.int32) - offset
    pos_b[...] = row_b.astype(jnp.int32) - offset

    loads[5].wait()
    for part in range(items_rows // QUARTER):
        rows = pl.ds(part * QUARTER, QUARTER)
        items_t[:, rows] = items_v[rows, :].T

    tiles = [slice(r, r + TILE) for r in range(0, items_rows, TILE)]
    ids = lax.broadcasted_iota(jnp.int32, (TILE, HALF), 0)

    def half_of(xx):
        return pl.ds(pl.multiple_of(xx * HALF, HALF), HALF)

    def fold(values, op):
        return op(values.reshape(TILE // 8, 8, HALF), axis=0)

    def scores(q, xx):
        users = q[xx].reshape(HALF, E)
        return lax.dot_general(
            items_v[...], users, (((1,), (1,)), ((), ())), preferred_element_type=F32
        )

    zero = jnp.zeros((8, HALF), F32)
    least = jnp.full((8, HALF), -jnp.inf, F32)

    def half_b(xx):
        probs[xx] = scores(qb, xx)

        top = least
        for rows in tiles:
            top = jnp.maximum(top, fold(probs[xx, rows, :], jnp.max))
        top = jnp.max(top, axis=0, keepdims=True)
        total = zero
        for rows in tiles:
            p = jnp.exp(probs[xx, rows, :] - top)
            probs[xx, rows, :] = p
            total = total + fold(p, jnp.sum)
        total = jnp.sum(total, axis=0, keepdims=True)
        tops[:, half_of(xx)] = top
        zb[z, :, half_of(xx)] = top + jnp.log(total)

    def tops_a(xx):
        score_a[...] = scores(qa, xx)
        pos = pos_a[:, half_of(xx)]
        top, hit = least, zero
        for rows in tiles:
            score = score_a[rows, :]
            top = jnp.maximum(top, fold(score, jnp.max))
            hit = hit + fold(jnp.where(ids == pos - rows.start, score, 0.0), jnp.sum)
        top_a[...] = jnp.max(top, axis=0, keepdims=True)
        za[z, 1:2, half_of(xx)] = jnp.sum(hit, axis=0, keepdims=True)

    def sums_a(xx):
        top, total = top_a[...], zero
        for rows in tiles:
            total = total + fold(jnp.exp(score_a[rows, :] - top), jnp.sum)
        total = jnp.sum(total, axis=0, keepdims=True)
        za[z, 0:1, half_of(xx)] = top + jnp.log(total)

    def z_round(buf, ss, rs):
        @pl.loop(1, NZ)
        def _(k):
            remote(buf.at[z], buf.at[z], ss, rs, at(z_peer(k), y, x)).start()

    def plane_round(buf, ss, rs):
        @pl.loop(1, NY * NX)
        def _(k):
            p = plane_peer(k)
            remote(buf.at[place], buf.at[place], ss, rs, at(z, p // NX, p % NX)).start()

    arrived(qb.at[x, pl.ds(0, NY - 1)], b2_s, b2_r.at[x])
    half_b(x)
    arrived(qb.at[1 - x], b2_s, b2_r.at[1 - x])
    half_b(1 - x)
    z_round(zb, b_zs, b_zr)
    gather_a_bulk(1 - x)
    sent(qb.at[x, y, others], b1_s, b1_r)
    sent(qa.at[x, y, others], a1_s, a1_r)
    sent(qb.at[0], b2_s, b2_r.at[0])
    sent(qb.at[0, pl.ds(0, NY - 1)], b2_s, b2_r.at[0])
    arrived(qa.at[x, :, others], a2_s, a2_r.at[x])
    tops_a(x)
    arrived(zb.at[others], b_zs, b_zr)
    yb[place] = lse_of(zb[...])
    plane_round(yb, b_ys, b_yr)
    sums_a(x)
    sent(zb.at[others], b_zs, b_zr)

    arrived(yb.at[others], b_ys, b_yr)
    lse_b = lse_of(yb[...])
    tops[...] = weight[...] * jnp.exp(tops[...] - lse_b)

    def quarter_of(ff, cc):
        return pl.ds(pl.multiple_of((ff * 2 + cc) * QUARTER, QUARTER), QUARTER)

    def dscores(xx, ff, cc):
        cols = half_of(xx)
        start = (ff * 2 + cc) * QUARTER
        pos, scale, ratio = pos_b[:, cols] - start, weight[:, cols], tops[:, cols]
        for r in range(0, QUARTER, TILE):
            rows = pl.ds(pl.multiple_of(start + r, TILE), TILE)
            match = jnp.where(ids == pos - r, scale, 0.0)
            dsc[rows, cols] = (probs[xx, rows, :] * ratio - match).astype(BF16)

    def far_copy():
        return remote(gi_s, gi_far, far_s, far_r, other_far)

    def core_copy(n):
        return remote(gi_f.at[n, 1 - core], gi_core.at[n], gi_ss.at[n], gi_rs.at[n], other_core)

    def item_grads(n, ff, cc):
        gi_f[n, cc] = jnp.dot(
            dsc[quarter_of(ff, cc), :], qb[...].reshape(GROUP, E), preferred_element_type=F32
        )

    def query_grads(xx):
        block = jnp.dot(
            items_t[...], dsc[:, half_of(xx)], preferred_element_type=F32
        ).T.reshape(NY, NZ, OWN, E)
        gq_f[xx] = block
        gq_s[xx] = block.astype(BF16)

    def plane_send(xx, yy):
        remote(gq_s.at[xx, yy], r1.at[x, y], s1s, s1r.at[x], at(z, yy, xx)).start()

    def own_sends():
        @pl.loop(1, NY)
        def _(k):
            plane_send(x, y_peer(k))

    def other_sends():
        @pl.when(core == 0)
        def _():
            @pl.loop(0, NY)
            def _(k):
                plane_send(1 - x, y_peer(k))

        @pl.when(core == 1)
        def _():
            @pl.loop(1, NZ)
            def _(k):
                zz = z_peer(k)
                remote(gq_s.at[1 - x, :, zz], rz.at[z], zs, zr, at(zz, y, x)).start()

    for quarter in range(4):
        dscores(1 - x, quarter // 2, quarter % 2)
    query_grads(1 - x)
    other_sends()
    dscores(x, 1 - far, 1 - core)
    item_grads(0, 1 - far, 1 - core)
    core_copy(0).start()
    dscores(x, 1 - far, core)
    item_grads(0, 1 - far, core)
    dscores(x, far, 1 - core)
    dscores(x, far, core)
    query_grads(x)
    own_sends()
    core_copy(0).wait_recv()
    gi_s[...] = (gi_f[0, core] + gi_core[0]).astype(BF16)
    far_copy().start()

    item_grads(1, far, 1 - core)
    core_copy(1).start()
    item_grads(1, far, core)

    arrived(qa.at[1 - x, :, others], a2_s, a2_r.at[1 - x])
    tops_a(1 - x)
    sums_a(1 - x)
    z_round(za, a_zs, a_zr)

    r1[x, y] = jnp.zeros((NZ, OWN, E), BF16)
    rz[z] = jnp.zeros((NY, OWN, E), BF16)
    r2[z] = jnp.zeros((OWN, E), F32)
    arrived(r1.at[x, pl.ds(0, NY - 1)], s1s, s1r.at[x])
    gq_h[...] = gq_f[x, y] + jnp.sum(r1[x].astype(F32), axis=0)

    @pl.when(core == 0)
    def _():
        arrived(r1.at[1 - x], s1s, s1r.at[1 - x])
        gq_h[...] += jnp.sum(r1[1 - x].astype(F32), axis=0)

    @pl.loop(1, NZ)
    def _(k):
        zz = z_peer(k)
        remote(gq_h.at[zz], r2.at[z], s2s, s2r, at(zz, y, x)).start()

    @pl.when(core == 1)
    def _():
        arrived(rz.at[others], zs, zr)
        gq_p[...] = gq_f[1 - x, :, z] + jnp.sum(rz[...].astype(F32), axis=0)

        @pl.loop(0, NY)
        def _(k):
            yy = y_peer(k)
            remote(gq_p.at[yy], r3.at[y], s3s, s3r, at(z, yy, 1 - x)).start()

    arrived(za.at[others], a_zs, a_zr)
    z_parts = za[...]
    ya[place, 0:1] = lse_of(z_parts[:, 0:1])
    ya[place, 1:2] = jnp.sum(z_parts[:, 1:2], axis=0)
    plane_round(ya, a_ys, a_yr)

    core_copy(1).wait_recv()
    gi_out[...] = gi_f[1, core] + gi_core[1]
    sent(qa.at[0, :, others], a2_s, a2_r.at[0])
    sent(qa.at[1, :, others], a2_s, a2_r.at[0])
    sent(yb.at[others], b_ys, b_yr)
    sent(za.at[others], a_zs, a_zr)
    sent(r1.at[0, pl.ds(0, NY - 1)], s1s, s1r.at[0])

    @pl.when(core == 0)
    def _():
        sent(r1.at[0], s1s, s1r.at[0])

    @pl.when(core == 1)
    def _():
        sent(rz.at[others], zs, zr)

    core_copy(0).wait_send()
    core_copy(1).wait_send()
    far_copy().wait_recv()
    gi_out[...] += gi_far[...].astype(F32)

    arrived(ya.at[others], a_ys, a_yr)
    y_parts = ya[...]
    tops[...] = lse_of(y_parts[:, 0:1]) - jnp.sum(y_parts[:, 1:2], axis=0)
    mine = tops[:, pl.ds(pl.multiple_of((x * NY + y) * NZ * OWN, NZ * OWN), NZ * OWN)]
    loss_out[...] = pltpu.roll(
        jnp.broadcast_to(mine, (8, NZ * OWN)), (NZ - z) * OWN % (NZ * OWN), 1
    )[0:1, 0:OWN]

    arrived(r2.at[others], s2s, s2r)
    gq_out[...] = gq_h[z] + jnp.sum(r2[...], axis=0)

    @pl.when(core == 1)
    def _():
        arrived(r3, s3s, s3r)
        gq_out[...] += jnp.sum(r3[...], axis=0)
        sent(r3, s3s, s3r)


    sent(ya.at[others], a_ys, a_yr)
    sent(r2.at[others], s2s, s2r)

    far_copy().wait_send()


def hand_over(*refs):
    copies = [
        pltpu.make_async_copy(source, target, refs[6].at[n])
        for n, (source, target) in enumerate(zip(refs[:3], refs[3:6]))
    ]
    for copy in copies:
        copy.start()
    for copy in copies:
        copy.wait()


def per_device(query_a, query_b, items, positive_a, positive_b, loss_cotangent):
    rows = items.shape[0]
    hbm, vmem = pl.BlockSpec(memory_space=pltpu.HBM), pl.BlockSpec(memory_space=pltpu.VMEM)
    results = (
        jax.ShapeDtypeStruct((1, OWN), F32),
        jax.ShapeDtypeStruct((OWN, E), F32),
        jax.ShapeDtypeStruct((QUARTER, E), F32),
    )
    dma = pltpu.SemaphoreType.DMA
    block = (NX, NY, NZ, OWN, E)
    loss, gq, gi = pl.pallas_call(
        kernel,
        out_shape=[pltpu.VMEM(r.shape, r.dtype) for r in results],
        in_specs=[hbm] * 6,
        out_specs=[vmem] * 3,
        scratch_shapes=[
            pltpu.VMEM((rows, E), BF16),
            pltpu.VMEM((E, rows), BF16),
            pltpu.VMEM(block, BF16),
            pltpu.VMEM(block, BF16),
            pltpu.VMEM((32, 128), jnp.int32),
            pltpu.VMEM((32, 128), jnp.int32),
            pltpu.VMEM((32, 128), F32),
            pltpu.VMEM((1, GROUP), jnp.int32),
            pltpu.VMEM((1, GROUP), jnp.int32),
            pltpu.VMEM((1, GROUP), F32),
            pltpu.VMEM((NX, rows, HALF), F32),
            pltpu.VMEM((rows, HALF), F32),
            pltpu.VMEM((rows, GROUP), BF16),
            pltpu.VMEM(block, F32),
            pltpu.VMEM(block, BF16),
            pltpu.VMEM(block, BF16),
            pltpu.VMEM((NZ, NY, OWN, E), BF16),
            pltpu.VMEM((NZ, OWN, E), F32),
            pltpu.VMEM((NY, OWN, E), F32),
            pltpu.VMEM((NZ, OWN, E), F32),
            pltpu.VMEM((NY, OWN, E), F32),
            pltpu.VMEM((2, 2, QUARTER, E), F32),
            pltpu.VMEM((QUARTER, E), BF16),
            pltpu.VMEM((2, QUARTER, E), F32),
            pltpu.VMEM((QUARTER, E), BF16),
            pltpu.VMEM((NZ, 1, GROUP), F32),
            pltpu.VMEM((NY * NX, 1, GROUP), F32),
            pltpu.VMEM((NZ, 2, GROUP), F32),
            pltpu.VMEM((NY * NX, 2, GROUP), F32),
            pltpu.VMEM((1, GROUP), F32),
            pltpu.VMEM((1, HALF), F32),
            dma((6,)),
            dma, dma,
            dma, dma((NX,)),
            dma, dma,
            dma, dma((NX,)),
            dma, dma,
            dma, dma,
            dma, dma,
            dma, dma,
            dma, dma((NX,)),
            dma, dma,
            dma, dma,
            dma, dma,
            dma((2,)), dma((2,)),
            dma, dma,
        ],
        compiler_params=pltpu.CompilerParams(
            collective_id=0, has_side_effects=True, vmem_limit_bytes=56 * 1024 * 1024
        ),
    )(
        *(
            pltpu.with_memory_space_constraint(operand, pltpu.HBM)
            for operand in (
                query_a,
                query_b,
                items,
                positive_a.reshape(32, 128),
                positive_b.reshape(32, 128),
                loss_cotangent.reshape(32, 128),
            )
        )
    )
    loss, gq, gi = pl.pallas_call(
        hand_over,
        out_shape=results,
        in_specs=[vmem] * 3,
        out_specs=[hbm] * 3,
        scratch_shapes=[dma((3,))],
        compiler_params=pltpu.CompilerParams(vmem_limit_bytes=1024 * 1024),
    )(*(pltpu.with_memory_space_constraint(result, pltpu.VMEM) for result in (loss, gq, gi)))
    return loss.reshape(OWN), gq, gi


def solution(mesh):
    return jax.shard_map(
        per_device,
        mesh=mesh,
        in_specs=(
            P(("item", "user"), None),
            P(("item", "user"), None),
            P("item", None),
            P(),
            P(),
            P(),
        ),
        out_specs=(P(("item", "user")), P(("item", "user"), None), P(("item", "user"), None)),
        check_vma=False,
    )
```

```python
import functools

import jax
import jax.numpy as jnp
from jax import lax
from jax.experimental import pallas as pl
from jax.experimental.pallas import tpu as pltpu
from jax.sharding import PartitionSpec as P

MESH = pl.DeviceIdType.MESH
F32 = jnp.float32
BF16 = jnp.bfloat16

NZ, NY, NX = 8, 4, 2
OWN = 16
E = 256
GROUP = NZ * NY * NX * OWN
HALF = GROUP // NX
TILE = 32
QUARTER = 512


def remote(src, dst, send_sem, recv_sem, device):
    return pltpu.make_async_remote_copy(
        src_ref=src,
        dst_ref=dst,
        send_sem=send_sem,
        recv_sem=recv_sem,
        device_id=device,
        device_id_type=MESH,
    )


def exact_parts(table):
    if table.dtype == jnp.int32:
        parts = (table & 63, table & (63 << 6), table & (63 << 12))
        return [part.astype(F32).astype(BF16) for part in parts]
    high = table.astype(BF16)
    rest = table - high.astype(F32)
    middle = rest.astype(BF16)
    return [high, middle, (rest - middle.astype(F32)).astype(BF16)]


def group_rows(tables, selector, row_of):
    parts = [part for table in tables for part in exact_parts(table)]
    picked = jnp.dot(jnp.concatenate(parts, axis=0), selector, preferred_element_type=F32)
    picked = picked.reshape(len(tables), 3, 32, GROUP)
    rows = lax.broadcasted_iota(jnp.int32, (32, GROUP), 0) == row_of
    return [
        jnp.sum(jnp.where(rows, (p[0] + p[1]) + p[2], 0.0), axis=0, keepdims=True) for p in picked
    ]


def lse_of(parts):
    top = jnp.max(parts, axis=0)
    return top + jnp.log(jnp.sum(jnp.exp(parts - top[None]), axis=0))


def kernel(
    qa_in, qb_in, items_in, pa_in, pb_in, w_in,
    loss_out, gq_out, gi_out,
    items_v, items_t, qa, qb, pa_v, pb_v, w_v, pos_a, pos_b, weight,
    probs, score_a, dsc, gq_f, gq_s,
    r1, rz, gq_h, gq_p, r2, r3,
    gi_f, gi_s, gi_core, gi_far,
    zb, yb, za, ya,
    tops, top_a,
    in_sem, b1_s, b1_r, b2_s, b2_r, a1_s, a1_r, a2_s, a2_r,
    b_zs, b_zr, b_ys, b_yr, a_zs, a_zr, a_ys, a_yr,
    s1s, s1r, zs, zr, s2s, s2r, s3s, s3r, gi_ss, gi_rs, far_s, far_r,
):
    item = lax.axis_index("item")
    user = lax.axis_index("user")
    z, y, x = item // (NY * NX), (item // NX) % NY, item % NX
    place = y * NX + x
    far, core = user // 2, user % 2
    items_rows = items_v.shape[0]
    offset = item * items_rows

    def at(zz, yy, xx):
        return {"item": (zz * NY + yy) * NX + xx}

    def z_peer(k):
        return lax.rem(z + k, NZ)

    def y_peer(k):
        return lax.rem(y + k, NY)

    def plane_peer(k):
        return lax.rem(place + k, NY * NX)

    loads = [
        pltpu.make_async_copy(source, target, in_sem.at[n])
        for n, (source, target) in enumerate(
            (
                (qb_in, qb.at[x, y, z]),
                (qa_in, qa.at[x, y, z]),
                (pa_in, pa_v),
                (pb_in, pb_v),
                (w_in, w_v),
                (items_in, items_v),
            )
        )
    ]

    barrier = pltpu.get_barrier_semaphore()

    @pl.loop(1, NZ)
    def _(k):
        pl.semaphore_signal(barrier, inc=1, device_id=at(z_peer(k), y, x), device_id_type=MESH)

    @pl.loop(1, NY * NX)
    def _(k):
        p = plane_peer(k)
        pl.semaphore_signal(barrier, inc=1, device_id=at(z, p // NX, p % NX), device_id_type=MESH)

    other_core = {"user": far * 2 + 1 - core}
    other_far = {"user": (1 - far) * 2 + core}
    pl.semaphore_signal(barrier, inc=1, device_id=other_core, device_id_type=MESH)
    pl.semaphore_signal(barrier, inc=1, device_id=other_far, device_id_type=MESH)

    for load in loads:
        load.start()

    pl.semaphore_wait(barrier, (NZ - 1) + (NY * NX - 1) + 2)

    def sent(refs, send_sem, recv_sem):
        remote(refs, refs, send_sem, recv_sem, other_core).wait_send()

    def arrived(refs, send_sem, recv_sem):
        remote(refs, refs, send_sem, recv_sem, other_core).wait_recv()

    others = pl.ds(0, NZ - 1)

    def on_core(number):
        return pl.when(core == number)

    def small_z(source, q, ss, rs):
        @pl.loop(1, NZ)
        def _(k):
            remote(source, q.at[x, y, z], ss, rs, at(z_peer(k), y, x)).start()

    def small_plane(source, q, ss, rs):
        @pl.loop(1, NY * NX)
        def _(k):
            p = plane_peer(k)
            remote(source, q.at[x, y, z], ss, rs, at(z, p // NX, p % NX)).start()

    def bulk_plane(q, ss, rs):
        block = q.at[x, y]

        @pl.loop(1, NY)
        def _(k):
            remote(block, block, ss, rs.at[x], at(z, y_peer(k), x)).start()

        @pl.loop(0, NY)
        def _(k):
            remote(block, block, ss, rs.at[x], at(z, y_peer(k), 1 - x)).start()

    def bulk_z(q, ss, rs, xx):
        block = q.at[xx, :, z]

        @pl.loop(1, NZ)
        def _(k):
            remote(block, block, ss, rs.at[xx], at(z_peer(k), y, x)).start()

    def plane_own_wait(q, ss, rs):
        arrived(q.at[x, pl.ds(0, NY - 1)], ss, rs.at[x])

    def plane_other_wait(q, ss, rs):
        arrived(q.at[1 - x], ss, rs.at[1 - x])

    def z_wait(q, ss, rs, xx):
        arrived(q.at[xx, :, others], ss, rs.at[xx])

    def plane_drain(q, ss, rs):
        sent(q.at[0], ss, rs.at[0])
        sent(q.at[0, pl.ds(0, NY - 1)], ss, rs.at[0])

    def z_drain(q, ss, rs):
        sent(q.at[0, :, others], ss, rs.at[0])
        sent(q.at[1, :, others], ss, rs.at[0])

    bulk_b, bulk_a = (qb, b2_s, b2_r), (qa, a2_s, a2_r)

    @on_core(0)
    def _():
        small_z(qb_in, qb, b1_s, b1_r)
        small_plane(qa_in, qa, a1_s, a1_r)

    @on_core(1)
    def _():
        small_plane(qb_in, qb, b1_s, b1_r)
        small_z(qa_in, qa, a1_s, a1_r)

    loads[0].wait()
    arrived(qb.at[x, y, others], b1_s, b1_r)

    @on_core(0)
    def _():
        bulk_plane(*bulk_b)

    @on_core(1)
    def _():
        bulk_z(*bulk_b, x)
        bulk_z(*bulk_b, 1 - x)

    loads[1].wait()
    arrived(qa.at[x, y, others], a1_s, a1_r)

    lanes = lax.broadcasted_iota(jnp.int32, (1, GROUP), 1)
    own_of = lanes % OWN
    z_of = (lanes // OWN) % NZ
    y_of = (lanes // (OWN * NZ)) % NY
    x_of = lanes // (OWN * NZ * NY)
    ks = lax.broadcasted_iota(jnp.int32, (128, GROUP), 0)
    selector = (ks == x_of * (4 * OWN) + user * OWN + own_of).astype(F32).astype(BF16)
    for load in loads[2:5]:
        load.wait()
    row_a, row_b, weight[...] = group_rows(
        (pa_v[...], pb_v[...], w_v[...]), selector, z_of * NY + y_of
    )
    pos_a[...] = row_a.astype(jnp.int32) - offset
    pos_b[...] = row_b.astype(jnp.int32) - offset

    loads[5].wait()
    for part in range(items_rows // QUARTER):
        rows = pl.ds(part * QUARTER, QUARTER)
        items_t[:, rows] = items_v[rows, :].T

    tiles = [slice(r, r + TILE) for r in range(0, items_rows, TILE)]
    ids = lax.broadcasted_iota(jnp.int32, (TILE, HALF), 0)

    def half_of(xx):
        return pl.ds(pl.multiple_of(xx * HALF, HALF), HALF)

    def fold(values, op):
        return op(values.reshape(TILE // 8, 8, HALF), axis=0)

    def scores(q, xx):
        users = q[xx].reshape(HALF, E)
        return lax.dot_general(
            items_v[...], users, (((1,), (1,)), ((), ())), preferred_element_type=F32
        )

    zero = jnp.zeros((8, HALF), F32)
    least = jnp.full((8, HALF), -jnp.inf, F32)

    def half_b(xx):
        probs[xx] = scores(qb, xx)

        top = least
        for rows in tiles:
            top = jnp.maximum(top, fold(probs[xx, rows, :], jnp.max))
        top = jnp.max(top, axis=0, keepdims=True)
        total = zero
        for rows in tiles:
            p = jnp.exp(probs[xx, rows, :] - top)
            probs[xx, rows, :] = p
            total = total + fold(p, jnp.sum)
        total = jnp.sum(total, axis=0, keepdims=True)
        tops[:, half_of(xx)] = top
        zb[z, :, half_of(xx)] = top + jnp.log(total)

    def tops_a(xx):
        score_a[...] = scores(qa, xx)
        pos = pos_a[:, half_of(xx)]
        top, hit = least, zero
        for rows in tiles:
            score = score_a[rows, :]
            top = jnp.maximum(top, fold(score, jnp.max))
            hit = hit + fold(jnp.where(ids == pos - rows.start, score, 0.0), jnp.sum)
        top_a[...] = jnp.max(top, axis=0, keepdims=True)
        za[z, 1:2, half_of(xx)] = jnp.sum(hit, axis=0, keepdims=True)

    def sums_a(xx):
        top, total = top_a[...], zero
        for rows in tiles:
            total = total + fold(jnp.exp(score_a[rows, :] - top), jnp.sum)
        total = jnp.sum(total, axis=0, keepdims=True)
        za[z, 0:1, half_of(xx)] = top + jnp.log(total)

    def z_round(buf, ss, rs):
        @pl.loop(1, NZ)
        def _(k):
            remote(buf.at[z], buf.at[z], ss, rs, at(z_peer(k), y, x)).start()

    def plane_round(buf, ss, rs):
        @pl.loop(1, NY * NX)
        def _(k):
            p = plane_peer(k)
            remote(buf.at[place], buf.at[place], ss, rs, at(z, p // NX, p % NX)).start()

    @on_core(0)
    def _():
        plane_own_wait(*bulk_b)
        bulk_z(*bulk_a, x)

    @on_core(1)
    def _():
        z_wait(*bulk_b, x)

    half_b(x)

    @on_core(0)
    def _():
        plane_other_wait(*bulk_b)

    @on_core(1)
    def _():
        z_wait(*bulk_b, 1 - x)
        bulk_plane(*bulk_a)

    half_b(1 - x)
    z_round(zb, b_zs, b_zr)
    sent(qb.at[x, y, others], b1_s, b1_r)
    sent(qa.at[x, y, others], a1_s, a1_r)

    @on_core(0)
    def _():
        bulk_z(*bulk_a, 1 - x)
        plane_drain(*bulk_b)
        z_wait(*bulk_a, x)

    @on_core(1)
    def _():
        z_drain(*bulk_b)
        plane_own_wait(*bulk_a)

    tops_a(x)
    arrived(zb.at[others], b_zs, b_zr)
    yb[place] = lse_of(zb[...])
    plane_round(yb, b_ys, b_yr)
    sums_a(x)
    sent(zb.at[others], b_zs, b_zr)

    arrived(yb.at[others], b_ys, b_yr)
    lse_b = lse_of(yb[...])
    tops[...] = weight[...] * jnp.exp(tops[...] - lse_b)

    def quarter_of(ff, cc):
        return pl.ds(pl.multiple_of((ff * 2 + cc) * QUARTER, QUARTER), QUARTER)

    def dscores(xx, ff, cc):
        cols = half_of(xx)
        start = (ff * 2 + cc) * QUARTER
        pos, scale, ratio = pos_b[:, cols] - start, weight[:, cols], tops[:, cols]
        for r in range(0, QUARTER, TILE):
            rows = pl.ds(pl.multiple_of(start + r, TILE), TILE)
            match = jnp.where(ids == pos - r, scale, 0.0)
            dsc[rows, cols] = (probs[xx, rows, :] * ratio - match).astype(BF16)

    def far_copy():
        return remote(gi_s, gi_far, far_s, far_r, other_far)

    def core_copy(n):
        return remote(gi_f.at[n, 1 - core], gi_core.at[n], gi_ss.at[n], gi_rs.at[n], other_core)

    def item_grads(n, ff, cc):
        gi_f[n, cc] = jnp.dot(
            dsc[quarter_of(ff, cc), :], qb[...].reshape(GROUP, E), preferred_element_type=F32
        )

    def query_grads(xx):
        block = jnp.dot(
            items_t[...], dsc[:, half_of(xx)], preferred_element_type=F32
        ).T.reshape(NY, NZ, OWN, E)
        gq_f[xx] = block
        gq_s[xx] = block.astype(BF16)

    def plane_send(xx, yy):
        remote(gq_s.at[xx, yy], r1.at[x, y], s1s, s1r.at[x], at(z, yy, xx)).start()

    def own_sends():
        @pl.loop(1, NY)
        def _(k):
            plane_send(x, y_peer(k))

    def other_sends():
        @pl.when(core == 0)
        def _():
            @pl.loop(0, NY)
            def _(k):
                plane_send(1 - x, y_peer(k))

        @pl.when(core == 1)
        def _():
            @pl.loop(1, NZ)
            def _(k):
                zz = z_peer(k)
                remote(gq_s.at[1 - x, :, zz], rz.at[z], zs, zr, at(zz, y, x)).start()

    for quarter in range(4):
        dscores(1 - x, quarter // 2, quarter % 2)
    query_grads(1 - x)
    other_sends()
    dscores(x, 1 - far, 1 - core)
    item_grads(0, 1 - far, 1 - core)
    core_copy(0).start()
    dscores(x, 1 - far, core)
    item_grads(0, 1 - far, core)
    dscores(x, far, 1 - core)
    dscores(x, far, core)
    query_grads(x)
    own_sends()
    core_copy(0).wait_recv()
    gi_s[...] = (gi_f[0, core] + gi_core[0]).astype(BF16)
    far_copy().start()

    item_grads(1, far, 1 - core)
    core_copy(1).start()
    item_grads(1, far, core)

    @on_core(0)
    def _():
        z_wait(*bulk_a, 1 - x)

    @on_core(1)
    def _():
        plane_other_wait(*bulk_a)

    tops_a(1 - x)
    sums_a(1 - x)
    z_round(za, a_zs, a_zr)

    r1[x, y] = jnp.zeros((NZ, OWN, E), BF16)
    rz[z] = jnp.zeros((NY, OWN, E), BF16)
    r2[z] = jnp.zeros((OWN, E), F32)
    arrived(r1.at[x, pl.ds(0, NY - 1)], s1s, s1r.at[x])
    gq_h[...] = gq_f[x, y] + jnp.sum(r1[x].astype(F32), axis=0)

    @pl.when(core == 0)
    def _():
        arrived(r1.at[1 - x], s1s, s1r.at[1 - x])
        gq_h[...] += jnp.sum(r1[1 - x].astype(F32), axis=0)

    @pl.loop(1, NZ)
    def _(k):
        zz = z_peer(k)
        remote(gq_h.at[zz], r2.at[z], s2s, s2r, at(zz, y, x)).start()

    @pl.when(core == 1)
    def _():
        arrived(rz.at[others], zs, zr)
        gq_p[...] = gq_f[1 - x, :, z] + jnp.sum(rz[...].astype(F32), axis=0)

        @pl.loop(0, NY)
        def _(k):
            yy = y_peer(k)
            remote(gq_p.at[yy], r3.at[y], s3s, s3r, at(z, yy, 1 - x)).start()

    arrived(za.at[others], a_zs, a_zr)
    z_parts = za[...]
    ya[place, 0:1] = lse_of(z_parts[:, 0:1])
    ya[place, 1:2] = jnp.sum(z_parts[:, 1:2], axis=0)
    plane_round(ya, a_ys, a_yr)

    core_copy(1).wait_recv()
    gi_out[...] = gi_f[1, core] + gi_core[1]

    @on_core(0)
    def _():
        z_drain(*bulk_a)

    @on_core(1)
    def _():
        plane_drain(*bulk_a)

    sent(yb.at[others], b_ys, b_yr)
    sent(za.at[others], a_zs, a_zr)
    sent(r1.at[0, pl.ds(0, NY - 1)], s1s, s1r.at[0])

    @pl.when(core == 0)
    def _():
        sent(r1.at[0], s1s, s1r.at[0])

    @pl.when(core == 1)
    def _():
        sent(rz.at[others], zs, zr)

    core_copy(0).wait_send()
    core_copy(1).wait_send()
    far_copy().wait_recv()
    gi_out[...] += gi_far[...].astype(F32)

    arrived(ya.at[others], a_ys, a_yr)
    y_parts = ya[...]
    tops[...] = lse_of(y_parts[:, 0:1]) - jnp.sum(y_parts[:, 1:2], axis=0)
    mine = tops[:, pl.ds(pl.multiple_of((x * NY + y) * NZ * OWN, NZ * OWN), NZ * OWN)]
    loss_out[...] = pltpu.roll(
        jnp.broadcast_to(mine, (8, NZ * OWN)), (NZ - z) * OWN % (NZ * OWN), 1
    )[0:1, 0:OWN]

    arrived(r2.at[others], s2s, s2r)
    gq_out[...] = gq_h[z] + jnp.sum(r2[...], axis=0)

    @pl.when(core == 1)
    def _():
        arrived(r3, s3s, s3r)
        gq_out[...] += jnp.sum(r3[...], axis=0)
        sent(r3, s3s, s3r)


    sent(ya.at[others], a_ys, a_yr)
    sent(r2.at[others], s2s, s2r)

    far_copy().wait_send()


def hand_over(*refs):
    copies = [
        pltpu.make_async_copy(source, target, refs[6].at[n])
        for n, (source, target) in enumerate(zip(refs[:3], refs[3:6]))
    ]
    for copy in copies:
        copy.start()
    for copy in copies:
        copy.wait()


def per_device(query_a, query_b, items, positive_a, positive_b, loss_cotangent):
    rows = items.shape[0]
    hbm, vmem = pl.BlockSpec(memory_space=pltpu.HBM), pl.BlockSpec(memory_space=pltpu.VMEM)
    results = (
        jax.ShapeDtypeStruct((1, OWN), F32),
        jax.ShapeDtypeStruct((OWN, E), F32),
        jax.ShapeDtypeStruct((QUARTER, E), F32),
    )
    dma = pltpu.SemaphoreType.DMA
    block = (NX, NY, NZ, OWN, E)
    loss, gq, gi = pl.pallas_call(
        kernel,
        out_shape=[pltpu.VMEM(r.shape, r.dtype) for r in results],
        in_specs=[hbm] * 6,
        out_specs=[vmem] * 3,
        scratch_shapes=[
            pltpu.VMEM((rows, E), BF16),
            pltpu.VMEM((E, rows), BF16),
            pltpu.VMEM(block, BF16),
            pltpu.VMEM(block, BF16),
            pltpu.VMEM((32, 128), jnp.int32),
            pltpu.VMEM((32, 128), jnp.int32),
            pltpu.VMEM((32, 128), F32),
            pltpu.VMEM((1, GROUP), jnp.int32),
            pltpu.VMEM((1, GROUP), jnp.int32),
            pltpu.VMEM((1, GROUP), F32),
            pltpu.VMEM((NX, rows, HALF), F32),
            pltpu.VMEM((rows, HALF), F32),
            pltpu.VMEM((rows, GROUP), BF16),
            pltpu.VMEM(block, F32),
            pltpu.VMEM(block, BF16),
            pltpu.VMEM(block, BF16),
            pltpu.VMEM((NZ, NY, OWN, E), BF16),
            pltpu.VMEM((NZ, OWN, E), F32),
            pltpu.VMEM((NY, OWN, E), F32),
            pltpu.VMEM((NZ, OWN, E), F32),
            pltpu.VMEM((NY, OWN, E), F32),
            pltpu.VMEM((2, 2, QUARTER, E), F32),
            pltpu.VMEM((QUARTER, E), BF16),
            pltpu.VMEM((2, QUARTER, E), F32),
            pltpu.VMEM((QUARTER, E), BF16),
            pltpu.VMEM((NZ, 1, GROUP), F32),
            pltpu.VMEM((NY * NX, 1, GROUP), F32),
            pltpu.VMEM((NZ, 2, GROUP), F32),
            pltpu.VMEM((NY * NX, 2, GROUP), F32),
            pltpu.VMEM((1, GROUP), F32),
            pltpu.VMEM((1, HALF), F32),
            dma((6,)),
            dma, dma,
            dma, dma((NX,)),
            dma, dma,
            dma, dma((NX,)),
            dma, dma,
            dma, dma,
            dma, dma,
            dma, dma,
            dma, dma((NX,)),
            dma, dma,
            dma, dma,
            dma, dma,
            dma((2,)), dma((2,)),
            dma, dma,
        ],
        compiler_params=pltpu.CompilerParams(
            collective_id=0, has_side_effects=True, vmem_limit_bytes=56 * 1024 * 1024
        ),
    )(
        *(
            pltpu.with_memory_space_constraint(operand, pltpu.HBM)
            for operand in (
                query_a,
                query_b,
                items,
                positive_a.reshape(32, 128),
                positive_b.reshape(32, 128),
                loss_cotangent.reshape(32, 128),
            )
        )
    )
    loss, gq, gi = pl.pallas_call(
        hand_over,
        out_shape=results,
        in_specs=[vmem] * 3,
        out_specs=[hbm] * 3,
        scratch_shapes=[dma((3,))],
        compiler_params=pltpu.CompilerParams(vmem_limit_bytes=1024 * 1024),
    )(*(pltpu.with_memory_space_constraint(result, pltpu.VMEM) for result in (loss, gq, gi)))
    return loss.reshape(OWN), gq, gi


def solution(mesh):
    return jax.shard_map(
        per_device,
        mesh=mesh,
        in_specs=(
            P(("item", "user"), None),
            P(("item", "user"), None),
            P("item", None),
            P(),
            P(),
            P(),
        ),
        out_specs=(P(("item", "user")), P(("item", "user"), None), P(("item", "user"), None)),
        check_vma=False,
    )
```

```python
import functools

import jax
import jax.numpy as jnp
from jax import lax
from jax.experimental import pallas as pl
from jax.experimental.pallas import tpu as pltpu
from jax.sharding import PartitionSpec as P

MESH = pl.DeviceIdType.MESH
F32 = jnp.float32
BF16 = jnp.bfloat16

NZ, NY, NX = 8, 4, 2
OWN = 16
E = 256
GROUP = NZ * NY * NX * OWN
HALF = GROUP // NX
TILE = 32
QUARTER = 512


def remote(src, dst, send_sem, recv_sem, device):
    return pltpu.make_async_remote_copy(
        src_ref=src,
        dst_ref=dst,
        send_sem=send_sem,
        recv_sem=recv_sem,
        device_id=device,
        device_id_type=MESH,
    )


def exact_parts(table):
    if table.dtype == jnp.int32:
        parts = (table & 63, table & (63 << 6), table & (63 << 12))
        return [part.astype(F32).astype(BF16) for part in parts]
    high = table.astype(BF16)
    rest = table - high.astype(F32)
    middle = rest.astype(BF16)
    return [high, middle, (rest - middle.astype(F32)).astype(BF16)]


def group_rows(tables, selector, row_of):
    parts = [part for table in tables for part in exact_parts(table)]
    picked = jnp.dot(jnp.concatenate(parts, axis=0), selector, preferred_element_type=F32)
    picked = picked.reshape(len(tables), 3, 32, GROUP)
    rows = lax.broadcasted_iota(jnp.int32, (32, GROUP), 0) == row_of
    return [
        jnp.sum(jnp.where(rows, (p[0] + p[1]) + p[2], 0.0), axis=0, keepdims=True) for p in picked
    ]


def lse_of(parts):
    top = jnp.max(parts, axis=0)
    return top + jnp.log(jnp.sum(jnp.exp(parts - top[None]), axis=0))


def kernel(
    qa_in, qb_in, items_in, pa_in, pb_in, w_in,
    loss_out, gq_out, gi_out,
    items_v, items_t, qa, qb, pa_v, pb_v, w_v, pos_a, pos_b, weight,
    probs, score_a, dsc, gq_f, gq_s,
    r1, rz, gq_h, gq_p, r2, r3,
    gi_f, gi_s, gi_core, gi_far,
    zb, yb, za, ya,
    tops, top_a,
    in_sem, b1_s, b1_r, b2_s, b2_r, a1_s, a1_r, a2_s, a2_r,
    b_zs, b_zr, b_ys, b_yr, a_zs, a_zr, a_ys, a_yr,
    s1s, s1r, zs, zr, s2s, s2r, s3s, s3r, gi_ss, gi_rs, far_s, far_r,
):
    item = lax.axis_index("item")
    user = lax.axis_index("user")
    z, y, x = item // (NY * NX), (item // NX) % NY, item % NX
    place = y * NX + x
    far, core = user // 2, user % 2
    items_rows = items_v.shape[0]
    offset = item * items_rows

    def at(zz, yy, xx):
        return {"item": (zz * NY + yy) * NX + xx}

    def z_peer(k):
        return lax.rem(z + k, NZ)

    def y_peer(k):
        return lax.rem(y + k, NY)

    def plane_peer(k):
        return lax.rem(place + k, NY * NX)

    loads = [
        pltpu.make_async_copy(source, target, in_sem.at[n])
        for n, (source, target) in enumerate(
            (
                (qb_in, qb.at[x, y, z]),
                (qa_in, qa.at[x, y, z]),
                (pa_in, pa_v),
                (pb_in, pb_v),
                (w_in, w_v),
                (items_in, items_v),
            )
        )
    ]

    barrier = pltpu.get_barrier_semaphore()

    @pl.loop(1, NZ)
    def _(k):
        pl.semaphore_signal(barrier, inc=1, device_id=at(z_peer(k), y, x), device_id_type=MESH)

    @pl.loop(1, NY * NX)
    def _(k):
        p = plane_peer(k)
        pl.semaphore_signal(barrier, inc=1, device_id=at(z, p // NX, p % NX), device_id_type=MESH)

    other_core = {"user": far * 2 + 1 - core}
    other_far = {"user": (1 - far) * 2 + core}
    pl.semaphore_signal(barrier, inc=1, device_id=other_core, device_id_type=MESH)
    pl.semaphore_signal(barrier, inc=1, device_id=other_far, device_id_type=MESH)

    for load in loads:
        load.start()

    pl.semaphore_wait(barrier, (NZ - 1) + (NY * NX - 1) + 2)

    def sent(refs, send_sem, recv_sem):
        remote(refs, refs, send_sem, recv_sem, other_core).wait_send()

    def arrived(refs, send_sem, recv_sem):
        remote(refs, refs, send_sem, recv_sem, other_core).wait_recv()

    others = pl.ds(0, NZ - 1)

    def on_core(number):
        return pl.when(core == number)

    def small_z(source, q, ss, rs):
        @pl.loop(1, NZ)
        def _(k):
            remote(source, q.at[x, y, z], ss, rs, at(z_peer(k), y, x)).start()

    def small_plane(source, q, ss, rs):
        @pl.loop(1, NY * NX)
        def _(k):
            p = plane_peer(k)
            remote(source, q.at[x, y, z], ss, rs, at(z, p // NX, p % NX)).start()

    def bulk_plane(q, ss, rs):
        block = q.at[x, y]

        @pl.loop(1, NY)
        def _(k):
            remote(block, block, ss, rs.at[x], at(z, y_peer(k), x)).start()

        @pl.loop(0, NY)
        def _(k):
            remote(block, block, ss, rs.at[x], at(z, y_peer(k), 1 - x)).start()

    def bulk_z(q, ss, rs, xx):
        block = q.at[xx, :, z]

        @pl.loop(1, NZ)
        def _(k):
            remote(block, block, ss, rs.at[xx], at(z_peer(k), y, x)).start()

    def plane_own_wait(q, ss, rs):
        arrived(q.at[x, pl.ds(0, NY - 1)], ss, rs.at[x])

    def plane_other_wait(q, ss, rs):
        arrived(q.at[1 - x], ss, rs.at[1 - x])

    def z_wait(q, ss, rs, xx):
        arrived(q.at[xx, :, others], ss, rs.at[xx])

    def plane_drain(q, ss, rs):
        sent(q.at[0], ss, rs.at[0])
        sent(q.at[0, pl.ds(0, NY - 1)], ss, rs.at[0])

    def z_drain(q, ss, rs):
        sent(q.at[0, :, others], ss, rs.at[0])
        sent(q.at[1, :, others], ss, rs.at[0])

    bulk_b, bulk_a = (qb, b2_s, b2_r), (qa, a2_s, a2_r)

    @on_core(0)
    def _():
        small_z(qb_in, qb, b1_s, b1_r)
        small_plane(qa_in, qa, a1_s, a1_r)

    @on_core(1)
    def _():
        small_plane(qb_in, qb, b1_s, b1_r)
        small_z(qa_in, qa, a1_s, a1_r)

    loads[0].wait()
    arrived(qb.at[x, y, others], b1_s, b1_r)

    @on_core(0)
    def _():
        bulk_plane(*bulk_b)

    @on_core(1)
    def _():
        bulk_z(*bulk_b, x)
        bulk_z(*bulk_b, 1 - x)

    loads[1].wait()
    arrived(qa.at[x, y, others], a1_s, a1_r)

    lanes = lax.broadcasted_iota(jnp.int32, (1, GROUP), 1)
    own_of = lanes % OWN
    z_of = (lanes // OWN) % NZ
    y_of = (lanes // (OWN * NZ)) % NY
    x_of = lanes // (OWN * NZ * NY)
    ks = lax.broadcasted_iota(jnp.int32, (128, GROUP), 0)
    selector = (ks == x_of * (4 * OWN) + user * OWN + own_of).astype(F32).astype(BF16)
    for load in loads[2:5]:
        load.wait()
    row_a, row_b, weight[...] = group_rows(
        (pa_v[...], pb_v[...], w_v[...]), selector, z_of * NY + y_of
    )
    pos_a[...] = row_a.astype(jnp.int32) - offset
    pos_b[...] = row_b.astype(jnp.int32) - offset

    loads[5].wait()
    for part in range(items_rows // QUARTER):
        rows = pl.ds(part * QUARTER, QUARTER)
        items_t[:, rows] = items_v[rows, :].T

    tiles = [slice(r, r + TILE) for r in range(0, items_rows, TILE)]
    ids = lax.broadcasted_iota(jnp.int32, (TILE, HALF), 0)

    def half_of(xx):
        return pl.ds(pl.multiple_of(xx * HALF, HALF), HALF)

    def fold(values, op):
        return op(values.reshape(TILE // 8, 8, HALF), axis=0)

    def scores(q, xx):
        users = q[xx].reshape(HALF, E)
        return lax.dot_general(
            items_v[...], users, (((1,), (1,)), ((), ())), preferred_element_type=F32
        )

    zero = jnp.zeros((8, HALF), F32)
    least = jnp.full((8, HALF), -jnp.inf, F32)

    def half_b(xx):
        probs[xx] = scores(qb, xx)

        top = least
        for rows in tiles:
            top = jnp.maximum(top, fold(probs[xx, rows, :], jnp.max))
        top = jnp.max(top, axis=0, keepdims=True)
        total = zero
        for rows in tiles:
            p = jnp.exp(probs[xx, rows, :] - top)
            probs[xx, rows, :] = p
            total = total + fold(p, jnp.sum)
        total = jnp.sum(total, axis=0, keepdims=True)
        tops[:, half_of(xx)] = top
        zb[z, :, half_of(xx)] = top + jnp.log(total)

    def tops_a(xx):
        score_a[...] = scores(qa, xx)
        pos = pos_a[:, half_of(xx)]
        top, hit = least, zero
        for rows in tiles:
            score = score_a[rows, :]
            top = jnp.maximum(top, fold(score, jnp.max))
            hit = hit + fold(jnp.where(ids == pos - rows.start, score, 0.0), jnp.sum)
        top_a[...] = jnp.max(top, axis=0, keepdims=True)
        za[z, 1:2, half_of(xx)] = jnp.sum(hit, axis=0, keepdims=True)

    def sums_a(xx):
        top, total = top_a[...], zero
        for rows in tiles:
            total = total + fold(jnp.exp(score_a[rows, :] - top), jnp.sum)
        total = jnp.sum(total, axis=0, keepdims=True)
        za[z, 0:1, half_of(xx)] = top + jnp.log(total)

    def z_round(buf, ss, rs):
        @pl.loop(1, NZ)
        def _(k):
            remote(buf.at[z], buf.at[z], ss, rs, at(z_peer(k), y, x)).start()

    def plane_round(buf, ss, rs):
        @pl.loop(1, NY * NX)
        def _(k):
            p = plane_peer(k)
            remote(buf.at[place], buf.at[place], ss, rs, at(z, p // NX, p % NX)).start()

    @on_core(0)
    def _():
        plane_own_wait(*bulk_b)
        bulk_z(*bulk_a, x)

    @on_core(1)
    def _():
        z_wait(*bulk_b, x)

    half_b(x)

    @on_core(0)
    def _():
        plane_other_wait(*bulk_b)

    @on_core(1)
    def _():
        z_wait(*bulk_b, 1 - x)
        bulk_plane(*bulk_a)

    half_b(1 - x)
    z_round(zb, b_zs, b_zr)
    sent(qb.at[x, y, others], b1_s, b1_r)
    sent(qa.at[x, y, others], a1_s, a1_r)

    @on_core(0)
    def _():
        bulk_z(*bulk_a, 1 - x)
        plane_drain(*bulk_b)
        z_wait(*bulk_a, x)

    @on_core(1)
    def _():
        z_drain(*bulk_b)
        plane_own_wait(*bulk_a)

    tops_a(x)
    arrived(zb.at[others], b_zs, b_zr)
    yb[place] = lse_of(zb[...])
    plane_round(yb, b_ys, b_yr)
    sums_a(x)
    sent(zb.at[others], b_zs, b_zr)

    arrived(yb.at[others], b_ys, b_yr)
    lse_b = lse_of(yb[...])
    tops[...] = weight[...] * jnp.exp(tops[...] - lse_b)

    def quarter_of(ff, cc):
        return pl.ds(pl.multiple_of((ff * 2 + cc) * QUARTER, QUARTER), QUARTER)

    def dscores(xx, ff, cc):
        cols = half_of(xx)
        start = (ff * 2 + cc) * QUARTER
        pos, scale, ratio = pos_b[:, cols] - start, weight[:, cols], tops[:, cols]
        for r in range(0, QUARTER, TILE):
            rows = pl.ds(pl.multiple_of(start + r, TILE), TILE)
            match = jnp.where(ids == pos - r, scale, 0.0)
            dsc[rows, cols] = (probs[xx, rows, :] * ratio - match).astype(BF16)

    def far_copy():
        return remote(gi_s, gi_far, far_s, far_r, other_far)

    def core_copy(n):
        return remote(gi_f.at[n, 1 - core], gi_core.at[n], gi_ss.at[n], gi_rs.at[n], other_core)

    def item_grads(n, ff, cc):
        gi_f[n, cc] = jnp.dot(
            dsc[quarter_of(ff, cc), :], qb[...].reshape(GROUP, E), preferred_element_type=F32
        )

    def query_grads(xx):
        block = jnp.dot(
            items_t[...], dsc[:, half_of(xx)], preferred_element_type=F32
        ).T.reshape(NY, NZ, OWN, E)
        gq_f[xx] = block
        gq_s[xx] = block.astype(BF16)

    def plane_send(xx, yy):
        remote(gq_s.at[xx, yy], r1.at[x, y], s1s, s1r.at[x], at(z, yy, xx)).start()

    def own_sends():
        @pl.loop(1, NY)
        def _(k):
            plane_send(x, y_peer(k))

    def other_sends():
        @pl.when(core == 0)
        def _():
            @pl.loop(0, NY)
            def _(k):
                plane_send(1 - x, y_peer(k))

        @pl.when(core == 1)
        def _():
            @pl.loop(1, NZ)
            def _(k):
                zz = z_peer(k)
                remote(gq_s.at[1 - x, :, zz], rz.at[z], zs, zr, at(zz, y, x)).start()

    for cc in (1 - core, core):
        dscores(1 - x, 1 - far, cc)
        dscores(x, 1 - far, cc)
        item_grads(0, 1 - far, cc)
        if cc is not core:
            core_copy(0).start()
    dscores(1 - x, far, 0)
    dscores(1 - x, far, 1)
    query_grads(1 - x)
    other_sends()
    core_copy(0).wait_recv()
    gi_s[...] = (gi_f[0, core] + gi_core[0]).astype(BF16)
    far_copy().start()
    dscores(x, far, 0)
    dscores(x, far, 1)
    query_grads(x)
    own_sends()
    item_grads(1, far, 1 - core)
    core_copy(1).start()
    item_grads(1, far, core)

    @on_core(0)
    def _():
        z_wait(*bulk_a, 1 - x)

    @on_core(1)
    def _():
        plane_other_wait(*bulk_a)

    tops_a(1 - x)
    sums_a(1 - x)
    z_round(za, a_zs, a_zr)

    r1[x, y] = jnp.zeros((NZ, OWN, E), BF16)
    rz[z] = jnp.zeros((NY, OWN, E), BF16)
    r2[z] = jnp.zeros((OWN, E), F32)
    arrived(r1.at[x, pl.ds(0, NY - 1)], s1s, s1r.at[x])
    gq_h[...] = gq_f[x, y] + jnp.sum(r1[x].astype(F32), axis=0)

    @pl.when(core == 0)
    def _():
        arrived(r1.at[1 - x], s1s, s1r.at[1 - x])
        gq_h[...] += jnp.sum(r1[1 - x].astype(F32), axis=0)

    @pl.loop(1, NZ)
    def _(k):
        zz = z_peer(k)
        remote(gq_h.at[zz], r2.at[z], s2s, s2r, at(zz, y, x)).start()

    @pl.when(core == 1)
    def _():
        arrived(rz.at[others], zs, zr)
        gq_p[...] = gq_f[1 - x, :, z] + jnp.sum(rz[...].astype(F32), axis=0)

        @pl.loop(0, NY)
        def _(k):
            yy = y_peer(k)
            remote(gq_p.at[yy], r3.at[y], s3s, s3r, at(z, yy, 1 - x)).start()

    arrived(za.at[others], a_zs, a_zr)
    z_parts = za[...]
    ya[place, 0:1] = lse_of(z_parts[:, 0:1])
    ya[place, 1:2] = jnp.sum(z_parts[:, 1:2], axis=0)
    plane_round(ya, a_ys, a_yr)

    core_copy(1).wait_recv()
    gi_out[...] = gi_f[1, core] + gi_core[1]

    @on_core(0)
    def _():
        z_drain(*bulk_a)

    @on_core(1)
    def _():
        plane_drain(*bulk_a)

    sent(yb.at[others], b_ys, b_yr)
    sent(za.at[others], a_zs, a_zr)
    sent(r1.at[0, pl.ds(0, NY - 1)], s1s, s1r.at[0])

    @pl.when(core == 0)
    def _():
        sent(r1.at[0], s1s, s1r.at[0])

    @pl.when(core == 1)
    def _():
        sent(rz.at[others], zs, zr)

    core_copy(0).wait_send()
    core_copy(1).wait_send()
    far_copy().wait_recv()
    gi_out[...] += gi_far[...].astype(F32)

    arrived(ya.at[others], a_ys, a_yr)
    y_parts = ya[...]
    tops[...] = lse_of(y_parts[:, 0:1]) - jnp.sum(y_parts[:, 1:2], axis=0)
    mine = tops[:, pl.ds(pl.multiple_of((x * NY + y) * NZ * OWN, NZ * OWN), NZ * OWN)]
    loss_out[...] = pltpu.roll(
        jnp.broadcast_to(mine, (8, NZ * OWN)), (NZ - z) * OWN % (NZ * OWN), 1
    )[0:1, 0:OWN]

    arrived(r2.at[others], s2s, s2r)
    gq_out[...] = gq_h[z] + jnp.sum(r2[...], axis=0)

    @pl.when(core == 1)
    def _():
        arrived(r3, s3s, s3r)
        gq_out[...] += jnp.sum(r3[...], axis=0)
        sent(r3, s3s, s3r)


    sent(ya.at[others], a_ys, a_yr)
    sent(r2.at[others], s2s, s2r)

    far_copy().wait_send()


def hand_over(*refs):
    copies = [
        pltpu.make_async_copy(source, target, refs[6].at[n])
        for n, (source, target) in enumerate(zip(refs[:3], refs[3:6]))
    ]
    for copy in copies:
        copy.start()
    for copy in copies:
        copy.wait()


def per_device(query_a, query_b, items, positive_a, positive_b, loss_cotangent):
    rows = items.shape[0]
    hbm, vmem = pl.BlockSpec(memory_space=pltpu.HBM), pl.BlockSpec(memory_space=pltpu.VMEM)
    results = (
        jax.ShapeDtypeStruct((1, OWN), F32),
        jax.ShapeDtypeStruct((OWN, E), F32),
        jax.ShapeDtypeStruct((QUARTER, E), F32),
    )
    dma = pltpu.SemaphoreType.DMA
    block = (NX, NY, NZ, OWN, E)
    loss, gq, gi = pl.pallas_call(
        kernel,
        out_shape=[pltpu.VMEM(r.shape, r.dtype) for r in results],
        in_specs=[hbm] * 6,
        out_specs=[vmem] * 3,
        scratch_shapes=[
            pltpu.VMEM((rows, E), BF16),
            pltpu.VMEM((E, rows), BF16),
            pltpu.VMEM(block, BF16),
            pltpu.VMEM(block, BF16),
            pltpu.VMEM((32, 128), jnp.int32),
            pltpu.VMEM((32, 128), jnp.int32),
            pltpu.VMEM((32, 128), F32),
            pltpu.VMEM((1, GROUP), jnp.int32),
            pltpu.VMEM((1, GROUP), jnp.int32),
            pltpu.VMEM((1, GROUP), F32),
            pltpu.VMEM((NX, rows, HALF), F32),
            pltpu.VMEM((rows, HALF), F32),
            pltpu.VMEM((rows, GROUP), BF16),
            pltpu.VMEM(block, F32),
            pltpu.VMEM(block, BF16),
            pltpu.VMEM(block, BF16),
            pltpu.VMEM((NZ, NY, OWN, E), BF16),
            pltpu.VMEM((NZ, OWN, E), F32),
            pltpu.VMEM((NY, OWN, E), F32),
            pltpu.VMEM((NZ, OWN, E), F32),
            pltpu.VMEM((NY, OWN, E), F32),
            pltpu.VMEM((2, 2, QUARTER, E), F32),
            pltpu.VMEM((QUARTER, E), BF16),
            pltpu.VMEM((2, QUARTER, E), F32),
            pltpu.VMEM((QUARTER, E), BF16),
            pltpu.VMEM((NZ, 1, GROUP), F32),
            pltpu.VMEM((NY * NX, 1, GROUP), F32),
            pltpu.VMEM((NZ, 2, GROUP), F32),
            pltpu.VMEM((NY * NX, 2, GROUP), F32),
            pltpu.VMEM((1, GROUP), F32),
            pltpu.VMEM((1, HALF), F32),
            dma((6,)),
            dma, dma,
            dma, dma((NX,)),
            dma, dma,
            dma, dma((NX,)),
            dma, dma,
            dma, dma,
            dma, dma,
            dma, dma,
            dma, dma((NX,)),
            dma, dma,
            dma, dma,
            dma, dma,
            dma((2,)), dma((2,)),
            dma, dma,
        ],
        compiler_params=pltpu.CompilerParams(
            collective_id=0, has_side_effects=True, vmem_limit_bytes=56 * 1024 * 1024
        ),
    )(
        *(
            pltpu.with_memory_space_constraint(operand, pltpu.HBM)
            for operand in (
                query_a,
                query_b,
                items,
                positive_a.reshape(32, 128),
                positive_b.reshape(32, 128),
                loss_cotangent.reshape(32, 128),
            )
        )
    )
    loss, gq, gi = pl.pallas_call(
        hand_over,
        out_shape=results,
        in_specs=[vmem] * 3,
        out_specs=[hbm] * 3,
        scratch_shapes=[dma((3,))],
        compiler_params=pltpu.CompilerParams(vmem_limit_bytes=1024 * 1024),
    )(*(pltpu.with_memory_space_constraint(result, pltpu.VMEM) for result in (loss, gq, gi)))
    return loss.reshape(OWN), gq, gi


def solution(mesh):
    return jax.shard_map(
        per_device,
        mesh=mesh,
        in_specs=(
            P(("item", "user"), None),
            P(("item", "user"), None),
            P("item", None),
            P(),
            P(),
            P(),
        ),
        out_specs=(P(("item", "user")), P(("item", "user"), None), P(("item", "user"), None)),
        check_vma=False,
    )
```

```python
import functools

import jax
import jax.numpy as jnp
from jax import lax
from jax.experimental import pallas as pl
from jax.experimental.pallas import tpu as pltpu
from jax.sharding import PartitionSpec as P

MESH = pl.DeviceIdType.MESH
F32 = jnp.float32
BF16 = jnp.bfloat16

NZ, NY, NX = 8, 4, 2
OWN = 16
E = 256
GROUP = NZ * NY * NX * OWN
HALF = GROUP // NX
TILE = 32
QUARTER = 512


def remote(src, dst, send_sem, recv_sem, device):
    return pltpu.make_async_remote_copy(
        src_ref=src,
        dst_ref=dst,
        send_sem=send_sem,
        recv_sem=recv_sem,
        device_id=device,
        device_id_type=MESH,
    )


def exact_parts(table):
    if table.dtype == jnp.int32:
        parts = (table & 63, table & (63 << 6), table & (63 << 12))
        return [part.astype(F32).astype(BF16) for part in parts]
    high = table.astype(BF16)
    rest = table - high.astype(F32)
    middle = rest.astype(BF16)
    return [high, middle, (rest - middle.astype(F32)).astype(BF16)]


def group_rows(tables, selector, row_of):
    parts = [part for table in tables for part in exact_parts(table)]
    picked = jnp.dot(jnp.concatenate(parts, axis=0), selector, preferred_element_type=F32)
    picked = picked.reshape(len(tables), 3, 32, GROUP)
    rows = lax.broadcasted_iota(jnp.int32, (32, GROUP), 0) == row_of
    return [
        jnp.sum(jnp.where(rows, (p[0] + p[1]) + p[2], 0.0), axis=0, keepdims=True) for p in picked
    ]


def lse_of(parts):
    top = jnp.max(parts, axis=0)
    return top + jnp.log(jnp.sum(jnp.exp(parts - top[None]), axis=0))


def kernel(
    qa_in, qb_in, items_in, pa_in, pb_in, w_in,
    loss_out, gq_out, gi_out,
    items_v, items_t, qa, qb, pa_v, pb_v, w_v, pos_a, pos_b, weight,
    probs, score_a, dsc, gq_f, gq_s,
    r1, rz, gq_h, gq_p, r2, r3,
    gi_f, gi_s, gi_core, gi_far,
    zb, yb, za, ya,
    tops, top_a,
    in_sem, b1_s, b1_r, b2_s, b2_r, a1_s, a1_r, a2_s, a2_r,
    b_zs, b_zr, b_ys, b_yr, a_zs, a_zr, a_ys, a_yr,
    s1s, s1r, zs, zr, s2s, s2r, s3s, s3r, gi_ss, gi_rs, far_s, far_r,
):
    item = lax.axis_index("item")
    user = lax.axis_index("user")
    z, y, x = item // (NY * NX), (item // NX) % NY, item % NX
    place = y * NX + x
    far, core = user // 2, user % 2
    items_rows = items_v.shape[0]
    offset = item * items_rows

    def at(zz, yy, xx):
        return {"item": (zz * NY + yy) * NX + xx}

    def z_peer(k):
        return lax.rem(z + k, NZ)

    def y_peer(k):
        return lax.rem(y + k, NY)

    def plane_peer(k):
        return lax.rem(place + k, NY * NX)

    loads = [
        pltpu.make_async_copy(source, target, in_sem.at[n])
        for n, (source, target) in enumerate(
            (
                (qb_in, qb.at[x, y, z]),
                (qa_in, qa.at[x, y, z]),
                (pa_in, pa_v),
                (pb_in, pb_v),
                (w_in, w_v),
                (items_in, items_v),
            )
        )
    ]

    barrier = pltpu.get_barrier_semaphore()

    @pl.loop(1, NZ)
    def _(k):
        pl.semaphore_signal(barrier, inc=1, device_id=at(z_peer(k), y, x), device_id_type=MESH)

    @pl.loop(1, NY * NX)
    def _(k):
        p = plane_peer(k)
        pl.semaphore_signal(barrier, inc=1, device_id=at(z, p // NX, p % NX), device_id_type=MESH)

    other_core = {"user": far * 2 + 1 - core}
    other_far = {"user": (1 - far) * 2 + core}
    pl.semaphore_signal(barrier, inc=1, device_id=other_core, device_id_type=MESH)
    pl.semaphore_signal(barrier, inc=1, device_id=other_far, device_id_type=MESH)

    for load in loads:
        load.start()

    pl.semaphore_wait(barrier, (NZ - 1) + (NY * NX - 1) + 2)

    def sent(refs, send_sem, recv_sem):
        remote(refs, refs, send_sem, recv_sem, other_core).wait_send()

    def arrived(refs, send_sem, recv_sem):
        remote(refs, refs, send_sem, recv_sem, other_core).wait_recv()

    others = pl.ds(0, NZ - 1)

    def on_core(number):
        return pl.when(core == number)

    def small_z(source, q, ss, rs):
        @pl.loop(1, NZ)
        def _(k):
            remote(source, q.at[x, y, z], ss, rs, at(z_peer(k), y, x)).start()

    def small_plane(source, q, ss, rs):
        @pl.loop(1, NY * NX)
        def _(k):
            p = plane_peer(k)
            remote(source, q.at[x, y, z], ss, rs, at(z, p // NX, p % NX)).start()

    def bulk_plane(q, ss, rs):
        block = q.at[x, y]

        @pl.loop(1, NY)
        def _(k):
            remote(block, block, ss, rs.at[x], at(z, y_peer(k), x)).start()

        @pl.loop(0, NY)
        def _(k):
            remote(block, block, ss, rs.at[x], at(z, y_peer(k), 1 - x)).start()

    def bulk_z(q, ss, rs, xx):
        block = q.at[xx, :, z]

        @pl.loop(1, NZ)
        def _(k):
            remote(block, block, ss, rs.at[xx], at(z_peer(k), y, x)).start()

    def plane_own_wait(q, ss, rs):
        arrived(q.at[x, pl.ds(0, NY - 1)], ss, rs.at[x])

    def plane_other_wait(q, ss, rs):
        arrived(q.at[1 - x], ss, rs.at[1 - x])

    def z_wait(q, ss, rs, xx):
        arrived(q.at[xx, :, others], ss, rs.at[xx])

    def plane_drain(q, ss, rs):
        sent(q.at[0], ss, rs.at[0])
        sent(q.at[0, pl.ds(0, NY - 1)], ss, rs.at[0])

    def z_drain(q, ss, rs):
        sent(q.at[0, :, others], ss, rs.at[0])
        sent(q.at[1, :, others], ss, rs.at[0])

    bulk_b, bulk_a = (qb, b2_s, b2_r), (qa, a2_s, a2_r)

    @on_core(0)
    def _():
        small_z(qb_in, qb, b1_s, b1_r)
        small_plane(qa_in, qa, a1_s, a1_r)

    @on_core(1)
    def _():
        small_plane(qb_in, qb, b1_s, b1_r)
        small_z(qa_in, qa, a1_s, a1_r)

    loads[0].wait()
    arrived(qb.at[x, y, others], b1_s, b1_r)

    @on_core(0)
    def _():
        bulk_plane(*bulk_b)

    @on_core(1)
    def _():
        bulk_z(*bulk_b, x)
        bulk_z(*bulk_b, 1 - x)

    loads[1].wait()
    arrived(qa.at[x, y, others], a1_s, a1_r)

    lanes = lax.broadcasted_iota(jnp.int32, (1, GROUP), 1)
    own_of = lanes % OWN
    z_of = (lanes // OWN) % NZ
    y_of = (lanes // (OWN * NZ)) % NY
    x_of = lanes // (OWN * NZ * NY)
    ks = lax.broadcasted_iota(jnp.int32, (128, GROUP), 0)
    selector = (ks == x_of * (4 * OWN) + user * OWN + own_of).astype(F32).astype(BF16)
    for load in loads[2:5]:
        load.wait()
    row_a, row_b, weight[...] = group_rows(
        (pa_v[...], pb_v[...], w_v[...]), selector, z_of * NY + y_of
    )
    pos_a[...] = row_a.astype(jnp.int32) - offset
    pos_b[...] = row_b.astype(jnp.int32) - offset

    loads[5].wait()
    for part in range(items_rows // QUARTER):
        rows = pl.ds(part * QUARTER, QUARTER)
        items_t[:, rows] = items_v[rows, :].T

    tiles = [slice(r, r + TILE) for r in range(0, items_rows, TILE)]
    ids = lax.broadcasted_iota(jnp.int32, (TILE, HALF), 0)

    def half_of(xx):
        return pl.ds(pl.multiple_of(xx * HALF, HALF), HALF)

    def fold(values, op):
        return op(values.reshape(TILE // 8, 8, HALF), axis=0)

    def scores(q, xx):
        users = q[xx].reshape(HALF, E)
        return lax.dot_general(
            items_v[...], users, (((1,), (1,)), ((), ())), preferred_element_type=F32
        )

    zero = jnp.zeros((8, HALF), F32)
    least = jnp.full((8, HALF), -jnp.inf, F32)

    def half_b(xx):
        probs[xx] = scores(qb, xx)

        top = least
        for rows in tiles:
            top = jnp.maximum(top, fold(probs[xx, rows, :], jnp.max))
        top = jnp.max(top, axis=0, keepdims=True)
        total = zero
        for rows in tiles:
            p = jnp.exp(probs[xx, rows, :] - top)
            probs[xx, rows, :] = p
            total = total + fold(p, jnp.sum)
        total = jnp.sum(total, axis=0, keepdims=True)
        tops[:, half_of(xx)] = top
        zb[z, :, half_of(xx)] = top + jnp.log(total)

    def tops_a(xx):
        score_a[...] = scores(qa, xx)
        pos = pos_a[:, half_of(xx)]
        top, hit = least, zero
        for rows in tiles:
            score = score_a[rows, :]
            top = jnp.maximum(top, fold(score, jnp.max))
            hit = hit + fold(jnp.where(ids == pos - rows.start, score, 0.0), jnp.sum)
        top_a[...] = jnp.max(top, axis=0, keepdims=True)
        za[z, 1:2, half_of(xx)] = jnp.sum(hit, axis=0, keepdims=True)

    def sums_a(xx):
        top, total = top_a[...], zero
        for rows in tiles:
            total = total + fold(jnp.exp(score_a[rows, :] - top), jnp.sum)
        total = jnp.sum(total, axis=0, keepdims=True)
        za[z, 0:1, half_of(xx)] = top + jnp.log(total)

    def z_round(buf, ss, rs):
        @pl.loop(1, NZ)
        def _(k):
            remote(buf.at[z], buf.at[z], ss, rs, at(z_peer(k), y, x)).start()

    def plane_round(buf, ss, rs):
        @pl.loop(1, NY * NX)
        def _(k):
            p = plane_peer(k)
            remote(buf.at[place], buf.at[place], ss, rs, at(z, p // NX, p % NX)).start()

    @on_core(0)
    def _():
        plane_own_wait(*bulk_b)
        bulk_z(*bulk_a, x)

    @on_core(1)
    def _():
        z_wait(*bulk_b, x)

    half_b(x)

    @on_core(0)
    def _():
        plane_other_wait(*bulk_b)

    @on_core(1)
    def _():
        z_wait(*bulk_b, 1 - x)
        bulk_plane(*bulk_a)

    half_b(1 - x)
    z_round(zb, b_zs, b_zr)
    sent(qb.at[x, y, others], b1_s, b1_r)
    sent(qa.at[x, y, others], a1_s, a1_r)

    @on_core(0)
    def _():
        bulk_z(*bulk_a, 1 - x)
        plane_drain(*bulk_b)
        z_wait(*bulk_a, x)

    @on_core(1)
    def _():
        z_drain(*bulk_b)
        plane_own_wait(*bulk_a)

    tops_a(x)
    arrived(zb.at[others], b_zs, b_zr)
    yb[place] = lse_of(zb[...])
    plane_round(yb, b_ys, b_yr)
    sums_a(x)
    sent(zb.at[others], b_zs, b_zr)

    arrived(yb.at[others], b_ys, b_yr)
    lse_b = lse_of(yb[...])
    tops[...] = weight[...] * jnp.exp(tops[...] - lse_b)

    def quarter_of(ff, cc):
        return pl.ds(pl.multiple_of((ff * 2 + cc) * QUARTER, QUARTER), QUARTER)

    def dscores(xx, ff, cc):
        cols = half_of(xx)
        start = (ff * 2 + cc) * QUARTER
        pos, scale, ratio = pos_b[:, cols] - start, weight[:, cols], tops[:, cols]
        for r in range(0, QUARTER, TILE):
            rows = pl.ds(pl.multiple_of(start + r, TILE), TILE)
            match = jnp.where(ids == pos - r, scale, 0.0)
            dsc[rows, cols] = (probs[xx, rows, :] * ratio - match).astype(BF16)

    def far_copy():
        return remote(gi_s, gi_far, far_s, far_r, other_far)

    def core_copy(n):
        return remote(gi_f.at[n, 1 - core], gi_core.at[n], gi_ss.at[n], gi_rs.at[n], other_core)

    def item_grads(n, ff, cc):
        gi_f[n, cc] = jnp.dot(
            dsc[quarter_of(ff, cc), :], qb[...].reshape(GROUP, E), preferred_element_type=F32
        )

    def query_grads(xx):
        block = jnp.dot(
            items_t[...], dsc[:, half_of(xx)], preferred_element_type=F32
        ).T.reshape(NY, NZ, OWN, E)
        gq_f[xx] = block
        gq_s[xx] = block.astype(BF16)

    def plane_send(xx, yy):
        remote(gq_s.at[xx, yy], r1.at[x, y], s1s, s1r.at[x], at(z, yy, xx)).start()

    def own_sends():
        @pl.loop(1, NY)
        def _(k):
            plane_send(x, y_peer(k))

    def other_sends():
        @pl.when(core == 0)
        def _():
            @pl.loop(0, NY)
            def _(k):
                plane_send(1 - x, y_peer(k))

        @pl.when(core == 1)
        def _():
            @pl.loop(1, NZ)
            def _(k):
                zz = z_peer(k)
                remote(gq_s.at[1 - x, :, zz], rz.at[z], zs, zr, at(zz, y, x)).start()

    for cc in (1 - core, core):
        dscores(1 - x, 1 - far, cc)
        dscores(x, 1 - far, cc)
        item_grads(0, 1 - far, cc)
        if cc is not core:
            core_copy(0).start()
    dscores(1 - x, far, 0)
    dscores(1 - x, far, 1)
    query_grads(1 - x)
    other_sends()
    core_copy(0).wait_recv()
    gi_s[...] = (gi_f[0, core] + gi_core[0]).astype(BF16)
    far_copy().start()
    dscores(x, far, 0)
    dscores(x, far, 1)
    query_grads(x)
    own_sends()

    @on_core(0)
    def _():
        z_wait(*bulk_a, 1 - x)

    @on_core(1)
    def _():
        plane_other_wait(*bulk_a)

    tops_a(1 - x)
    sums_a(1 - x)
    z_round(za, a_zs, a_zr)

    item_grads(1, far, 1 - core)
    core_copy(1).start()
    item_grads(1, far, core)

    r1[x, y] = jnp.zeros((NZ, OWN, E), BF16)
    rz[z] = jnp.zeros((NY, OWN, E), BF16)
    r2[z] = jnp.zeros((OWN, E), F32)
    arrived(r1.at[x, pl.ds(0, NY - 1)], s1s, s1r.at[x])
    gq_h[...] = gq_f[x, y] + jnp.sum(r1[x].astype(F32), axis=0)

    @pl.when(core == 0)
    def _():
        arrived(r1.at[1 - x], s1s, s1r.at[1 - x])
        gq_h[...] += jnp.sum(r1[1 - x].astype(F32), axis=0)

    @pl.loop(1, NZ)
    def _(k):
        zz = z_peer(k)
        remote(gq_h.at[zz], r2.at[z], s2s, s2r, at(zz, y, x)).start()

    @pl.when(core == 1)
    def _():
        arrived(rz.at[others], zs, zr)
        gq_p[...] = gq_f[1 - x, :, z] + jnp.sum(rz[...].astype(F32), axis=0)

        @pl.loop(0, NY)
        def _(k):
            yy = y_peer(k)
            remote(gq_p.at[yy], r3.at[y], s3s, s3r, at(z, yy, 1 - x)).start()

    arrived(za.at[others], a_zs, a_zr)
    z_parts = za[...]
    ya[place, 0:1] = lse_of(z_parts[:, 0:1])
    ya[place, 1:2] = jnp.sum(z_parts[:, 1:2], axis=0)
    plane_round(ya, a_ys, a_yr)

    core_copy(1).wait_recv()
    gi_out[...] = gi_f[1, core] + gi_core[1]

    @on_core(0)
    def _():
        z_drain(*bulk_a)

    @on_core(1)
    def _():
        plane_drain(*bulk_a)

    sent(yb.at[others], b_ys, b_yr)
    sent(za.at[others], a_zs, a_zr)
    sent(r1.at[0, pl.ds(0, NY - 1)], s1s, s1r.at[0])

    @pl.when(core == 0)
    def _():
        sent(r1.at[0], s1s, s1r.at[0])

    @pl.when(core == 1)
    def _():
        sent(rz.at[others], zs, zr)

    core_copy(0).wait_send()
    core_copy(1).wait_send()
    far_copy().wait_recv()
    gi_out[...] += gi_far[...].astype(F32)

    arrived(ya.at[others], a_ys, a_yr)
    y_parts = ya[...]
    tops[...] = lse_of(y_parts[:, 0:1]) - jnp.sum(y_parts[:, 1:2], axis=0)
    mine = tops[:, pl.ds(pl.multiple_of((x * NY + y) * NZ * OWN, NZ * OWN), NZ * OWN)]
    loss_out[...] = pltpu.roll(
        jnp.broadcast_to(mine, (8, NZ * OWN)), (NZ - z) * OWN % (NZ * OWN), 1
    )[0:1, 0:OWN]

    arrived(r2.at[others], s2s, s2r)
    gq_out[...] = gq_h[z] + jnp.sum(r2[...], axis=0)

    @pl.when(core == 1)
    def _():
        arrived(r3, s3s, s3r)
        gq_out[...] += jnp.sum(r3[...], axis=0)
        sent(r3, s3s, s3r)


    sent(ya.at[others], a_ys, a_yr)
    sent(r2.at[others], s2s, s2r)

    far_copy().wait_send()


def hand_over(*refs):
    copies = [
        pltpu.make_async_copy(source, target, refs[6].at[n])
        for n, (source, target) in enumerate(zip(refs[:3], refs[3:6]))
    ]
    for copy in copies:
        copy.start()
    for copy in copies:
        copy.wait()


def per_device(query_a, query_b, items, positive_a, positive_b, loss_cotangent):
    rows = items.shape[0]
    hbm, vmem = pl.BlockSpec(memory_space=pltpu.HBM), pl.BlockSpec(memory_space=pltpu.VMEM)
    results = (
        jax.ShapeDtypeStruct((1, OWN), F32),
        jax.ShapeDtypeStruct((OWN, E), F32),
        jax.ShapeDtypeStruct((QUARTER, E), F32),
    )
    dma = pltpu.SemaphoreType.DMA
    block = (NX, NY, NZ, OWN, E)
    loss, gq, gi = pl.pallas_call(
        kernel,
        out_shape=[pltpu.VMEM(r.shape, r.dtype) for r in results],
        in_specs=[hbm] * 6,
        out_specs=[vmem] * 3,
        scratch_shapes=[
            pltpu.VMEM((rows, E), BF16),
            pltpu.VMEM((E, rows), BF16),
            pltpu.VMEM(block, BF16),
            pltpu.VMEM(block, BF16),
            pltpu.VMEM((32, 128), jnp.int32),
            pltpu.VMEM((32, 128), jnp.int32),
            pltpu.VMEM((32, 128), F32),
            pltpu.VMEM((1, GROUP), jnp.int32),
            pltpu.VMEM((1, GROUP), jnp.int32),
            pltpu.VMEM((1, GROUP), F32),
            pltpu.VMEM((NX, rows, HALF), F32),
            pltpu.VMEM((rows, HALF), F32),
            pltpu.VMEM((rows, GROUP), BF16),
            pltpu.VMEM(block, F32),
            pltpu.VMEM(block, BF16),
            pltpu.VMEM(block, BF16),
            pltpu.VMEM((NZ, NY, OWN, E), BF16),
            pltpu.VMEM((NZ, OWN, E), F32),
            pltpu.VMEM((NY, OWN, E), F32),
            pltpu.VMEM((NZ, OWN, E), F32),
            pltpu.VMEM((NY, OWN, E), F32),
            pltpu.VMEM((2, 2, QUARTER, E), F32),
            pltpu.VMEM((QUARTER, E), BF16),
            pltpu.VMEM((2, QUARTER, E), F32),
            pltpu.VMEM((QUARTER, E), BF16),
            pltpu.VMEM((NZ, 1, GROUP), F32),
            pltpu.VMEM((NY * NX, 1, GROUP), F32),
            pltpu.VMEM((NZ, 2, GROUP), F32),
            pltpu.VMEM((NY * NX, 2, GROUP), F32),
            pltpu.VMEM((1, GROUP), F32),
            pltpu.VMEM((1, HALF), F32),
            dma((6,)),
            dma, dma,
            dma, dma((NX,)),
            dma, dma,
            dma, dma((NX,)),
            dma, dma,
            dma, dma,
            dma, dma,
            dma, dma,
            dma, dma((NX,)),
            dma, dma,
            dma, dma,
            dma, dma,
            dma((2,)), dma((2,)),
            dma, dma,
        ],
        compiler_params=pltpu.CompilerParams(
            collective_id=0, has_side_effects=True, vmem_limit_bytes=56 * 1024 * 1024
        ),
    )(
        *(
            pltpu.with_memory_space_constraint(operand, pltpu.HBM)
            for operand in (
                query_a,
                query_b,
                items,
                positive_a.reshape(32, 128),
                positive_b.reshape(32, 128),
                loss_cotangent.reshape(32, 128),
            )
        )
    )
    loss, gq, gi = pl.pallas_call(
        hand_over,
        out_shape=results,
        in_specs=[vmem] * 3,
        out_specs=[hbm] * 3,
        scratch_shapes=[dma((3,))],
        compiler_params=pltpu.CompilerParams(vmem_limit_bytes=1024 * 1024),
    )(*(pltpu.with_memory_space_constraint(result, pltpu.VMEM) for result in (loss, gq, gi)))
    return loss.reshape(OWN), gq, gi


def solution(mesh):
    return jax.shard_map(
        per_device,
        mesh=mesh,
        in_specs=(
            P(("item", "user"), None),
            P(("item", "user"), None),
            P("item", None),
            P(),
            P(),
            P(),
        ),
        out_specs=(P(("item", "user")), P(("item", "user"), None), P(("item", "user"), None)),
        check_vma=False,
    )
```

```python
import functools

import jax
import jax.numpy as jnp
from jax import lax
from jax.experimental import pallas as pl
from jax.experimental.pallas import tpu as pltpu
from jax.sharding import PartitionSpec as P

MESH = pl.DeviceIdType.MESH
F32 = jnp.float32
BF16 = jnp.bfloat16

NZ, NY, NX = 8, 4, 2
OWN = 16
E = 256
GROUP = NZ * NY * NX * OWN
HALF = GROUP // NX
TILE = 16
QUARTER = 512


def remote(src, dst, send_sem, recv_sem, device):
    return pltpu.make_async_remote_copy(
        src_ref=src,
        dst_ref=dst,
        send_sem=send_sem,
        recv_sem=recv_sem,
        device_id=device,
        device_id_type=MESH,
    )


def exact_parts(table):
    if table.dtype == jnp.int32:
        parts = (table & 63, table & (63 << 6), table & (63 << 12))
        return [part.astype(F32).astype(BF16) for part in parts]
    high = table.astype(BF16)
    rest = table - high.astype(F32)
    middle = rest.astype(BF16)
    return [high, middle, (rest - middle.astype(F32)).astype(BF16)]


def group_rows(tables, selector, row_of):
    parts = [part for table in tables for part in exact_parts(table)]
    picked = jnp.dot(jnp.concatenate(parts, axis=0), selector, preferred_element_type=F32)
    picked = picked.reshape(len(tables), 3, 32, GROUP)
    rows = lax.broadcasted_iota(jnp.int32, (32, GROUP), 0) == row_of
    return [
        jnp.sum(jnp.where(rows, (p[0] + p[1]) + p[2], 0.0), axis=0, keepdims=True) for p in picked
    ]


def lse_of(parts):
    top = jnp.max(parts, axis=0)
    return top + jnp.log(jnp.sum(jnp.exp(parts - top[None]), axis=0))


def kernel(
    qa_in, qb_in, items_in, pa_in, pb_in, w_in,
    loss_out, gq_out, gi_out,
    items_v, items_t, qa, qb, pa_v, pb_v, w_v, pos_a, pos_b, weight,
    probs, score_a, dsc, gq_f, gq_s,
    r1, rz, gq_h, gq_p, r2, r3,
    gi_f, gi_s, gi_core, gi_far,
    zb, yb, za, ya,
    tops, top_a,
    in_sem, b1_s, b1_r, b2_s, b2_r, a1_s, a1_r, a2_s, a2_r,
    b_zs, b_zr, b_ys, b_yr, a_zs, a_zr, a_ys, a_yr,
    s1s, s1r, zs, zr, s2s, s2r, s3s, s3r, gi_ss, gi_rs, far_s, far_r,
):
    item = lax.axis_index("item")
    user = lax.axis_index("user")
    z, y, x = item // (NY * NX), (item // NX) % NY, item % NX
    place = y * NX + x
    far, core = user // 2, user % 2
    items_rows = items_v.shape[0]
    offset = item * items_rows

    def at(zz, yy, xx):
        return {"item": (zz * NY + yy) * NX + xx}

    def z_peer(k):
        return lax.rem(z + k, NZ)

    def y_peer(k):
        return lax.rem(y + k, NY)

    def plane_peer(k):
        return lax.rem(place + k, NY * NX)

    loads = [
        pltpu.make_async_copy(source, target, in_sem.at[n])
        for n, (source, target) in enumerate(
            (
                (qb_in, qb.at[x, y, z]),
                (qa_in, qa.at[x, y, z]),
                (pa_in, pa_v),
                (pb_in, pb_v),
                (w_in, w_v),
                (items_in, items_v),
            )
        )
    ]

    barrier = pltpu.get_barrier_semaphore()

    @pl.loop(1, NZ)
    def _(k):
        pl.semaphore_signal(barrier, inc=1, device_id=at(z_peer(k), y, x), device_id_type=MESH)

    @pl.loop(1, NY * NX)
    def _(k):
        p = plane_peer(k)
        pl.semaphore_signal(barrier, inc=1, device_id=at(z, p // NX, p % NX), device_id_type=MESH)

    other_core = {"user": far * 2 + 1 - core}
    other_far = {"user": (1 - far) * 2 + core}
    pl.semaphore_signal(barrier, inc=1, device_id=other_core, device_id_type=MESH)
    pl.semaphore_signal(barrier, inc=1, device_id=other_far, device_id_type=MESH)

    for load in loads:
        load.start()

    pl.semaphore_wait(barrier, (NZ - 1) + (NY * NX - 1) + 2)

    def sent(refs, send_sem, recv_sem):
        remote(refs, refs, send_sem, recv_sem, other_core).wait_send()

    def arrived(refs, send_sem, recv_sem):
        remote(refs, refs, send_sem, recv_sem, other_core).wait_recv()

    others = pl.ds(0, NZ - 1)

    def on_core(number):
        return pl.when(core == number)

    def small_z(source, q, ss, rs):
        @pl.loop(1, NZ)
        def _(k):
            remote(source, q.at[x, y, z], ss, rs, at(z_peer(k), y, x)).start()

    def small_plane(source, q, ss, rs):
        @pl.loop(1, NY * NX)
        def _(k):
            p = plane_peer(k)
            remote(source, q.at[x, y, z], ss, rs, at(z, p // NX, p % NX)).start()

    def bulk_plane(q, ss, rs):
        block = q.at[x, y]

        @pl.loop(1, NY)
        def _(k):
            remote(block, block, ss, rs.at[x], at(z, y_peer(k), x)).start()

        @pl.loop(0, NY)
        def _(k):
            remote(block, block, ss, rs.at[x], at(z, y_peer(k), 1 - x)).start()

    def bulk_z(q, ss, rs, xx):
        block = q.at[xx, :, z]

        @pl.loop(1, NZ)
        def _(k):
            remote(block, block, ss, rs.at[xx], at(z_peer(k), y, x)).start()

    def plane_own_wait(q, ss, rs):
        arrived(q.at[x, pl.ds(0, NY - 1)], ss, rs.at[x])

    def plane_other_wait(q, ss, rs):
        arrived(q.at[1 - x], ss, rs.at[1 - x])

    def z_wait(q, ss, rs, xx):
        arrived(q.at[xx, :, others], ss, rs.at[xx])

    def plane_drain(q, ss, rs):
        sent(q.at[0], ss, rs.at[0])
        sent(q.at[0, pl.ds(0, NY - 1)], ss, rs.at[0])

    def z_drain(q, ss, rs):
        sent(q.at[0, :, others], ss, rs.at[0])
        sent(q.at[1, :, others], ss, rs.at[0])

    bulk_b, bulk_a = (qb, b2_s, b2_r), (qa, a2_s, a2_r)

    @on_core(0)
    def _():
        small_z(qb_in, qb, b1_s, b1_r)
        small_plane(qa_in, qa, a1_s, a1_r)

    @on_core(1)
    def _():
        small_plane(qb_in, qb, b1_s, b1_r)
        small_z(qa_in, qa, a1_s, a1_r)

    loads[0].wait()
    arrived(qb.at[x, y, others], b1_s, b1_r)

    @on_core(0)
    def _():
        bulk_plane(*bulk_b)

    @on_core(1)
    def _():
        bulk_z(*bulk_b, x)
        bulk_z(*bulk_b, 1 - x)

    loads[1].wait()
    arrived(qa.at[x, y, others], a1_s, a1_r)

    lanes = lax.broadcasted_iota(jnp.int32, (1, GROUP), 1)
    own_of = lanes % OWN
    z_of = (lanes // OWN) % NZ
    y_of = (lanes // (OWN * NZ)) % NY
    x_of = lanes // (OWN * NZ * NY)
    ks = lax.broadcasted_iota(jnp.int32, (128, GROUP), 0)
    selector = (ks == x_of * (4 * OWN) + user * OWN + own_of).astype(F32).astype(BF16)
    for load in loads[2:5]:
        load.wait()
    row_a, row_b, weight[...] = group_rows(
        (pa_v[...], pb_v[...], w_v[...]), selector, z_of * NY + y_of
    )
    pos_a[...] = row_a.astype(jnp.int32) - offset
    pos_b[...] = row_b.astype(jnp.int32) - offset

    loads[5].wait()
    for part in range(items_rows // QUARTER):
        rows = pl.ds(part * QUARTER, QUARTER)
        items_t[:, rows] = items_v[rows, :].T

    tiles = [slice(r, r + TILE) for r in range(0, items_rows, TILE)]
    ids = lax.broadcasted_iota(jnp.int32, (TILE, HALF), 0)

    def half_of(xx):
        return pl.ds(pl.multiple_of(xx * HALF, HALF), HALF)

    def fold(values, op):
        return op(values.reshape(TILE // 8, 8, HALF), axis=0)

    def scores(q, xx):
        users = q[xx].reshape(HALF, E)
        return lax.dot_general(
            items_v[...], users, (((1,), (1,)), ((), ())), preferred_element_type=F32
        )

    zero = jnp.zeros((8, HALF), F32)
    least = jnp.full((8, HALF), -jnp.inf, F32)

    def half_b(xx):
        probs[xx] = scores(qb, xx)

        top = least
        for rows in tiles:
            top = jnp.maximum(top, fold(probs[xx, rows, :], jnp.max))
        top = jnp.max(top, axis=0, keepdims=True)
        total = zero
        for rows in tiles:
            p = jnp.exp(probs[xx, rows, :] - top)
            probs[xx, rows, :] = p
            total = total + fold(p, jnp.sum)
        total = jnp.sum(total, axis=0, keepdims=True)
        tops[:, half_of(xx)] = top
        zb[z, :, half_of(xx)] = top + jnp.log(total)

    def tops_a(xx):
        score_a[...] = scores(qa, xx)
        pos = pos_a[:, half_of(xx)]
        top, hit = least, zero
        for rows in tiles:
            score = score_a[rows, :]
            top = jnp.maximum(top, fold(score, jnp.max))
            hit = hit + fold(jnp.where(ids == pos - rows.start, score, 0.0), jnp.sum)
        top_a[...] = jnp.max(top, axis=0, keepdims=True)
        za[z, 1:2, half_of(xx)] = jnp.sum(hit, axis=0, keepdims=True)

    def sums_a(xx):
        top, total = top_a[...], zero
        for rows in tiles:
            total = total + fold(jnp.exp(score_a[rows, :] - top), jnp.sum)
        total = jnp.sum(total, axis=0, keepdims=True)
        za[z, 0:1, half_of(xx)] = top + jnp.log(total)

    def z_round(buf, ss, rs):
        @pl.loop(1, NZ)
        def _(k):
            remote(buf.at[z], buf.at[z], ss, rs, at(z_peer(k), y, x)).start()

    def plane_round(buf, ss, rs):
        @pl.loop(1, NY * NX)
        def _(k):
            p = plane_peer(k)
            remote(buf.at[place], buf.at[place], ss, rs, at(z, p // NX, p % NX)).start()

    @on_core(0)
    def _():
        plane_own_wait(*bulk_b)
        bulk_z(*bulk_a, x)

    @on_core(1)
    def _():
        z_wait(*bulk_b, x)

    half_b(x)

    @on_core(0)
    def _():
        plane_other_wait(*bulk_b)

    @on_core(1)
    def _():
        z_wait(*bulk_b, 1 - x)
        bulk_plane(*bulk_a)

    half_b(1 - x)
    z_round(zb, b_zs, b_zr)
    sent(qb.at[x, y, others], b1_s, b1_r)
    sent(qa.at[x, y, others], a1_s, a1_r)

    @on_core(0)
    def _():
        bulk_z(*bulk_a, 1 - x)
        plane_drain(*bulk_b)
        z_wait(*bulk_a, x)

    @on_core(1)
    def _():
        z_drain(*bulk_b)
        plane_own_wait(*bulk_a)

    tops_a(x)
    arrived(zb.at[others], b_zs, b_zr)
    yb[place] = lse_of(zb[...])
    plane_round(yb, b_ys, b_yr)
    sums_a(x)
    sent(zb.at[others], b_zs, b_zr)

    arrived(yb.at[others], b_ys, b_yr)
    lse_b = lse_of(yb[...])
    tops[...] = weight[...] * jnp.exp(tops[...] - lse_b)

    def quarter_of(ff, cc):
        return pl.ds(pl.multiple_of((ff * 2 + cc) * QUARTER, QUARTER), QUARTER)

    def dscores(xx, ff, cc):
        cols = half_of(xx)
        start = (ff * 2 + cc) * QUARTER
        pos, scale, ratio = pos_b[:, cols] - start, weight[:, cols], tops[:, cols]
        for r in range(0, QUARTER, TILE):
            rows = pl.ds(pl.multiple_of(start + r, TILE), TILE)
            match = jnp.where(ids == pos - r, scale, 0.0)
            dsc[rows, cols] = (probs[xx, rows, :] * ratio - match).astype(BF16)

    def far_copy():
        return remote(gi_s, gi_far, far_s, far_r, other_far)

    def core_copy(n):
        return remote(gi_f.at[n, 1 - core], gi_core.at[n], gi_ss.at[n], gi_rs.at[n], other_core)

    def item_grads(n, ff, cc):
        gi_f[n, cc] = jnp.dot(
            dsc[quarter_of(ff, cc), :], qb[...].reshape(GROUP, E), preferred_element_type=F32
        )

    def query_grads(xx):
        block = jnp.dot(
            items_t[...], dsc[:, half_of(xx)], preferred_element_type=F32
        ).T.reshape(NY, NZ, OWN, E)
        gq_f[xx] = block
        gq_s[xx] = block.astype(BF16)

    def plane_send(xx, yy):
        remote(gq_s.at[xx, yy], r1.at[x, y], s1s, s1r.at[x], at(z, yy, xx)).start()

    def own_sends():
        @pl.loop(1, NY)
        def _(k):
            plane_send(x, y_peer(k))

    def other_sends():
        @pl.when(core == 0)
        def _():
            @pl.loop(0, NY)
            def _(k):
                plane_send(1 - x, y_peer(k))

        @pl.when(core == 1)
        def _():
            @pl.loop(1, NZ)
            def _(k):
                zz = z_peer(k)
                remote(gq_s.at[1 - x, :, zz], rz.at[z], zs, zr, at(zz, y, x)).start()

    for cc in (1 - core, core):
        dscores(1 - x, 1 - far, cc)
        dscores(x, 1 - far, cc)
        item_grads(0, 1 - far, cc)
        if cc is not core:
            core_copy(0).start()
    dscores(1 - x, far, 0)
    dscores(1 - x, far, 1)
    query_grads(1 - x)
    other_sends()
    core_copy(0).wait_recv()
    gi_s[...] = (gi_f[0, core] + gi_core[0]).astype(BF16)
    far_copy().start()
    dscores(x, far, 0)
    dscores(x, far, 1)
    query_grads(x)
    own_sends()

    @on_core(0)
    def _():
        z_wait(*bulk_a, 1 - x)

    @on_core(1)
    def _():
        plane_other_wait(*bulk_a)

    tops_a(1 - x)
    sums_a(1 - x)
    z_round(za, a_zs, a_zr)

    item_grads(1, far, 1 - core)
    core_copy(1).start()
    item_grads(1, far, core)

    r1[x, y] = jnp.zeros((NZ, OWN, E), BF16)
    rz[z] = jnp.zeros((NY, OWN, E), BF16)
    r2[z] = jnp.zeros((OWN, E), F32)
    arrived(r1.at[x, pl.ds(0, NY - 1)], s1s, s1r.at[x])
    gq_h[...] = gq_f[x, y] + jnp.sum(r1[x].astype(F32), axis=0)

    @pl.when(core == 0)
    def _():
        arrived(r1.at[1 - x], s1s, s1r.at[1 - x])
        gq_h[...] += jnp.sum(r1[1 - x].astype(F32), axis=0)

    @pl.loop(1, NZ)
    def _(k):
        zz = z_peer(k)
        remote(gq_h.at[zz], r2.at[z], s2s, s2r, at(zz, y, x)).start()

    @pl.when(core == 1)
    def _():
        arrived(rz.at[others], zs, zr)
        gq_p[...] = gq_f[1 - x, :, z] + jnp.sum(rz[...].astype(F32), axis=0)

        @pl.loop(0, NY)
        def _(k):
            yy = y_peer(k)
            remote(gq_p.at[yy], r3.at[y], s3s, s3r, at(z, yy, 1 - x)).start()

    arrived(za.at[others], a_zs, a_zr)
    z_parts = za[...]
    ya[place, 0:1] = lse_of(z_parts[:, 0:1])
    ya[place, 1:2] = jnp.sum(z_parts[:, 1:2], axis=0)
    plane_round(ya, a_ys, a_yr)

    core_copy(1).wait_recv()
    gi_out[...] = gi_f[1, core] + gi_core[1]

    @on_core(0)
    def _():
        z_drain(*bulk_a)

    @on_core(1)
    def _():
        plane_drain(*bulk_a)

    sent(yb.at[others], b_ys, b_yr)
    sent(za.at[others], a_zs, a_zr)
    sent(r1.at[0, pl.ds(0, NY - 1)], s1s, s1r.at[0])

    @pl.when(core == 0)
    def _():
        sent(r1.at[0], s1s, s1r.at[0])

    @pl.when(core == 1)
    def _():
        sent(rz.at[others], zs, zr)

    core_copy(0).wait_send()
    core_copy(1).wait_send()
    far_copy().wait_recv()
    gi_out[...] += gi_far[...].astype(F32)

    arrived(ya.at[others], a_ys, a_yr)
    y_parts = ya[...]
    tops[...] = lse_of(y_parts[:, 0:1]) - jnp.sum(y_parts[:, 1:2], axis=0)
    mine = tops[:, pl.ds(pl.multiple_of((x * NY + y) * NZ * OWN, NZ * OWN), NZ * OWN)]
    loss_out[...] = pltpu.roll(
        jnp.broadcast_to(mine, (8, NZ * OWN)), (NZ - z) * OWN % (NZ * OWN), 1
    )[0:1, 0:OWN]

    arrived(r2.at[others], s2s, s2r)
    gq_out[...] = gq_h[z] + jnp.sum(r2[...], axis=0)

    @pl.when(core == 1)
    def _():
        arrived(r3, s3s, s3r)
        gq_out[...] += jnp.sum(r3[...], axis=0)
        sent(r3, s3s, s3r)


    sent(ya.at[others], a_ys, a_yr)
    sent(r2.at[others], s2s, s2r)

    far_copy().wait_send()


def hand_over(*refs):
    copies = [
        pltpu.make_async_copy(source, target, refs[6].at[n])
        for n, (source, target) in enumerate(zip(refs[:3], refs[3:6]))
    ]
    for copy in copies:
        copy.start()
    for copy in copies:
        copy.wait()


def per_device(query_a, query_b, items, positive_a, positive_b, loss_cotangent):
    rows = items.shape[0]
    hbm, vmem = pl.BlockSpec(memory_space=pltpu.HBM), pl.BlockSpec(memory_space=pltpu.VMEM)
    results = (
        jax.ShapeDtypeStruct((1, OWN), F32),
        jax.ShapeDtypeStruct((OWN, E), F32),
        jax.ShapeDtypeStruct((QUARTER, E), F32),
    )
    dma = pltpu.SemaphoreType.DMA
    block = (NX, NY, NZ, OWN, E)
    loss, gq, gi = pl.pallas_call(
        kernel,
        out_shape=[pltpu.VMEM(r.shape, r.dtype) for r in results],
        in_specs=[hbm] * 6,
        out_specs=[vmem] * 3,
        scratch_shapes=[
            pltpu.VMEM((rows, E), BF16),
            pltpu.VMEM((E, rows), BF16),
            pltpu.VMEM(block, BF16),
            pltpu.VMEM(block, BF16),
            pltpu.VMEM((32, 128), jnp.int32),
            pltpu.VMEM((32, 128), jnp.int32),
            pltpu.VMEM((32, 128), F32),
            pltpu.VMEM((1, GROUP), jnp.int32),
            pltpu.VMEM((1, GROUP), jnp.int32),
            pltpu.VMEM((1, GROUP), F32),
            pltpu.VMEM((NX, rows, HALF), F32),
            pltpu.VMEM((rows, HALF), F32),
            pltpu.VMEM((rows, GROUP), BF16),
            pltpu.VMEM(block, F32),
            pltpu.VMEM(block, BF16),
            pltpu.VMEM(block, BF16),
            pltpu.VMEM((NZ, NY, OWN, E), BF16),
            pltpu.VMEM((NZ, OWN, E), F32),
            pltpu.VMEM((NY, OWN, E), F32),
            pltpu.VMEM((NZ, OWN, E), F32),
            pltpu.VMEM((NY, OWN, E), F32),
            pltpu.VMEM((2, 2, QUARTER, E), F32),
            pltpu.VMEM((QUARTER, E), BF16),
            pltpu.VMEM((2, QUARTER, E), F32),
            pltpu.VMEM((QUARTER, E), BF16),
            pltpu.VMEM((NZ, 1, GROUP), F32),
            pltpu.VMEM((NY * NX, 1, GROUP), F32),
            pltpu.VMEM((NZ, 2, GROUP), F32),
            pltpu.VMEM((NY * NX, 2, GROUP), F32),
            pltpu.VMEM((1, GROUP), F32),
            pltpu.VMEM((1, HALF), F32),
            dma((6,)),
            dma, dma,
            dma, dma((NX,)),
            dma, dma,
            dma, dma((NX,)),
            dma, dma,
            dma, dma,
            dma, dma,
            dma, dma,
            dma, dma((NX,)),
            dma, dma,
            dma, dma,
            dma, dma,
            dma((2,)), dma((2,)),
            dma, dma,
        ],
        compiler_params=pltpu.CompilerParams(
            collective_id=0, has_side_effects=True, vmem_limit_bytes=56 * 1024 * 1024
        ),
    )(
        *(
            pltpu.with_memory_space_constraint(operand, pltpu.HBM)
            for operand in (
                query_a,
                query_b,
                items,
                positive_a.reshape(32, 128),
                positive_b.reshape(32, 128),
                loss_cotangent.reshape(32, 128),
            )
        )
    )
    loss, gq, gi = pl.pallas_call(
        hand_over,
        out_shape=results,
        in_specs=[vmem] * 3,
        out_specs=[hbm] * 3,
        scratch_shapes=[dma((3,))],
        compiler_params=pltpu.CompilerParams(vmem_limit_bytes=1024 * 1024),
    )(*(pltpu.with_memory_space_constraint(result, pltpu.VMEM) for result in (loss, gq, gi)))
    return loss.reshape(OWN), gq, gi


def solution(mesh):
    return jax.shard_map(
        per_device,
        mesh=mesh,
        in_specs=(
            P(("item", "user"), None),
            P(("item", "user"), None),
            P("item", None),
            P(),
            P(),
            P(),
        ),
        out_specs=(P(("item", "user")), P(("item", "user"), None), P(("item", "user"), None)),
        check_vma=False,
    )
```
